32 devices in a mesh: fsdp: 8 (over y, x, core), blk: 4 (over z).
Axes of the slice: x: 2, y: 2, z: 4, core: 2. Of those that a mesh axis runs over, the one named last changes fastest.
Arguments:
- block_input: bfloat16 [32, 256, 2048], P('fsdp', 'blk'), may hold values from -6 to 6
- cotangent: bfloat16 [32, 256, 2048], P('fsdp', 'blk'), may hold values from -6 to 6
- bin_ids: int32 [32], P('fsdp'), may hold values from 0 to 63
- image_counts: int32 [8], P('fsdp'), may hold values from 1 to 4, as said below
- attn_weight: float32 [2048, 8192], P('fsdp')
- mlp_weight: float32 [2048, 16384], P('fsdp')
- noise_table: float32 [64, 2048], P(None, 'fsdp'), may hold values from -6 to 6
- mod_weight: float32 [2048, 12288], P('fsdp'), may hold values from -0.125 to 0.125
- mod_bias: float32 [12288], P('fsdp'), may hold values from -3 to 3
Outputs:
- block_out: bfloat16 [32, 256, 2048], P('fsdp', 'blk')
- input_grad: float32 [32, 256, 2048], P('fsdp', 'blk')
- attn_weight_grad: float32 [2048, 8192], P('fsdp')
- mlp_weight_grad: float32 [2048, 16384], P('fsdp')
- noise_grad: float32 [64, 2048], P(None, 'fsdp')
- mod_weight_grad: float32 [2048, 12288], P('fsdp')
- mod_bias_grad: float32 [12288], P('fsdp')
The draws below stay inside these ranges and needn't reach their ends.
Inputs may be any that keep to these rules, and one draw needn't show every extreme that they name: `image_counts`: slots at and beyond the count hold no image; some index of fsdp holds all 4.
All inputs are finite; a program needn't handle non-finite values.
Results may differ from the reference program's by a relative error of at most 0.017.
Values may be sent and summed in bfloat16 or wider, within the bound.
A program may use at most 576 MiB of HBM per device.

```python
import math
import jax
import jax.numpy as jnp
from jax import lax

D = 2048
HEADS = 16
HD = 128
FF = 8192
TOKI = 256
SLOTS = 4
BINS = 64
GROUPS = 8
IMAGES = 32


def draw_attn_weight(key, part):
    key = jax.random.fold_in(key, 11)
    normal = jax.random.normal(key, (D, 4 * D), jnp.float32)
    column = jnp.arange(4 * D)
    factor = jnp.where(column < 3 * D, 1.0, 8.0) * D ** (-0.5)
    return normal * factor[None, :]


def draw_mlp_weight(key, part):
    key = jax.random.fold_in(key, 12)
    normal = jax.random.normal(key, (D, 2 * FF), jnp.float32)
    column = jnp.arange(2 * FF)
    factor = jnp.where(column < FF, D ** (-0.5), FF ** (-0.5))
    return normal * factor[None, :]


def draw_image_counts(key, part):
    key = jax.random.fold_in(key, 13)
    first_key, second_key = jax.random.split(key)
    counts = jax.random.randint(first_key, (GROUPS,), 1, SLOTS + 1)
    fullest = jax.random.randint(second_key, (), 0, GROUPS)
    return jnp.where(jnp.arange(GROUPS) == fullest, SLOTS, counts).astype(jnp.int32)


def place_ends(array, own_key, smallest, top_value):
    extent = array.shape
    index_at = [jax.random.randint(jax.random.fold_in(own_key, axis), (), 0, extent[axis]) for axis in range(len(extent))]
    array = array.at[tuple(index_at)].set(smallest)
    longest = extent.index(max(extent))
    index_at[longest] = (index_at[longest] + 1) % extent[longest]
    return array.at[tuple(index_at)].set(top_value)


def steps_of(key, shape, cuts, least, high):
    factor_of, own = 1.0, jax.random.fold_in(key, 6)
    for position, parts in cuts:
        steps = jnp.exp(jax.random.uniform(jax.random.fold_in(own, position), (parts,), jnp.float32, least / len(cuts), high / len(cuts)))
        factor_of = factor_of * jnp.repeat(steps, shape[position] // parts).reshape([-1 if axis == position else 1 for axis in range(len(shape))])
    return factor_of


def normal_values(own_key, dims, scale, reach, cuts=(), held_as=jnp.bfloat16):
    array = scale * jax.random.normal(own_key, dims, jnp.float32)
    if cuts:
        array = array * steps_of(own_key, dims, cuts, -0.22, 0.18)
    return jnp.clip(array, -reach, reach).astype(held_as)


def setup_inputs(seed: int = 0) -> dict:
    splits = jax.random.split(jax.random.key(seed), 10)
    block_input = normal_values(splits[0], (IMAGES, TOKI, D), 1.0, 6.0, ((0, 8), (1, 4)))
    cotangent = normal_values(splits[1], (IMAGES, TOKI, D), 1.0, 6.0, ((0, 8), (1, 4)))
    bin_ids = place_ends(jax.random.randint(splits[2], (IMAGES,), 0, BINS), jax.random.fold_in(splits[2], 1), 0, BINS - 1).astype(jnp.int32)
    image_counts = draw_image_counts(jax.random.fold_in(splits[9], 71), 0)
    attn_weight = draw_attn_weight(jax.random.fold_in(splits[9], 71), 0)
    mlp_weight = draw_mlp_weight(jax.random.fold_in(splits[9], 71), 0)
    noise_table = normal_values(splits[6], (BINS, D), 1.0, 6.0, ((1, 8),), jnp.float32)
    mod_weight = normal_values(splits[7], (D, 6 * D), D ** -0.5, 0.125, ((0, 8),), jnp.float32)
    mod_bias = normal_values(splits[8], (6 * D,), 0.5, 3.0, ((0, 8),), jnp.float32)
    return {"block_input": block_input, "cotangent": cotangent, "bin_ids": bin_ids, "image_counts": image_counts, "attn_weight": attn_weight, "mlp_weight": mlp_weight, "noise_table": noise_table, "mod_weight": mod_weight, "mod_bias": mod_bias}


EPSILON = 1e-06
PRECISE = lax.Precision.HIGHEST

@jax.custom_vjp
def low(v):
    return lax.optimization_barrier(v.astype(jnp.bfloat16)).astype(jnp.float32)

@jax.custom_vjp
def low_back(v):
    return v

def low_keep(v):
    return (low(v), None)

def low_pass(kept, grad):
    return (grad,)

def back_keep(v):
    return (v, None)

def back_low(kept, grad):
    return (low(grad),)
low.defvjp(low_keep, low_pass)
low_back.defvjp(back_keep, back_low)

def norm_mod(features, scaling, shifting):
    normed = features * lax.rsqrt(lax.optimization_barrier(jnp.mean(features * features, axis=-1, keepdims=True)) + EPSILON)
    return normed * (1.0 + scaling) + shifting

def group_block(group_input, group_mod, group_live, attn_bf, mlp_bf):
    images = group_input.shape[0]
    shift_one, scale_one, gate_one, shift_two, scale_two, gate_two = [member[:, None, :] for member in jnp.split(group_mod, 6, axis=-1)]
    h_one = low(norm_mod(group_input, scale_one, shift_one))
    projected = low_back(low(jnp.einsum('gtd,de->gte', h_one, attn_bf[:, :3 * D], precision=PRECISE)))
    queries = projected[..., :D].reshape(images, TOKI, HEADS, HD)
    key_rows = projected[..., D:2 * D].reshape(images, TOKI, HEADS, HD)
    value_rows = projected[..., 2 * D:].reshape(images, TOKI, HEADS, HD)
    scores = low_back(jnp.einsum('gqhd,gkhd->ghqk', queries, key_rows, precision=PRECISE) * HD ** (-0.5))
    exponent = jnp.exp(scores - lax.optimization_barrier(jnp.max(scores, axis=-1, keepdims=True)))
    attention = exponent / lax.optimization_barrier(jnp.sum(exponent, axis=-1, keepdims=True))
    attended = low_back(low(jnp.einsum('ghqk,gkhd->gqhd', low(attention), value_rows, precision=PRECISE))).reshape(images, TOKI, D)
    attn_out = low_back(jnp.einsum('gte,ed->gtd', attended, attn_bf[:, 3 * D:], precision=PRECISE))
    first_sum = group_input + gate_one * attn_out
    h_two = low(norm_mod(first_sum, scale_two, shift_two))
    pre_gelu = low_back(jnp.einsum('gtd,df->gtf', h_two, mlp_bf[:, :FF], precision=PRECISE))
    hidden = low(jax.nn.gelu(pre_gelu))
    mlp_out = low_back(jnp.einsum('gtf,df->gtd', hidden, mlp_bf[:, FF:], precision=PRECISE))
    second_sum = first_sum + gate_two * mlp_out
    return group_live[:, None, None] * second_sum

def reference(block_input, cotangent, bin_ids, image_counts, attn_weight, mlp_weight, noise_table, mod_weight, mod_bias):
    image_index = jnp.arange(IMAGES, dtype=jnp.int32)
    live_mask = (image_index % SLOTS < jnp.take(image_counts, image_index // SLOTS)).astype(jnp.float32)
    onehot = (bin_ids[:, None] == jnp.arange(BINS, dtype=jnp.int32)[None, :]).astype(jnp.float32)
    per_group = math.gcd(IMAGES, 16)
    groups = IMAGES // per_group

    def forward(inputs, attn_w, mlp_w, emb_table, weight, bias_vec):
        mod_table = jnp.dot(jax.nn.silu(emb_table), weight, precision=PRECISE) + bias_vec
        mod_image = jnp.dot(onehot, mod_table, precision=PRECISE)
        attn_bf = low(attn_w)
        mlp_bf = low(mlp_w)
        checked = jax.checkpoint(group_block)

        def group_step(running, sliced):
            return (running, checked(sliced[0], sliced[1], sliced[2], attn_bf, mlp_bf))
        running, stacked = lax.scan(group_step, jnp.zeros((), jnp.float32), (inputs.reshape(groups, per_group, TOKI, D), mod_image.reshape(groups, per_group, 6 * D), live_mask.reshape(groups, per_group)))
        return stacked.reshape(IMAGES, TOKI, D)
    result, pullback = jax.vjp(forward, block_input.astype(jnp.float32), attn_weight, mlp_weight, noise_table, mod_weight, mod_bias)
    gradients = pullback(cotangent.astype(jnp.float32))
    return (result.astype(jnp.bfloat16), gradients[0], gradients[1], gradients[2], gradients[3], gradients[4], gradients[5])
```

```python
import functools
import math

import jax
import jax.numpy as jnp
from jax import lax
from jax.experimental import pallas as pl
from jax.experimental.pallas import tpu as pltpu
from jax.sharding import PartitionSpec as P

HD = 128


EPSILON = 1e-06
PRECISE = lax.Precision.HIGHEST


def norm_mod(features, scaling, shifting):
    normed = features * lax.rsqrt(jnp.mean(features * features, axis=-1, keepdims=True) + EPSILON)
    return normed * (1.0 + scaling) + shifting


def rows_product(left_rows, right_rows):
    return lax.dot_general(
        left_rows, right_rows, (((0,), (0,)), ((), ())), preferred_element_type=jnp.float32
    )


def body(
    block_input,
    cotangent,
    bin_ids,
    image_counts,
    attn_weight,
    mlp_weight,
    noise_table,
    mod_weight,
    mod_bias,
):
    slot_count, local_tok, model_width = block_input.shape
    row_count = slot_count * local_tok
    feed_width = mlp_weight.shape[1] // 2
    head_count = model_width // HD
    blk_size = lax.axis_size("blk")
    image_tok = local_tok * blk_size
    score_scale = HD ** (-0.5)
    bias_piece = mod_bias.shape[0]
    activated = jax.nn.silu(noise_table)
    partial_mod = jnp.dot(activated, mod_weight, precision=PRECISE)
    bias_full = lax.dynamic_update_slice_in_dim(
        jnp.zeros((6 * model_width,), jnp.float32), mod_bias, lax.axis_index("fsdp") * bias_piece, 0
    )
    mod_table = lax.psum(partial_mod + bias_full[None, :], "fsdp")
    onehot = (
        bin_ids[:, None] == jnp.arange(noise_table.shape[0], dtype=jnp.int32)[None, :]
    ).astype(jnp.float32)
    mod_image = jnp.dot(onehot, mod_table, precision=PRECISE)
    shift_one, scale_one, gate_one, shift_two, scale_two, gate_two = [
        member[:, None, :] for member in jnp.split(mod_image, 6, axis=-1)
    ]
    live_mask = (jnp.arange(slot_count) < image_counts[0]).astype(jnp.float32)[:, None, None]
    features = block_input.astype(jnp.float32)
    h_one = (
        norm_mod(features, scale_one, shift_one)
        .astype(jnp.bfloat16)
        .reshape(row_count, model_width)
    )
    attn_full = lax.all_gather(attn_weight.astype(jnp.bfloat16), "fsdp", axis=0, tiled=True)
    projected = jnp.dot(
        h_one, attn_full[:, : 3 * model_width], preferred_element_type=jnp.float32
    ).astype(jnp.bfloat16)
    queries = projected[:, :model_width].reshape(slot_count, local_tok, head_count, HD)
    key_rows = projected[:, model_width : 2 * model_width].reshape(
        slot_count, local_tok, model_width
    )
    value_rows = projected[:, 2 * model_width :].reshape(slot_count, local_tok, model_width)
    all_keys, all_values = (
        lax.all_gather(key_rows, "blk", axis=1, tiled=True),
        lax.all_gather(value_rows, "blk", axis=1, tiled=True),
    )
    all_keys = all_keys.reshape(slot_count, image_tok, head_count, HD)
    all_values = all_values.reshape(slot_count, image_tok, head_count, HD)

    def scores_of(query_rows):
        return (
            jnp.einsum("sqhd,skhd->shqk", query_rows, all_keys, preferred_element_type=jnp.float32)
            * score_scale
        )

    scores = scores_of(queries)
    maximum = jnp.max(scores, axis=-1, keepdims=True)
    exponent = jnp.exp(scores - maximum)
    denominator = jnp.sum(exponent, axis=-1, keepdims=True)
    attention = exponent / denominator
    log_total = maximum + jnp.log(denominator)
    attended = (
        jnp.einsum(
            "shqk,skhd->sqhd",
            attention.astype(jnp.bfloat16),
            all_values,
            preferred_element_type=jnp.float32,
        )
        .astype(jnp.bfloat16)
        .reshape(row_count, model_width)
    )
    attn_out = jnp.dot(
        attended, attn_full[:, 3 * model_width :], preferred_element_type=jnp.float32
    ).reshape(slot_count, local_tok, model_width)
    first_sum = features + gate_one * attn_out
    h_two = (
        norm_mod(first_sum, scale_two, shift_two)
        .astype(jnp.bfloat16)
        .reshape(row_count, model_width)
    )
    mlp_full = lax.all_gather(mlp_weight.astype(jnp.bfloat16), "fsdp", axis=0, tiled=True)
    pre_gelu = jnp.dot(h_two, mlp_full[:, :feed_width], preferred_element_type=jnp.float32)
    hidden = jax.nn.gelu(pre_gelu).astype(jnp.bfloat16)
    mlp_out = jnp.einsum(
        "rf,df->rd", hidden, mlp_full[:, feed_width:], preferred_element_type=jnp.float32
    ).reshape(slot_count, local_tok, model_width)
    second_sum = first_sum + gate_two * mlp_out
    block_out = (live_mask * second_sum).astype(jnp.bfloat16)
    grad_out = cotangent.astype(jnp.float32) * live_mask
    grad_mlp = (gate_two * grad_out).astype(jnp.bfloat16).reshape(row_count, model_width)
    grad_gate_two = jnp.sum(grad_out * mlp_out, axis=1)
    grad_hidden = jnp.dot(grad_mlp, mlp_full[:, feed_width:], preferred_element_type=jnp.float32)
    grad_pre = jax.vjp(jax.nn.gelu, pre_gelu)[1](grad_hidden)[0].astype(jnp.bfloat16)
    grad_h_two = jnp.einsum(
        "rf,df->rd", grad_pre, mlp_full[:, :feed_width], preferred_element_type=jnp.float32
    ).reshape(slot_count, local_tok, model_width)
    grad_first, grad_scale_two, grad_shift_two = jax.vjp(norm_mod, first_sum, scale_two, shift_two)[
        1
    ](grad_h_two)
    grad_first = grad_first + grad_out
    grad_attn_out = (gate_one * grad_first).astype(jnp.bfloat16).reshape(row_count, model_width)
    grad_gate_one = jnp.sum(grad_first * attn_out, axis=1)
    grad_attended = jnp.einsum(
        "rd,ed->re",
        grad_attn_out,
        attn_full[:, 3 * model_width :],
        preferred_element_type=jnp.float32,
    ).astype(jnp.bfloat16)
    grad_heads = grad_attended.reshape(slot_count, local_tok, head_count, HD)
    recomputed = jnp.exp(scores_of(queries) - log_total)
    grad_weights = jnp.einsum(
        "sqhd,skhd->shqk", grad_heads, all_values, preferred_element_type=jnp.float32
    )
    row_delta = jnp.sum(recomputed * grad_weights, axis=-1, keepdims=True)
    grad_scores = (recomputed * (grad_weights - row_delta)).astype(jnp.bfloat16)
    grad_queries = (
        jnp.einsum("shqk,skhd->sqhd", grad_scores, all_keys, preferred_element_type=jnp.float32)
        * score_scale
    )
    grad_keys_all = (
        jnp.einsum("shqk,sqhd->skhd", grad_scores, queries, preferred_element_type=jnp.float32)
        * score_scale
    )
    grad_values_all = jnp.einsum(
        "shqk,sqhd->skhd",
        recomputed.astype(jnp.bfloat16),
        grad_heads,
        preferred_element_type=jnp.float32,
    )
    grad_keys, grad_values = (
        lax.psum_scatter(
            grad_keys_all.reshape(slot_count, image_tok, model_width).astype(jnp.bfloat16),
            "blk",
            scatter_dimension=1,
            tiled=True,
        ).astype(jnp.float32),
        lax.psum_scatter(
            grad_values_all.reshape(slot_count, image_tok, model_width).astype(jnp.bfloat16),
            "blk",
            scatter_dimension=1,
            tiled=True,
        ).astype(jnp.float32),
    )
    grad_qkv = jnp.concatenate(
        [
            grad_queries.reshape(row_count, model_width).astype(jnp.bfloat16),
            grad_keys.reshape(row_count, model_width).astype(jnp.bfloat16),
            grad_values.reshape(row_count, model_width).astype(jnp.bfloat16),
        ],
        axis=1,
    )
    grad_h_one = jnp.einsum(
        "rc,dc->rd", grad_qkv, attn_full[:, : 3 * model_width], preferred_element_type=jnp.float32
    ).reshape(slot_count, local_tok, model_width)
    grad_input, grad_scale_one, grad_shift_one = jax.vjp(norm_mod, features, scale_one, shift_one)[
        1
    ](grad_h_one)
    input_grad = grad_input + grad_first
    grad_mod = jnp.concatenate(
        [
            grad_shift_one[:, 0, :],
            grad_scale_one[:, 0, :],
            grad_gate_one,
            grad_shift_two[:, 0, :],
            grad_scale_two[:, 0, :],
            grad_gate_two,
        ],
        axis=-1,
    )
    bin_terms = lax.dot_general(onehot, grad_mod, (((0,), (0,)), ((), ())), precision=PRECISE)
    grad_bins = lax.psum(bin_terms, ("fsdp", "blk"))
    table_term = jnp.einsum("be,de->bd", grad_bins, mod_weight, precision=PRECISE)
    noise_grad = jax.vjp(jax.nn.silu, noise_table)[1](table_term)[0]
    mod_weight_grad = lax.dot_general(
        activated, grad_bins, (((0,), (0,)), ((), ())), precision=PRECISE
    )
    mod_bias_grad = lax.dynamic_slice_in_dim(
        jnp.sum(grad_bins, axis=0), lax.axis_index("fsdp") * bias_piece, bias_piece
    )
    h_part = h_one
    attn_part = lax.psum_scatter(
        jnp.concatenate(
            [rows_product(h_part, grad_qkv), rows_product(attended, grad_attn_out)], axis=1
        ).astype(jnp.bfloat16),
        "fsdp",
        scatter_dimension=0,
        tiled=True,
    )
    h_part = h_two
    mlp_part = lax.psum_scatter(
        jnp.concatenate(
            [rows_product(h_part, grad_pre), rows_product(grad_mlp, hidden)], axis=1
        ).astype(jnp.bfloat16),
        "fsdp",
        scatter_dimension=0,
        tiled=True,
    )
    attn_weight_grad, mlp_weight_grad = (
        lax.psum(attn_part, "blk").astype(jnp.float32),
        lax.psum(mlp_part, "blk").astype(jnp.float32),
    )
    return (
        block_out,
        input_grad,
        attn_weight_grad,
        mlp_weight_grad,
        noise_grad,
        mod_weight_grad,
        mod_bias_grad,
    )


MESH_ID = pl.DeviceIdType.MESH
VMEM_BYTES = 56 * 1024 * 1024


def contract(left, right, left_dim, right_dim):
    return lax.dot_general(
        left, right, (((left_dim,), (right_dim,)), ((), ())), preferred_element_type=jnp.float32
    )


def plane_places():
    mine = lax.axis_index("fsdp")
    plane = lax.axis_index("blk")
    core = lax.rem(mine, 2)
    col = lax.rem(mine // 2, 2)
    row = mine // 4

    def at(flip):
        flip_row, flip_col, flip_core = flip // 4, (flip // 2) % 2, flip % 2
        new_row = 1 - row if flip_row else row
        new_col = 1 - col if flip_col else col
        new_core = 1 - core if flip_core else core
        return new_row * 4 + new_col * 2 + new_core

    return mine, plane, at


def greet(places):
    barrier = pltpu.get_barrier_semaphore()
    for place in places:
        pl.semaphore_signal(barrier, inc=1, device_id=place, device_id_type=MESH_ID)
    pl.semaphore_wait(barrier, len(places))


def remote(src, dst, send_sem, recv_sem, place):
    return pltpu.make_async_remote_copy(
        src_ref=src,
        dst_ref=dst,
        send_sem=send_sem,
        recv_sem=recv_sem,
        device_id=place,
        device_id_type=MESH_ID,
    )


PIECES = 4


def gather_kernel(block_ref, out_ref, own_sem, send_sems, recv_sems):
    mine, plane, at = plane_places()
    piece = block_ref.shape[0] // PIECES
    greet([(at(flip), plane) for flip in (1, 2, 4)])
    own = pltpu.make_async_copy(block_ref, out_ref.at[mine], own_sem)
    own.start()
    started = []

    def send(src, owner, part, flip, slot):
        copy = remote(
            src,
            out_ref.at[owner, pl.ds(part * piece, piece)],
            send_sems.at[slot],
            recv_sems.at[slot],
            (at(flip), plane),
        )
        copy.start()
        started.append(copy)

    def arrived(owner, part, slot):
        ref = out_ref.at[owner, pl.ds(part * piece, piece)]
        remote(ref, ref, send_sems.at[slot], recv_sems.at[slot], (mine, plane)).wait_recv()
        return ref

    for part in range(PIECES):
        src = block_ref.at[pl.ds(part * piece, piece)]
        send(src, mine, part, 2, part)
        send(src, mine, part, 4, PIECES + part)
        send(src, mine, part, 1, 3 * PIECES + part)
    for part in range(PIECES):
        got = arrived(at(2), part, part)
        if part < PIECES // 2:
            send(got, at(2), part, 4, 2 * PIECES + part)
        send(got, at(2), part, 1, 4 * PIECES + part)
        got = arrived(at(4), part, PIECES + part)
        if part >= PIECES // 2:
            send(got, at(4), part, 2, 2 * PIECES + part)
        send(got, at(4), part, 1, 5 * PIECES + part)
    for part in range(PIECES):
        got = arrived(at(6), part, 2 * PIECES + part)
        send(got, at(6), part, 1, 6 * PIECES + part)
    for number, flip in enumerate((1, 3, 5, 7)):
        for part in range(PIECES):
            arrived(at(flip), part, (3 + number) * PIECES + part)
    own.wait()
    for copy in started:
        copy.wait_send()


def plane_gather(block):
    rows, width = block.shape
    return pl.pallas_call(
        gather_kernel,
        out_shape=jax.ShapeDtypeStruct((8, rows, width), block.dtype),
        in_specs=[pl.BlockSpec(memory_space=pl.ANY)],
        out_specs=pl.BlockSpec(memory_space=pl.ANY),
        scratch_shapes=[
            pltpu.SemaphoreType.DMA,
            pltpu.SemaphoreType.DMA((7 * PIECES,)),
            pltpu.SemaphoreType.DMA((7 * PIECES,)),
        ],
        compiler_params=pltpu.CompilerParams(collective_id=0, has_side_effects=True),
        name="plane_gather",
    )(block)


def scatter_kernel(
    part_ref,
    out_ref,
    own,
    peer,
    far,
    near,
    load_sems,
    core_send,
    core_recv,
    far_send,
    far_recv,
    near_send,
    near_recv,
):
    mine, plane, at = plane_places()
    rows = part_ref.shape[1]
    half = rows // 2
    greet([(at(flip), plane) for flip in (1, 2, 4)])
    order = (6, 2, 4, 0)
    loads, pairs = [], []
    for slot, flip in enumerate(order):
        copy = remote(
            part_ref.at[at(flip ^ 1)],
            peer.at[slot],
            core_send.at[slot],
            core_recv.at[slot],
            (at(1), plane),
        )
        copy.start()
        pairs.append(copy)
        load = pltpu.make_async_copy(part_ref.at[at(flip)], own.at[slot], load_sems.at[slot])
        load.start()
        loads.append(load)

    def pair_sum(slot, start, count):
        rows_at = pl.ds(start, count)
        total = own[slot, rows_at, :].astype(jnp.float32) + peer[slot, rows_at, :].astype(
            jnp.float32
        )
        return total

    low, high = pl.ds(0, half), pl.ds(half, half)
    far_copies, near_copies = [], []
    loads[0].wait()
    pairs[0].wait_recv()
    own[0] = pair_sum(0, 0, rows).astype(jnp.bfloat16)
    for number, (flip, rows_at) in enumerate(((2, low), (4, high))):
        copy = remote(
            own.at[0, rows_at],
            far.at[number],
            far_send.at[number],
            far_recv.at[number],
            (at(flip), plane),
        )
        copy.start()
        far_copies.append(copy)

    def send_near(slot, flip, part, rows_at):
        index = (slot - 1) * 2 + part
        copy = remote(
            own.at[slot, rows_at],
            near.at[slot - 1, rows_at],
            near_send.at[index],
            near_recv.at[index],
            (at(flip), plane),
        )
        copy.start()
        near_copies.append(copy)

    loads[1].wait()
    pairs[1].wait_recv()
    own[1, low, :] = pair_sum(1, 0, half).astype(jnp.bfloat16)
    send_near(1, 2, 0, low)
    loads[2].wait()
    pairs[2].wait_recv()
    own[2, high, :] = pair_sum(2, half, half).astype(jnp.bfloat16)
    send_near(2, 4, 1, high)
    far_copies[0].wait_recv()
    own[2, low, :] = (pair_sum(2, 0, half) + far[0].astype(jnp.float32)).astype(jnp.bfloat16)
    send_near(2, 4, 0, low)
    far_copies[1].wait_recv()
    own[1, high, :] = (pair_sum(1, half, half) + far[1].astype(jnp.float32)).astype(jnp.bfloat16)
    send_near(1, 2, 1, high)
    loads[3].wait()
    pairs[3].wait_recv()
    for copy in near_copies:
        copy.wait_recv()
    out_ref[...] = (
        pair_sum(3, 0, rows) + near[0].astype(jnp.float32) + near[1].astype(jnp.float32)
    )
    for copy in pairs + far_copies + near_copies:
        copy.wait_send()


def plane_scatter(partial_sums):
    _, rows, width = partial_sums.shape
    kind = partial_sums.dtype
    return pl.pallas_call(
        scatter_kernel,
        out_shape=jax.ShapeDtypeStruct((rows, width), jnp.float32),
        in_specs=[pl.BlockSpec(memory_space=pl.ANY)],
        out_specs=pl.BlockSpec(memory_space=pltpu.VMEM),
        scratch_shapes=[
            pltpu.VMEM((4, rows, width), kind),
            pltpu.VMEM((4, rows, width), kind),
            pltpu.VMEM((2, rows // 2, width), kind),
            pltpu.VMEM((2, rows, width), kind),
            pltpu.SemaphoreType.DMA((4,)),
            pltpu.SemaphoreType.DMA((4,)),
            pltpu.SemaphoreType.DMA((4,)),
            pltpu.SemaphoreType.DMA((2,)),
            pltpu.SemaphoreType.DMA((2,)),
            pltpu.SemaphoreType.DMA((4,)),
            pltpu.SemaphoreType.DMA((4,)),
        ],
        compiler_params=pltpu.CompilerParams(
            collective_id=1, has_side_effects=True, vmem_limit_bytes=VMEM_BYTES
        ),
        name="plane_scatter",
    )(partial_sums)


def exchange_kernel(count, *refs):
    sources, results = refs[:count], refs[count : 2 * count]
    own_sems, send_sems, recv_sems = refs[2 * count :]
    mine, plane, at = plane_places()
    greet([(at(flip), plane) for flip in range(1, 8)])
    waits = []
    for number, (src, dst) in enumerate(zip(sources, results)):
        own = pltpu.make_async_copy(src.at[mine], dst.at[mine], own_sems.at[number])
        own.start()
        waits.append(own)
        for flip in (6, 7, 2, 4, 3, 5, 1):
            copy = remote(
                src.at[at(flip)],
                dst.at[mine],
                send_sems.at[number, flip],
                recv_sems.at[number, flip],
                (at(flip), plane),
            )
            copy.start()
            waits.append(copy)
    for copy in waits:
        copy.wait()


def plane_exchange(sources, number):
    count = len(sources)
    return pl.pallas_call(
        functools.partial(exchange_kernel, count),
        out_shape=[jax.ShapeDtypeStruct(source.shape, source.dtype) for source in sources],
        in_specs=[pl.BlockSpec(memory_space=pl.ANY)] * count,
        out_specs=[pl.BlockSpec(memory_space=pl.ANY)] * count,
        scratch_shapes=[
            pltpu.SemaphoreType.DMA((count,)),
            pltpu.SemaphoreType.DMA((count, 8)),
            pltpu.SemaphoreType.DMA((count, 8)),
        ],
        compiler_params=pltpu.CompilerParams(collective_id=number, has_side_effects=True),
        name="plane_exchange",
    )(*sources)


def softmax_rows(queries, key_rows):
    scores = contract(queries, key_rows, 1, 1) * HD ** (-0.5)
    exponent = jnp.exp(scores - jnp.max(scores, axis=-1, keepdims=True))
    return exponent / jnp.sum(exponent, axis=-1, keepdims=True)


def attention_kernel(h_ref, qkv_weight_ref, out_weight_ref, qkv_ref, attended_ref, partial_ref):
    width = qkv_ref.shape[-1] // 3
    projected = contract(h_ref[0], qkv_weight_ref[...], 1, 0).astype(jnp.bfloat16)
    qkv_ref[0] = projected
    for head in range(width // HD):
        at = head * HD
        queries = projected[:, at : at + HD]
        key_rows = projected[:, width + at : width + at + HD]
        value_rows = projected[:, 2 * width + at : 2 * width + at + HD]
        attention = softmax_rows(queries, key_rows).astype(jnp.bfloat16)
        attended_ref[0, :, at : at + HD] = contract(attention, value_rows, 1, 0).astype(
            jnp.bfloat16
        )
    partial_ref[0] = contract(attended_ref[0], out_weight_ref[...], 1, 0).astype(jnp.bfloat16)


def whole(shape):
    return pl.BlockSpec(shape, lambda image: (0,) * len(shape))


def per_image(shape):
    return pl.BlockSpec((1,) + shape, lambda image: (image,) + (0,) * len(shape))


def attention_forward(h_all, qkv_weight, out_weight):
    images, rows, width = h_all.shape
    columns = qkv_weight.shape[1]
    return pl.pallas_call(
        attention_kernel,
        grid=(images,),
        out_shape=[
            jax.ShapeDtypeStruct((images, rows, columns), jnp.bfloat16),
            jax.ShapeDtypeStruct((images, rows, columns // 3), jnp.bfloat16),
            jax.ShapeDtypeStruct((images, rows, width), jnp.bfloat16),
        ],
        in_specs=[
            per_image((rows, width)),
            whole(qkv_weight.shape),
            whole(out_weight.shape),
        ],
        out_specs=[
            per_image((rows, columns)),
            per_image((rows, columns // 3)),
            per_image((rows, width)),
        ],
        compiler_params=pltpu.CompilerParams(vmem_limit_bytes=VMEM_BYTES),
        name="attention_forward",
    )(h_all, qkv_weight, out_weight)


def attention_back_kernel(
    grad_ref, qkv_ref, qkv_weight_ref, out_weight_ref, grad_qkv_ref, partial_ref
):
    width = qkv_ref.shape[-1] // 3
    scale = HD ** (-0.5)
    grad_attended = contract(grad_ref[0], out_weight_ref[...], 1, 1).astype(jnp.bfloat16)
    for head in range(width // HD):
        at = head * HD
        queries = qkv_ref[0, :, at : at + HD]
        key_rows = qkv_ref[0, :, width + at : width + at + HD]
        value_rows = qkv_ref[0, :, 2 * width + at : 2 * width + at + HD]
        grad_head = grad_attended[:, at : at + HD]
        attention = softmax_rows(queries, key_rows)
        grad_weights = contract(grad_head, value_rows, 1, 1)
        row_delta = jnp.sum(attention * grad_weights, axis=-1, keepdims=True)
        grad_scores = (attention * (grad_weights - row_delta)).astype(jnp.bfloat16)
        grad_qkv_ref[0, :, at : at + HD] = (contract(grad_scores, key_rows, 1, 0) * scale).astype(
            jnp.bfloat16
        )
        grad_qkv_ref[0, :, width + at : width + at + HD] = (
            contract(grad_scores, queries, 0, 0) * scale
        ).astype(jnp.bfloat16)
        grad_qkv_ref[0, :, 2 * width + at : 2 * width + at + HD] = contract(
            attention.astype(jnp.bfloat16), grad_head, 0, 0
        ).astype(jnp.bfloat16)
    partial_ref[0] = contract(grad_qkv_ref[0], qkv_weight_ref[...], 1, 1).astype(jnp.bfloat16)


def attention_backward(grad_all, qkv_all, qkv_weight, out_weight):
    images, rows, width = grad_all.shape
    columns = qkv_weight.shape[1]
    return pl.pallas_call(
        attention_back_kernel,
        grid=(images,),
        out_shape=[
            jax.ShapeDtypeStruct((images, rows, columns), jnp.bfloat16),
            jax.ShapeDtypeStruct((images, rows, width), jnp.bfloat16),
        ],
        in_specs=[
            per_image((rows, width)),
            per_image((rows, columns)),
            whole(qkv_weight.shape),
            whole(out_weight.shape),
        ],
        out_specs=[per_image((rows, columns)), per_image((rows, width))],
        compiler_params=pltpu.CompilerParams(vmem_limit_bytes=VMEM_BYTES),
        name="attention_backward",
    )(grad_all, qkv_all, qkv_weight, out_weight)


GELU_SCALE = (2.0 / math.pi) ** 0.5


def feed_kernel(
    h_ref, grad_ref, up_ref, down_ref, hidden_ref, grad_pre_ref, partial_out_ref, partial_grad_ref
):
    pre = contract(h_ref[0], up_ref[...], 1, 0)
    grad_hidden = contract(grad_ref[0], down_ref[...], 1, 0)
    squared = pre * pre
    bend = jnp.tanh(GELU_SCALE * (pre + 0.044715 * (squared * pre)))
    rise = 0.5 * (1.0 + bend)
    hidden_ref[0] = (pre * rise).astype(jnp.bfloat16)
    slope = rise + 0.5 * pre * (1.0 - bend * bend) * (
        GELU_SCALE * (1.0 + 3.0 * 0.044715 * squared)
    )
    grad_pre_ref[0] = (grad_hidden * slope).astype(jnp.bfloat16)
    partial_out_ref[0] = contract(hidden_ref[0], down_ref[...], 1, 1).astype(jnp.bfloat16)
    partial_grad_ref[0] = contract(grad_pre_ref[0], up_ref[...], 1, 1).astype(jnp.bfloat16)


def feed_both(h_all, grad_all, up_weight, down_weight):
    images, rows, width = h_all.shape
    columns = up_weight.shape[1]
    return pl.pallas_call(
        feed_kernel,
        grid=(images,),
        out_shape=[
            jax.ShapeDtypeStruct((images, rows, columns), jnp.bfloat16),
            jax.ShapeDtypeStruct((images, rows, columns), jnp.bfloat16),
            jax.ShapeDtypeStruct((images, rows, width), jnp.bfloat16),
            jax.ShapeDtypeStruct((images, rows, width), jnp.bfloat16),
        ],
        in_specs=[
            per_image((rows, width)),
            per_image((rows, width)),
            whole(up_weight.shape),
            whole(down_weight.shape),
        ],
        out_specs=[
            per_image((rows, columns)),
            per_image((rows, columns)),
            per_image((rows, width)),
            per_image((rows, width)),
        ],
        compiler_params=pltpu.CompilerParams(vmem_limit_bytes=VMEM_BYTES),
        name="feed_both",
    )(h_all, grad_all, up_weight, down_weight)


def rms_scale(features):
    return lax.rsqrt(jnp.mean(features * features, axis=-1, keepdims=True) + EPSILON)


def norm_back(features, grad_h, scaling):
    inverse = rms_scale(features)
    unit = features * inverse
    inner = grad_h * (1.0 + scaling)
    grad = (inner - unit * jnp.mean(inner * unit, axis=-1, keepdims=True)) * inverse
    grad_scaling = jnp.sum(grad_h * unit, axis=0)
    grad_shifting = jnp.sum(grad_h, axis=0)
    return grad, grad_scaling, grad_shifting


def plane_sum(weight_part, number):
    depth, columns = weight_part.shape
    rows = depth // 8
    place = lax.axis_index("blk")
    received = lax.ppermute(weight_part, "blk", [(0, 1), (3, 2)])
    total = (weight_part.astype(jnp.float32) + received.astype(jnp.float32)).astype(jnp.bfloat16)
    halves = total.reshape(8, 2, rows // 2, columns)
    kept = lax.dynamic_index_in_dim(halves, jnp.where(place == 1, 0, 1), 1, keepdims=False)
    sent = lax.dynamic_index_in_dim(halves, jnp.where(place == 1, 1, 0), 1, keepdims=False)
    received = lax.ppermute(sent, "blk", [(1, 2), (2, 1)])
    total = (kept.astype(jnp.float32) + received.astype(jnp.float32)).astype(jnp.bfloat16)
    (mine,) = plane_exchange([total], number)
    other = lax.ppermute(mine, "blk", [(1, 2), (2, 1)])
    both = jnp.where(place == 1, jnp.stack([mine, other]), jnp.stack([other, mine]))
    given = lax.ppermute(both, "blk", [(1, 0), (2, 3)])
    result = jnp.where((place == 1) | (place == 2), both, given)
    return result.transpose(0, 2, 1, 3).reshape(rows, 8 * columns).astype(jnp.float32)


def plane_body(
    block_input,
    cotangent,
    bin_ids,
    image_counts,
    attn_weight,
    mlp_weight,
    noise_table,
    mod_weight,
    mod_bias,
):
    _, local_tok, model_width = block_input.shape
    feed_width = mlp_weight.shape[1] // 2
    rows = attn_weight.shape[0]
    bins = noise_table.shape[0]
    bias_piece = mod_bias.shape[0]
    mine, place = lax.axis_index("fsdp"), lax.axis_index("blk")

    def to_images(tokens):
        return lax.all_to_all(tokens, "blk", split_axis=0, concat_axis=1, tiled=True)[0]

    def to_tokens(image):
        return lax.all_to_all(
            image.reshape(1, -1, model_width), "blk", split_axis=1, concat_axis=0, tiled=True
        )

    features = to_images(block_input).astype(jnp.float32)
    incoming = to_images(cotangent).astype(jnp.float32)
    live = (place < image_counts[0]).astype(jnp.float32)

    all_bins = lax.all_gather(bin_ids, "fsdp", axis=0)
    plane_bins = lax.dynamic_index_in_dim(all_bins, place, 1, keepdims=False)
    activated = jax.nn.silu(noise_table)
    onehot = (plane_bins[:, None] == jnp.arange(bins, dtype=jnp.int32)[None, :]).astype(jnp.float32)
    chosen = jnp.dot(onehot, activated, precision=PRECISE)
    partial_mod = jnp.dot(chosen, mod_weight, precision=PRECISE)
    bias_full = lax.dynamic_update_slice_in_dim(
        jnp.zeros((6 * model_width,), jnp.float32), mod_bias, mine * bias_piece, 0
    )
    partial_mod = partial_mod + bias_full[None, :]
    mod_parts, qkv_weight = plane_exchange(
        [
            partial_mod.reshape(8, 6, model_width),
            attn_weight[:, : 3 * model_width]
            .astype(jnp.bfloat16)
            .reshape(rows, 3, 8, model_width // 8)
            .transpose(2, 0, 1, 3)
            .reshape(8, rows, 3 * model_width // 8),
        ],
        2,
    )
    mod_image = jnp.sum(mod_parts, axis=0)
    shift_one, scale_one, gate_one, shift_two, scale_two, gate_two = [
        mod_image[number][None, :] for number in range(6)
    ]
    qkv_weight = qkv_weight.reshape(model_width, 3 * model_width // 8)
    out_weight = attn_weight[:, 3 * model_width :].astype(jnp.bfloat16)
    feed_piece = feed_width // 8

    def columns_apart(weight):
        return weight.astype(jnp.bfloat16).reshape(rows, 8, feed_piece).transpose(1, 0, 2)

    h_one = (features * rms_scale(features) * (1.0 + scale_one) + shift_one).astype(jnp.bfloat16)
    h_one_all = plane_gather(h_one)
    qkv_all, attended_all, partial = attention_forward(h_one_all, qkv_weight, out_weight)
    attn_out = plane_scatter(partial)
    up_weight, down_weight = plane_exchange(
        [columns_apart(mlp_weight[:, :feed_width]), columns_apart(mlp_weight[:, feed_width:])], 3
    )
    up_weight = up_weight.reshape(model_width, feed_piece)
    down_weight = down_weight.reshape(model_width, feed_piece)
    first_sum = features + gate_one * attn_out
    h_two = (first_sum * rms_scale(first_sum) * (1.0 + scale_two) + shift_two).astype(jnp.bfloat16)
    grad_out = incoming * live
    grad_mlp = (gate_two * grad_out).astype(jnp.bfloat16)
    grad_mlp_all = plane_gather(grad_mlp)
    h_two_all = plane_gather(h_two)
    hidden_all, grad_pre_all, partial_out, partial_grad = feed_both(
        h_two_all, grad_mlp_all, up_weight, down_weight
    )

    def flat(array):
        return array.reshape(-1, array.shape[-1])

    def rows_low(left, right):
        return rows_product(flat(left), flat(right)).astype(jnp.bfloat16)

    down_grad = plane_sum(rows_low(grad_mlp_all, hidden_all), 4)
    up_grad = plane_sum(rows_low(h_two_all, grad_pre_all), 5)
    grad_h_two = plane_scatter(partial_grad)
    grad_first, grad_scale_two, grad_shift_two = norm_back(first_sum, grad_h_two, scale_two)
    grad_first = grad_first + grad_out
    grad_attn_out = (gate_one * grad_first).astype(jnp.bfloat16)
    grad_gate_one = jnp.sum(grad_first * attn_out, axis=0)
    grad_attn_all = plane_gather(grad_attn_out)
    grad_qkv_all, partial_h_one = attention_backward(
        grad_attn_all, qkv_all, qkv_weight, out_weight
    )
    qkv_grad = plane_sum(rows_low(h_one_all, grad_qkv_all), 6)
    qkv_grad = (
        qkv_grad.reshape(rows, 8, 3, model_width // 8)
        .transpose(0, 2, 1, 3)
        .reshape(rows, 3 * model_width)
    )
    out_grad = lax.psum(rows_low(attended_all, grad_attn_all), "blk").astype(jnp.float32)
    attn_weight_grad = jnp.concatenate([qkv_grad, out_grad], axis=1)
    mlp_weight_grad = jnp.concatenate([up_grad, down_grad], axis=1)
    grad_h_one = plane_scatter(partial_h_one)
    grad_input, grad_scale_one, grad_shift_one = norm_back(features, grad_h_one, scale_one)
    input_grad = to_tokens((grad_input + grad_first).astype(jnp.bfloat16)).astype(jnp.float32)
    mlp_out = plane_scatter(partial_out)
    block_out = to_tokens((live * (first_sum + gate_two * mlp_out)).astype(jnp.bfloat16))
    grad_gate_two = jnp.sum(grad_out * mlp_out, axis=0)

    grad_mod = jnp.concatenate(
        [
            grad_shift_one,
            grad_scale_one,
            grad_gate_one,
            grad_shift_two,
            grad_scale_two,
            grad_gate_two,
        ]
    )
    grad_images = lax.all_gather(
        lax.all_gather(grad_mod, "blk", axis=0), "fsdp", axis=0, tiled=True
    )
    onehot_all = (
        all_bins.reshape(-1)[:, None] == jnp.arange(bins, dtype=jnp.int32)[None, :]
    ).astype(jnp.float32)
    chosen_all = jnp.dot(onehot_all, activated, precision=PRECISE)
    mod_weight_grad = lax.dot_general(
        chosen_all, grad_images, (((0,), (0,)), ((), ())), precision=PRECISE
    )
    image_term = lax.dot_general(
        grad_images, mod_weight, (((1,), (1,)), ((), ())), precision=PRECISE
    )
    table_term = lax.dot_general(onehot_all, image_term, (((0,), (0,)), ((), ())), precision=PRECISE)
    noise_grad = jax.vjp(jax.nn.silu, noise_table)[1](table_term)[0]
    mod_bias_grad = lax.dynamic_slice_in_dim(
        jnp.sum(grad_images, axis=0), mine * bias_piece, bias_piece
    )
    return (
        block_out,
        input_grad,
        attn_weight_grad,
        mlp_weight_grad,
        noise_grad,
        mod_weight_grad,
        mod_bias_grad,
    )


def solution(mesh):
    fits = mesh.shape["fsdp"] == 8 and mesh.shape["blk"] == 4
    return jax.shard_map(
        plane_body if fits else body,
        mesh=mesh,
        in_specs=(
            P("fsdp", "blk", None),
            P("fsdp", "blk", None),
            P("fsdp"),
            P("fsdp"),
            P("fsdp", None),
            P("fsdp", None),
            P(None, "fsdp"),
            P("fsdp", None),
            P("fsdp"),
        ),
        out_specs=(
            P("fsdp", "blk", None),
            P("fsdp", "blk", None),
            P("fsdp", None),
            P("fsdp", None),
            P(None, "fsdp"),
            P("fsdp", None),
            P("fsdp"),
        ),
        check_vma=False,
    )
```

```python
import functools
import math

import jax
import jax.numpy as jnp
from jax import lax
from jax.experimental import pallas as pl
from jax.experimental.pallas import tpu as pltpu
from jax.sharding import PartitionSpec as P

HD = 128


EPSILON = 1e-06
PRECISE = lax.Precision.HIGHEST


def norm_mod(features, scaling, shifting):
    normed = features * lax.rsqrt(jnp.mean(features * features, axis=-1, keepdims=True) + EPSILON)
    return normed * (1.0 + scaling) + shifting


def rows_product(left_rows, right_rows):
    return lax.dot_general(
        left_rows, right_rows, (((0,), (0,)), ((), ())), preferred_element_type=jnp.float32
    )


def body(
    block_input,
    cotangent,
    bin_ids,
    image_counts,
    attn_weight,
    mlp_weight,
    noise_table,
    mod_weight,
    mod_bias,
):
    slot_count, local_tok, model_width = block_input.shape
    row_count = slot_count * local_tok
    feed_width = mlp_weight.shape[1] // 2
    head_count = model_width // HD
    blk_size = lax.axis_size("blk")
    image_tok = local_tok * blk_size
    score_scale = HD ** (-0.5)
    bias_piece = mod_bias.shape[0]
    activated = jax.nn.silu(noise_table)
    partial_mod = jnp.dot(activated, mod_weight, precision=PRECISE)
    bias_full = lax.dynamic_update_slice_in_dim(
        jnp.zeros((6 * model_width,), jnp.float32), mod_bias, lax.axis_index("fsdp") * bias_piece, 0
    )
    mod_table = lax.psum(partial_mod + bias_full[None, :], "fsdp")
    onehot = (
        bin_ids[:, None] == jnp.arange(noise_table.shape[0], dtype=jnp.int32)[None, :]
    ).astype(jnp.float32)
    mod_image = jnp.dot(onehot, mod_table, precision=PRECISE)
    shift_one, scale_one, gate_one, shift_two, scale_two, gate_two = [
        member[:, None, :] for member in jnp.split(mod_image, 6, axis=-1)
    ]
    live_mask = (jnp.arange(slot_count) < image_counts[0]).astype(jnp.float32)[:, None, None]
    features = block_input.astype(jnp.float32)
    h_one = (
        norm_mod(features, scale_one, shift_one)
        .astype(jnp.bfloat16)
        .reshape(row_count, model_width)
    )
    attn_full = lax.all_gather(attn_weight.astype(jnp.bfloat16), "fsdp", axis=0, tiled=True)
    projected = jnp.dot(
        h_one, attn_full[:, : 3 * model_width], preferred_element_type=jnp.float32
    ).astype(jnp.bfloat16)
    queries = projected[:, :model_width].reshape(slot_count, local_tok, head_count, HD)
    key_rows = projected[:, model_width : 2 * model_width].reshape(
        slot_count, local_tok, model_width
    )
    value_rows = projected[:, 2 * model_width :].reshape(slot_count, local_tok, model_width)
    all_keys, all_values = (
        lax.all_gather(key_rows, "blk", axis=1, tiled=True),
        lax.all_gather(value_rows, "blk", axis=1, tiled=True),
    )
    all_keys = all_keys.reshape(slot_count, image_tok, head_count, HD)
    all_values = all_values.reshape(slot_count, image_tok, head_count, HD)

    def scores_of(query_rows):
        return (
            jnp.einsum("sqhd,skhd->shqk", query_rows, all_keys, preferred_element_type=jnp.float32)
            * score_scale
        )

    scores = scores_of(queries)
    maximum = jnp.max(scores, axis=-1, keepdims=True)
    exponent = jnp.exp(scores - maximum)
    denominator = jnp.sum(exponent, axis=-1, keepdims=True)
    attention = exponent / denominator
    log_total = maximum + jnp.log(denominator)
    attended = (
        jnp.einsum(
            "shqk,skhd->sqhd",
            attention.astype(jnp.bfloat16),
            all_values,
            preferred_element_type=jnp.float32,
        )
        .astype(jnp.bfloat16)
        .reshape(row_count, model_width)
    )
    attn_out = jnp.dot(
        attended, attn_full[:, 3 * model_width :], preferred_element_type=jnp.float32
    ).reshape(slot_count, local_tok, model_width)
    first_sum = features + gate_one * attn_out
    h_two = (
        norm_mod(first_sum, scale_two, shift_two)
        .astype(jnp.bfloat16)
        .reshape(row_count, model_width)
    )
    mlp_full = lax.all_gather(mlp_weight.astype(jnp.bfloat16), "fsdp", axis=0, tiled=True)
    pre_gelu = jnp.dot(h_two, mlp_full[:, :feed_width], preferred_element_type=jnp.float32)
    hidden = jax.nn.gelu(pre_gelu).astype(jnp.bfloat16)
    mlp_out = jnp.einsum(
        "rf,df->rd", hidden, mlp_full[:, feed_width:], preferred_element_type=jnp.float32
    ).reshape(slot_count, local_tok, model_width)
    second_sum = first_sum + gate_two * mlp_out
    block_out = (live_mask * second_sum).astype(jnp.bfloat16)
    grad_out = cotangent.astype(jnp.float32) * live_mask
    grad_mlp = (gate_two * grad_out).astype(jnp.bfloat16).reshape(row_count, model_width)
    grad_gate_two = jnp.sum(grad_out * mlp_out, axis=1)
    grad_hidden = jnp.dot(grad_mlp, mlp_full[:, feed_width:], preferred_element_type=jnp.float32)
    grad_pre = jax.vjp(jax.nn.gelu, pre_gelu)[1](grad_hidden)[0].astype(jnp.bfloat16)
    grad_h_two = jnp.einsum(
        "rf,df->rd", grad_pre, mlp_full[:, :feed_width], preferred_element_type=jnp.float32
    ).reshape(slot_count, local_tok, model_width)
    grad_first, grad_scale_two, grad_shift_two = jax.vjp(norm_mod, first_sum, scale_two, shift_two)[
        1
    ](grad_h_two)
    grad_first = grad_first + grad_out
    grad_attn_out = (gate_one * grad_first).astype(jnp.bfloat16).reshape(row_count, model_width)
    grad_gate_one = jnp.sum(grad_first * attn_out, axis=1)
    grad_attended = jnp.einsum(
        "rd,ed->re",
        grad_attn_out,
        attn_full[:, 3 * model_width :],
        preferred_element_type=jnp.float32,
    ).astype(jnp.bfloat16)
    grad_heads = grad_attended.reshape(slot_count, local_tok, head_count, HD)
    recomputed = jnp.exp(scores_of(queries) - log_total)
    grad_weights = jnp.einsum(
        "sqhd,skhd->shqk", grad_heads, all_values, preferred_element_type=jnp.float32
    )
    row_delta = jnp.sum(recomputed * grad_weights, axis=-1, keepdims=True)
    grad_scores = (recomputed * (grad_weights - row_delta)).astype(jnp.bfloat16)
    grad_queries = (
        jnp.einsum("shqk,skhd->sqhd", grad_scores, all_keys, preferred_element_type=jnp.float32)
        * score_scale
    )
    grad_keys_all = (
        jnp.einsum("shqk,sqhd->skhd", grad_scores, queries, preferred_element_type=jnp.float32)
        * score_scale
    )
    grad_values_all = jnp.einsum(
        "shqk,sqhd->skhd",
        recomputed.astype(jnp.bfloat16),
        grad_heads,
        preferred_element_type=jnp.float32,
    )
    grad_keys, grad_values = (
        lax.psum_scatter(
            grad_keys_all.reshape(slot_count, image_tok, model_width).astype(jnp.bfloat16),
            "blk",
            scatter_dimension=1,
            tiled=True,
        ).astype(jnp.float32),
        lax.psum_scatter(
            grad_values_all.reshape(slot_count, image_tok, model_width).astype(jnp.bfloat16),
            "blk",
            scatter_dimension=1,
            tiled=True,
        ).astype(jnp.float32),
    )
    grad_qkv = jnp.concatenate(
        [
            grad_queries.reshape(row_count, model_width).astype(jnp.bfloat16),
            grad_keys.reshape(row_count, model_width).astype(jnp.bfloat16),
            grad_values.reshape(row_count, model_width).astype(jnp.bfloat16),
        ],
        axis=1,
    )
    grad_h_one = jnp.einsum(
        "rc,dc->rd", grad_qkv, attn_full[:, : 3 * model_width], preferred_element_type=jnp.float32
    ).reshape(slot_count, local_tok, model_width)
    grad_input, grad_scale_one, grad_shift_one = jax.vjp(norm_mod, features, scale_one, shift_one)[
        1
    ](grad_h_one)
    input_grad = grad_input + grad_first
    grad_mod = jnp.concatenate(
        [
            grad_shift_one[:, 0, :],
            grad_scale_one[:, 0, :],
            grad_gate_one,
            grad_shift_two[:, 0, :],
            grad_scale_two[:, 0, :],
            grad_gate_two,
        ],
        axis=-1,
    )
    bin_terms = lax.dot_general(onehot, grad_mod, (((0,), (0,)), ((), ())), precision=PRECISE)
    grad_bins = lax.psum(bin_terms, ("fsdp", "blk"))
    table_term = jnp.einsum("be,de->bd", grad_bins, mod_weight, precision=PRECISE)
    noise_grad = jax.vjp(jax.nn.silu, noise_table)[1](table_term)[0]
    mod_weight_grad = lax.dot_general(
        activated, grad_bins, (((0,), (0,)), ((), ())), precision=PRECISE
    )
    mod_bias_grad = lax.dynamic_slice_in_dim(
        jnp.sum(grad_bins, axis=0), lax.axis_index("fsdp") * bias_piece, bias_piece
    )
    h_part = h_one
    attn_part = lax.psum_scatter(
        jnp.concatenate(
            [rows_product(h_part, grad_qkv), rows_product(attended, grad_attn_out)], axis=1
        ).astype(jnp.bfloat16),
        "fsdp",
        scatter_dimension=0,
        tiled=True,
    )
    h_part = h_two
    mlp_part = lax.psum_scatter(
        jnp.concatenate(
            [rows_product(h_part, grad_pre), rows_product(grad_mlp, hidden)], axis=1
        ).astype(jnp.bfloat16),
        "fsdp",
        scatter_dimension=0,
        tiled=True,
    )
    attn_weight_grad, mlp_weight_grad = (
        lax.psum(attn_part, "blk").astype(jnp.float32),
        lax.psum(mlp_part, "blk").astype(jnp.float32),
    )
    return (
        block_out,
        input_grad,
        attn_weight_grad,
        mlp_weight_grad,
        noise_grad,
        mod_weight_grad,
        mod_bias_grad,
    )


MESH_ID = pl.DeviceIdType.MESH
VMEM_BYTES = 56 * 1024 * 1024


def contract(left, right, left_dim, right_dim):
    return lax.dot_general(
        left, right, (((left_dim,), (right_dim,)), ((), ())), preferred_element_type=jnp.float32
    )


def plane_places():
    mine = lax.axis_index("fsdp")
    plane = lax.axis_index("blk")
    core = lax.rem(mine, 2)
    col = lax.rem(mine // 2, 2)
    row = mine // 4

    def at(flip):
        flip_row, flip_col, flip_core = flip // 4, (flip // 2) % 2, flip % 2
        new_row = 1 - row if flip_row else row
        new_col = 1 - col if flip_col else col
        new_core = 1 - core if flip_core else core
        return new_row * 4 + new_col * 2 + new_core

    return mine, plane, at


def greet(places):
    barrier = pltpu.get_barrier_semaphore()
    for place in places:
        pl.semaphore_signal(barrier, inc=1, device_id=place, device_id_type=MESH_ID)
    pl.semaphore_wait(barrier, len(places))


def remote(src, dst, send_sem, recv_sem, place):
    return pltpu.make_async_remote_copy(
        src_ref=src,
        dst_ref=dst,
        send_sem=send_sem,
        recv_sem=recv_sem,
        device_id=place,
        device_id_type=MESH_ID,
    )


PIECES = 4


def gather_kernel(block_ref, out_ref, own_sem, send_sems, recv_sems):
    mine, plane, at = plane_places()
    piece = block_ref.shape[0] // PIECES
    greet([(at(flip), plane) for flip in (1, 2, 4)])
    own = pltpu.make_async_copy(block_ref, out_ref.at[mine], own_sem)
    own.start()
    started = []

    def send(src, owner, part, flip, slot):
        copy = remote(
            src,
            out_ref.at[owner, pl.ds(part * piece, piece)],
            send_sems.at[slot],
            recv_sems.at[slot],
            (at(flip), plane),
        )
        copy.start()
        started.append(copy)

    def arrived(owner, part, slot):
        ref = out_ref.at[owner, pl.ds(part * piece, piece)]
        remote(ref, ref, send_sems.at[slot], recv_sems.at[slot], (mine, plane)).wait_recv()
        return ref

    for part in range(PIECES):
        src = block_ref.at[pl.ds(part * piece, piece)]
        send(src, mine, part, 2, part)
        send(src, mine, part, 4, PIECES + part)
        send(src, mine, part, 1, 3 * PIECES + part)
    for part in range(PIECES):
        got = arrived(at(2), part, part)
        if part < PIECES // 2:
            send(got, at(2), part, 4, 2 * PIECES + part)
        send(got, at(2), part, 1, 4 * PIECES + part)
        got = arrived(at(4), part, PIECES + part)
        if part >= PIECES // 2:
            send(got, at(4), part, 2, 2 * PIECES + part)
        send(got, at(4), part, 1, 5 * PIECES + part)
    for part in range(PIECES):
        got = arrived(at(6), part, 2 * PIECES + part)
        send(got, at(6), part, 1, 6 * PIECES + part)
    for number, flip in enumerate((1, 3, 5, 7)):
        for part in range(PIECES):
            arrived(at(flip), part, (3 + number) * PIECES + part)
    own.wait()
    for copy in started:
        copy.wait_send()


def plane_gather(block):
    rows, width = block.shape
    return pl.pallas_call(
        gather_kernel,
        out_shape=jax.ShapeDtypeStruct((8, rows, width), block.dtype),
        in_specs=[pl.BlockSpec(memory_space=pl.ANY)],
        out_specs=pl.BlockSpec(memory_space=pl.ANY),
        scratch_shapes=[
            pltpu.SemaphoreType.DMA,
            pltpu.SemaphoreType.DMA((7 * PIECES,)),
            pltpu.SemaphoreType.DMA((7 * PIECES,)),
        ],
        compiler_params=pltpu.CompilerParams(collective_id=0, has_side_effects=True),
        name="plane_gather",
    )(block)


def scatter_kernel(
    part_ref,
    out_ref,
    own,
    peer,
    far,
    near,
    load_sems,
    core_send,
    core_recv,
    far_send,
    far_recv,
    near_send,
    near_recv,
):
    mine, plane, at = plane_places()
    rows = part_ref.shape[1]
    half = rows // 2
    greet([(at(flip), plane) for flip in (1, 2, 4)])
    order = (6, 2, 4, 0)
    loads, pairs = [], []
    for slot, flip in enumerate(order):
        copy = remote(
            part_ref.at[at(flip ^ 1)],
            peer.at[slot],
            core_send.at[slot],
            core_recv.at[slot],
            (at(1), plane),
        )
        copy.start()
        pairs.append(copy)
        load = pltpu.make_async_copy(part_ref.at[at(flip)], own.at[slot], load_sems.at[slot])
        load.start()
        loads.append(load)

    def pair_sum(slot, start, count):
        rows_at = pl.ds(start, count)
        total = own[slot, rows_at, :].astype(jnp.float32) + peer[slot, rows_at, :].astype(
            jnp.float32
        )
        return total

    low, high = pl.ds(0, half), pl.ds(half, half)
    far_copies, near_copies = [], []
    loads[0].wait()
    pairs[0].wait_recv()
    own[0] = pair_sum(0, 0, rows).astype(jnp.bfloat16)
    for number, (flip, rows_at) in enumerate(((2, low), (4, high))):
        copy = remote(
            own.at[0, rows_at],
            far.at[number],
            far_send.at[number],
            far_recv.at[number],
            (at(flip), plane),
        )
        copy.start()
        far_copies.append(copy)

    def send_near(slot, flip, part, rows_at):
        index = (slot - 1) * 2 + part
        copy = remote(
            own.at[slot, rows_at],
            near.at[slot - 1, rows_at],
            near_send.at[index],
            near_recv.at[index],
            (at(flip), plane),
        )
        copy.start()
        near_copies.append(copy)

    loads[1].wait()
    pairs[1].wait_recv()
    own[1, low, :] = pair_sum(1, 0, half).astype(jnp.bfloat16)
    send_near(1, 2, 0, low)
    loads[2].wait()
    pairs[2].wait_recv()
    own[2, high, :] = pair_sum(2, half, half).astype(jnp.bfloat16)
    send_near(2, 4, 1, high)
    far_copies[0].wait_recv()
    own[2, low, :] = (pair_sum(2, 0, half) + far[0].astype(jnp.float32)).astype(jnp.bfloat16)
    send_near(2, 4, 0, low)
    far_copies[1].wait_recv()
    own[1, high, :] = (pair_sum(1, half, half) + far[1].astype(jnp.float32)).astype(jnp.bfloat16)
    send_near(1, 2, 1, high)
    loads[3].wait()
    pairs[3].wait_recv()
    for copy in near_copies:
        copy.wait_recv()
    out_ref[...] = (
        pair_sum(3, 0, rows) + near[0].astype(jnp.float32) + near[1].astype(jnp.float32)
    )
    for copy in pairs + far_copies + near_copies:
        copy.wait_send()


def plane_scatter(partial_sums):
    _, rows, width = partial_sums.shape
    kind = partial_sums.dtype
    return pl.pallas_call(
        scatter_kernel,
        out_shape=jax.ShapeDtypeStruct((rows, width), jnp.float32),
        in_specs=[pl.BlockSpec(memory_space=pl.ANY)],
        out_specs=pl.BlockSpec(memory_space=pltpu.VMEM),
        scratch_shapes=[
            pltpu.VMEM((4, rows, width), kind),
            pltpu.VMEM((4, rows, width), kind),
            pltpu.VMEM((2, rows // 2, width), kind),
            pltpu.VMEM((2, rows, width), kind),
            pltpu.SemaphoreType.DMA((4,)),
            pltpu.SemaphoreType.DMA((4,)),
            pltpu.SemaphoreType.DMA((4,)),
            pltpu.SemaphoreType.DMA((2,)),
            pltpu.SemaphoreType.DMA((2,)),
            pltpu.SemaphoreType.DMA((4,)),
            pltpu.SemaphoreType.DMA((4,)),
        ],
        compiler_params=pltpu.CompilerParams(
            collective_id=1, has_side_effects=True, vmem_limit_bytes=VMEM_BYTES
        ),
        name="plane_scatter",
    )(partial_sums)


def exchange_kernel(count, *refs):
    sources, results = refs[:count], refs[count : 2 * count]
    own_sems, send_sems, recv_sems = refs[2 * count :]
    mine, plane, at = plane_places()
    greet([(at(flip), plane) for flip in range(1, 8)])
    waits = []
    for number, (src, dst) in enumerate(zip(sources, results)):
        own = pltpu.make_async_copy(src.at[mine], dst.at[mine], own_sems.at[number])
        own.start()
        waits.append(own)
        for flip in (6, 7, 2, 4, 3, 5, 1):
            copy = remote(
                src.at[at(flip)],
                dst.at[mine],
                send_sems.at[number, flip],
                recv_sems.at[number, flip],
                (at(flip), plane),
            )
            copy.start()
            waits.append(copy)
    for copy in waits:
        copy.wait()


def plane_exchange(sources, number):
    count = len(sources)
    return pl.pallas_call(
        functools.partial(exchange_kernel, count),
        out_shape=[jax.ShapeDtypeStruct(source.shape, source.dtype) for source in sources],
        in_specs=[pl.BlockSpec(memory_space=pl.ANY)] * count,
        out_specs=[pl.BlockSpec(memory_space=pl.ANY)] * count,
        scratch_shapes=[
            pltpu.SemaphoreType.DMA((count,)),
            pltpu.SemaphoreType.DMA((count, 8)),
            pltpu.SemaphoreType.DMA((count, 8)),
        ],
        compiler_params=pltpu.CompilerParams(collective_id=number, has_side_effects=True),
        name="plane_exchange",
    )(*sources)


def softmax_rows(queries, key_rows):
    scores = contract(queries, key_rows, 1, 1) * HD ** (-0.5)
    exponent = jnp.exp(scores - jnp.max(scores, axis=-1, keepdims=True))
    return exponent / jnp.sum(exponent, axis=-1, keepdims=True)


def attention_kernel(h_ref, qkv_weight_ref, out_weight_ref, qkv_ref, attended_ref, partial_ref):
    width = qkv_ref.shape[-1] // 3
    projected = contract(h_ref[0], qkv_weight_ref[...], 1, 0).astype(jnp.bfloat16)
    qkv_ref[0] = projected
    for head in range(width // HD):
        at = head * HD
        queries = projected[:, at : at + HD]
        key_rows = projected[:, width + at : width + at + HD]
        value_rows = projected[:, 2 * width + at : 2 * width + at + HD]
        attention = softmax_rows(queries, key_rows).astype(jnp.bfloat16)
        attended_ref[0, :, at : at + HD] = contract(attention, value_rows, 1, 0).astype(
            jnp.bfloat16
        )
    partial_ref[0] = contract(attended_ref[0], out_weight_ref[...], 1, 0).astype(jnp.bfloat16)


def whole(shape):
    return pl.BlockSpec(shape, lambda image: (0,) * len(shape))


def per_image(shape):
    return pl.BlockSpec((1,) + shape, lambda image: (image,) + (0,) * len(shape))


def attention_forward(h_all, qkv_weight, out_weight):
    images, rows, width = h_all.shape
    columns = qkv_weight.shape[1]
    return pl.pallas_call(
        attention_kernel,
        grid=(images,),
        out_shape=[
            jax.ShapeDtypeStruct((images, rows, columns), jnp.bfloat16),
            jax.ShapeDtypeStruct((images, rows, columns // 3), jnp.bfloat16),
            jax.ShapeDtypeStruct((images, rows, width), jnp.bfloat16),
        ],
        in_specs=[
            per_image((rows, width)),
            whole(qkv_weight.shape),
            whole(out_weight.shape),
        ],
        out_specs=[
            per_image((rows, columns)),
            per_image((rows, columns // 3)),
            per_image((rows, width)),
        ],
        compiler_params=pltpu.CompilerParams(vmem_limit_bytes=VMEM_BYTES),
        name="attention_forward",
    )(h_all, qkv_weight, out_weight)


def attention_back_kernel(
    grad_ref, qkv_ref, qkv_weight_ref, out_weight_ref, grad_qkv_ref, partial_ref
):
    width = qkv_ref.shape[-1] // 3
    scale = HD ** (-0.5)
    grad_attended = contract(grad_ref[0], out_weight_ref[...], 1, 1).astype(jnp.bfloat16)
    for head in range(width // HD):
        at = head * HD
        queries = qkv_ref[0, :, at : at + HD]
        key_rows = qkv_ref[0, :, width + at : width + at + HD]
        value_rows = qkv_ref[0, :, 2 * width + at : 2 * width + at + HD]
        grad_head = grad_attended[:, at : at + HD]
        attention = softmax_rows(queries, key_rows)
        grad_weights = contract(grad_head, value_rows, 1, 1)
        row_delta = jnp.sum(attention * grad_weights, axis=-1, keepdims=True)
        grad_scores = (attention * (grad_weights - row_delta)).astype(jnp.bfloat16)
        grad_qkv_ref[0, :, at : at + HD] = (contract(grad_scores, key_rows, 1, 0) * scale).astype(
            jnp.bfloat16
        )
        grad_qkv_ref[0, :, width + at : width + at + HD] = (
            contract(grad_scores, queries, 0, 0) * scale
        ).astype(jnp.bfloat16)
        grad_qkv_ref[0, :, 2 * width + at : 2 * width + at + HD] = contract(
            attention.astype(jnp.bfloat16), grad_head, 0, 0
        ).astype(jnp.bfloat16)
    partial_ref[0] = contract(grad_qkv_ref[0], qkv_weight_ref[...], 1, 1).astype(jnp.bfloat16)


def attention_backward(grad_all, qkv_all, qkv_weight, out_weight):
    images, rows, width = grad_all.shape
    columns = qkv_weight.shape[1]
    return pl.pallas_call(
        attention_back_kernel,
        grid=(images,),
        out_shape=[
            jax.ShapeDtypeStruct((images, rows, columns), jnp.bfloat16),
            jax.ShapeDtypeStruct((images, rows, width), jnp.bfloat16),
        ],
        in_specs=[
            per_image((rows, width)),
            per_image((rows, columns)),
            whole(qkv_weight.shape),
            whole(out_weight.shape),
        ],
        out_specs=[per_image((rows, columns)), per_image((rows, width))],
        compiler_params=pltpu.CompilerParams(vmem_limit_bytes=VMEM_BYTES),
        name="attention_backward",
    )(grad_all, qkv_all, qkv_weight, out_weight)


GELU_SCALE = (2.0 / math.pi) ** 0.5


def feed_kernel(
    h_ref, grad_ref, up_ref, down_ref, hidden_ref, grad_pre_ref, partial_out_ref, partial_grad_ref
):
    pre = contract(h_ref[0], up_ref[...], 1, 0)
    grad_hidden = contract(grad_ref[0], down_ref[...], 1, 0)
    squared = pre * pre
    bend = jnp.tanh(GELU_SCALE * (pre + 0.044715 * (squared * pre)))
    rise = 0.5 * (1.0 + bend)
    hidden_ref[0] = (pre * rise).astype(jnp.bfloat16)
    slope = rise + 0.5 * pre * (1.0 - bend * bend) * (
        GELU_SCALE * (1.0 + 3.0 * 0.044715 * squared)
    )
    grad_pre_ref[0] = (grad_hidden * slope).astype(jnp.bfloat16)
    partial_out_ref[0] = contract(hidden_ref[0], down_ref[...], 1, 1).astype(jnp.bfloat16)
    partial_grad_ref[0] = contract(grad_pre_ref[0], up_ref[...], 1, 1).astype(jnp.bfloat16)


def feed_both(h_all, grad_all, up_weight, down_weight):
    images, rows, width = h_all.shape
    columns = up_weight.shape[1]
    return pl.pallas_call(
        feed_kernel,
        grid=(images,),
        out_shape=[
            jax.ShapeDtypeStruct((images, rows, columns), jnp.bfloat16),
            jax.ShapeDtypeStruct((images, rows, columns), jnp.bfloat16),
            jax.ShapeDtypeStruct((images, rows, width), jnp.bfloat16),
            jax.ShapeDtypeStruct((images, rows, width), jnp.bfloat16),
        ],
        in_specs=[
            per_image((rows, width)),
            per_image((rows, width)),
            whole(up_weight.shape),
            whole(down_weight.shape),
        ],
        out_specs=[
            per_image((rows, columns)),
            per_image((rows, columns)),
            per_image((rows, width)),
            per_image((rows, width)),
        ],
        compiler_params=pltpu.CompilerParams(vmem_limit_bytes=VMEM_BYTES),
        name="feed_both",
    )(h_all, grad_all, up_weight, down_weight)


def rms_scale(features):
    return lax.rsqrt(jnp.mean(features * features, axis=-1, keepdims=True) + EPSILON)


CHUNKS = 12
EARLY = 8
HALF_ROWS = 128
BAND = 32


def flipped(mine, flip):
    total = 0
    for bit in (1, 2, 4):
        total = total + lax.rem(mine // bit + flip // bit, 2) * bit
    return total


def bands(count, step):
    @pl.loop(0, count // BAND)
    def _(index):
        step(pl.ds(pl.multiple_of(index * BAND, BAND), BAND))


def plain(ref, rows):
    return ref[rows, :].astype(jnp.float32)


class Plane:
    def __init__(self):
        self.mine, self.place, self.at = plane_places()

    def to(self, flip):
        return (self.at(flip), self.place)

    def got(self, ref, sem):
        remote(ref, ref, sem, sem, (self.mine, self.place)).wait_recv()

    def gone(self, ref, sem):
        remote(ref, ref, sem, sem, (self.mine, self.place)).wait_send()


def scatter_flow(plane, own_of, fetch, peer, far, near, sems, finish):
    core_recv, far_send, far_recv, near_send, near_recv = sems
    rows = near.shape[1]
    half = rows // 2
    sent = []

    def add(slot, start, count, extra=None):
        own = own_of(slot)

        def step(band):
            at = pl.ds(pl.multiple_of(start + band.start, BAND), BAND)
            total = plain(own, at) + plain(peer.at[slot], at)
            if extra is not None:
                total = total + plain(extra, band)
            peer[slot, at, :] = total.astype(jnp.bfloat16)

        bands(count, step)

    def send(src, dst, flip, send_sem, recv_sem):
        copy = remote(src, dst, send_sem, recv_sem, plane.to(flip))
        copy.start()
        sent.append(copy)

    def send_near(slot, part):
        at = pl.ds(part * half, half)
        index = (slot - 1) * 2 + part
        send(
            peer.at[slot, at],
            near.at[slot - 1, at],
            2 * slot,
            near_send.at[index],
            near_recv.at[index],
        )

    fetch(3)
    plane.got(peer.at[3], core_recv.at[3])
    add(3, 0, rows)
    send(peer.at[3, pl.ds(0, half)], far.at[0], 2, far_send.at[0], far_recv.at[0])
    send(peer.at[3, pl.ds(half, half)], far.at[1], 4, far_send.at[1], far_recv.at[1])
    fetch(1)
    plane.got(peer.at[1], core_recv.at[1])
    add(1, 0, half)
    send_near(1, 0)
    fetch(2)
    plane.got(peer.at[2], core_recv.at[2])
    add(2, half, half)
    send_near(2, 1)
    yield
    plane.got(far.at[0], far_recv.at[0])
    add(2, 0, half, far.at[0])
    send_near(2, 0)
    plane.got(far.at[1], far_recv.at[1])
    add(1, half, half, far.at[1])
    send_near(1, 1)
    fetch(0)
    plane.got(peer.at[0], core_recv.at[0])
    yield
    for slot in (1, 2):
        for part in (0, 1):
            at = pl.ds(part * half, half)
            plane.got(near.at[slot - 1, at], near_recv.at[(slot - 1) * 2 + part])
    own = own_of(0)

    def step(at):
        finish(
            at,
            plain(own, at)
            + plain(peer.at[0], at)
            + plain(near.at[0], at)
            + plain(near.at[1], at),
        )

    bands(rows, step)
    for copy in sent:
        copy.wait_send()


def back_kernel(
    partial_grad,
    partial_out,
    early,
    h_all,
    qkv_all,
    attended_all,
    qkv_weight,
    out_weight,
    features,
    first_sum,
    attn_out,
    grad_out,
    mod,
    shares,
    token_out,
    token_grad,
    mod_out,
    late,
    land_a,
    land_b,
    first_buf,
    second_buf,
    stage,
    own_grad,
    grad_all,
    grad_first,
    image_out,
    image_grad,
    grad_qkv,
    h_cols,
    qkv_buf,
    attended_buf,
    late_buf,
    out_sum,
    sum_buf,
    in_buf,
    half_buf,
    half_in,
    mod_sum,
    mod_land,
    core_send,
    core_recv,
    far_send,
    far_recv,
    near_send,
    near_recv,
    stage_sems,
    gather_send,
    gather_recv,
    load_sems,
    late_sems,
    z_sems,
    x_sems,
    zload_sems,
    token_sems,
    mod_sems,
):
    plane = Plane()
    mine, place = plane.mine, plane.place
    rows, width = features.shape
    at = plane.at
    is_mid = (place == 1) | (place == 2)
    my_half = pl.ds(pl.multiple_of(jnp.where(place == 2, HALF_ROWS, 0), HALF_ROWS), HALF_ROWS)
    other_half = pl.ds(pl.multiple_of(jnp.where(place == 2, 0, HALF_ROWS), HALF_ROWS), HALF_ROWS)
    partner = (mine, 3 - place)
    outer = (mine, jnp.where(place == 1, 0, 3))
    inner = (mine, jnp.where(place == 0, 1, 2))
    others = [lax.rem(place + step, 4) for step in (1, 2, 3)]
    greet([plane.to(flip) for flip in range(1, 8)] + [(mine, other) for other in others])

    def z_copy(kind, chunk, src, dst, target):
        return remote(src, dst, z_sems.at[0, kind, chunk], z_sems.at[1, kind, chunk], target)

    def start_outward(chunk):
        if isinstance(chunk, int) and chunk >= EARLY:
            src = late.at[chunk - EARLY]
        else:
            src = early.at[chunk]
        z_copy(0, chunk, src, land_a.at[chunk], inner).start()

    def stage_d(k):
        region = shares.at[k, :, other_half]
        plane.got(region, z_sems.at[1, 2, k])
        z_copy(4, k, region, region, outer).start()

    def stage_x(k):
        region = shares.at[k, :, my_half]
        plane.got(region, x_sems.at[1, k])
        z_copy(2, k, region, region, partner).start()
        z_copy(3, k, region, region, outer).start()

    def stage_f(k):
        slot = k % 2
        load = pltpu.make_async_copy(land_b.at[k], half_in, zload_sems.at[2])
        plane.got(land_b.at[k], z_sems.at[1, 1, k])
        load.start()
        if k >= 2:
            plane.gone(half_buf.at[slot, pl.ds(0, 7)], x_sems.at[0, k - 2])
        load.wait()

        @pl.loop(0, 8)
        def _(block):
            half_buf[slot, block] = (
                sum_buf[slot, block, my_half, :].astype(jnp.float32)
                + half_in[block].astype(jnp.float32)
            ).astype(jnp.bfloat16)

        if k == CHUNKS - 1:
            pltpu.make_async_copy(
                half_buf.at[slot], shares.at[k, :, my_half], x_sems.at[1, k]
            ).start()
            return
        pltpu.make_async_copy(
            half_buf.at[slot, mine], shares.at[k, mine, my_half], x_sems.at[1, k]
        ).start()
        for flip in (6, 7, 2, 4, 3, 5, 1):
            remote(
                half_buf.at[slot, at(flip)],
                shares.at[k, mine, my_half],
                x_sems.at[0, k],
                x_sems.at[1, k],
                plane.to(flip),
            ).start()

    def stage_s(k):
        slot = k % 2
        if k >= 2:
            plane.gone(sum_buf.at[slot, :, other_half], z_sems.at[0, 1, k - 2])
        src = late.at[k - EARLY] if k >= EARLY else early.at[k]
        own_load = pltpu.make_async_copy(src, sum_buf.at[slot], zload_sems.at[0])
        own_load.start()
        in_load = pltpu.make_async_copy(land_a.at[k], in_buf, zload_sems.at[1])
        plane.got(land_a.at[k], z_sems.at[1, 0, k])
        in_load.start()
        own_load.wait()
        in_load.wait()

        @pl.loop(0, 8)
        def _(block):
            sum_buf[slot, block] = (
                sum_buf[slot, block].astype(jnp.float32) + in_buf[block].astype(jnp.float32)
            ).astype(jnp.bfloat16)

        z_copy(1, k, sum_buf.at[slot, :, other_half], land_b.at[k], partner).start()

    def tick(now):
        @pl.when(jnp.logical_not(is_mid))
        def _():
            if now < CHUNKS:
                plane.gone(land_a.at[now], z_sems.at[0, 0, now])
            if now + 2 < CHUNKS:
                start_outward(now + 2)

        @pl.when(is_mid)
        def _():
            if 0 <= now - 3 < CHUNKS:
                stage_d(now - 3)
            if 0 <= now - 2 < CHUNKS:
                stage_x(now - 2)
            if 0 <= now - 1 < CHUNKS:
                stage_f(now - 1)
            if now < CHUNKS:
                stage_s(now)

    @pl.when(jnp.logical_not(is_mid))
    def _():
        start_outward(0)
        start_outward(1)

    attended_load = pltpu.make_async_copy(attended_all, attended_buf, load_sems.at[0])
    attended_load.start()
    mod_sum[...] = jnp.zeros_like(mod_sum)
    row = {
        name: number
        for number, name in enumerate(
            ("shift_one", "scale_one", "gate_one", "shift_two", "scale_two", "gate_two", "live")
        )
    }

    def mod_row(name):
        return mod[pl.ds(row[name], 1), :]

    def accumulate(name, value):
        mod_sum[pl.ds(row[name], 1), :] += jnp.sum(value, axis=0, keepdims=True)

    def sems(number):
        return (
            core_recv.at[number],
            far_send.at[number],
            far_recv.at[number],
            near_send.at[number],
            near_recv.at[number],
        )

    class Halves:
        def __init__(self, ref):
            self.ref = ref

        @property
        def at(self):
            return self

        def __getitem__(self, number):
            return self.ref.at[pl.ds(number * (rows // 2), rows // 2)]

    def give(src, buf, number, slot):
        remote(
            src, buf.at[slot], core_send.at[number, slot], core_recv.at[number, slot], plane.to(1)
        ).start()

    def staged_flow(source, buf, number, finish):
        for slot in (3, 1, 2, 0):
            give(source.at[at((2 * slot) ^ 1)], buf, number, slot)
        order = {3: 0, 1: 1, 2: 0, 0: 1}

        def load(slot):
            return pltpu.make_async_copy(
                source.at[at(2 * slot)], stage.at[order[slot]], stage_sems.at[number, slot]
            )

        load(3).start()
        load(1).start()

        def fetch(slot):
            if slot == 2:
                load(2).start()
            if slot == 0:
                load(0).start()
            load(slot).wait()

        return scatter_flow(
            plane,
            lambda slot: stage.at[order[slot]],
            fetch,
            buf.at[pl.ds(0, 4)],
            Halves(buf.at[6]),
            buf.at[pl.ds(4, 2)],
            sems(number),
            finish,
        )

    def run(flow, first_tick):
        for step, _ in enumerate(flow):
            tick(first_tick + step)

    def finish_out(where, value):
        base = first_sum[where, :]
        image_out[where, :] = (
            mod_row("live") * (base + mod_row("gate_two") * value)
        ).astype(jnp.bfloat16)
        accumulate("gate_two", plain(grad_out, where) * value)

    token_copies = []

    def return_tokens(image, result, number):
        piece = rows // 4
        own = pltpu.make_async_copy(
            image.at[pl.ds(pl.multiple_of(place * piece, piece), piece)],
            result.at[place],
            token_sems.at[0, number, 0],
        )
        own.start()
        token_copies.append(own)
        for step, other in enumerate(others):
            copy = remote(
                image.at[pl.ds(pl.multiple_of(other * piece, piece), piece)],
                result.at[place],
                token_sems.at[0, number, step + 1],
                token_sems.at[1, number, step + 1],
                (mine, other),
            )
            copy.start()
            token_copies.append(copy)

    run(staged_flow(partial_out, first_buf, 0, finish_out), 0)
    return_tokens(image_out, token_out, 0)

    def back_norm(source, value, scale_name, shift_name):
        inverse = rms_scale(source)
        unit = source * inverse
        inner = value * (1.0 + mod_row(scale_name))
        accumulate(scale_name, value * unit)
        accumulate(shift_name, value)
        return (inner - unit * jnp.mean(inner * unit, axis=-1, keepdims=True)) * inverse

    def finish_feed(where, value):
        total = back_norm(first_sum[where, :], value, "scale_two", "shift_two") + plain(
            grad_out, where
        )
        grad_first[where, :] = total
        accumulate("gate_one", total * attn_out[where, :])
        low_grad = (mod_row("gate_one") * total).astype(jnp.bfloat16)
        own_grad[where, :] = low_grad
        grad_all[mine, where, :] = low_grad

    run(staged_flow(partial_grad, second_buf, 1, finish_feed), 2)

    piece = rows // PIECES

    def forward(src, owner, part, flip, slot):
        copy = remote(
            src,
            grad_all.at[owner, pl.ds(part * piece, piece)],
            gather_send.at[slot],
            gather_recv.at[slot],
            plane.to(flip),
        )
        copy.start()

    def arrived(owner, part, slot):
        ref = grad_all.at[owner, pl.ds(part * piece, piece)]
        plane.got(ref, gather_recv.at[slot])
        return ref

    for part in range(PIECES):
        src = own_grad.at[pl.ds(part * piece, piece)]
        forward(src, mine, part, 2, part)
        forward(src, mine, part, 4, PIECES + part)
        forward(src, mine, part, 1, 3 * PIECES + part)

    def arrive(step):
        if step == 2:
            for part in range(PIECES):
                got = arrived(at(2), part, part)
                if part < PIECES // 2:
                    forward(got, at(2), part, 4, 2 * PIECES + part)
                forward(got, at(2), part, 1, 4 * PIECES + part)
                got = arrived(at(4), part, PIECES + part)
                if part >= PIECES // 2:
                    forward(got, at(4), part, 2, 2 * PIECES + part)
                forward(got, at(4), part, 1, 5 * PIECES + part)
        if step == 6:
            for part in range(PIECES):
                got = arrived(at(6), part, 2 * PIECES + part)
                forward(got, at(6), part, 1, 6 * PIECES + part)
        if step % 2:
            for part in range(PIECES):
                arrived(at(step), part, (3 + step // 2) * PIECES + part)

    def qkv_load(step):
        return pltpu.make_async_copy(
            qkv_all.at[flipped(mine, step)], qkv_buf.at[lax.rem(step, 2)], load_sems.at[1 + lax.rem(step, 2)]
        )

    qkv_load(0).start()
    attended_load.wait()
    out_sum[...] = jnp.zeros_like(out_sum)
    columns = qkv_buf.shape[-1]
    third = columns // 3
    scale = HD ** (-0.5)

    @pl.loop(0, 8)
    def _(step):
        for number in range(8):

            @pl.when(step == number)
            def _(number=number):
                arrive(number)

        image = flipped(mine, step)
        slot = lax.rem(step, 2)
        qkv_load(step).wait()

        @pl.when(step < 7)
        def _():
            qkv_load(step + 1).start()

        grad = grad_all[image]
        grad_attended = contract(grad, out_weight[...], 1, 1).astype(jnp.bfloat16)
        image_rows = pl.ds(pl.multiple_of(image * rows, rows), rows)
        for head in range(third // HD):
            begin = head * HD
            queries = qkv_buf[slot, :, begin : begin + HD]
            key_rows = qkv_buf[slot, :, third + begin : third + begin + HD]
            value_rows = qkv_buf[slot, :, 2 * third + begin : 2 * third + begin + HD]
            grad_head = grad_attended[:, begin : begin + HD]
            attention = softmax_rows(queries, key_rows)
            grad_weights = contract(grad_head, value_rows, 1, 1)
            row_delta = jnp.sum(attention * grad_weights, axis=-1, keepdims=True)
            grad_scores = (attention * (grad_weights - row_delta)).astype(jnp.bfloat16)
            grad_qkv[image_rows, begin : begin + HD] = (
                contract(grad_scores, key_rows, 1, 0) * scale
            ).astype(jnp.bfloat16)
            grad_qkv[image_rows, third + begin : third + begin + HD] = (
                contract(grad_scores, queries, 0, 0) * scale
            ).astype(jnp.bfloat16)
            grad_qkv[image_rows, 2 * third + begin : 2 * third + begin + HD] = contract(
                attention.astype(jnp.bfloat16), grad_head, 0, 0
            ).astype(jnp.bfloat16)
        out_sum[...] += contract(attended_buf[image], grad, 0, 0)
        second_buf[step] = contract(grad_qkv[image_rows, :], qkv_weight[...], 1, 1).astype(
            jnp.bfloat16
        )
        for number in (1, 3, 5, 7):

            @pl.when(step == number)
            def _(number=number):
                give(second_buf.at[number], first_buf, 2, number // 2)

        for number, now in ((2, 4), (5, 5)):

            @pl.when(step == number)
            def _(now=now):
                tick(now)

    for slot in range(7 * PIECES):
        plane.gone(own_grad.at[pl.ds(0, piece)], gather_send.at[slot])

    def cols_load(block):
        return pltpu.make_async_copy(
            h_all.at[:, :, pl.ds(pl.multiple_of(block * rows, rows), rows)],
            h_cols.at[lax.rem(block, 2)],
            load_sems.at[3 + lax.rem(block, 2)],
        )

    cols_load(0).start()
    for block in range(8):
        late_buf[3, block] = out_sum[:, block * rows : (block + 1) * rows].astype(jnp.bfloat16)

    @pl.loop(0, 8)
    def _(block):
        cols_load(block).wait()

        @pl.when(block < 7)
        def _():
            cols_load(block + 1).start()

        cols = h_cols[lax.rem(block, 2)].reshape(8 * rows, rows)
        product = contract(cols, grad_qkv[...], 0, 0)
        for number in range(3):
            late_buf[number, block] = product[:, number * third : (number + 1) * third].astype(
                jnp.bfloat16
            )

    late_copy = pltpu.make_async_copy(late_buf, late, late_sems)
    late_copy.start()

    def finish_input(where, value):
        total = back_norm(plain(features, where), value, "scale_one", "shift_one")
        image_grad[where, :] = (total + grad_first[where, :]).astype(jnp.bfloat16)

    late_copy.wait()
    run(
        scatter_flow(
            plane,
            lambda slot: second_buf.at[2 * slot],
            lambda slot: None,
            first_buf.at[pl.ds(0, 4)],
            Halves(first_buf.at[6]),
            first_buf.at[pl.ds(4, 2)],
            sems(2),
            finish_input,
        ),
        6,
    )
    return_tokens(image_grad, token_grad, 1)

    mod_copies = []
    mod_land[place] = mod_sum[...]
    for step, other in enumerate(others):
        copy = remote(
            mod_sum, mod_land.at[place], mod_sems.at[0, step], mod_sems.at[1, step], (mine, other)
        )
        copy.start()
        mod_copies.append(copy)
    tick(8)
    for copy in mod_copies:
        copy.wait_recv()
    own = pltpu.make_async_copy(mod_land, mod_out.at[mine], mod_sems.at[0, 3])
    own.start()
    plane_copies = []
    for flip in range(1, 8):
        copy = remote(
            mod_land,
            mod_out.at[mine],
            mod_sems.at[0, 3 + flip],
            mod_sems.at[1, 3 + flip],
            plane.to(flip),
        )
        copy.start()
        plane_copies.append(copy)
    for now in range(9, CHUNKS + 3):
        tick(now)
    own.wait()
    for copy in mod_copies:
        copy.wait_send()
    for copy in plane_copies:
        copy.wait()
    for copy in token_copies:
        copy.wait()
    for number in range(3):
        for slot in range(4):
            plane.gone(second_buf.at[slot], core_send.at[number, slot])

    @pl.when(is_mid)
    def _():
        for k in (CHUNKS - 2, CHUNKS - 1):
            plane.gone(sum_buf.at[k % 2, :, other_half], z_sems.at[0, 1, k])
        plane.gone(half_buf.at[0, pl.ds(0, 7)], x_sems.at[0, CHUNKS - 2])
        for k in range(CHUNKS):
            plane.gone(shares.at[k, :, my_half], z_sems.at[0, 2, k])
            plane.gone(shares.at[k, :, my_half], z_sems.at[0, 3, k])
            plane.gone(shares.at[k, :, other_half], z_sems.at[0, 4, k])

    @pl.when(jnp.logical_not(is_mid))
    def _():
        first = pl.ds(pl.multiple_of(jnp.where(place == 0, 0, HALF_ROWS), HALF_ROWS), HALF_ROWS)
        second = pl.ds(pl.multiple_of(jnp.where(place == 0, HALF_ROWS, 0), HALF_ROWS), HALF_ROWS)
        for k in range(CHUNKS):
            plane.got(shares.at[k, :, first], z_sems.at[1, 3, k])
            plane.got(shares.at[k, :, second], z_sems.at[1, 4, k])


def back_part(
    partial_grad,
    partial_out,
    early,
    h_all,
    qkv_all,
    attended_all,
    qkv_weight,
    out_weight,
    features,
    first_sum,
    attn_out,
    grad_out,
    mod,
):
    images, rows, width = h_all.shape
    columns = qkv_weight.shape[1]
    low, full = jnp.bfloat16, jnp.float32
    dma = pltpu.SemaphoreType.DMA
    anywhere, inside = pl.BlockSpec(memory_space=pl.ANY), pl.BlockSpec(memory_space=pltpu.VMEM)
    return pl.pallas_call(
        back_kernel,
        out_shape=[
            jax.ShapeDtypeStruct((CHUNKS, 8, rows, rows), low),
            jax.ShapeDtypeStruct((4, rows // 4, width), low),
            jax.ShapeDtypeStruct((4, rows // 4, width), low),
            jax.ShapeDtypeStruct((8, 4, 8, width), full),
            jax.ShapeDtypeStruct((CHUNKS - EARLY, 8, rows, rows), low),
            jax.ShapeDtypeStruct((CHUNKS, 8, rows, rows), low),
            jax.ShapeDtypeStruct((CHUNKS, 8, HALF_ROWS, rows), low),
        ],
        in_specs=[anywhere] * 6 + [inside] * 7,
        out_specs=[anywhere] * 7,
        scratch_shapes=[
            pltpu.VMEM((7, rows, width), low),
            pltpu.VMEM((8, rows, width), low),
            pltpu.VMEM((2, rows, width), low),
            pltpu.VMEM((rows, width), low),
            pltpu.VMEM((8, rows, width), low),
            pltpu.VMEM((rows, width), full),
            pltpu.VMEM((rows, width), low),
            pltpu.VMEM((rows, width), low),
            pltpu.VMEM((8 * rows, columns), low),
            pltpu.VMEM((2, 8, rows, rows), low),
            pltpu.VMEM((2, rows, columns), low),
            pltpu.VMEM((8, rows, columns // 3), low),
            pltpu.VMEM((4, 8, rows, rows), low),
            pltpu.VMEM((columns // 3, width), full),
            pltpu.VMEM((2, 8, rows, rows), low),
            pltpu.VMEM((8, rows, rows), low),
            pltpu.VMEM((2, 8, HALF_ROWS, rows), low),
            pltpu.VMEM((8, HALF_ROWS, rows), low),
            pltpu.VMEM((8, width), full),
            pltpu.VMEM((4, 8, width), full),
            dma((3, 4)),
            dma((3, 4)),
            dma((3, 2)),
            dma((3, 2)),
            dma((3, 4)),
            dma((3, 4)),
            dma((2, 4)),
            dma((7 * PIECES,)),
            dma((7 * PIECES,)),
            dma((5,)),
            dma,
            dma((2, 5, CHUNKS)),
            dma((2, CHUNKS)),
            dma((3,)),
            dma((2, 2, 4)),
            dma((2, 11)),
        ],
        compiler_params=pltpu.CompilerParams(
            collective_id=4, has_side_effects=True, vmem_limit_bytes=63 * 1024 * 1024
        ),
        name="back_part",
    )(
        partial_grad,
        partial_out,
        early,
        h_all,
        qkv_all,
        attended_all,
        qkv_weight,
        out_weight,
        features,
        first_sum,
        attn_out,
        grad_out,
        mod,
    )


def early_kernel(grad_mlp, h_two, hidden, grad_pre, out_ref):
    step = pl.program_id(0)

    def product(left, right):
        for block in range(8):
            size = out_ref.shape[-1]
            out_ref[0, block] = contract(
                left[:, block * size : (block + 1) * size], right[...], 0, 0
            ).astype(jnp.bfloat16)

    @pl.when(step < 4)
    def _():
        product(grad_mlp, hidden)

    @pl.when(step >= 4)
    def _():
        product(h_two, grad_pre)


def early_grads(grad_mlp, h_two, hidden, grad_pre):
    tokens, width = grad_mlp.shape
    size = width // 8
    once = pl.Buffered(1)
    return pl.pallas_call(
        early_kernel,
        grid=(EARLY,),
        out_shape=jax.ShapeDtypeStruct((EARLY, 8, size, size), jnp.bfloat16),
        in_specs=[
            pl.BlockSpec((tokens, width), lambda step: (0, 0), pipeline_mode=once),
            pl.BlockSpec((tokens, width), lambda step: (0, 0), pipeline_mode=once),
            pl.BlockSpec((tokens, size), lambda step: (0, jnp.minimum(step, 3))),
            pl.BlockSpec((tokens, size), lambda step: (0, jnp.maximum(step - 4, 0))),
        ],
        out_specs=pl.BlockSpec((1, 8, size, size), lambda step: (step, 0, 0, 0)),
        compiler_params=pltpu.CompilerParams(vmem_limit_bytes=VMEM_BYTES),
        name="early_grads",
    )(grad_mlp, h_two, hidden, grad_pre)


def mlp_spread_kernel(share_ref, out_ref):
    size = share_ref.shape[-1]
    for number in range(4):
        out_ref[:, number * size : (number + 1) * size] = share_ref[number, 0].astype(jnp.float32)


def mlp_spread(shares):
    rows = shares.shape[2]
    return pl.pallas_call(
        mlp_spread_kernel,
        grid=(2, 8),
        out_shape=jax.ShapeDtypeStruct((rows, 64 * rows), jnp.float32),
        in_specs=[pl.BlockSpec((4, 1, rows, rows), lambda part, block: (1 - part, block, 0, 0))],
        out_specs=pl.BlockSpec((rows, 4 * rows), lambda part, block: (0, part * 8 + block)),
        compiler_params=pltpu.CompilerParams(vmem_limit_bytes=VMEM_BYTES),
        name="mlp_spread",
    )(shares)


def attn_spread_kernel(share_ref, out_ref):
    size = share_ref.shape[-1]
    for number in range(8):
        out_ref[:, number * size : (number + 1) * size] = share_ref[0, number].astype(jnp.float32)


def attn_spread(shares):
    rows = shares.shape[2]
    return pl.pallas_call(
        attn_spread_kernel,
        grid=(4,),
        out_shape=jax.ShapeDtypeStruct((rows, 32 * rows), jnp.float32),
        in_specs=[pl.BlockSpec((1, 8, rows, rows), lambda part: (EARLY + part, 0, 0, 0))],
        out_specs=pl.BlockSpec((rows, 8 * rows), lambda part: (0, part)),
        compiler_params=pltpu.CompilerParams(vmem_limit_bytes=VMEM_BYTES),
        name="attn_spread",
    )(shares)


def plane_body(
    block_input,
    cotangent,
    bin_ids,
    image_counts,
    attn_weight,
    mlp_weight,
    noise_table,
    mod_weight,
    mod_bias,
):
    _, local_tok, model_width = block_input.shape
    feed_width = mlp_weight.shape[1] // 2
    rows = attn_weight.shape[0]
    bins = noise_table.shape[0]
    bias_piece = mod_bias.shape[0]
    mine, place = lax.axis_index("fsdp"), lax.axis_index("blk")

    def to_images(tokens):
        return lax.all_to_all(tokens, "blk", split_axis=0, concat_axis=1, tiled=True)[0]

    features = to_images(block_input).astype(jnp.float32)
    incoming = to_images(cotangent).astype(jnp.float32)
    live = (place < image_counts[0]).astype(jnp.float32)

    all_bins = lax.all_gather(bin_ids, "fsdp", axis=0)
    plane_bins = lax.dynamic_index_in_dim(all_bins, place, 1, keepdims=False)
    activated = jax.nn.silu(noise_table)
    onehot = (plane_bins[:, None] == jnp.arange(bins, dtype=jnp.int32)[None, :]).astype(jnp.float32)
    chosen = jnp.dot(onehot, activated, precision=PRECISE)
    partial_mod = jnp.dot(chosen, mod_weight, precision=PRECISE)
    bias_full = lax.dynamic_update_slice_in_dim(
        jnp.zeros((6 * model_width,), jnp.float32), mod_bias, mine * bias_piece, 0
    )
    partial_mod = partial_mod + bias_full[None, :]
    mod_parts, qkv_weight = plane_exchange(
        [
            partial_mod.reshape(8, 6, model_width),
            attn_weight[:, : 3 * model_width]
            .astype(jnp.bfloat16)
            .reshape(rows, 3, 8, model_width // 8)
            .transpose(2, 0, 1, 3)
            .reshape(8, rows, 3 * model_width // 8),
        ],
        2,
    )
    mod_image = jnp.sum(mod_parts, axis=0)
    shift_one, scale_one, gate_one, shift_two, scale_two, gate_two = [
        mod_image[number][None, :] for number in range(6)
    ]
    qkv_weight = qkv_weight.reshape(model_width, 3 * model_width // 8)
    out_weight = attn_weight[:, 3 * model_width :].astype(jnp.bfloat16)
    feed_piece = feed_width // 8

    def columns_apart(weight):
        return weight.astype(jnp.bfloat16).reshape(rows, 8, feed_piece).transpose(1, 0, 2)

    up_weight, down_weight = [
        lax.all_to_all(
            columns_apart(weight), "fsdp", split_axis=0, concat_axis=0, tiled=True
        ).reshape(model_width, feed_piece)
        for weight in (mlp_weight[:, :feed_width], mlp_weight[:, feed_width:])
    ]
    grad_out = incoming * live
    grad_mlp = (gate_two * grad_out).astype(jnp.bfloat16)
    grad_mlp_all = lax.all_gather(grad_mlp, "fsdp", axis=0)
    h_one = (features * rms_scale(features) * (1.0 + scale_one) + shift_one).astype(jnp.bfloat16)
    h_one_all = plane_gather(h_one)
    qkv_all, attended_all, partial = attention_forward(h_one_all, qkv_weight, out_weight)
    attn_out = plane_scatter(partial)
    first_sum = features + gate_one * attn_out
    h_two = (first_sum * rms_scale(first_sum) * (1.0 + scale_two) + shift_two).astype(jnp.bfloat16)
    h_two_all = plane_gather(h_two)
    hidden_all, grad_pre_all, partial_out, partial_grad = feed_both(
        h_two_all, grad_mlp_all, up_weight, down_weight
    )

    def flat(array):
        return array.reshape(-1, array.shape[-1])

    early = early_grads(
        flat(grad_mlp_all), flat(h_two_all), flat(hidden_all), flat(grad_pre_all)
    )
    mod_rows = jnp.concatenate(
        [
            mod_image.reshape(6, model_width),
            jnp.full((2, model_width), live, jnp.float32),
        ]
    )
    shares, token_out, token_grad, mod_out, _, _, _ = back_part(
        partial_grad,
        partial_out,
        early,
        h_one_all,
        qkv_all,
        attended_all,
        qkv_weight,
        out_weight,
        features.astype(jnp.bfloat16),
        first_sum,
        attn_out,
        grad_out.astype(jnp.bfloat16),
        mod_rows,
    )
    block_out, input_grad = token_out, token_grad.astype(jnp.float32)
    attn_weight_grad, mlp_weight_grad = attn_spread(shares), mlp_spread(shares)
    grad_images = mod_out[:, :, :6].reshape(-1, 6 * model_width)
    onehot_all = (
        all_bins.reshape(-1)[:, None] == jnp.arange(bins, dtype=jnp.int32)[None, :]
    ).astype(jnp.float32)
    chosen_all = jnp.dot(onehot_all, activated, precision=PRECISE)
    mod_weight_grad = lax.dot_general(
        chosen_all, grad_images, (((0,), (0,)), ((), ())), precision=PRECISE
    )
    image_term = lax.dot_general(
        grad_images, mod_weight, (((1,), (1,)), ((), ())), precision=PRECISE
    )
    table_term = lax.dot_general(onehot_all, image_term, (((0,), (0,)), ((), ())), precision=PRECISE)
    noise_grad = jax.vjp(jax.nn.silu, noise_table)[1](table_term)[0]
    mod_bias_grad = lax.dynamic_slice_in_dim(
        jnp.sum(grad_images, axis=0), mine * bias_piece, bias_piece
    )
    return (
        block_out,
        input_grad,
        attn_weight_grad,
        mlp_weight_grad,
        noise_grad,
        mod_weight_grad,
        mod_bias_grad,
    )


def solution(mesh):
    fits = mesh.shape["fsdp"] == 8 and mesh.shape["blk"] == 4
    return jax.shard_map(
        plane_body if fits else body,
        mesh=mesh,
        in_specs=(
            P("fsdp", "blk", None),
            P("fsdp", "blk", None),
            P("fsdp"),
            P("fsdp"),
            P("fsdp", None),
            P("fsdp", None),
            P(None, "fsdp"),
            P("fsdp", None),
            P("fsdp"),
        ),
        out_specs=(
            P("fsdp", "blk", None),
            P("fsdp", "blk", None),
            P("fsdp", None),
            P("fsdp", None),
            P(None, "fsdp"),
            P("fsdp", None),
            P("fsdp"),
        ),
        check_vma=False,
    )
```

```python
import functools
import math

import jax
import jax.numpy as jnp
from jax import lax
from jax.experimental import pallas as pl
from jax.experimental.pallas import tpu as pltpu
from jax.sharding import PartitionSpec as P

HD = 128


EPSILON = 1e-06
PRECISE = lax.Precision.HIGHEST


def norm_mod(features, scaling, shifting):
    normed = features * lax.rsqrt(jnp.mean(features * features, axis=-1, keepdims=True) + EPSILON)
    return normed * (1.0 + scaling) + shifting


def rows_product(left_rows, right_rows):
    return lax.dot_general(
        left_rows, right_rows, (((0,), (0,)), ((), ())), preferred_element_type=jnp.float32
    )


def body(
    block_input,
    cotangent,
    bin_ids,
    image_counts,
    attn_weight,
    mlp_weight,
    noise_table,
    mod_weight,
    mod_bias,
):
    slot_count, local_tok, model_width = block_input.shape
    row_count = slot_count * local_tok
    feed_width = mlp_weight.shape[1] // 2
    head_count = model_width // HD
    blk_size = lax.axis_size("blk")
    image_tok = local_tok * blk_size
    score_scale = HD ** (-0.5)
    bias_piece = mod_bias.shape[0]
    activated = jax.nn.silu(noise_table)
    partial_mod = jnp.dot(activated, mod_weight, precision=PRECISE)
    bias_full = lax.dynamic_update_slice_in_dim(
        jnp.zeros((6 * model_width,), jnp.float32), mod_bias, lax.axis_index("fsdp") * bias_piece, 0
    )
    mod_table = lax.psum(partial_mod + bias_full[None, :], "fsdp")
    onehot = (
        bin_ids[:, None] == jnp.arange(noise_table.shape[0], dtype=jnp.int32)[None, :]
    ).astype(jnp.float32)
    mod_image = jnp.dot(onehot, mod_table, precision=PRECISE)
    shift_one, scale_one, gate_one, shift_two, scale_two, gate_two = [
        member[:, None, :] for member in jnp.split(mod_image, 6, axis=-1)
    ]
    live_mask = (jnp.arange(slot_count) < image_counts[0]).astype(jnp.float32)[:, None, None]
    features = block_input.astype(jnp.float32)
    h_one = (
        norm_mod(features, scale_one, shift_one)
        .astype(jnp.bfloat16)
        .reshape(row_count, model_width)
    )
    attn_full = lax.all_gather(attn_weight.astype(jnp.bfloat16), "fsdp", axis=0, tiled=True)
    projected = jnp.dot(
        h_one, attn_full[:, : 3 * model_width], preferred_element_type=jnp.float32
    ).astype(jnp.bfloat16)
    queries = projected[:, :model_width].reshape(slot_count, local_tok, head_count, HD)
    key_rows = projected[:, model_width : 2 * model_width].reshape(
        slot_count, local_tok, model_width
    )
    value_rows = projected[:, 2 * model_width :].reshape(slot_count, local_tok, model_width)
    all_keys, all_values = (
        lax.all_gather(key_rows, "blk", axis=1, tiled=True),
        lax.all_gather(value_rows, "blk", axis=1, tiled=True),
    )
    all_keys = all_keys.reshape(slot_count, image_tok, head_count, HD)
    all_values = all_values.reshape(slot_count, image_tok, head_count, HD)

    def scores_of(query_rows):
        return (
            jnp.einsum("sqhd,skhd->shqk", query_rows, all_keys, preferred_element_type=jnp.float32)
            * score_scale
        )

    scores = scores_of(queries)
    maximum = jnp.max(scores, axis=-1, keepdims=True)
    exponent = jnp.exp(scores - maximum)
    denominator = jnp.sum(exponent, axis=-1, keepdims=True)
    attention = exponent / denominator
    log_total = maximum + jnp.log(denominator)
    attended = (
        jnp.einsum(
            "shqk,skhd->sqhd",
            attention.astype(jnp.bfloat16),
            all_values,
            preferred_element_type=jnp.float32,
        )
        .astype(jnp.bfloat16)
        .reshape(row_count, model_width)
    )
    attn_out = jnp.dot(
        attended, attn_full[:, 3 * model_width :], preferred_element_type=jnp.float32
    ).reshape(slot_count, local_tok, model_width)
    first_sum = features + gate_one * attn_out
    h_two = (
        norm_mod(first_sum, scale_two, shift_two)
        .astype(jnp.bfloat16)
        .reshape(row_count, model_width)
    )
    mlp_full = lax.all_gather(mlp_weight.astype(jnp.bfloat16), "fsdp", axis=0, tiled=True)
    pre_gelu = jnp.dot(h_two, mlp_full[:, :feed_width], preferred_element_type=jnp.float32)
    hidden = jax.nn.gelu(pre_gelu).astype(jnp.bfloat16)
    mlp_out = jnp.einsum(
        "rf,df->rd", hidden, mlp_full[:, feed_width:], preferred_element_type=jnp.float32
    ).reshape(slot_count, local_tok, model_width)
    second_sum = first_sum + gate_two * mlp_out
    block_out = (live_mask * second_sum).astype(jnp.bfloat16)
    grad_out = cotangent.astype(jnp.float32) * live_mask
    grad_mlp = (gate_two * grad_out).astype(jnp.bfloat16).reshape(row_count, model_width)
    grad_gate_two = jnp.sum(grad_out * mlp_out, axis=1)
    grad_hidden = jnp.dot(grad_mlp, mlp_full[:, feed_width:], preferred_element_type=jnp.float32)
    grad_pre = jax.vjp(jax.nn.gelu, pre_gelu)[1](grad_hidden)[0].astype(jnp.bfloat16)
    grad_h_two = jnp.einsum(
        "rf,df->rd", grad_pre, mlp_full[:, :feed_width], preferred_element_type=jnp.float32
    ).reshape(slot_count, local_tok, model_width)
    grad_first, grad_scale_two, grad_shift_two = jax.vjp(norm_mod, first_sum, scale_two, shift_two)[
        1
    ](grad_h_two)
    grad_first = grad_first + grad_out
    grad_attn_out = (gate_one * grad_first).astype(jnp.bfloat16).reshape(row_count, model_width)
    grad_gate_one = jnp.sum(grad_first * attn_out, axis=1)
    grad_attended = jnp.einsum(
        "rd,ed->re",
        grad_attn_out,
        attn_full[:, 3 * model_width :],
        preferred_element_type=jnp.float32,
    ).astype(jnp.bfloat16)
    grad_heads = grad_attended.reshape(slot_count, local_tok, head_count, HD)
    recomputed = jnp.exp(scores_of(queries) - log_total)
    grad_weights = jnp.einsum(
        "sqhd,skhd->shqk", grad_heads, all_values, preferred_element_type=jnp.float32
    )
    row_delta = jnp.sum(recomputed * grad_weights, axis=-1, keepdims=True)
    grad_scores = (recomputed * (grad_weights - row_delta)).astype(jnp.bfloat16)
    grad_queries = (
        jnp.einsum("shqk,skhd->sqhd", grad_scores, all_keys, preferred_element_type=jnp.float32)
        * score_scale
    )
    grad_keys_all = (
        jnp.einsum("shqk,sqhd->skhd", grad_scores, queries, preferred_element_type=jnp.float32)
        * score_scale
    )
    grad_values_all = jnp.einsum(
        "shqk,sqhd->skhd",
        recomputed.astype(jnp.bfloat16),
        grad_heads,
        preferred_element_type=jnp.float32,
    )
    grad_keys, grad_values = (
        lax.psum_scatter(
            grad_keys_all.reshape(slot_count, image_tok, model_width).astype(jnp.bfloat16),
            "blk",
            scatter_dimension=1,
            tiled=True,
        ).astype(jnp.float32),
        lax.psum_scatter(
            grad_values_all.reshape(slot_count, image_tok, model_width).astype(jnp.bfloat16),
            "blk",
            scatter_dimension=1,
            tiled=True,
        ).astype(jnp.float32),
    )
    grad_qkv = jnp.concatenate(
        [
            grad_queries.reshape(row_count, model_width).astype(jnp.bfloat16),
            grad_keys.reshape(row_count, model_width).astype(jnp.bfloat16),
            grad_values.reshape(row_count, model_width).astype(jnp.bfloat16),
        ],
        axis=1,
    )
    grad_h_one = jnp.einsum(
        "rc,dc->rd", grad_qkv, attn_full[:, : 3 * model_width], preferred_element_type=jnp.float32
    ).reshape(slot_count, local_tok, model_width)
    grad_input, grad_scale_one, grad_shift_one = jax.vjp(norm_mod, features, scale_one, shift_one)[
        1
    ](grad_h_one)
    input_grad = grad_input + grad_first
    grad_mod = jnp.concatenate(
        [
            grad_shift_one[:, 0, :],
            grad_scale_one[:, 0, :],
            grad_gate_one,
            grad_shift_two[:, 0, :],
            grad_scale_two[:, 0, :],
            grad_gate_two,
        ],
        axis=-1,
    )
    bin_terms = lax.dot_general(onehot, grad_mod, (((0,), (0,)), ((), ())), precision=PRECISE)
    grad_bins = lax.psum(bin_terms, ("fsdp", "blk"))
    table_term = jnp.einsum("be,de->bd", grad_bins, mod_weight, precision=PRECISE)
    noise_grad = jax.vjp(jax.nn.silu, noise_table)[1](table_term)[0]
    mod_weight_grad = lax.dot_general(
        activated, grad_bins, (((0,), (0,)), ((), ())), precision=PRECISE
    )
    mod_bias_grad = lax.dynamic_slice_in_dim(
        jnp.sum(grad_bins, axis=0), lax.axis_index("fsdp") * bias_piece, bias_piece
    )
    h_part = h_one
    attn_part = lax.psum_scatter(
        jnp.concatenate(
            [rows_product(h_part, grad_qkv), rows_product(attended, grad_attn_out)], axis=1
        ).astype(jnp.bfloat16),
        "fsdp",
        scatter_dimension=0,
        tiled=True,
    )
    h_part = h_two
    mlp_part = lax.psum_scatter(
        jnp.concatenate(
            [rows_product(h_part, grad_pre), rows_product(grad_mlp, hidden)], axis=1
        ).astype(jnp.bfloat16),
        "fsdp",
        scatter_dimension=0,
        tiled=True,
    )
    attn_weight_grad, mlp_weight_grad = (
        lax.psum(attn_part, "blk").astype(jnp.float32),
        lax.psum(mlp_part, "blk").astype(jnp.float32),
    )
    return (
        block_out,
        input_grad,
        attn_weight_grad,
        mlp_weight_grad,
        noise_grad,
        mod_weight_grad,
        mod_bias_grad,
    )


MESH_ID = pl.DeviceIdType.MESH
VMEM_BYTES = 56 * 1024 * 1024


def contract(left, right, left_dim, right_dim):
    return lax.dot_general(
        left, right, (((left_dim,), (right_dim,)), ((), ())), preferred_element_type=jnp.float32
    )


def plane_places():
    mine = lax.axis_index("fsdp")
    plane = lax.axis_index("blk")
    core = lax.rem(mine, 2)
    col = lax.rem(mine // 2, 2)
    row = mine // 4

    def at(flip):
        flip_row, flip_col, flip_core = flip // 4, (flip // 2) % 2, flip % 2
        new_row = 1 - row if flip_row else row
        new_col = 1 - col if flip_col else col
        new_core = 1 - core if flip_core else core
        return new_row * 4 + new_col * 2 + new_core

    return mine, plane, at


def greet(places):
    barrier = pltpu.get_barrier_semaphore()
    for place in places:
        pl.semaphore_signal(barrier, inc=1, device_id=place, device_id_type=MESH_ID)
    pl.semaphore_wait(barrier, len(places))


def remote(src, dst, send_sem, recv_sem, place):
    return pltpu.make_async_remote_copy(
        src_ref=src,
        dst_ref=dst,
        send_sem=send_sem,
        recv_sem=recv_sem,
        device_id=place,
        device_id_type=MESH_ID,
    )


PIECES = 4


def softmax_rows(queries, key_rows):
    scores = contract(queries, key_rows, 1, 1) * HD ** (-0.5)
    exponent = jnp.exp(scores - jnp.max(scores, axis=-1, keepdims=True))
    return exponent / jnp.sum(exponent, axis=-1, keepdims=True)


def rms_scale(features):
    return lax.rsqrt(jnp.mean(features * features, axis=-1, keepdims=True) + EPSILON)


CHUNKS = 12
FIRST = 4
UP_TICK = 4
LATE_TICK = 8
EARLY = 8
HALF_ROWS = 128
BAND = 32


def flipped(mine, flip):
    total = 0
    for bit in (1, 2, 4):
        total = total + lax.rem(mine // bit + flip // bit, 2) * bit
    return total


def bands(count, step):
    @pl.loop(0, count // BAND)
    def _(index):
        step(pl.ds(pl.multiple_of(index * BAND, BAND), BAND))


def plain(ref, rows):
    return ref[rows, :].astype(jnp.float32)


def column_products(source, right, cols, staged, result, load_sems, store_sems):
    rows = cols.shape[-1]
    count = result.shape[0]

    def load(block):
        slot = lax.rem(block, 2)
        return pltpu.make_async_copy(
            source.at[:, :, pl.ds(pl.multiple_of(block * rows, rows), rows)],
            cols.at[slot],
            load_sems.at[slot],
        )

    def store(block):
        slot = lax.rem(block, 2)
        return pltpu.make_async_copy(
            staged.at[slot, pl.ds(0, count)], result.at[:, block], store_sems.at[slot]
        )

    load(0).start()

    @pl.loop(0, 8)
    def _(block):
        slot = lax.rem(block, 2)
        load(block).wait()

        @pl.when(block < 7)
        def _():
            load(block + 1).start()

        @pl.when(block >= 2)
        def _():
            store(block - 2).wait()

        product = contract(cols[slot].reshape(8 * rows, rows), right[...], 0, 0)
        for number in range(count):
            staged[slot, number] = product[:, number * rows : (number + 1) * rows].astype(
                jnp.bfloat16
            )
        store(block).start()

    store(6).wait()
    store(7).wait()


GELU_SCALE = (2.0 / math.pi) ** 0.5


def gelu_and_slope(pre):
    squared = pre * pre
    bend = jnp.tanh(GELU_SCALE * (pre + 0.044715 * (squared * pre)))
    rise = 0.5 * (1.0 + bend)
    slope = rise + 0.5 * pre * (1.0 - bend * bend) * (GELU_SCALE * (1.0 + 3.0 * 0.044715 * squared))
    return pre * rise, slope


class Plane:
    def __init__(self):
        self.mine, self.place, self.at = plane_places()

    def to(self, flip):
        return (self.at(flip), self.place)

    def got(self, ref, sem):
        remote(ref, ref, sem, sem, (self.mine, self.place)).wait_recv()

    def gone(self, ref, sem):
        remote(ref, ref, sem, sem, (self.mine, self.place)).wait_send()


def scatter_flow(plane, own_of, fetch, peer, far, near, sems, finish):
    core_recv, far_send, far_recv, near_send, near_recv = sems
    rows = near.shape[1]
    half = rows // 2
    sent = []

    def add(slot, start, count, extra=None):
        own = own_of(slot)

        def step(band):
            at = pl.ds(pl.multiple_of(start + band.start, BAND), BAND)
            total = plain(own, at) + plain(peer.at[slot], at)
            if extra is not None:
                total = total + plain(extra, band)
            peer[slot, at, :] = total.astype(jnp.bfloat16)

        bands(count, step)

    def send(src, dst, flip, send_sem, recv_sem):
        copy = remote(src, dst, send_sem, recv_sem, plane.to(flip))
        copy.start()
        sent.append(copy)

    def send_near(slot, part):
        at = pl.ds(part * half, half)
        index = (slot - 1) * 2 + part
        send(
            peer.at[slot, at],
            near.at[slot - 1, at],
            2 * slot,
            near_send.at[index],
            near_recv.at[index],
        )

    fetch(3)
    plane.got(peer.at[3], core_recv.at[3])
    add(3, 0, rows)
    send(peer.at[3, pl.ds(0, half)], far.at[0], 2, far_send.at[0], far_recv.at[0])
    send(peer.at[3, pl.ds(half, half)], far.at[1], 4, far_send.at[1], far_recv.at[1])
    fetch(1)
    plane.got(peer.at[1], core_recv.at[1])
    add(1, 0, half)
    send_near(1, 0)
    fetch(2)
    plane.got(peer.at[2], core_recv.at[2])
    add(2, half, half)
    send_near(2, 1)
    yield
    plane.got(far.at[0], far_recv.at[0])
    add(2, 0, half, far.at[0])
    send_near(2, 0)
    plane.got(far.at[1], far_recv.at[1])
    add(1, half, half, far.at[1])
    send_near(1, 1)
    fetch(0)
    plane.got(peer.at[0], core_recv.at[0])
    yield
    for slot in (1, 2):
        for part in (0, 1):
            at = pl.ds(part * half, half)
            plane.got(near.at[slot - 1, at], near_recv.at[(slot - 1) * 2 + part])
    own = own_of(0)

    def step(at):
        finish(
            at,
            plain(own, at)
            + plain(peer.at[0], at)
            + plain(near.at[0], at)
            + plain(near.at[1], at),
        )

    bands(rows, step)
    for copy in sent:
        copy.wait_send()


def back_kernel(
    down_low,
    up_weight,
    hidden_all,
    slope_all,
    grad_mlp_all,
    h_two_all,
    first_grads,
    h_all,
    qkv_all,
    attended_all,
    qkv_weight,
    out_weight,
    features,
    first_sum,
    attn_out,
    grad_out,
    mod,
    shares,
    token_out,
    token_grad,
    mod_out,
    more,
    partial_out,
    land_a,
    land_b,
    first_buf,
    second_buf,
    stage,
    own_pair,
    grad_all,
    grad_first,
    saved_grad,
    cols_buf,
    qkv_buf,
    attended_buf,
    staged_buf,
    out_sum,
    sum_buf,
    in_buf,
    half_buf,
    half_in,
    mod_sum,
    mod_land,
    core_send,
    core_recv,
    far_send,
    far_recv,
    near_send,
    near_recv,
    stage_sems,
    gather_send,
    gather_recv,
    load_sems,
    weight_sems,
    z_sems,
    x_sems,
    zload_sems,
    token_sems,
    mod_sems,
    mod_gather_sems,
):
    plane = Plane()
    mine, place = plane.mine, plane.place
    rows, width = features.shape
    at = plane.at
    own_grad, image_out = own_pair.at[0], own_pair.at[1]
    is_mid = (place == 1) | (place == 2)
    my_half = pl.ds(pl.multiple_of(jnp.where(place == 2, HALF_ROWS, 0), HALF_ROWS), HALF_ROWS)
    other_half = pl.ds(pl.multiple_of(jnp.where(place == 2, 0, HALF_ROWS), HALF_ROWS), HALF_ROWS)
    partner = (mine, 3 - place)
    outer = (mine, jnp.where(place == 1, 0, 3))
    inner = (mine, jnp.where(place == 0, 1, 2))
    others = [lax.rem(place + step, 4) for step in (1, 2, 3)]
    greet([plane.to(flip) for flip in range(1, 8)] + [(mine, other) for other in others])

    def z_copy(kind, chunk, src, dst, target):
        return remote(src, dst, z_sems.at[0, kind, chunk], z_sems.at[1, kind, chunk], target)

    def own_chunk(chunk):
        return first_grads.at[chunk] if chunk < FIRST else more.at[chunk - FIRST]

    def start_outward(chunk):
        z_copy(0, chunk, own_chunk(chunk), land_a.at[chunk], inner).start()

    def stage_d(k):
        region = shares.at[k, :, other_half]
        plane.got(region, z_sems.at[1, 2, k])
        z_copy(4, k, region, region, outer).start()

    def stage_x(k):
        region = shares.at[k, :, my_half]
        plane.got(region, x_sems.at[1, k])
        z_copy(2, k, region, region, partner).start()
        z_copy(3, k, region, region, outer).start()

    def stage_f(k):
        slot = k % 2
        load = pltpu.make_async_copy(land_b.at[k], half_in, zload_sems.at[2])
        plane.got(land_b.at[k], z_sems.at[1, 1, k])
        load.start()
        if k >= 2:
            plane.gone(half_buf.at[slot, pl.ds(0, 7)], x_sems.at[0, k - 2])
        load.wait()

        @pl.loop(0, 8)
        def _(block):
            half_buf[slot, block] = (
                sum_buf[slot, block, my_half, :].astype(jnp.float32)
                + half_in[block].astype(jnp.float32)
            ).astype(jnp.bfloat16)

        if k == CHUNKS - 1:
            pltpu.make_async_copy(
                half_buf.at[slot], shares.at[k, :, my_half], x_sems.at[1, k]
            ).start()
            return
        pltpu.make_async_copy(
            half_buf.at[slot, mine], shares.at[k, mine, my_half], x_sems.at[1, k]
        ).start()
        for flip in (6, 7, 2, 4, 3, 5, 1):
            remote(
                half_buf.at[slot, at(flip)],
                shares.at[k, mine, my_half],
                x_sems.at[0, k],
                x_sems.at[1, k],
                plane.to(flip),
            ).start()

    def stage_s(k):
        slot = k % 2
        if k >= 2:
            plane.gone(sum_buf.at[slot, :, other_half], z_sems.at[0, 1, k - 2])
        own_load = pltpu.make_async_copy(own_chunk(k), sum_buf.at[slot], zload_sems.at[0])
        own_load.start()
        in_load = pltpu.make_async_copy(land_a.at[k], in_buf, zload_sems.at[1])
        plane.got(land_a.at[k], z_sems.at[1, 0, k])
        in_load.start()
        own_load.wait()
        in_load.wait()

        @pl.loop(0, 8)
        def _(block):
            sum_buf[slot, block] = (
                sum_buf[slot, block].astype(jnp.float32) + in_buf[block].astype(jnp.float32)
            ).astype(jnp.bfloat16)

        z_copy(1, k, sum_buf.at[slot, :, other_half], land_b.at[k], partner).start()

    def start_tick(chunk):
        return LATE_TICK if chunk >= EARLY else (UP_TICK if chunk >= FIRST else -1)

    def tick(now):
        @pl.when(jnp.logical_not(is_mid))
        def _():
            for chunk in range(CHUNKS):
                if start_tick(chunk) == now:
                    start_outward(chunk)

        @pl.when(is_mid)
        def _():
            if 0 <= now - 3 < CHUNKS:
                stage_d(now - 3)
            if 0 <= now - 2 < CHUNKS:
                stage_x(now - 2)
            if 0 <= now - 1 < CHUNKS:
                stage_f(now - 1)
            if now < CHUNKS:
                stage_s(now)

    @pl.when(jnp.logical_not(is_mid))
    def _():
        for chunk in range(CHUNKS):
            if start_tick(chunk) < 0:
                start_outward(chunk)

    attended_load = pltpu.make_async_copy(attended_all, attended_buf, load_sems.at[0])
    attended_load.start()
    feed = up_weight.shape[-1]
    down_part, up_part = pl.ds(0, feed), pl.ds(feed, feed)

    pltpu.make_async_copy(
        down_low.at[mine], grad_all.at[mine, :, down_part], weight_sems.at[0, 0]
    ).start()
    for flip in (6, 7, 2, 4, 3, 5, 1):
        remote(
            down_low.at[at(flip)],
            grad_all.at[mine, :, down_part],
            weight_sems.at[0, flip],
            weight_sems.at[1, flip],
            plane.to(flip),
        ).start()
    up_load = pltpu.make_async_copy(up_weight, grad_all.at[:, :, up_part], load_sems.at[5])
    up_load.start()
    mod_sum[...] = jnp.zeros_like(mod_sum)
    row = {
        name: number
        for number, name in enumerate(
            ("shift_one", "scale_one", "gate_one", "shift_two", "scale_two", "gate_two", "live")
        )
    }

    def mod_row(name):
        return mod[pl.ds(row[name], 1), :]

    def accumulate(name, value):
        mod_sum[pl.ds(row[name], 1), :] += jnp.sum(value, axis=0, keepdims=True)

    def sems(number):
        return (
            core_recv.at[number],
            far_send.at[number],
            far_recv.at[number],
            near_send.at[number],
            near_recv.at[number],
        )

    def give(src, buf, number, slot):
        remote(
            src, buf.at[slot], core_send.at[number, slot], core_recv.at[number, slot], plane.to(1)
        ).start()

    def staged_flow(source, buf, number, finish):
        for slot in (3, 1, 2, 0):
            give(source.at[at((2 * slot) ^ 1)], buf, number, slot)
        order = {3: 0, 1: 1, 2: 0, 0: 1}

        def load(slot):
            return pltpu.make_async_copy(
                source.at[at(2 * slot)], stage.at[order[slot]], stage_sems.at[number, slot]
            )

        load(3).start()
        load(1).start()

        def fetch(slot):
            if slot == 2:
                load(2).start()
            if slot == 0:
                load(0).start()
            load(slot).wait()

        return scatter_flow(
            plane,
            lambda slot: stage.at[order[slot]],
            fetch,
            buf.at[pl.ds(0, 4)],
            Halves(buf.at[6], rows // 2),
            buf.at[pl.ds(4, 2)],
            sems(number),
            finish,
        )

    def run(flow, first_tick):
        for step, _ in enumerate(flow):
            tick(first_tick + step)

    def finish_out(where, value):
        base = first_sum[where, :]
        own_pair[1, where, :] = (
            mod_row("live") * (base + mod_row("gate_two") * value)
        ).astype(jnp.bfloat16)
        accumulate("gate_two", plain(grad_out, where) * value)

    token_copies = []

    def return_tokens(image, result, number):
        piece = rows // 4
        own = pltpu.make_async_copy(
            image.at[pl.ds(pl.multiple_of(place * piece, piece), piece)],
            result.at[place],
            token_sems.at[0, number, 0],
        )
        own.start()
        token_copies.append(own)
        for step, other in enumerate(others):
            copy = remote(
                image.at[pl.ds(pl.multiple_of(other * piece, piece), piece)],
                result.at[place],
                token_sems.at[0, number, step + 1],
                token_sems.at[1, number, step + 1],
                (mine, other),
            )
            copy.start()
            token_copies.append(copy)


    def back_norm(source, value, scale_name, shift_name):
        inverse = rms_scale(source)
        unit = source * inverse
        inner = value * (1.0 + mod_row(scale_name))
        accumulate(scale_name, value * unit)
        accumulate(shift_name, value)
        return (inner - unit * jnp.mean(inner * unit, axis=-1, keepdims=True)) * inverse

    def finish_feed(where, value):
        total = back_norm(first_sum[where, :], value, "scale_two", "shift_two") + plain(
            grad_out, where
        )
        grad_first[where, :] = total
        accumulate("gate_one", total * plain(attn_out, where))
        low_grad = (mod_row("gate_one") * total).astype(jnp.bfloat16)
        own_pair[0, where, :] = low_grad
        grad_all[mine, where, :] = low_grad

    up_load.wait()
    pltpu.make_async_copy(
        down_low.at[mine], grad_all.at[mine, :, down_part], weight_sems.at[0, 0]
    ).wait()
    tick(0)
    tick(1)
    for flip in range(1, 8):
        plane.got(grad_all.at[at(flip), :, down_part], weight_sems.at[1, flip])
        plane.gone(down_low.at[0], weight_sems.at[0, flip])

    def image_loads(step):
        image = flipped(mine, step)
        return [
            pltpu.make_async_copy(
                hidden_all.at[image], stage.at[0, :, pl.ds(0, feed)], load_sems.at[6]
            ),
            pltpu.make_async_copy(
                slope_all.at[image], stage.at[0, :, pl.ds(feed, feed)], load_sems.at[7]
            ),
            pltpu.make_async_copy(grad_mlp_all.at[image], stage.at[1], load_sems.at[8]),
        ]

    def out_store(step):
        return pltpu.make_async_copy(
            own_pair.at[lax.rem(step, 2)],
            partial_out.at[flipped(mine, step)],
            load_sems.at[9 + lax.rem(step, 2)],
        )

    for load in image_loads(0):
        load.start()

    @pl.loop(0, 8)
    def _(step):
        for load in image_loads(step):
            load.wait()
        image = flipped(mine, step)
        image_rows = pl.ds(pl.multiple_of(image * rows, rows), rows)

        @pl.when(step >= 2)
        def _():
            out_store(step - 2).wait()

        down = grad_all[:, :, 0:feed].reshape(8 * rows, feed)
        grad_hidden = contract(stage[1], down, 1, 0)
        saved_grad[image_rows, :] = (
            grad_hidden * stage[0, :, feed : 2 * feed].astype(jnp.float32)
        ).astype(jnp.bfloat16)
        own_pair[lax.rem(step, 2)] = contract(stage[0, :, 0:feed], down, 1, 1).astype(jnp.bfloat16)
        out_store(step).start()

        @pl.when(step < 7)
        def _():
            for load in image_loads(step + 1):
                load.start()

        up = grad_all[:, :, feed : 2 * feed].reshape(8 * rows, feed)
        second_buf[step] = contract(saved_grad[image_rows, :], up, 1, 1).astype(jnp.bfloat16)
        for number in (1, 3, 5, 7):

            @pl.when(step == number)
            def _(number=number):
                give(second_buf.at[number], first_buf, 1, number // 2)

        @pl.when(step == 3)
        def _():
            tick(2)

    out_store(6).wait()
    out_store(7).wait()
    tick(3)
    column_products(
        h_two_all,
        saved_grad,
        cols_buf,
        staged_buf,
        more.at[pl.ds(0, 4)],
        load_sems.at[pl.ds(3, 2)],
        load_sems.at[pl.ds(11, 2)],
    )

    def own_flow(number, finish):
        return scatter_flow(
            plane,
            lambda slot: second_buf.at[2 * slot],
            lambda slot: None,
            first_buf.at[pl.ds(0, 4)],
            Halves(first_buf.at[6], rows // 2),
            first_buf.at[pl.ds(4, 2)],
            sems(number),
            finish,
        )

    run(own_flow(1, finish_feed), 4)
    for slot in range(4):
        plane.gone(second_buf.at[slot], core_send.at[1, slot])

    gather = Gather(plane, own_grad, grad_all, gather_send, gather_recv)
    gather.start()

    def qkv_load(step):
        return pltpu.make_async_copy(
            qkv_all.at[flipped(mine, step)], qkv_buf.at[lax.rem(step, 2)], load_sems.at[1 + lax.rem(step, 2)]
        )

    qkv_load(0).start()
    attended_load.wait()
    out_sum[...] = jnp.zeros_like(out_sum)
    columns = qkv_buf.shape[-1]
    third = columns // 3
    scale = HD ** (-0.5)

    @pl.loop(0, 8)
    def _(step):
        for number in range(8):

            @pl.when(step == number)
            def _(number=number):
                gather.step(number)
                if number == 7:
                    gather.finish()

        image = flipped(mine, step)
        slot = lax.rem(step, 2)
        qkv_load(step).wait()

        @pl.when(step < 7)
        def _():
            qkv_load(step + 1).start()

        grad = grad_all[image]
        grad_attended = contract(grad, out_weight[...], 1, 1).astype(jnp.bfloat16)
        image_rows = pl.ds(pl.multiple_of(image * rows, rows), rows)
        for head in range(third // HD):
            begin = head * HD
            queries = qkv_buf[slot, :, begin : begin + HD]
            key_rows = qkv_buf[slot, :, third + begin : third + begin + HD]
            value_rows = qkv_buf[slot, :, 2 * third + begin : 2 * third + begin + HD]
            grad_head = grad_attended[:, begin : begin + HD]
            attention = softmax_rows(queries, key_rows)
            grad_weights = contract(grad_head, value_rows, 1, 1)
            row_delta = jnp.sum(attention * grad_weights, axis=-1, keepdims=True)
            grad_scores = (attention * (grad_weights - row_delta)).astype(jnp.bfloat16)
            saved_grad[image_rows, begin : begin + HD] = (
                contract(grad_scores, key_rows, 1, 0) * scale
            ).astype(jnp.bfloat16)
            saved_grad[image_rows, third + begin : third + begin + HD] = (
                contract(grad_scores, queries, 0, 0) * scale
            ).astype(jnp.bfloat16)
            saved_grad[image_rows, 2 * third + begin : 2 * third + begin + HD] = contract(
                attention.astype(jnp.bfloat16), grad_head, 0, 0
            ).astype(jnp.bfloat16)
        out_sum[...] += contract(attended_buf[image], grad, 0, 0)
        second_buf[step] = contract(saved_grad[image_rows, 0:columns], qkv_weight[...], 1, 1).astype(
            jnp.bfloat16
        )
        for number in (1, 3, 5, 7):

            @pl.when(step == number)
            def _(number=number):
                give(second_buf.at[number], first_buf, 2, number // 2)

        for number, now in ((2, 6), (5, 7)):

            @pl.when(step == number)
            def _(now=now):
                tick(now)

    for block in range(8):
        staged_buf[0, 0] = out_sum[:, block * rows : (block + 1) * rows].astype(jnp.bfloat16)
        pltpu.sync_copy(staged_buf.at[0, 0], more.at[7, block])
    column_products(
        h_all,
        saved_grad.at[:, pl.ds(0, columns)],
        cols_buf,
        staged_buf,
        more.at[pl.ds(4, 3)],
        load_sems.at[pl.ds(3, 2)],
        load_sems.at[pl.ds(11, 2)],
    )

    def finish_input(where, value):
        total = back_norm(plain(features, where), value, "scale_one", "shift_one")
        own_pair[0, where, :] = (total + grad_first[where, :]).astype(jnp.bfloat16)

    run(own_flow(2, finish_input), 8)
    return_tokens(own_grad, token_grad, 1)
    run(staged_flow(partial_out, grad_all, 0, finish_out), 10)
    return_tokens(image_out, token_out, 0)

    mod_copies = []
    mod_sum[7:8, :] = mod[7:8, :]
    mod_rows = pl.ds(pl.multiple_of(place * 8, 8), 8)
    mod_land[mod_rows, :] = mod_sum[...]
    for step, other in enumerate(others):
        copy = remote(
            mod_sum, mod_land.at[mod_rows], mod_sems.at[0, step], mod_sems.at[1, step], (mine, other)
        )
        copy.start()
        mod_copies.append(copy)
    tick(12)
    for copy in mod_copies:
        copy.wait_recv()
    own = pltpu.make_async_copy(mod_land, mod_out.at[mine], mod_sems.at[0, 3])
    own.start()
    mod_gather = Gather(plane, mod_land, mod_out, mod_gather_sems.at[0], mod_gather_sems.at[1])
    mod_gather.start()
    tick(13)
    mod_gather.middle()
    mod_gather.far()
    for flip in (1, 3, 5, 7):
        mod_gather.crossed(flip)
    mod_gather.finish()
    tick(14)
    own.wait()
    for copy in mod_copies:
        copy.wait_send()
    for copy in token_copies:
        copy.wait()
    for number in (0, 2):
        for slot in range(4):
            plane.gone(second_buf.at[slot], core_send.at[number, slot])

    @pl.when(is_mid)
    def _():
        for k in (CHUNKS - 2, CHUNKS - 1):
            plane.gone(sum_buf.at[k % 2, :, other_half], z_sems.at[0, 1, k])
        plane.gone(half_buf.at[0, pl.ds(0, 7)], x_sems.at[0, CHUNKS - 2])
        for k in range(CHUNKS):
            plane.gone(shares.at[k, :, my_half], z_sems.at[0, 2, k])
            plane.gone(shares.at[k, :, my_half], z_sems.at[0, 3, k])
            plane.gone(shares.at[k, :, other_half], z_sems.at[0, 4, k])

    @pl.when(jnp.logical_not(is_mid))
    def _():
        first = pl.ds(pl.multiple_of(jnp.where(place == 0, 0, HALF_ROWS), HALF_ROWS), HALF_ROWS)
        second = pl.ds(pl.multiple_of(jnp.where(place == 0, HALF_ROWS, 0), HALF_ROWS), HALF_ROWS)
        for k in range(CHUNKS):
            plane.gone(land_a.at[k], z_sems.at[0, 0, k])
            plane.got(shares.at[k, :, first], z_sems.at[1, 3, k])
            plane.got(shares.at[k, :, second], z_sems.at[1, 4, k])


def back_part(*operands):
    h_all, qkv_weight = operands[7], operands[10]
    _, rows, width = h_all.shape
    columns = qkv_weight.shape[1]
    feed = operands[1].shape[-1]
    low, full = jnp.bfloat16, jnp.float32
    dma = pltpu.SemaphoreType.DMA
    anywhere, inside = pl.BlockSpec(memory_space=pl.ANY), pl.BlockSpec(memory_space=pltpu.VMEM)
    return pl.pallas_call(
        back_kernel,
        out_shape=[
            jax.ShapeDtypeStruct((CHUNKS, 8, rows, rows), low),
            jax.ShapeDtypeStruct((4, rows // 4, width), low),
            jax.ShapeDtypeStruct((4, rows // 4, width), low),
            jax.ShapeDtypeStruct((8, 32, width), full),
            jax.ShapeDtypeStruct((CHUNKS - FIRST, 8, rows, rows), low),
            jax.ShapeDtypeStruct((8, rows, width), low),
            jax.ShapeDtypeStruct((CHUNKS, 8, rows, rows), low),
            jax.ShapeDtypeStruct((CHUNKS, 8, HALF_ROWS, rows), low),
        ],
        in_specs=[anywhere] * 10 + [inside] * 7,
        out_specs=[anywhere] * 8,
        scratch_shapes=[
            pltpu.VMEM((7, rows, width), low),
            pltpu.VMEM((8, rows, width), low),
            pltpu.VMEM((2, rows, width), low),
            pltpu.VMEM((2, rows, width), low),
            pltpu.VMEM((8, rows, width), low),
            pltpu.VMEM((rows, width), full),
            pltpu.VMEM((8 * rows, feed), low),
            pltpu.VMEM((2, 8, rows, rows), low),
            pltpu.VMEM((2, rows, columns), low),
            pltpu.VMEM((8, rows, columns // 3), low),
            pltpu.VMEM((2, 4, rows, rows), low),
            pltpu.VMEM((columns // 3, width), full),
            pltpu.VMEM((2, 8, rows, rows), low),
            pltpu.VMEM((8, rows, rows), low),
            pltpu.VMEM((2, 8, HALF_ROWS, rows), low),
            pltpu.VMEM((8, HALF_ROWS, rows), low),
            pltpu.VMEM((8, width), full),
            pltpu.VMEM((32, width), full),
            dma((3, 4)),
            dma((3, 4)),
            dma((3, 2)),
            dma((3, 2)),
            dma((3, 4)),
            dma((3, 4)),
            dma((2, 4)),
            dma((7 * PIECES,)),
            dma((7 * PIECES,)),
            dma((13,)),
            dma((2, 8)),
            dma((2, 5, CHUNKS)),
            dma((2, CHUNKS)),
            dma((3,)),
            dma((2, 2, 4)),
            dma((2, 4)),
            dma((2, 7 * PIECES)),
        ],
        compiler_params=pltpu.CompilerParams(
            collective_id=4, has_side_effects=True, vmem_limit_bytes=63 * 1024 * 1024
        ),
        name="back_part",
    )(*operands)


def mlp_spread_kernel(share_ref, out_ref):
    size = share_ref.shape[-1]
    for number in range(4):
        out_ref[:, number * size : (number + 1) * size] = share_ref[number, 0].astype(jnp.float32)


def mlp_spread(shares):
    rows = shares.shape[2]
    return pl.pallas_call(
        mlp_spread_kernel,
        grid=(2, 8),
        out_shape=jax.ShapeDtypeStruct((rows, 64 * rows), jnp.float32),
        in_specs=[pl.BlockSpec((4, 1, rows, rows), lambda part, block: (1 - part, block, 0, 0))],
        out_specs=pl.BlockSpec((rows, 4 * rows), lambda part, block: (0, part * 8 + block)),
        compiler_params=pltpu.CompilerParams(vmem_limit_bytes=VMEM_BYTES),
        name="mlp_spread",
    )(shares)


def attn_spread_kernel(share_ref, out_ref):
    size = share_ref.shape[-1]
    for number in range(8):
        out_ref[:, number * size : (number + 1) * size] = share_ref[0, number].astype(jnp.float32)


def attn_spread(shares):
    rows = shares.shape[2]
    return pl.pallas_call(
        attn_spread_kernel,
        grid=(4,),
        out_shape=jax.ShapeDtypeStruct((rows, 32 * rows), jnp.float32),
        in_specs=[pl.BlockSpec((1, 8, rows, rows), lambda part: (EARLY + part, 0, 0, 0))],
        out_specs=pl.BlockSpec((rows, 8 * rows), lambda part: (0, part)),
        compiler_params=pltpu.CompilerParams(vmem_limit_bytes=VMEM_BYTES),
        name="attn_spread",
    )(shares)


class Gather:
    def __init__(self, plane, own, result, send_sems, recv_sems):
        self.plane, self.own, self.result = plane, own, result
        self.send_sems, self.recv_sems = send_sems, recv_sems
        self.piece = own.shape[0] // PIECES

    def put(self, src, owner, part, flip, slot):
        remote(
            src,
            self.result.at[owner, pl.ds(part * self.piece, self.piece)],
            self.send_sems.at[slot],
            self.recv_sems.at[slot],
            self.plane.to(flip),
        ).start()

    def arrived(self, flip, part, slot):
        ref = self.result.at[self.plane.at(flip), pl.ds(part * self.piece, self.piece)]
        self.plane.got(ref, self.recv_sems.at[slot])
        return ref

    def start(self):
        mine = self.plane.mine
        for part in range(PIECES):
            src = self.own.at[pl.ds(part * self.piece, self.piece)]
            self.put(src, mine, part, 2, part)
            self.put(src, mine, part, 4, PIECES + part)
            self.put(src, mine, part, 1, 3 * PIECES + part)

    def middle(self):
        at = self.plane.at
        for part in range(PIECES):
            got = self.arrived(2, part, part)
            if part < PIECES // 2:
                self.put(got, at(2), part, 4, 2 * PIECES + part)
            self.put(got, at(2), part, 1, 4 * PIECES + part)
            got = self.arrived(4, part, PIECES + part)
            if part >= PIECES // 2:
                self.put(got, at(4), part, 2, 2 * PIECES + part)
            self.put(got, at(4), part, 1, 5 * PIECES + part)

    def far(self):
        for part in range(PIECES):
            got = self.arrived(6, part, 2 * PIECES + part)
            self.put(got, self.plane.at(6), part, 1, 6 * PIECES + part)

    def crossed(self, flip):
        for part in range(PIECES):
            self.arrived(flip, part, (3 + flip // 2) * PIECES + part)

    def step(self, number):
        if number == 2:
            self.middle()
        if number == 6:
            self.far()
        if number % 2:
            self.crossed(number)

    def finish(self):
        for slot in range(7 * PIECES):
            self.plane.gone(self.own.at[pl.ds(0, self.piece)], self.send_sems.at[slot])


class Halves:
    def __init__(self, ref, half):
        self.ref, self.half = ref, half

    @property
    def at(self):
        return self

    def __getitem__(self, number):
        return self.ref.at[pl.ds(number * self.half, self.half)]


def front_kernel(
    bin_ids,
    image_counts,
    noise,
    mod_bias,
    block_input,
    cotangent,
    attn_weight,
    mlp_weight,
    mod_weight,
    qkv_weight,
    out_weight,
    up_weight,
    down_low,
    h_one_all,
    h_two_all,
    grad_mlp_all,
    qkv_all,
    attended_all,
    hidden_all,
    slope_all,
    first_grads,
    features,
    first_sum,
    attn_out,
    grad_out,
    mod,
    load_buf,
    qkv_stage,
    up_stage,
    weight_buf,
    hidden_buf,
    cols_buf,
    staged_buf,
    h_all,
    qkv_buf,
    attended_buf,
    part_buf,
    scatter_buf,
    own_h,
    own_grad,
    own_next,
    bin_row,
    bin_land,
    mod_part,
    mod_land,
    load_sems,
    token_sems,
    bin_sems,
    mod_sems,
    weight_sems,
    gather_sems,
    core_send,
    core_recv,
    far_send,
    far_recv,
    near_send,
    near_recv,
    copy_sems,
):
    plane = Plane()
    mine, place, at = plane.mine, plane.place, plane.at
    rows, width = own_h.shape
    feed = up_stage.shape[-1]
    columns = qkv_stage.shape[-1]
    third = columns // 3
    piece = rows // 4
    others = [lax.rem(place + step, 4) for step in (1, 2, 3)]
    flips = (6, 7, 2, 4, 3, 5, 1, 0)
    greet([plane.to(flip) for flip in range(1, 8)] + [(mine, other) for other in others])

    token_copies = []
    my_rows = pl.ds(pl.multiple_of(place * piece, piece), piece)
    for number, (source, result) in enumerate(((block_input, features), (cotangent, grad_out))):
        copies = [
            pltpu.make_async_copy(
                source.at[place], result.at[my_rows], token_sems.at[0, number, 0]
            )
        ]
        for step, other in enumerate(others):
            copies.append(
                remote(
                    source.at[other],
                    result.at[my_rows],
                    token_sems.at[0, number, step + 1],
                    token_sems.at[1, number, step + 1],
                    (mine, other),
                )
            )
        for copy in copies:
            copy.start()
        token_copies.append(copies)

    lanes = lax.broadcasted_iota(jnp.int32, bin_row.shape, 1)
    bin_row[...] = jnp.where(lanes == bin_ids[place], 1.0, 0.0).astype(jnp.float32)
    bin_land[mine] = bin_row[...]
    bin_copies = [
        remote(
            bin_row, bin_land.at[mine], bin_sems.at[0, flip], bin_sems.at[1, flip], plane.to(flip)
        )
        for flip in range(1, 8)
    ]
    for copy in bin_copies:
        copy.start()

    def load_columns(source, slot, begins, size):
        return [
            pltpu.make_async_copy(
                source.at[:, pl.ds(begin, size)],
                load_buf.at[slot, :, pl.ds(number * size, size)],
                load_sems.at[slot, number],
            )
            for number, begin in enumerate(begins)
        ]

    def cast_and_send(source, begins_of, size, stage, result, kind):
        loads = [load_columns(source, step % 2, begins_of(at(flip)), size) for step, flip in enumerate(flips)]
        total = size * len(loads[0])
        for load in loads[0]:
            load.start()
        for step, flip in enumerate(flips):
            if step + 1 < len(flips):
                for load in loads[step + 1]:
                    load.start()
            for load in loads[step]:
                load.wait()

            def cast(band, step=step):
                stage[step, band, :] = load_buf[step % 2, band, :total].astype(jnp.bfloat16)

            bands(rows, cast)
            if flip:
                remote(
                    stage.at[step],
                    result.at[mine],
                    weight_sems.at[0, kind, flip],
                    weight_sems.at[1, kind, flip],
                    plane.to(flip),
                ).start()
            else:
                pltpu.make_async_copy(
                    stage.at[step], result.at[mine], weight_sems.at[0, kind, 0]
                ).start()

    def weights_arrived(result, kind):
        for flip in range(1, 8):
            plane.got(result.at[at(flip)], weight_sems.at[1, kind, flip])

    def weights_gone(stage, result, kind):
        pltpu.make_async_copy(stage.at[7], result.at[mine], weight_sems.at[0, kind, 0]).wait()
        for flip in range(1, 8):
            plane.gone(stage.at[0], weight_sems.at[0, kind, flip])

    cast_and_send(
        attn_weight,
        lambda owner: [number * width + owner * third for number in range(3)],
        third,
        qkv_stage,
        qkv_weight,
        0,
    )

    for copy in bin_copies:
        copy.wait_recv()
    bins = noise.shape[0]
    activated = noise[...] / (1.0 + jnp.exp(-noise[...]))
    chosen = jnp.dot(
        bin_land[:, 0, :bins], activated, precision=PRECISE, preferred_element_type=jnp.float32
    )

    def load_mod(number):
        return pltpu.make_async_copy(
            mod_weight.at[:, pl.ds(number * width, width)],
            load_buf.at[number % 2],
            load_sems.at[number % 2, 0],
        )

    load_mod(0).start()
    mod_part[...] = jnp.zeros_like(mod_part)
    for number in range(6):
        if number < 5:
            load_mod(number + 1).start()
        load_mod(number).wait()
        mod_part[:, number, :] = jnp.dot(
            chosen, load_buf[number % 2], precision=PRECISE, preferred_element_type=jnp.float32
        )
    quarter = width // 4
    for number in range(3):
        index = 3 * mine + number
        where = pl.ds(pl.multiple_of(lax.rem(index, 4) * quarter, quarter), quarter)
        for image in range(8):
            mod_part[image, pl.ds(index // 4, 1), where] += mod_bias[
                :, number * quarter : (number + 1) * quarter
            ]
    mod_copies = [
        remote(
            mod_part.at[at(flip)],
            mod_land.at[mine],
            mod_sems.at[0, flip],
            mod_sems.at[1, flip],
            plane.to(flip),
        )
        for flip in range(1, 8)
    ]
    for copy in mod_copies:
        copy.start()
    mod_land[mine] = mod_part[mine]
    for copy in mod_copies:
        copy.wait_recv()
    total = mod_land[0]
    for number in range(1, 8):
        total = total + mod_land[number]
    mod[...] = total
    live = jnp.where(place < image_counts[0], 1.0, 0.0).astype(jnp.float32)
    mod[6:7, :] = jnp.full((1, width), 1.0, jnp.float32) * live
    mod[7:8, :] = jnp.zeros((1, width), jnp.float32)
    mod[7:8, :128] = bin_row[0:1, :]

    def mod_row(number):
        return mod[number : number + 1, :]

    def tokens_arrived(number):
        for copy in token_copies[number]:
            if copy is token_copies[number][0]:
                copy.wait()
            else:
                copy.wait_recv()

    tokens_arrived(0)

    def first_norm(band):
        source = plain(features, band)
        normed = (source * rms_scale(source) * (1.0 + mod_row(1)) + mod_row(0)).astype(jnp.bfloat16)
        own_h[band, :] = normed
        h_all[mine, band, :] = normed

    bands(rows, first_norm)
    h_gather = Gather(plane, own_h, h_all, gather_sems.at[0, 0], gather_sems.at[0, 1])
    h_gather.start()
    cast_and_send(
        mlp_weight, lambda owner: [owner * feed], feed, up_stage, up_weight, 1
    )

    tokens_arrived(1)

    def feed_grad(band):
        scaled = plain(grad_out, band) * mod_row(6)
        grad_out[band, :] = scaled.astype(jnp.bfloat16)
        own_grad[band, :] = (mod_row(5) * scaled).astype(jnp.bfloat16)

    bands(rows, feed_grad)
    grad_own = pltpu.make_async_copy(own_grad, grad_mlp_all.at[mine], copy_sems.at[0])
    grad_own.start()
    grad_gather = Gather(plane, own_grad, grad_mlp_all, gather_sems.at[1, 0], gather_sems.at[1, 1])
    grad_gather.start()
    def down_load(owner):
        return pltpu.make_async_copy(
            mlp_weight.at[:, pl.ds((8 + owner) * feed, feed)],
            load_buf.at[owner % 2, :, pl.ds(0, feed)],
            load_sems.at[owner % 2, 0],
        )

    def down_store(owner):
        return pltpu.make_async_copy(
            part_buf.at[owner, :, pl.ds(0, feed)], down_low.at[owner], copy_sems.at[6 + owner]
        )

    down_load(0).start()
    for owner in range(8):
        if owner < 7:
            down_load(owner + 1).start()
        down_load(owner).wait()

        def cast_down(band, owner=owner):
            part_buf[owner, band, 0:feed] = load_buf[owner % 2, band, 0:feed].astype(jnp.bfloat16)

        bands(rows, cast_down)
        down_store(owner).start()
    for owner in range(8):
        down_store(owner).wait()
    load = pltpu.make_async_copy(
        attn_weight.at[:, pl.ds(3 * width, width)], load_buf.at[0], load_sems.at[0, 0]
    )
    load.start()
    load.wait()

    def cast_out(band):
        out_weight[band, :] = load_buf[0, band, :].astype(jnp.bfloat16)

    bands(rows, cast_out)

    weights_arrived(qkv_weight, 0)
    weights_gone(qkv_stage, qkv_weight, 0)
    load = pltpu.make_async_copy(qkv_weight, weight_buf, copy_sems.at[1])
    load.start()
    load.wait()

    @pl.loop(0, 8)
    def _(step):
        for number in range(8):

            @pl.when(step == number)
            def _(number=number):
                h_gather.step(number)

        image = flipped(mine, step)
        pltpu.make_async_copy(h_all.at[image], h_one_all.at[image], copy_sems.at[2]).start()
        projected = contract(
            h_all[image], weight_buf[...].reshape(8 * rows, columns), 1, 0
        ).astype(jnp.bfloat16)
        qkv_buf[image] = projected
        for head in range(third // HD):
            begin = head * HD
            queries = projected[:, begin : begin + HD]
            key_rows = projected[:, third + begin : third + begin + HD]
            value_rows = projected[:, 2 * third + begin : 2 * third + begin + HD]
            attention = softmax_rows(queries, key_rows).astype(jnp.bfloat16)
            attended_buf[image, :, begin : begin + HD] = contract(
                attention, value_rows, 1, 0
            ).astype(jnp.bfloat16)
        part_buf[step] = contract(attended_buf[image], out_weight[...], 1, 0).astype(jnp.bfloat16)
        pltpu.make_async_copy(h_all.at[image], h_one_all.at[image], copy_sems.at[2]).wait()

        @pl.when(step == 7)
        def _():
            h_gather.finish()

        for number in (1, 3, 5, 7):

            @pl.when(step == number)
            def _(number=number):
                slot = number // 2
                remote(
                    part_buf.at[number],
                    scatter_buf.at[slot],
                    core_send.at[slot],
                    core_recv.at[slot],
                    plane.to(1),
                ).start()

    keeps = [
        pltpu.make_async_copy(qkv_buf, qkv_all, copy_sems.at[3]),
        pltpu.make_async_copy(attended_buf, attended_all, copy_sems.at[4]),
    ]
    for copy in keeps:
        copy.start()

    def second_norm(band, value):
        attn_out[band, :] = value.astype(jnp.bfloat16)
        source = plain(features, band) + mod_row(2) * value
        first_sum[band, :] = source
        normed = (source * rms_scale(source) * (1.0 + mod_row(4)) + mod_row(3)).astype(jnp.bfloat16)
        own_next[band, :] = normed
        h_all[mine, band, :] = normed

    flow = scatter_flow(
        plane,
        lambda slot: part_buf.at[2 * slot],
        lambda slot: None,
        scatter_buf.at[pl.ds(0, 4)],
        Halves(scatter_buf.at[6], rows // 2),
        scatter_buf.at[pl.ds(4, 2)],
        (core_recv, far_send, far_recv, near_send, near_recv),
        second_norm,
    )
    for number, _ in enumerate(flow):
        if number == 1:
            grad_gather.middle()
    for slot in range(4):
        plane.gone(part_buf.at[slot], core_send.at[slot])
    next_gather = Gather(plane, own_next, h_all, gather_sems.at[2, 0], gather_sems.at[2, 1])
    next_gather.start()
    grad_gather.far()
    weights_arrived(up_weight, 1)
    weights_gone(up_stage, up_weight, 1)
    load = pltpu.make_async_copy(up_weight, up_stage, copy_sems.at[1])
    load.start()
    load.wait()

    @pl.loop(0, 8)
    def _(step):
        for number in range(8):

            @pl.when(step == number)
            def _(number=number):
                next_gather.step(number)

        image = flipped(mine, step)
        pre = contract(h_all[image], up_stage[...].reshape(8 * rows, feed), 1, 0)
        hidden, slope = gelu_and_slope(pre)
        hidden_buf[pl.ds(pl.multiple_of(image * rows, rows), rows), :] = hidden.astype(jnp.bfloat16)
        part_buf[image, :, 0:feed] = slope.astype(jnp.bfloat16)

    keeps.append(pltpu.make_async_copy(h_all, h_two_all, copy_sems.at[2]))
    keeps.append(pltpu.make_async_copy(hidden_buf, hidden_all, copy_sems.at[5]))
    keeps.append(
        pltpu.make_async_copy(part_buf.at[:, :, pl.ds(0, feed)], slope_all, copy_sems.at[1])
    )
    for copy in keeps[-3:]:
        copy.start()
    for flip in (1, 3, 5, 7):
        grad_gather.crossed(flip)
    grad_own.wait()
    column_products(
        grad_mlp_all,
        hidden_buf,
        cols_buf,
        staged_buf,
        first_grads,
        copy_sems.at[pl.ds(6, 2)],
        copy_sems.at[pl.ds(8, 2)],
    )
    for gather in (grad_gather, next_gather):
        gather.finish()
    for copy in keeps:
        copy.wait()
    for copies in token_copies:
        for copy in copies[1:]:
            copy.wait_send()
    for copy in bin_copies + mod_copies:
        copy.wait_send()


def front_part(
    bin_ids,
    image_counts,
    noise,
    mod_bias,
    block_input,
    cotangent,
    attn_weight,
    mlp_weight,
    mod_weight,
):
    slots, local_tok, width = block_input.shape
    rows = slots * local_tok
    columns, feed = 3 * width // 8, mlp_weight.shape[1] // 16
    low, full = jnp.bfloat16, jnp.float32
    dma = pltpu.SemaphoreType.DMA
    anywhere, inside = pl.BlockSpec(memory_space=pl.ANY), pl.BlockSpec(memory_space=pltpu.VMEM)
    scalars = pl.BlockSpec(memory_space=pltpu.SMEM)
    return pl.pallas_call(
        front_kernel,
        out_shape=[
            jax.ShapeDtypeStruct((8, rows, columns), low),
            jax.ShapeDtypeStruct((rows, width), low),
            jax.ShapeDtypeStruct((8, rows, feed), low),
            jax.ShapeDtypeStruct((8, rows, feed), low),
            jax.ShapeDtypeStruct((8, rows, width), low),
            jax.ShapeDtypeStruct((8, rows, width), low),
            jax.ShapeDtypeStruct((8, rows, width), low),
            jax.ShapeDtypeStruct((8, rows, columns), low),
            jax.ShapeDtypeStruct((8, rows, columns // 3), low),
            jax.ShapeDtypeStruct((8 * rows, feed), low),
            jax.ShapeDtypeStruct((8, rows, feed), low),
            jax.ShapeDtypeStruct((FIRST, 8, rows, rows), low),
            jax.ShapeDtypeStruct((rows, width), low),
            jax.ShapeDtypeStruct((rows, width), full),
            jax.ShapeDtypeStruct((rows, width), low),
            jax.ShapeDtypeStruct((rows, width), low),
            jax.ShapeDtypeStruct((8, width), full),
        ],
        in_specs=[scalars] * 2 + [inside] * 2 + [anywhere] * 5,
        out_specs=[anywhere, inside] + [anywhere] * 10 + [inside] * 5,
        scratch_shapes=[
            pltpu.VMEM((2, rows, width), full),
            pltpu.VMEM((8, rows, columns), low),
            pltpu.VMEM((8, rows, feed), low),
            pltpu.VMEM((8, rows, columns), low),
            pltpu.VMEM((8 * rows, feed), low),
            pltpu.VMEM((2, 8, rows, rows), low),
            pltpu.VMEM((2, 4, rows, rows), low),
            pltpu.VMEM((8, rows, width), low),
            pltpu.VMEM((8, rows, columns), low),
            pltpu.VMEM((8, rows, columns // 3), low),
            pltpu.VMEM((8, rows, width), low),
            pltpu.VMEM((7, rows, width), low),
            pltpu.VMEM((rows, width), low),
            pltpu.VMEM((rows, width), low),
            pltpu.VMEM((rows, width), low),
            pltpu.VMEM((8, 128), full),
            pltpu.VMEM((8, 8, 128), full),
            pltpu.VMEM((8, 8, width), full),
            pltpu.VMEM((8, 8, width), full),
            dma((2, 3)),
            dma((2, 2, 4)),
            dma((2, 8)),
            dma((2, 8)),
            dma((2, 2, 8)),
            dma((3, 2, 7 * PIECES)),
            dma((4,)),
            dma((4,)),
            dma((2,)),
            dma((2,)),
            dma((4,)),
            dma((4,)),
            dma((14,)),
        ],
        compiler_params=pltpu.CompilerParams(
            collective_id=5, has_side_effects=True, vmem_limit_bytes=63 * 1024 * 1024
        ),
        name="front_part",
    )(
        bin_ids,
        image_counts,
        noise,
        mod_bias,
        block_input,
        cotangent,
        attn_weight,
        mlp_weight,
        mod_weight,
    )


def plane_body(
    block_input,
    cotangent,
    bin_ids,
    image_counts,
    attn_weight,
    mlp_weight,
    noise_table,
    mod_weight,
    mod_bias,
):
    model_width = block_input.shape[2]
    rows = attn_weight.shape[0]
    bins = noise_table.shape[0]
    bias_piece = mod_bias.shape[0]
    mine = lax.axis_index("fsdp")
    (
        qkv_weight,
        out_weight,
        up_weight,
        down_low,
        h_one_all,
        h_two_all,
        grad_mlp_all,
        qkv_all,
        attended_all,
        hidden_all,
        slope_all,
        first_grads,
        features,
        first_sum,
        attn_out,
        grad_out,
        mod_rows,
    ) = front_part(
        bin_ids,
        image_counts,
        noise_table,
        mod_bias.reshape(1, bias_piece),
        block_input,
        cotangent,
        attn_weight,
        mlp_weight,
        mod_weight,
    )

    def flat(array):
        return array.reshape(-1, array.shape[-1])

    shares, token_out, token_grad, mod_out, _, _, _, _ = back_part(
        down_low,
        up_weight,
        hidden_all.reshape(8, rows, -1),
        slope_all,
        grad_mlp_all,
        h_two_all,
        first_grads,
        h_one_all,
        qkv_all,
        attended_all,
        flat(qkv_weight),
        out_weight,
        features,
        first_sum,
        attn_out,
        grad_out,
        mod_rows,
    )
    mod_out = mod_out.reshape(8, 4, 8, model_width)
    block_out, input_grad = token_out, token_grad.astype(jnp.float32)
    attn_weight_grad, mlp_weight_grad = attn_spread(shares), mlp_spread(shares)
    grad_images = mod_out[:, :, :6].reshape(-1, 6 * model_width)
    onehot_all = mod_out[:, :, 7, :bins].reshape(-1, bins)
    activated = jax.nn.silu(noise_table)
    chosen_all = jnp.dot(onehot_all, activated, precision=PRECISE)
    mod_weight_grad = lax.dot_general(
        chosen_all, grad_images, (((0,), (0,)), ((), ())), precision=PRECISE
    )
    image_term = lax.dot_general(
        grad_images, mod_weight, (((1,), (1,)), ((), ())), precision=PRECISE
    )
    table_term = lax.dot_general(onehot_all, image_term, (((0,), (0,)), ((), ())), precision=PRECISE)
    noise_grad = jax.vjp(jax.nn.silu, noise_table)[1](table_term)[0]
    mod_bias_grad = lax.dynamic_slice_in_dim(
        jnp.sum(grad_images, axis=0), mine * bias_piece, bias_piece
    )
    return (
        block_out,
        input_grad,
        attn_weight_grad,
        mlp_weight_grad,
        noise_grad,
        mod_weight_grad,
        mod_bias_grad,
    )


def solution(mesh):
    fits = mesh.shape["fsdp"] == 8 and mesh.shape["blk"] == 4
    return jax.shard_map(
        plane_body if fits else body,
        mesh=mesh,
        in_specs=(
            P("fsdp", "blk", None),
            P("fsdp", "blk", None),
            P("fsdp"),
            P("fsdp"),
            P("fsdp", None),
            P("fsdp", None),
            P(None, "fsdp"),
            P("fsdp", None),
            P("fsdp"),
        ),
        out_specs=(
            P("fsdp", "blk", None),
            P("fsdp", "blk", None),
            P("fsdp", None),
            P("fsdp", None),
            P(None, "fsdp"),
            P("fsdp", None),
            P("fsdp"),
        ),
        check_vma=False,
    )
```

```python
import functools
import math

import jax
import jax.numpy as jnp
from jax import lax
from jax.experimental import pallas as pl
from jax.experimental.pallas import tpu as pltpu
from jax.sharding import PartitionSpec as P

HD = 128


EPSILON = 1e-06
PRECISE = lax.Precision.HIGHEST


def norm_mod(features, scaling, shifting):
    normed = features * lax.rsqrt(jnp.mean(features * features, axis=-1, keepdims=True) + EPSILON)
    return normed * (1.0 + scaling) + shifting


def rows_product(left_rows, right_rows):
    return lax.dot_general(
        left_rows, right_rows, (((0,), (0,)), ((), ())), preferred_element_type=jnp.float32
    )


def body(
    block_input,
    cotangent,
    bin_ids,
    image_counts,
    attn_weight,
    mlp_weight,
    noise_table,
    mod_weight,
    mod_bias,
):
    slot_count, local_tok, model_width = block_input.shape
    row_count = slot_count * local_tok
    feed_width = mlp_weight.shape[1] // 2
    head_count = model_width // HD
    blk_size = lax.axis_size("blk")
    image_tok = local_tok * blk_size
    score_scale = HD ** (-0.5)
    bias_piece = mod_bias.shape[0]
    activated = jax.nn.silu(noise_table)
    partial_mod = jnp.dot(activated, mod_weight, precision=PRECISE)
    bias_full = lax.dynamic_update_slice_in_dim(
        jnp.zeros((6 * model_width,), jnp.float32), mod_bias, lax.axis_index("fsdp") * bias_piece, 0
    )
    mod_table = lax.psum(partial_mod + bias_full[None, :], "fsdp")
    onehot = (
        bin_ids[:, None] == jnp.arange(noise_table.shape[0], dtype=jnp.int32)[None, :]
    ).astype(jnp.float32)
    mod_image = jnp.dot(onehot, mod_table, precision=PRECISE)
    shift_one, scale_one, gate_one, shift_two, scale_two, gate_two = [
        member[:, None, :] for member in jnp.split(mod_image, 6, axis=-1)
    ]
    live_mask = (jnp.arange(slot_count) < image_counts[0]).astype(jnp.float32)[:, None, None]
    features = block_input.astype(jnp.float32)
    h_one = (
        norm_mod(features, scale_one, shift_one)
        .astype(jnp.bfloat16)
        .reshape(row_count, model_width)
    )
    attn_full = lax.all_gather(attn_weight.astype(jnp.bfloat16), "fsdp", axis=0, tiled=True)
    projected = jnp.dot(
        h_one, attn_full[:, : 3 * model_width], preferred_element_type=jnp.float32
    ).astype(jnp.bfloat16)
    queries = projected[:, :model_width].reshape(slot_count, local_tok, head_count, HD)
    key_rows = projected[:, model_width : 2 * model_width].reshape(
        slot_count, local_tok, model_width
    )
    value_rows = projected[:, 2 * model_width :].reshape(slot_count, local_tok, model_width)
    all_keys, all_values = (
        lax.all_gather(key_rows, "blk", axis=1, tiled=True),
        lax.all_gather(value_rows, "blk", axis=1, tiled=True),
    )
    all_keys = all_keys.reshape(slot_count, image_tok, head_count, HD)
    all_values = all_values.reshape(slot_count, image_tok, head_count, HD)

    def scores_of(query_rows):
        return (
            jnp.einsum("sqhd,skhd->shqk", query_rows, all_keys, preferred_element_type=jnp.float32)
            * score_scale
        )

    scores = scores_of(queries)
    maximum = jnp.max(scores, axis=-1, keepdims=True)
    exponent = jnp.exp(scores - maximum)
    denominator = jnp.sum(exponent, axis=-1, keepdims=True)
    attention = exponent / denominator
    log_total = maximum + jnp.log(denominator)
    attended = (
        jnp.einsum(
            "shqk,skhd->sqhd",
            attention.astype(jnp.bfloat16),
            all_values,
            preferred_element_type=jnp.float32,
        )
        .astype(jnp.bfloat16)
        .reshape(row_count, model_width)
    )
    attn_out = jnp.dot(
        attended, attn_full[:, 3 * model_width :], preferred_element_type=jnp.float32
    ).reshape(slot_count, local_tok, model_width)
    first_sum = features + gate_one * attn_out
    h_two = (
        norm_mod(first_sum, scale_two, shift_two)
        .astype(jnp.bfloat16)
        .reshape(row_count, model_width)
    )
    mlp_full = lax.all_gather(mlp_weight.astype(jnp.bfloat16), "fsdp", axis=0, tiled=True)
    pre_gelu = jnp.dot(h_two, mlp_full[:, :feed_width], preferred_element_type=jnp.float32)
    hidden = jax.nn.gelu(pre_gelu).astype(jnp.bfloat16)
    mlp_out = jnp.einsum(
        "rf,df->rd", hidden, mlp_full[:, feed_width:], preferred_element_type=jnp.float32
    ).reshape(slot_count, local_tok, model_width)
    second_sum = first_sum + gate_two * mlp_out
    block_out = (live_mask * second_sum).astype(jnp.bfloat16)
    grad_out = cotangent.astype(jnp.float32) * live_mask
    grad_mlp = (gate_two * grad_out).astype(jnp.bfloat16).reshape(row_count, model_width)
    grad_gate_two = jnp.sum(grad_out * mlp_out, axis=1)
    grad_hidden = jnp.dot(grad_mlp, mlp_full[:, feed_width:], preferred_element_type=jnp.float32)
    grad_pre = jax.vjp(jax.nn.gelu, pre_gelu)[1](grad_hidden)[0].astype(jnp.bfloat16)
    grad_h_two = jnp.einsum(
        "rf,df->rd", grad_pre, mlp_full[:, :feed_width], preferred_element_type=jnp.float32
    ).reshape(slot_count, local_tok, model_width)
    grad_first, grad_scale_two, grad_shift_two = jax.vjp(norm_mod, first_sum, scale_two, shift_two)[
        1
    ](grad_h_two)
    grad_first = grad_first + grad_out
    grad_attn_out = (gate_one * grad_first).astype(jnp.bfloat16).reshape(row_count, model_width)
    grad_gate_one = jnp.sum(grad_first * attn_out, axis=1)
    grad_attended = jnp.einsum(
        "rd,ed->re",
        grad_attn_out,
        attn_full[:, 3 * model_width :],
        preferred_element_type=jnp.float32,
    ).astype(jnp.bfloat16)
    grad_heads = grad_attended.reshape(slot_count, local_tok, head_count, HD)
    recomputed = jnp.exp(scores_of(queries) - log_total)
    grad_weights = jnp.einsum(
        "sqhd,skhd->shqk", grad_heads, all_values, preferred_element_type=jnp.float32
    )
    row_delta = jnp.sum(recomputed * grad_weights, axis=-1, keepdims=True)
    grad_scores = (recomputed * (grad_weights - row_delta)).astype(jnp.bfloat16)
    grad_queries = (
        jnp.einsum("shqk,skhd->sqhd", grad_scores, all_keys, preferred_element_type=jnp.float32)
        * score_scale
    )
    grad_keys_all = (
        jnp.einsum("shqk,sqhd->skhd", grad_scores, queries, preferred_element_type=jnp.float32)
        * score_scale
    )
    grad_values_all = jnp.einsum(
        "shqk,sqhd->skhd",
        recomputed.astype(jnp.bfloat16),
        grad_heads,
        preferred_element_type=jnp.float32,
    )
    grad_keys, grad_values = (
        lax.psum_scatter(
            grad_keys_all.reshape(slot_count, image_tok, model_width).astype(jnp.bfloat16),
            "blk",
            scatter_dimension=1,
            tiled=True,
        ).astype(jnp.float32),
        lax.psum_scatter(
            grad_values_all.reshape(slot_count, image_tok, model_width).astype(jnp.bfloat16),
            "blk",
            scatter_dimension=1,
            tiled=True,
        ).astype(jnp.float32),
    )
    grad_qkv = jnp.concatenate(
        [
            grad_queries.reshape(row_count, model_width).astype(jnp.bfloat16),
            grad_keys.reshape(row_count, model_width).astype(jnp.bfloat16),
            grad_values.reshape(row_count, model_width).astype(jnp.bfloat16),
        ],
        axis=1,
    )
    grad_h_one = jnp.einsum(
        "rc,dc->rd", grad_qkv, attn_full[:, : 3 * model_width], preferred_element_type=jnp.float32
    ).reshape(slot_count, local_tok, model_width)
    grad_input, grad_scale_one, grad_shift_one = jax.vjp(norm_mod, features, scale_one, shift_one)[
        1
    ](grad_h_one)
    input_grad = grad_input + grad_first
    grad_mod = jnp.concatenate(
        [
            grad_shift_one[:, 0, :],
            grad_scale_one[:, 0, :],
            grad_gate_one,
            grad_shift_two[:, 0, :],
            grad_scale_two[:, 0, :],
            grad_gate_two,
        ],
        axis=-1,
    )
    bin_terms = lax.dot_general(onehot, grad_mod, (((0,), (0,)), ((), ())), precision=PRECISE)
    grad_bins = lax.psum(bin_terms, ("fsdp", "blk"))
    table_term = jnp.einsum("be,de->bd", grad_bins, mod_weight, precision=PRECISE)
    noise_grad = jax.vjp(jax.nn.silu, noise_table)[1](table_term)[0]
    mod_weight_grad = lax.dot_general(
        activated, grad_bins, (((0,), (0,)), ((), ())), precision=PRECISE
    )
    mod_bias_grad = lax.dynamic_slice_in_dim(
        jnp.sum(grad_bins, axis=0), lax.axis_index("fsdp") * bias_piece, bias_piece
    )
    h_part = h_one
    attn_part = lax.psum_scatter(
        jnp.concatenate(
            [rows_product(h_part, grad_qkv), rows_product(attended, grad_attn_out)], axis=1
        ).astype(jnp.bfloat16),
        "fsdp",
        scatter_dimension=0,
        tiled=True,
    )
    h_part = h_two
    mlp_part = lax.psum_scatter(
        jnp.concatenate(
            [rows_product(h_part, grad_pre), rows_product(grad_mlp, hidden)], axis=1
        ).astype(jnp.bfloat16),
        "fsdp",
        scatter_dimension=0,
        tiled=True,
    )
    attn_weight_grad, mlp_weight_grad = (
        lax.psum(attn_part, "blk").astype(jnp.float32),
        lax.psum(mlp_part, "blk").astype(jnp.float32),
    )
    return (
        block_out,
        input_grad,
        attn_weight_grad,
        mlp_weight_grad,
        noise_grad,
        mod_weight_grad,
        mod_bias_grad,
    )


MESH_ID = pl.DeviceIdType.MESH
VMEM_BYTES = 56 * 1024 * 1024


def contract(left, right, left_dim, right_dim):
    return lax.dot_general(
        left, right, (((left_dim,), (right_dim,)), ((), ())), preferred_element_type=jnp.float32
    )


def plane_places():
    mine = lax.axis_index("fsdp")
    plane = lax.axis_index("blk")
    core = lax.rem(mine, 2)
    col = lax.rem(mine // 2, 2)
    row = mine // 4

    def at(flip):
        flip_row, flip_col, flip_core = flip // 4, (flip // 2) % 2, flip % 2
        new_row = 1 - row if flip_row else row
        new_col = 1 - col if flip_col else col
        new_core = 1 - core if flip_core else core
        return new_row * 4 + new_col * 2 + new_core

    return mine, plane, at


def greet(places):
    barrier = pltpu.get_barrier_semaphore()
    for place in places:
        pl.semaphore_signal(barrier, inc=1, device_id=place, device_id_type=MESH_ID)
    pl.semaphore_wait(barrier, len(places))


def remote(src, dst, send_sem, recv_sem, place):
    return pltpu.make_async_remote_copy(
        src_ref=src,
        dst_ref=dst,
        send_sem=send_sem,
        recv_sem=recv_sem,
        device_id=place,
        device_id_type=MESH_ID,
    )


PIECES = 4


def softmax_rows(queries, key_rows):
    scores = contract(queries, key_rows, 1, 1) * HD ** (-0.5)
    exponent = jnp.exp(scores - jnp.max(scores, axis=-1, keepdims=True))
    return exponent / jnp.sum(exponent, axis=-1, keepdims=True)


def rms_scale(features):
    return lax.rsqrt(jnp.mean(features * features, axis=-1, keepdims=True) + EPSILON)


CHUNKS = 12
FIRST = 4
EARLY = 8
HALF_ROWS = 128
BAND = 32


def flipped(mine, flip):
    total = 0
    for bit in (1, 2, 4):
        total = total + lax.rem(mine // bit + flip // bit, 2) * bit
    return total


def bands(count, step):
    @pl.loop(0, count // BAND)
    def _(index):
        step(pl.ds(pl.multiple_of(index * BAND, BAND), BAND))


def plain(ref, rows):
    return ref[rows, :].astype(jnp.float32)


def column_products(source, right, cols, staged, result, load_sems, store_sems, pieces=None, hook=None):
    rows = cols.shape[-1]
    count = result.shape[0]

    def load(block):
        slot = lax.rem(block, 2)
        return pltpu.make_async_copy(
            source.at[:, :, pl.ds(pl.multiple_of(block * rows, rows), rows)],
            cols.at[slot],
            load_sems.at[slot],
        )

    def store(block):
        slot = lax.rem(block, 2)
        return pltpu.make_async_copy(
            staged.at[slot, pl.ds(0, count)], result.at[:, block], store_sems.at[slot]
        )

    load(0).start()

    @pl.loop(0, 8)
    def _(block):
        slot = lax.rem(block, 2)
        load(block).wait()

        @pl.when(block < 7)
        def _():
            load(block + 1).start()

        @pl.when(block >= 2)
        def _():
            store(block - 2).wait()

        if hook:
            hook(block)
        product = contract(cols[slot].reshape(8 * rows, rows), right[...], 0, 0)
        for number in range(count):
            begins = pieces[number] if pieces else (number * rows,)
            size = rows // len(begins)
            for index, begin in enumerate(begins):
                staged[slot, number, :, index * size : (index + 1) * size] = product[
                    :, begin : begin + size
                ].astype(jnp.bfloat16)
        store(block).start()

    store(6).wait()
    store(7).wait()


GELU_SCALE = (2.0 / math.pi) ** 0.5


def gelu_and_slope(pre):
    squared = pre * pre
    bend = jnp.tanh(GELU_SCALE * (pre + 0.044715 * (squared * pre)))
    rise = 0.5 * (1.0 + bend)
    slope = rise + 0.5 * pre * (1.0 - bend * bend) * (GELU_SCALE * (1.0 + 3.0 * 0.044715 * squared))
    return pre * rise, slope


class Plane:
    def __init__(self):
        self.mine, self.place, self.at = plane_places()

    def to(self, flip):
        return (self.at(flip), self.place)

    def got(self, ref, sem):
        remote(ref, ref, sem, sem, (self.mine, self.place)).wait_recv()

    def gone(self, ref, sem):
        remote(ref, ref, sem, sem, (self.mine, self.place)).wait_send()


def scatter_flow(plane, own_of, fetch, peer, far, near, sems, finish):
    core_recv, far_send, far_recv, near_send, near_recv = sems
    rows = near.shape[1]
    half = rows // 2
    sent = []

    def add(slot, start, count, extra=None):
        own = own_of(slot)

        def step(band):
            at = pl.ds(pl.multiple_of(start + band.start, BAND), BAND)
            total = plain(own, at) + plain(peer.at[slot], at)
            if extra is not None:
                total = total + plain(extra, band)
            peer[slot, at, :] = total.astype(jnp.bfloat16)

        bands(count, step)

    def send(src, dst, flip, send_sem, recv_sem):
        copy = remote(src, dst, send_sem, recv_sem, plane.to(flip))
        copy.start()
        sent.append(copy)

    def send_near(slot, part):
        at = pl.ds(part * half, half)
        index = (slot - 1) * 2 + part
        send(
            peer.at[slot, at],
            near.at[slot - 1, at],
            2 * slot,
            near_send.at[index],
            near_recv.at[index],
        )

    fetch(3)
    plane.got(peer.at[3], core_recv.at[3])
    add(3, 0, rows)
    send(peer.at[3, pl.ds(0, half)], far.at[0], 2, far_send.at[0], far_recv.at[0])
    send(peer.at[3, pl.ds(half, half)], far.at[1], 4, far_send.at[1], far_recv.at[1])
    fetch(1)
    plane.got(peer.at[1], core_recv.at[1])
    add(1, 0, half)
    send_near(1, 0)
    fetch(2)
    plane.got(peer.at[2], core_recv.at[2])
    add(2, half, half)
    send_near(2, 1)
    yield
    plane.got(far.at[0], far_recv.at[0])
    add(2, 0, half, far.at[0])
    send_near(2, 0)
    plane.got(far.at[1], far_recv.at[1])
    add(1, half, half, far.at[1])
    send_near(1, 1)
    fetch(0)
    plane.got(peer.at[0], core_recv.at[0])
    yield
    for slot, part in ((1, 0), (2, 1), (2, 0), (1, 1)):
        at = pl.ds(part * half, half)
        plane.got(near.at[slot - 1, at], near_recv.at[(slot - 1) * 2 + part])
        if (slot, part) == (2, 1):
            yield
    own = own_of(0)

    def step(at):
        finish(
            at,
            plain(own, at)
            + plain(peer.at[0], at)
            + plain(near.at[0], at)
            + plain(near.at[1], at),
        )

    bands(rows, step)
    for copy in sent:
        copy.wait_send()


def back_kernel(
    down_low,
    up_weight,
    hidden_all,
    slope_all,
    grad_mlp_all,
    h_two_all,
    first_grads,
    h_all,
    qkv_all,
    attended_all,
    qkv_weight,
    out_weight,
    features,
    first_sum,
    attn_out,
    grad_out,
    mod,
    shares,
    token_out,
    token_grad,
    mod_out,
    more,
    partial_out,
    land_a,
    land_b,
    first_buf,
    second_buf,
    stage,
    own_pair,
    image_buf,
    grad_all,
    down_buf,
    grad_first,
    saved_grad,
    cols_buf,
    qkv_buf,
    attended_buf,
    staged_buf,
    out_sum,
    sum_buf,
    in_buf,
    half_buf,
    half_in,
    mod_sum,
    mod_land,
    core_send,
    core_recv,
    far_send,
    far_recv,
    near_send,
    near_recv,
    stage_sems,
    gather_send,
    gather_recv,
    load_sems,
    weight_sems,
    z_sems,
    x_sems,
    zload_sems,
    token_sems,
    mod_sems,
    mod_gather_sems,
):
    plane = Plane()
    mine, place = plane.mine, plane.place
    rows, width = features.shape
    at = plane.at
    own_grad, image_out = own_pair.at[0], own_pair.at[1]
    is_mid = (place == 1) | (place == 2)
    my_half = pl.ds(pl.multiple_of(jnp.where(place == 2, HALF_ROWS, 0), HALF_ROWS), HALF_ROWS)
    other_half = pl.ds(pl.multiple_of(jnp.where(place == 2, 0, HALF_ROWS), HALF_ROWS), HALF_ROWS)
    partner = (mine, 3 - place)
    outer = (mine, jnp.where(place == 1, 0, 3))
    inner = (mine, jnp.where(place == 0, 1, 2))
    others = [lax.rem(place + step, 4) for step in (1, 2, 3)]
    greet([plane.to(flip) for flip in range(1, 8)] + [(mine, other) for other in others])

    def z_copy(kind, chunk, src, dst, target):
        return remote(src, dst, z_sems.at[0, kind, chunk], z_sems.at[1, kind, chunk], target)

    def own_chunk(chunk):
        return first_grads.at[chunk] if chunk < FIRST else more.at[chunk - FIRST]

    def start_outward(chunk):
        z_copy(0, chunk, own_chunk(chunk), land_a.at[chunk], inner).start()

    def stage_d(k):
        region = shares.at[k, :, other_half]
        plane.got(region, z_sems.at[1, 2, k])
        z_copy(4, k, region, region, outer).start()

    def stage_x(k):
        region = shares.at[k, :, my_half]
        plane.got(region, x_sems.at[1, k])
        z_copy(2, k, region, region, partner).start()
        z_copy(3, k, region, region, outer).start()

    def stage_f(k):
        slot = k % 2
        load = pltpu.make_async_copy(land_b.at[k], half_in, zload_sems.at[2])
        plane.got(land_b.at[k], z_sems.at[1, 1, k])
        load.start()
        if k >= 2:
            plane.gone(half_buf.at[slot, pl.ds(0, 7)], x_sems.at[0, k - 2])
        load.wait()

        @pl.loop(0, 8)
        def _(block):
            half_buf[slot, block] = sum_buf[slot, block, my_half, :] + half_in[block]

        if k == CHUNKS - 1:
            pltpu.make_async_copy(
                half_buf.at[slot], shares.at[k, :, my_half], x_sems.at[1, k]
            ).start()
            return
        pltpu.make_async_copy(
            half_buf.at[slot, mine], shares.at[k, mine, my_half], x_sems.at[1, k]
        ).start()
        for flip in (6, 7, 2, 4, 3, 5, 1):
            remote(
                half_buf.at[slot, at(flip)],
                shares.at[k, mine, my_half],
                x_sems.at[0, k],
                x_sems.at[1, k],
                plane.to(flip),
            ).start()

    def stage_s(k):
        slot = k % 2
        if k >= 2:
            plane.gone(sum_buf.at[slot, :, other_half], z_sems.at[0, 1, k - 2])
        own_load = pltpu.make_async_copy(own_chunk(k), sum_buf.at[slot], zload_sems.at[0])
        own_load.start()
        in_load = pltpu.make_async_copy(land_a.at[k], in_buf, zload_sems.at[1])
        plane.got(land_a.at[k], z_sems.at[1, 0, k])
        in_load.start()
        own_load.wait()
        in_load.wait()

        @pl.loop(0, 8)
        def _(block):
            sum_buf[slot, block] = sum_buf[slot, block] + in_buf[block]

        z_copy(1, k, sum_buf.at[slot, :, other_half], land_b.at[k], partner).start()

    def send_outward(first, last):
        @pl.when(jnp.logical_not(is_mid))
        def _():
            for chunk in range(first, last):
                start_outward(chunk)

    def tick(now):
        k, odd = now // 2, now % 2

        def stage(work, chunk):
            if 0 <= chunk < CHUNKS:
                work(chunk)

        @pl.when(is_mid)
        def _():
            if odd:
                stage(stage_f, k - 1)
                stage(stage_d, k - 3)
            else:
                stage(stage_s, k)
                stage(stage_x, k - 2)

    send_outward(0, FIRST)

    attended_load = pltpu.make_async_copy(attended_all, attended_buf, load_sems.at[0])
    attended_load.start()
    feed = up_weight.shape[-1]

    pltpu.make_async_copy(
        down_low.at[mine], down_buf.at[mine], weight_sems.at[0, 0]
    ).start()
    for flip in (6, 7, 2, 4, 3, 5, 1):
        remote(
            down_low.at[at(flip)],
            down_buf.at[mine],
            weight_sems.at[0, flip],
            weight_sems.at[1, flip],
            plane.to(flip),
        ).start()
    up_load = pltpu.make_async_copy(up_weight, grad_all.at[:, :, pl.ds(0, feed)], load_sems.at[5])
    up_load.start()
    mod_sum[...] = jnp.zeros_like(mod_sum)
    row = {
        name: number
        for number, name in enumerate(
            ("shift_one", "scale_one", "gate_one", "shift_two", "scale_two", "gate_two", "live")
        )
    }

    def mod_row(name):
        return mod[pl.ds(row[name], 1), :]

    def accumulate(name, value):
        mod_sum[pl.ds(row[name], 1), :] += jnp.sum(value, axis=0, keepdims=True)

    def sems(number):
        return (
            core_recv.at[number],
            far_send.at[number],
            far_recv.at[number],
            near_send.at[number],
            near_recv.at[number],
        )

    def give(src, buf, number, slot):
        remote(
            src, buf.at[slot], core_send.at[number, slot], core_recv.at[number, slot], plane.to(1)
        ).start()

    def staged_flow(source, buf, number, finish):
        for slot in (3, 1, 2, 0):
            give(source.at[at((2 * slot) ^ 1)], buf, number, slot)
        order = {3: 0, 1: 1, 2: 0, 0: 1}

        def load(slot):
            return pltpu.make_async_copy(
                source.at[at(2 * slot)], stage.at[order[slot]], stage_sems.at[number, slot]
            )

        load(3).start()
        load(1).start()

        def fetch(slot):
            if slot == 2:
                load(2).start()
            if slot == 0:
                load(0).start()
            load(slot).wait()

        return scatter_flow(
            plane,
            lambda slot: stage.at[order[slot]],
            fetch,
            buf.at[pl.ds(0, 4)],
            Halves(buf.at[6], rows // 2),
            buf.at[pl.ds(4, 2)],
            sems(number),
            finish,
        )

    def run(flow, first_tick):
        for step, _ in enumerate(flow):
            tick(first_tick + step)

    def finish_out(where, value):
        base = first_sum[where, :]
        own_pair[1, where, :] = (
            mod_row("live") * (base + mod_row("gate_two") * value)
        ).astype(jnp.bfloat16)
        accumulate("gate_two", plain(grad_out, where) * value)

    token_copies = []

    def return_tokens(image, result, number):
        piece = rows // 4
        own = pltpu.make_async_copy(
            image.at[pl.ds(pl.multiple_of(place * piece, piece), piece)],
            result.at[place],
            token_sems.at[0, number, 0],
        )
        own.start()
        token_copies.append(own)
        for step, other in enumerate(others):
            copy = remote(
                image.at[pl.ds(pl.multiple_of(other * piece, piece), piece)],
                result.at[place],
                token_sems.at[0, number, step + 1],
                token_sems.at[1, number, step + 1],
                (mine, other),
            )
            copy.start()
            token_copies.append(copy)


    def back_norm(source, value, scale_name, shift_name):
        inverse = rms_scale(source)
        unit = source * inverse
        inner = value * (1.0 + mod_row(scale_name))
        accumulate(scale_name, value * unit)
        accumulate(shift_name, value)
        return (inner - unit * jnp.mean(inner * unit, axis=-1, keepdims=True)) * inverse

    def finish_feed(where, value):
        total = back_norm(first_sum[where, :], value, "scale_two", "shift_two") + plain(
            grad_out, where
        )
        grad_first[where, :] = total
        accumulate("gate_one", total * plain(attn_out, where))
        low_grad = (mod_row("gate_one") * total).astype(jnp.bfloat16)
        own_pair[0, where, :] = low_grad
        grad_all[mine, where, :] = low_grad

    up_load.wait()
    pltpu.make_async_copy(
        down_low.at[mine], down_buf.at[mine], weight_sems.at[0, 0]
    ).wait()
    for now in range(5):
        tick(now)
    for flip in range(1, 8):
        plane.got(down_buf.at[at(flip)], weight_sems.at[1, flip])
        plane.gone(down_low.at[0], weight_sems.at[0, flip])

    def image_loads(step):
        image, slot = flipped(mine, step), lax.rem(step, 2)
        return [
            pltpu.make_async_copy(
                slope_all.at[image], image_buf.at[slot, :, pl.ds(0, feed)], load_sems.at[6 + slot]
            ),
            pltpu.make_async_copy(grad_mlp_all.at[image], stage.at[slot], load_sems.at[8 + slot]),
        ]

    for load in image_loads(0):
        load.start()

    @pl.loop(0, 8)
    def _(step):
        @pl.when(step == 4)
        def _():
            tick(5)

        slot = lax.rem(step, 2)
        for load in image_loads(step):
            load.wait()

        @pl.when(step < 7)
        def _():
            for load in image_loads(step + 1):
                load.start()

        image_rows = pl.ds(pl.multiple_of(flipped(mine, step) * rows, rows), rows)
        grad_hidden = contract(stage[slot], down_buf[...].reshape(8 * rows, feed), 1, 0)
        saved_grad[image_rows, :] = (
            grad_hidden * image_buf[slot, :, 0:feed].astype(jnp.float32)
        ).astype(jnp.bfloat16)
        up = grad_all[:, :, 0:feed].reshape(8 * rows, feed)
        second_buf[step] = contract(saved_grad[image_rows, :], up, 1, 1).astype(jnp.bfloat16)
        for number in (1, 3, 5, 7):

            @pl.when(step == number)
            def _(number=number):
                give(second_buf.at[number], first_buf, 1, number // 2)


    def hidden_load(step):
        slot = lax.rem(step, 2)
        return pltpu.make_async_copy(
            hidden_all.at[step], image_buf.at[slot, :, pl.ds(0, feed)], load_sems.at[6 + slot]
        )

    def out_store(step):
        slot = lax.rem(step, 2)
        return pltpu.make_async_copy(own_pair.at[slot], partial_out.at[step], load_sems.at[8 + slot])

    def out_products():
        hidden_load(0).start()

        @pl.loop(0, 8)
        def _(step):
            slot = lax.rem(step, 2)
            hidden_load(step).wait()

            @pl.when(step < 7)
            def _():
                hidden_load(step + 1).start()

            @pl.when(step >= 2)
            def _():
                out_store(step - 2).wait()

            @pl.when(step == 5)
            def _():
                tick(9)

            own_pair[slot] = contract(
                image_buf[slot, :, 0:feed], down_buf[...].reshape(8 * rows, feed), 1, 1
            ).astype(jnp.bfloat16)
            out_store(step).start()

        out_store(6).wait()
        out_store(7).wait()

    def up_hook(block):
        @pl.when(block == 6)
        def _():
            tick(7)

    def up_products():
        column_products(
            h_two_all,
            saved_grad,
            cols_buf,
            staged_buf,
            more.at[pl.ds(0, 4)],
            load_sems.at[pl.ds(3, 2)],
            load_sems.at[pl.ds(11, 2)],
            hook=up_hook,
        )

    def own_flow(number, finish):
        return scatter_flow(
            plane,
            lambda slot: second_buf.at[2 * slot],
            lambda slot: None,
            first_buf.at[pl.ds(0, 4)],
            Halves(first_buf.at[6], rows // 2),
            first_buf.at[pl.ds(4, 2)],
            sems(number),
            finish,
        )

    tick(6)
    up_products()
    send_outward(FIRST, EARLY)
    for step, _ in enumerate(own_flow(1, finish_feed)):
        tick((8, 10, 11)[step])
        if step == 0:
            out_products()
    for slot in range(4):
        plane.gone(second_buf.at[slot], core_send.at[1, slot])

    gather = Gather(plane, own_grad, grad_all, gather_send, gather_recv)
    gather.start()

    def qkv_load(step):
        return pltpu.make_async_copy(
            qkv_all.at[flipped(mine, step)], qkv_buf.at[lax.rem(step, 2)], load_sems.at[1 + lax.rem(step, 2)]
        )

    qkv_load(0).start()
    attended_load.wait()
    out_sum[...] = jnp.zeros_like(out_sum)
    columns = qkv_buf.shape[-1]
    third = columns // 3
    scale = HD ** (-0.5)

    @pl.loop(0, 8)
    def _(step):
        for number in range(8):

            @pl.when(step == number)
            def _(number=number):
                if number in (1, 2, 4):
                    tick({1: 12, 2: 13, 4: 15}[number])
                if number == 2:
                    tick(14)
                gather.step(number)
                if number == 7:
                    gather.finish()

        image = flipped(mine, step)
        slot = lax.rem(step, 2)
        qkv_load(step).wait()

        @pl.when(step < 7)
        def _():
            qkv_load(step + 1).start()

        grad = grad_all[image]
        grad_attended = contract(grad, out_weight[...], 1, 1).astype(jnp.bfloat16)
        image_rows = pl.ds(pl.multiple_of(image * rows, rows), rows)
        for head in range(third // HD):
            begin, first = head * HD, 3 * head * HD
            queries = qkv_buf[slot, :, first : first + HD]
            key_rows = qkv_buf[slot, :, first + HD : first + 2 * HD]
            value_rows = qkv_buf[slot, :, first + 2 * HD : first + 3 * HD]
            grad_head = grad_attended[:, begin : begin + HD]
            attention = softmax_rows(queries, key_rows)
            grad_weights = contract(grad_head, value_rows, 1, 1)
            row_delta = jnp.sum(attention * grad_weights, axis=-1, keepdims=True)
            grad_scores = (attention * (grad_weights - row_delta)).astype(jnp.bfloat16)
            saved_grad[image_rows, first : first + HD] = (
                contract(grad_scores, key_rows, 1, 0) * scale
            ).astype(jnp.bfloat16)
            saved_grad[image_rows, first + HD : first + 2 * HD] = (
                contract(grad_scores, queries, 0, 0) * scale
            ).astype(jnp.bfloat16)
            saved_grad[image_rows, first + 2 * HD : first + 3 * HD] = contract(
                attention.astype(jnp.bfloat16), grad_head, 0, 0
            ).astype(jnp.bfloat16)
        out_sum[...] += contract(attended_buf[image], grad, 0, 0)
        second_buf[step] = contract(saved_grad[image_rows, 0:columns], qkv_weight[...], 1, 1).astype(
            jnp.bfloat16
        )
        for number in (1, 3, 5, 7):

            @pl.when(step == number)
            def _(number=number):
                give(second_buf.at[number], first_buf, 2, number // 2)


    for block in range(8):
        in_buf[block] = out_sum[:, block * rows : (block + 1) * rows].astype(jnp.bfloat16)
    out_copy = pltpu.make_async_copy(in_buf, more.at[7], load_sems.at[0])
    out_copy.start()
    column_products(
        h_all,
        saved_grad.at[:, pl.ds(0, columns)],
        cols_buf,
        staged_buf,
        more.at[pl.ds(4, 3)],
        load_sems.at[pl.ds(3, 2)],
        load_sems.at[pl.ds(11, 2)],
        [[(3 * head + number) * HD for head in range(third // HD)] for number in range(3)],
    )

    def finish_input(where, value):
        total = back_norm(plain(features, where), value, "scale_one", "shift_one")
        own_pair[0, where, :] = (total + grad_first[where, :]).astype(jnp.bfloat16)

    out_copy.wait()
    send_outward(EARLY, CHUNKS)
    tick(16)
    run(own_flow(2, finish_input), 17)
    return_tokens(own_grad, token_grad, 1)
    for step, _ in enumerate(staged_flow(partial_out, grad_all, 0, finish_out)):
        tick(20 + step)
    return_tokens(image_out, token_out, 0)

    mod_copies = []
    mod_sum[7:8, :] = mod[7:8, :]
    mod_rows = pl.ds(pl.multiple_of(place * 8, 8), 8)
    mod_land[mod_rows, :] = mod_sum[...]
    for step, other in enumerate(others):
        copy = remote(
            mod_sum, mod_land.at[mod_rows], mod_sems.at[0, step], mod_sems.at[1, step], (mine, other)
        )
        copy.start()
        mod_copies.append(copy)
    tick(23)
    tick(24)
    for copy in mod_copies:
        copy.wait_recv()
    own = pltpu.make_async_copy(mod_land, mod_out.at[mine], mod_sems.at[0, 3])
    own.start()
    mod_gather = Gather(plane, mod_land, mod_out, mod_gather_sems.at[0], mod_gather_sems.at[1])
    mod_gather.start()
    tick(25)
    tick(26)
    mod_gather.middle()
    mod_gather.far()
    for flip in (1, 3, 5, 7):
        mod_gather.crossed(flip)
    mod_gather.finish()
    for now in range(27, 2 * CHUNKS + 6):
        tick(now)
    own.wait()
    for copy in mod_copies:
        copy.wait_send()
    for copy in token_copies:
        copy.wait()
    for number in (0, 2):
        for slot in range(4):
            plane.gone(second_buf.at[slot], core_send.at[number, slot])

    @pl.when(is_mid)
    def _():
        for k in (CHUNKS - 2, CHUNKS - 1):
            plane.gone(sum_buf.at[k % 2, :, other_half], z_sems.at[0, 1, k])
        plane.gone(half_buf.at[0, pl.ds(0, 7)], x_sems.at[0, CHUNKS - 2])
        for k in range(CHUNKS):
            plane.gone(shares.at[k, :, my_half], z_sems.at[0, 2, k])
            plane.gone(shares.at[k, :, my_half], z_sems.at[0, 3, k])
            plane.gone(shares.at[k, :, other_half], z_sems.at[0, 4, k])

    @pl.when(jnp.logical_not(is_mid))
    def _():
        first = pl.ds(pl.multiple_of(jnp.where(place == 0, 0, HALF_ROWS), HALF_ROWS), HALF_ROWS)
        second = pl.ds(pl.multiple_of(jnp.where(place == 0, HALF_ROWS, 0), HALF_ROWS), HALF_ROWS)
        for k in range(CHUNKS):
            plane.gone(land_a.at[k], z_sems.at[0, 0, k])
            plane.got(shares.at[k, :, first], z_sems.at[1, 3, k])
            plane.got(shares.at[k, :, second], z_sems.at[1, 4, k])


def back_part(*operands):
    h_all, qkv_weight = operands[7], operands[10]
    _, rows, width = h_all.shape
    columns = qkv_weight.shape[1]
    feed = operands[1].shape[-1]
    low, full = jnp.bfloat16, jnp.float32
    dma = pltpu.SemaphoreType.DMA
    anywhere, inside = pl.BlockSpec(memory_space=pl.ANY), pl.BlockSpec(memory_space=pltpu.VMEM)
    return pl.pallas_call(
        back_kernel,
        out_shape=[
            jax.ShapeDtypeStruct((CHUNKS, 8, rows, rows), low),
            jax.ShapeDtypeStruct((4, rows // 4, width), low),
            jax.ShapeDtypeStruct((4, rows // 4, width), low),
            jax.ShapeDtypeStruct((8, 32, width), full),
            jax.ShapeDtypeStruct((CHUNKS - FIRST, 8, rows, rows), low),
            jax.ShapeDtypeStruct((8, rows, width), low),
            jax.ShapeDtypeStruct((CHUNKS, 8, rows, rows), low),
            jax.ShapeDtypeStruct((CHUNKS, 8, HALF_ROWS, rows), low),
        ],
        in_specs=[anywhere] * 10 + [inside] * 7,
        out_specs=[anywhere] * 8,
        scratch_shapes=[
            pltpu.VMEM((7, rows, width), low),
            pltpu.VMEM((8, rows, width), low),
            pltpu.VMEM((2, rows, width), low),
            pltpu.VMEM((2, rows, width), low),
            pltpu.VMEM((2, rows, feed), low),
            pltpu.VMEM((8, rows, width), low),
            pltpu.VMEM((8, rows, feed), low),
            pltpu.VMEM((rows, width), full),
            pltpu.VMEM((8 * rows, feed), low),
            pltpu.VMEM((2, 8, rows, rows), low),
            pltpu.VMEM((2, rows, columns), low),
            pltpu.VMEM((8, rows, columns // 3), low),
            pltpu.VMEM((2, 4, rows, rows), low),
            pltpu.VMEM((columns // 3, width), full),
            pltpu.VMEM((2, 8, rows, rows), low),
            pltpu.VMEM((8, rows, rows), low),
            pltpu.VMEM((2, 8, HALF_ROWS, rows), low),
            pltpu.VMEM((8, HALF_ROWS, rows), low),
            pltpu.VMEM((8, width), full),
            pltpu.VMEM((32, width), full),
            dma((3, 4)),
            dma((3, 4)),
            dma((3, 2)),
            dma((3, 2)),
            dma((3, 4)),
            dma((3, 4)),
            dma((2, 4)),
            dma((7 * PIECES,)),
            dma((7 * PIECES,)),
            dma((13,)),
            dma((2, 8)),
            dma((2, 5, CHUNKS)),
            dma((2, CHUNKS)),
            dma((3,)),
            dma((2, 2, 4)),
            dma((2, 4)),
            dma((2, 7 * PIECES)),
        ],
        compiler_params=pltpu.CompilerParams(
            collective_id=4, has_side_effects=True, vmem_limit_bytes=63 * 1024 * 1024
        ),
        name="back_part",
    )(*operands)


def mlp_spread_kernel(share_ref, out_ref):
    size = share_ref.shape[-1]
    for number in range(4):
        out_ref[:, number * size : (number + 1) * size] = share_ref[number, 0].astype(jnp.float32)


def mlp_spread(shares):
    rows = shares.shape[2]
    return pl.pallas_call(
        mlp_spread_kernel,
        grid=(2, 8),
        out_shape=jax.ShapeDtypeStruct((rows, 64 * rows), jnp.float32),
        in_specs=[pl.BlockSpec((4, 1, rows, rows), lambda part, block: (1 - part, block, 0, 0))],
        out_specs=pl.BlockSpec((rows, 4 * rows), lambda part, block: (0, part * 8 + block)),
        compiler_params=pltpu.CompilerParams(vmem_limit_bytes=VMEM_BYTES),
        name="mlp_spread",
    )(shares)


def attn_spread_kernel(share_ref, out_ref):
    size = share_ref.shape[-1]
    for number in range(8):
        out_ref[:, number * size : (number + 1) * size] = share_ref[0, number].astype(jnp.float32)


def attn_spread(shares):
    rows = shares.shape[2]
    return pl.pallas_call(
        attn_spread_kernel,
        grid=(4,),
        out_shape=jax.ShapeDtypeStruct((rows, 32 * rows), jnp.float32),
        in_specs=[pl.BlockSpec((1, 8, rows, rows), lambda part: (EARLY + part, 0, 0, 0))],
        out_specs=pl.BlockSpec((rows, 8 * rows), lambda part: (0, part)),
        compiler_params=pltpu.CompilerParams(vmem_limit_bytes=VMEM_BYTES),
        name="attn_spread",
    )(shares)


class Gather:
    def __init__(self, plane, own, result, send_sems, recv_sems):
        self.plane, self.own, self.result = plane, own, result
        self.send_sems, self.recv_sems = send_sems, recv_sems
        self.piece = own.shape[0] // PIECES

    def put(self, src, owner, part, flip, slot):
        remote(
            src,
            self.result.at[owner, pl.ds(part * self.piece, self.piece)],
            self.send_sems.at[slot],
            self.recv_sems.at[slot],
            self.plane.to(flip),
        ).start()

    def arrived(self, flip, part, slot):
        ref = self.result.at[self.plane.at(flip), pl.ds(part * self.piece, self.piece)]
        self.plane.got(ref, self.recv_sems.at[slot])
        return ref

    def start(self):
        mine = self.plane.mine
        for part in range(PIECES):
            src = self.own.at[pl.ds(part * self.piece, self.piece)]
            self.put(src, mine, part, 2, part)
            self.put(src, mine, part, 4, PIECES + part)
            self.put(src, mine, part, 1, 3 * PIECES + part)

    def middle(self):
        at = self.plane.at
        for part in range(PIECES):
            got = self.arrived(2, part, part)
            if part < PIECES // 2:
                self.put(got, at(2), part, 4, 2 * PIECES + part)
            self.put(got, at(2), part, 1, 4 * PIECES + part)
            got = self.arrived(4, part, PIECES + part)
            if part >= PIECES // 2:
                self.put(got, at(4), part, 2, 2 * PIECES + part)
            self.put(got, at(4), part, 1, 5 * PIECES + part)

    def far(self):
        for part in range(PIECES):
            got = self.arrived(6, part, 2 * PIECES + part)
            self.put(got, self.plane.at(6), part, 1, 6 * PIECES + part)

    def crossed(self, flip):
        for part in range(PIECES):
            self.arrived(flip, part, (3 + flip // 2) * PIECES + part)

    def step(self, number):
        if number == 2:
            self.middle()
        if number == 6:
            self.far()
        if number % 2:
            self.crossed(number)

    def finish(self):
        for slot in range(7 * PIECES):
            self.plane.gone(self.own.at[pl.ds(0, self.piece)], self.send_sems.at[slot])


class Halves:
    def __init__(self, ref, half):
        self.ref, self.half = ref, half

    @property
    def at(self):
        return self

    def __getitem__(self, number):
        return self.ref.at[pl.ds(number * self.half, self.half)]


def front_kernel(
    bin_ids,
    image_counts,
    noise,
    mod_bias,
    block_input,
    cotangent,
    attn_weight,
    mlp_weight,
    mod_weight,
    qkv_weight,
    out_weight,
    up_weight,
    down_low,
    h_one_all,
    h_two_all,
    grad_mlp_all,
    qkv_all,
    attended_all,
    hidden_all,
    slope_all,
    first_grads,
    features,
    first_sum,
    attn_out,
    grad_out,
    mod,
    load_buf,
    qkv_stage,
    up_stage,
    weight_buf,
    hidden_buf,
    cols_buf,
    staged_buf,
    h_all,
    qkv_buf,
    attended_buf,
    part_buf,
    scatter_buf,
    own_h,
    own_grad,
    own_next,
    bin_row,
    bin_land,
    mod_part,
    mod_land,
    load_sems,
    token_sems,
    bin_sems,
    mod_sems,
    weight_sems,
    beside_sems,
    gather_sems,
    core_send,
    core_recv,
    far_send,
    far_recv,
    near_send,
    near_recv,
    copy_sems,
):
    plane = Plane()
    mine, place, at = plane.mine, plane.place, plane.at
    rows, width = own_h.shape
    feed = up_stage.shape[-1]
    columns = qkv_stage.shape[-1]
    third = columns // 3
    piece = rows // 4
    others = [lax.rem(place + step, 4) for step in (1, 2, 3)]
    flips = (6, 7, 2, 4, 3, 5, 1, 0)
    greet([plane.to(flip) for flip in range(1, 8)] + [(mine, other) for other in others])

    token_copies = []
    my_rows = pl.ds(pl.multiple_of(place * piece, piece), piece)
    for number, (source, result) in enumerate(((block_input, features), (cotangent, grad_out))):
        copies = [
            pltpu.make_async_copy(
                source.at[place], result.at[my_rows], token_sems.at[0, number, 0]
            )
        ]
        for step, other in enumerate(others):
            copies.append(
                remote(
                    source.at[other],
                    result.at[my_rows],
                    token_sems.at[0, number, step + 1],
                    token_sems.at[1, number, step + 1],
                    (mine, other),
                )
            )
        for copy in copies:
            copy.start()
        token_copies.append(copies)

    lanes = lax.broadcasted_iota(jnp.int32, bin_row.shape, 1)
    bin_row[...] = jnp.where(lanes == bin_ids[place], 1.0, 0.0).astype(jnp.float32)
    bin_land[mine] = bin_row[...]
    bin_copies = [
        remote(
            bin_row, bin_land.at[mine], bin_sems.at[0, flip], bin_sems.at[1, flip], plane.to(flip)
        )
        for flip in range(1, 8)
    ]
    for copy in bin_copies:
        copy.start()

    parity = lax.rem(place, 2)
    beside = (mine, place + 1 - 2 * parity)

    def half_of(size):
        return pl.ds(pl.multiple_of(parity * size, size), size)

    def load_columns(source, slot, begins, size):
        return [
            pltpu.make_async_copy(
                source.at[:, pl.ds(pl.multiple_of(begin, HD), size)],
                load_buf.at[slot, :, pl.ds(number * size, size)],
                load_sems.at[slot, number],
            )
            for number, begin in enumerate(begins)
        ]

    def cast_and_send(source, begins_of, size, stage, result, kind):
        loads = [
            load_columns(source, step % 2, begins_of(at(flip)), size)
            for step, flip in enumerate(flips)
        ]
        total = size * len(loads[0])
        half = half_of(total)
        for load in loads[0]:
            load.start()
        for step, flip in enumerate(flips):
            if step + 1 < len(flips):
                for load in loads[step + 1]:
                    load.start()
            for load in loads[step]:
                load.wait()

            def cast(band, step=step):
                stage[step, band, 0:total] = load_buf[step % 2, band, 0:total].astype(jnp.bfloat16)

            bands(rows, cast)
            src = stage.at[step, :, pl.ds(0, total)]
            if flip:
                remote(
                    src,
                    result.at[mine, :, half],
                    weight_sems.at[0, kind, flip],
                    weight_sems.at[1, kind, flip],
                    plane.to(flip),
                ).start()
            else:
                pltpu.make_async_copy(
                    src, result.at[mine, :, half], weight_sems.at[0, kind, 0]
                ).start()

    def pass_on(stage, result, kind, total):
        half = half_of(total)
        pltpu.make_async_copy(
            stage.at[7, :, pl.ds(0, total)], result.at[mine, :, half], weight_sems.at[0, kind, 0]
        ).wait()
        for flip in (1, 2, 3, 4, 5, 6, 7, 0):
            piece = result.at[at(flip), :, half]
            if flip:
                plane.got(piece, weight_sems.at[1, kind, flip])
            remote(
                piece,
                piece,
                beside_sems.at[0, kind, flip],
                beside_sems.at[1, kind, flip],
                beside,
            ).start()

    def weights_ready(stage, result, kind, total):
        for flip in range(8):
            piece = result.at[at(flip), :, half_of(total)]
            plane.got(piece, beside_sems.at[1, kind, flip])
            plane.gone(piece, beside_sems.at[0, kind, flip])
            if flip:
                plane.gone(stage.at[0, :, pl.ds(0, total)], weight_sems.at[0, kind, flip])

    cast_and_send(
        attn_weight,
        lambda owner: [number * width + owner * third + parity * HD for number in range(3)],
        HD,
        qkv_stage,
        qkv_weight,
        0,
    )

    cast_and_send(
        mlp_weight,
        lambda owner: [owner * feed + parity * (feed // 2)],
        feed // 2,
        up_stage,
        up_weight,
        1,
    )

    for copy in bin_copies:
        copy.wait_recv()
    bins = noise.shape[0]
    activated = noise[...] / (1.0 + jnp.exp(-noise[...]))
    chosen = jnp.dot(
        bin_land[:, 0, :bins], activated, precision=PRECISE, preferred_element_type=jnp.float32
    )

    def load_mod(number):
        return pltpu.make_async_copy(
            mod_weight.at[:, pl.ds(number * width, width)],
            load_buf.at[number % 2],
            load_sems.at[number % 2, 0],
        )

    load_mod(0).start()
    mod_part[...] = jnp.zeros_like(mod_part)
    for number in range(6):
        if number < 5:
            load_mod(number + 1).start()
        load_mod(number).wait()
        mod_part[:, number, :] = jnp.dot(
            chosen, load_buf[number % 2], precision=PRECISE, preferred_element_type=jnp.float32
        )
    quarter = width // 4
    for number in range(3):
        index = 3 * mine + number
        where = pl.ds(pl.multiple_of(lax.rem(index, 4) * quarter, quarter), quarter)
        for image in range(8):
            mod_part[image, pl.ds(index // 4, 1), where] += mod_bias[
                :, number * quarter : (number + 1) * quarter
            ]
    mod_copies = [
        remote(
            mod_part.at[at(flip)],
            mod_land.at[mine],
            mod_sems.at[0, flip],
            mod_sems.at[1, flip],
            plane.to(flip),
        )
        for flip in range(1, 8)
    ]
    for copy in mod_copies:
        copy.start()
    pass_on(qkv_stage, qkv_weight, 0, 3 * HD)
    mod_land[mine] = mod_part[mine]
    for copy in mod_copies:
        copy.wait_recv()
    total = mod_land[0]
    for number in range(1, 8):
        total = total + mod_land[number]
    mod[...] = total
    live = jnp.where(place < image_counts[0], 1.0, 0.0).astype(jnp.float32)
    mod[6:7, :] = jnp.full((1, width), 1.0, jnp.float32) * live
    mod[7:8, :] = jnp.zeros((1, width), jnp.float32)
    mod[7:8, :128] = bin_row[0:1, :]

    def mod_row(number):
        return mod[number : number + 1, :]

    def tokens_arrived(number):
        for copy in token_copies[number]:
            if copy is token_copies[number][0]:
                copy.wait()
            else:
                copy.wait_recv()

    tokens_arrived(0)

    def first_norm(band):
        source = plain(features, band)
        normed = (source * rms_scale(source) * (1.0 + mod_row(1)) + mod_row(0)).astype(jnp.bfloat16)
        own_h[band, :] = normed
        h_all[mine, band, :] = normed

    bands(rows, first_norm)
    h_gather = Gather(plane, own_h, h_all, gather_sems.at[0, 0], gather_sems.at[0, 1])
    h_gather.start()

    tokens_arrived(1)

    def feed_grad(band):
        scaled = plain(grad_out, band) * mod_row(6)
        grad_out[band, :] = scaled.astype(jnp.bfloat16)
        own_grad[band, :] = (mod_row(5) * scaled).astype(jnp.bfloat16)

    bands(rows, feed_grad)
    grad_own = pltpu.make_async_copy(own_grad, grad_mlp_all.at[mine], copy_sems.at[0])
    grad_own.start()
    grad_gather = Gather(plane, own_grad, grad_mlp_all, gather_sems.at[1, 0], gather_sems.at[1, 1])
    grad_gather.start()
    def down_load(owner):
        return pltpu.make_async_copy(
            mlp_weight.at[:, pl.ds((8 + owner) * feed, feed)],
            load_buf.at[owner % 2, :, pl.ds(0, feed)],
            load_sems.at[owner % 2, 0],
        )

    def down_store(owner):
        return pltpu.make_async_copy(
            part_buf.at[owner, :, pl.ds(0, feed)], down_low.at[owner], copy_sems.at[6 + owner]
        )

    down_load(0).start()
    for owner in range(8):
        if owner < 7:
            down_load(owner + 1).start()
        down_load(owner).wait()

        def cast_down(band, owner=owner):
            part_buf[owner, band, 0:feed] = load_buf[owner % 2, band, 0:feed].astype(jnp.bfloat16)

        bands(rows, cast_down)
        down_store(owner).start()
    for owner in range(8):
        down_store(owner).wait()
    load = pltpu.make_async_copy(
        attn_weight.at[:, pl.ds(3 * width, width)], load_buf.at[0], load_sems.at[0, 0]
    )
    load.start()
    load.wait()

    def cast_out(band):
        out_weight[band, :] = load_buf[0, band, :].astype(jnp.bfloat16)

    bands(rows, cast_out)

    weights_ready(qkv_stage, qkv_weight, 0, 3 * HD)
    load = pltpu.make_async_copy(qkv_weight, weight_buf, copy_sems.at[1])
    load.start()
    load.wait()

    @pl.loop(0, 8)
    def _(step):
        for number in range(8):

            @pl.when(step == number)
            def _(number=number):
                h_gather.step(number)

        image = flipped(mine, step)
        pltpu.make_async_copy(h_all.at[image], h_one_all.at[image], copy_sems.at[2]).start()
        projected = contract(
            h_all[image], weight_buf[...].reshape(8 * rows, columns), 1, 0
        ).astype(jnp.bfloat16)
        qkv_buf[image] = projected
        for head in range(third // HD):
            begin, first = head * HD, 3 * head * HD
            queries = projected[:, first : first + HD]
            key_rows = projected[:, first + HD : first + 2 * HD]
            value_rows = projected[:, first + 2 * HD : first + 3 * HD]
            attention = softmax_rows(queries, key_rows).astype(jnp.bfloat16)
            attended_buf[image, :, begin : begin + HD] = contract(
                attention, value_rows, 1, 0
            ).astype(jnp.bfloat16)
        part_buf[step] = contract(attended_buf[image], out_weight[...], 1, 0).astype(jnp.bfloat16)
        pltpu.make_async_copy(h_all.at[image], h_one_all.at[image], copy_sems.at[2]).wait()

        @pl.when(step == 7)
        def _():
            h_gather.finish()

        for number in (1, 3, 5, 7):

            @pl.when(step == number)
            def _(number=number):
                slot = number // 2
                remote(
                    part_buf.at[number],
                    scatter_buf.at[slot],
                    core_send.at[slot],
                    core_recv.at[slot],
                    plane.to(1),
                ).start()

    pass_on(up_stage, up_weight, 1, feed // 2)
    keeps = [
        pltpu.make_async_copy(qkv_buf, qkv_all, copy_sems.at[3]),
        pltpu.make_async_copy(attended_buf, attended_all, copy_sems.at[4]),
    ]
    for copy in keeps:
        copy.start()

    def second_norm(band, value):
        attn_out[band, :] = value.astype(jnp.bfloat16)
        source = plain(features, band) + mod_row(2) * value
        first_sum[band, :] = source
        normed = (source * rms_scale(source) * (1.0 + mod_row(4)) + mod_row(3)).astype(jnp.bfloat16)
        own_next[band, :] = normed
        h_all[mine, band, :] = normed

    flow = scatter_flow(
        plane,
        lambda slot: part_buf.at[2 * slot],
        lambda slot: None,
        scatter_buf.at[pl.ds(0, 4)],
        Halves(scatter_buf.at[6], rows // 2),
        scatter_buf.at[pl.ds(4, 2)],
        (core_recv, far_send, far_recv, near_send, near_recv),
        second_norm,
    )
    for number, _ in enumerate(flow):
        if number == 1:
            grad_gather.middle()
    for slot in range(4):
        plane.gone(part_buf.at[slot], core_send.at[slot])
    next_gather = Gather(plane, own_next, h_all, gather_sems.at[2, 0], gather_sems.at[2, 1])
    next_gather.start()
    grad_gather.far()
    weights_ready(up_stage, up_weight, 1, feed // 2)
    load = pltpu.make_async_copy(up_weight, up_stage, copy_sems.at[1])
    load.start()
    load.wait()

    @pl.loop(0, 8)
    def _(step):
        for number in range(8):

            @pl.when(step == number)
            def _(number=number):
                next_gather.step(number)

        image = flipped(mine, step)
        pre = contract(h_all[image], up_stage[...].reshape(8 * rows, feed), 1, 0)
        hidden, slope = gelu_and_slope(pre)
        hidden_buf[pl.ds(pl.multiple_of(image * rows, rows), rows), :] = hidden.astype(jnp.bfloat16)
        part_buf[image, :, 0:feed] = slope.astype(jnp.bfloat16)

    keeps.append(pltpu.make_async_copy(h_all, h_two_all, copy_sems.at[2]))
    keeps.append(pltpu.make_async_copy(hidden_buf, hidden_all, copy_sems.at[5]))
    keeps.append(
        pltpu.make_async_copy(part_buf.at[:, :, pl.ds(0, feed)], slope_all, copy_sems.at[1])
    )
    for copy in keeps[-3:]:
        copy.start()
    for flip in (1, 3, 5, 7):
        grad_gather.crossed(flip)
    grad_own.wait()
    column_products(
        grad_mlp_all,
        hidden_buf,
        cols_buf,
        staged_buf,
        first_grads,
        copy_sems.at[pl.ds(6, 2)],
        copy_sems.at[pl.ds(8, 2)],
    )
    for gather in (grad_gather, next_gather):
        gather.finish()
    for copy in keeps:
        copy.wait()
    for copies in token_copies:
        for copy in copies[1:]:
            copy.wait_send()
    for copy in bin_copies + mod_copies:
        copy.wait_send()


def front_part(
    bin_ids,
    image_counts,
    noise,
    mod_bias,
    block_input,
    cotangent,
    attn_weight,
    mlp_weight,
    mod_weight,
):
    slots, local_tok, width = block_input.shape
    rows = slots * local_tok
    columns, feed = 3 * width // 8, mlp_weight.shape[1] // 16
    low, full = jnp.bfloat16, jnp.float32
    dma = pltpu.SemaphoreType.DMA
    anywhere, inside = pl.BlockSpec(memory_space=pl.ANY), pl.BlockSpec(memory_space=pltpu.VMEM)
    scalars = pl.BlockSpec(memory_space=pltpu.SMEM)
    return pl.pallas_call(
        front_kernel,
        out_shape=[
            jax.ShapeDtypeStruct((8, rows, columns), low),
            jax.ShapeDtypeStruct((rows, width), low),
            jax.ShapeDtypeStruct((8, rows, feed), low),
            jax.ShapeDtypeStruct((8, rows, feed), low),
            jax.ShapeDtypeStruct((8, rows, width), low),
            jax.ShapeDtypeStruct((8, rows, width), low),
            jax.ShapeDtypeStruct((8, rows, width), low),
            jax.ShapeDtypeStruct((8, rows, columns), low),
            jax.ShapeDtypeStruct((8, rows, columns // 3), low),
            jax.ShapeDtypeStruct((8 * rows, feed), low),
            jax.ShapeDtypeStruct((8, rows, feed), low),
            jax.ShapeDtypeStruct((FIRST, 8, rows, rows), low),
            jax.ShapeDtypeStruct((rows, width), low),
            jax.ShapeDtypeStruct((rows, width), full),
            jax.ShapeDtypeStruct((rows, width), low),
            jax.ShapeDtypeStruct((rows, width), low),
            jax.ShapeDtypeStruct((8, width), full),
        ],
        in_specs=[scalars] * 2 + [inside] * 2 + [anywhere] * 5,
        out_specs=[anywhere, inside] + [anywhere] * 10 + [inside] * 5,
        scratch_shapes=[
            pltpu.VMEM((2, rows, width), full),
            pltpu.VMEM((8, rows, columns), low),
            pltpu.VMEM((8, rows, feed), low),
            pltpu.VMEM((8, rows, columns), low),
            pltpu.VMEM((8 * rows, feed), low),
            pltpu.VMEM((2, 8, rows, rows), low),
            pltpu.VMEM((2, 4, rows, rows), low),
            pltpu.VMEM((8, rows, width), low),
            pltpu.VMEM((8, rows, columns), low),
            pltpu.VMEM((8, rows, columns // 3), low),
            pltpu.VMEM((8, rows, width), low),
            pltpu.VMEM((7, rows, width), low),
            pltpu.VMEM((rows, width), low),
            pltpu.VMEM((rows, width), low),
            pltpu.VMEM((rows, width), low),
            pltpu.VMEM((8, 128), full),
            pltpu.VMEM((8, 8, 128), full),
            pltpu.VMEM((8, 8, width), full),
            pltpu.VMEM((8, 8, width), full),
            dma((2, 3)),
            dma((2, 2, 4)),
            dma((2, 8)),
            dma((2, 8)),
            dma((2, 2, 8)),
            dma((2, 2, 8)),
            dma((3, 2, 7 * PIECES)),
            dma((4,)),
            dma((4,)),
            dma((2,)),
            dma((2,)),
            dma((4,)),
            dma((4,)),
            dma((14,)),
        ],
        compiler_params=pltpu.CompilerParams(
            collective_id=5, has_side_effects=True, vmem_limit_bytes=63 * 1024 * 1024
        ),
        name="front_part",
    )(
        bin_ids,
        image_counts,
        noise,
        mod_bias,
        block_input,
        cotangent,
        attn_weight,
        mlp_weight,
        mod_weight,
    )


def mod_grads_kernel(
    rows_ref, onehot_ref, noise_ref, weight_ref, weight_grad_ref, noise_grad_ref, bias_ref, chosen, total
):
    part = pl.program_id(0)
    noise = noise_ref[...]
    onehot = onehot_ref[...]
    rise = 1.0 / (1.0 + jnp.exp(-noise))

    def exact(left, right, left_dim, right_dim):
        return lax.dot_general(
            left,
            right,
            (((left_dim,), (right_dim,)), ((), ())),
            precision=PRECISE,
            preferred_element_type=jnp.float32,
        )

    @pl.when(part == 0)
    def _():
        chosen[...] = exact(onehot, noise * rise, 1, 0)
        total[...] = jnp.zeros_like(total)

    grads = rows_ref[0]
    bias_ref[...] = jnp.broadcast_to(jnp.sum(grads, axis=0, keepdims=True), bias_ref.shape)
    low = grads.astype(jnp.bfloat16)
    weight_grad_ref[...] = contract(chosen[...].astype(jnp.bfloat16), low, 0, 0)
    total[...] += contract(weight_ref[...].astype(jnp.bfloat16), low, 1, 1)

    @pl.when(part == pl.num_programs(0) - 1)
    def _():
        table = lax.dot_general(
            onehot,
            total[...],
            (((0,), (1,)), ((), ())),
            precision=PRECISE,
            preferred_element_type=jnp.float32,
        )
        noise_grad_ref[...] = table * (rise + noise * rise * (1.0 - rise))


def mod_grads(image_rows, onehot, noise, weight):
    images, _, width = image_rows.shape
    depth = weight.shape[0]
    return pl.pallas_call(
        mod_grads_kernel,
        grid=(12,),
        out_shape=[
            jax.ShapeDtypeStruct(weight.shape, jnp.float32),
            jax.ShapeDtypeStruct(noise.shape, jnp.float32),
            jax.ShapeDtypeStruct((8, 6 * width), jnp.float32),
        ],
        in_specs=[
            pl.BlockSpec((1, images, width // 2), lambda part: (part // 2, 0, part % 2)),
            pl.BlockSpec(onehot.shape, lambda part: (0, 0)),
            pl.BlockSpec(noise.shape, lambda part: (0, 0)),
            pl.BlockSpec((depth, width // 2), lambda part: (0, part)),
        ],
        out_specs=[
            pl.BlockSpec((depth, width // 2), lambda part: (0, part)),
            pl.BlockSpec(noise.shape, lambda part: (0, 0)),
            pl.BlockSpec((8, width // 2), lambda part: (0, part)),
        ],
        scratch_shapes=[
            pltpu.VMEM((images, depth), jnp.float32),
            pltpu.VMEM((depth, images), jnp.float32),
        ],
        compiler_params=pltpu.CompilerParams(vmem_limit_bytes=VMEM_BYTES),
        name="mod_grads",
    )(image_rows.transpose(1, 0, 2), onehot, noise, weight)


def plane_body(
    block_input,
    cotangent,
    bin_ids,
    image_counts,
    attn_weight,
    mlp_weight,
    noise_table,
    mod_weight,
    mod_bias,
):
    model_width = block_input.shape[2]
    rows = attn_weight.shape[0]
    bins = noise_table.shape[0]
    bias_piece = mod_bias.shape[0]
    mine = lax.axis_index("fsdp")
    (
        qkv_weight,
        out_weight,
        up_weight,
        down_low,
        h_one_all,
        h_two_all,
        grad_mlp_all,
        qkv_all,
        attended_all,
        hidden_all,
        slope_all,
        first_grads,
        features,
        first_sum,
        attn_out,
        grad_out,
        mod_rows,
    ) = front_part(
        bin_ids,
        image_counts,
        noise_table,
        mod_bias.reshape(1, bias_piece),
        block_input,
        cotangent,
        attn_weight,
        mlp_weight,
        mod_weight,
    )

    def flat(array):
        return array.reshape(-1, array.shape[-1])

    shares, token_out, token_grad, mod_out, _, _, _, _ = back_part(
        down_low,
        up_weight,
        hidden_all.reshape(8, rows, -1),
        slope_all,
        grad_mlp_all,
        h_two_all,
        first_grads,
        h_one_all,
        qkv_all,
        attended_all,
        flat(qkv_weight),
        out_weight,
        features,
        first_sum,
        attn_out,
        grad_out,
        mod_rows,
    )
    mod_out = mod_out.reshape(8, 4, 8, model_width)
    block_out, input_grad = token_out, token_grad.astype(jnp.float32)
    attn_weight_grad, mlp_weight_grad = attn_spread(shares), mlp_spread(shares)
    onehot_all = mod_out[:, :, 7, :bins].reshape(-1, bins)
    mod_weight_grad, noise_grad, bias_sums = mod_grads(
        mod_out.reshape(-1, 8, model_width), onehot_all, noise_table, mod_weight
    )
    mod_bias_grad = lax.dynamic_slice_in_dim(bias_sums[0], mine * bias_piece, bias_piece)
    return (
        block_out,
        input_grad,
        attn_weight_grad,
        mlp_weight_grad,
        noise_grad,
        mod_weight_grad,
        mod_bias_grad,
    )


def solution(mesh):
    fits = mesh.shape["fsdp"] == 8 and mesh.shape["blk"] == 4
    return jax.shard_map(
        plane_body if fits else body,
        mesh=mesh,
        in_specs=(
            P("fsdp", "blk", None),
            P("fsdp", "blk", None),
            P("fsdp"),
            P("fsdp"),
            P("fsdp", None),
            P("fsdp", None),
            P(None, "fsdp"),
            P("fsdp", None),
            P("fsdp"),
        ),
        out_specs=(
            P("fsdp", "blk", None),
            P("fsdp", "blk", None),
            P("fsdp", None),
            P("fsdp", None),
            P(None, "fsdp"),
            P("fsdp", None),
            P("fsdp"),
        ),
        check_vma=False,
    )
```

```python
import functools
import math

import jax
import jax.numpy as jnp
from jax import lax
from jax.experimental import pallas as pl
from jax.experimental.pallas import tpu as pltpu
from jax.sharding import PartitionSpec as P

HD = 128


EPSILON = 1e-06
PRECISE = lax.Precision.HIGHEST


def norm_mod(features, scaling, shifting):
    normed = features * lax.rsqrt(jnp.mean(features * features, axis=-1, keepdims=True) + EPSILON)
    return normed * (1.0 + scaling) + shifting


def rows_product(left_rows, right_rows):
    return lax.dot_general(
        left_rows, right_rows, (((0,), (0,)), ((), ())), preferred_element_type=jnp.float32
    )


def body(
    block_input,
    cotangent,
    bin_ids,
    image_counts,
    attn_weight,
    mlp_weight,
    noise_table,
    mod_weight,
    mod_bias,
):
    slot_count, local_tok, model_width = block_input.shape
    row_count = slot_count * local_tok
    feed_width = mlp_weight.shape[1] // 2
    head_count = model_width // HD
    blk_size = lax.axis_size("blk")
    image_tok = local_tok * blk_size
    score_scale = HD ** (-0.5)
    bias_piece = mod_bias.shape[0]
    activated = jax.nn.silu(noise_table)
    partial_mod = jnp.dot(activated, mod_weight, precision=PRECISE)
    bias_full = lax.dynamic_update_slice_in_dim(
        jnp.zeros((6 * model_width,), jnp.float32), mod_bias, lax.axis_index("fsdp") * bias_piece, 0
    )
    mod_table = lax.psum(partial_mod + bias_full[None, :], "fsdp")
    onehot = (
        bin_ids[:, None] == jnp.arange(noise_table.shape[0], dtype=jnp.int32)[None, :]
    ).astype(jnp.float32)
    mod_image = jnp.dot(onehot, mod_table, precision=PRECISE)
    shift_one, scale_one, gate_one, shift_two, scale_two, gate_two = [
        member[:, None, :] for member in jnp.split(mod_image, 6, axis=-1)
    ]
    live_mask = (jnp.arange(slot_count) < image_counts[0]).astype(jnp.float32)[:, None, None]
    features = block_input.astype(jnp.float32)
    h_one = (
        norm_mod(features, scale_one, shift_one)
        .astype(jnp.bfloat16)
        .reshape(row_count, model_width)
    )
    attn_full = lax.all_gather(attn_weight.astype(jnp.bfloat16), "fsdp", axis=0, tiled=True)
    projected = jnp.dot(
        h_one, attn_full[:, : 3 * model_width], preferred_element_type=jnp.float32
    ).astype(jnp.bfloat16)
    queries = projected[:, :model_width].reshape(slot_count, local_tok, head_count, HD)
    key_rows = projected[:, model_width : 2 * model_width].reshape(
        slot_count, local_tok, model_width
    )
    value_rows = projected[:, 2 * model_width :].reshape(slot_count, local_tok, model_width)
    all_keys, all_values = (
        lax.all_gather(key_rows, "blk", axis=1, tiled=True),
        lax.all_gather(value_rows, "blk", axis=1, tiled=True),
    )
    all_keys = all_keys.reshape(slot_count, image_tok, head_count, HD)
    all_values = all_values.reshape(slot_count, image_tok, head_count, HD)

    def scores_of(query_rows):
        return (
            jnp.einsum("sqhd,skhd->shqk", query_rows, all_keys, preferred_element_type=jnp.float32)
            * score_scale
        )

    scores = scores_of(queries)
    maximum = jnp.max(scores, axis=-1, keepdims=True)
    exponent = jnp.exp(scores - maximum)
    denominator = jnp.sum(exponent, axis=-1, keepdims=True)
    attention = exponent / denominator
    log_total = maximum + jnp.log(denominator)
    attended = (
        jnp.einsum(
            "shqk,skhd->sqhd",
            attention.astype(jnp.bfloat16),
            all_values,
            preferred_element_type=jnp.float32,
        )
        .astype(jnp.bfloat16)
        .reshape(row_count, model_width)
    )
    attn_out = jnp.dot(
        attended, attn_full[:, 3 * model_width :], preferred_element_type=jnp.float32
    ).reshape(slot_count, local_tok, model_width)
    first_sum = features + gate_one * attn_out
    h_two = (
        norm_mod(first_sum, scale_two, shift_two)
        .astype(jnp.bfloat16)
        .reshape(row_count, model_width)
    )
    mlp_full = lax.all_gather(mlp_weight.astype(jnp.bfloat16), "fsdp", axis=0, tiled=True)
    pre_gelu = jnp.dot(h_two, mlp_full[:, :feed_width], preferred_element_type=jnp.float32)
    hidden = jax.nn.gelu(pre_gelu).astype(jnp.bfloat16)
    mlp_out = jnp.einsum(
        "rf,df->rd", hidden, mlp_full[:, feed_width:], preferred_element_type=jnp.float32
    ).reshape(slot_count, local_tok, model_width)
    second_sum = first_sum + gate_two * mlp_out
    block_out = (live_mask * second_sum).astype(jnp.bfloat16)
    grad_out = cotangent.astype(jnp.float32) * live_mask
    grad_mlp = (gate_two * grad_out).astype(jnp.bfloat16).reshape(row_count, model_width)
    grad_gate_two = jnp.sum(grad_out * mlp_out, axis=1)
    grad_hidden = jnp.dot(grad_mlp, mlp_full[:, feed_width:], preferred_element_type=jnp.float32)
    grad_pre = jax.vjp(jax.nn.gelu, pre_gelu)[1](grad_hidden)[0].astype(jnp.bfloat16)
    grad_h_two = jnp.einsum(
        "rf,df->rd", grad_pre, mlp_full[:, :feed_width], preferred_element_type=jnp.float32
    ).reshape(slot_count, local_tok, model_width)
    grad_first, grad_scale_two, grad_shift_two = jax.vjp(norm_mod, first_sum, scale_two, shift_two)[
        1
    ](grad_h_two)
    grad_first = grad_first + grad_out
    grad_attn_out = (gate_one * grad_first).astype(jnp.bfloat16).reshape(row_count, model_width)
    grad_gate_one = jnp.sum(grad_first * attn_out, axis=1)
    grad_attended = jnp.einsum(
        "rd,ed->re",
        grad_attn_out,
        attn_full[:, 3 * model_width :],
        preferred_element_type=jnp.float32,
    ).astype(jnp.bfloat16)
    grad_heads = grad_attended.reshape(slot_count, local_tok, head_count, HD)
    recomputed = jnp.exp(scores_of(queries) - log_total)
    grad_weights = jnp.einsum(
        "sqhd,skhd->shqk", grad_heads, all_values, preferred_element_type=jnp.float32
    )
    row_delta = jnp.sum(recomputed * grad_weights, axis=-1, keepdims=True)
    grad_scores = (recomputed * (grad_weights - row_delta)).astype(jnp.bfloat16)
    grad_queries = (
        jnp.einsum("shqk,skhd->sqhd", grad_scores, all_keys, preferred_element_type=jnp.float32)
        * score_scale
    )
    grad_keys_all = (
        jnp.einsum("shqk,sqhd->skhd", grad_scores, queries, preferred_element_type=jnp.float32)
        * score_scale
    )
    grad_values_all = jnp.einsum(
        "shqk,sqhd->skhd",
        recomputed.astype(jnp.bfloat16),
        grad_heads,
        preferred_element_type=jnp.float32,
    )
    grad_keys, grad_values = (
        lax.psum_scatter(
            grad_keys_all.reshape(slot_count, image_tok, model_width).astype(jnp.bfloat16),
            "blk",
            scatter_dimension=1,
            tiled=True,
        ).astype(jnp.float32),
        lax.psum_scatter(
            grad_values_all.reshape(slot_count, image_tok, model_width).astype(jnp.bfloat16),
            "blk",
            scatter_dimension=1,
            tiled=True,
        ).astype(jnp.float32),
    )
    grad_qkv = jnp.concatenate(
        [
            grad_queries.reshape(row_count, model_width).astype(jnp.bfloat16),
            grad_keys.reshape(row_count, model_width).astype(jnp.bfloat16),
            grad_values.reshape(row_count, model_width).astype(jnp.bfloat16),
        ],
        axis=1,
    )
    grad_h_one = jnp.einsum(
        "rc,dc->rd", grad_qkv, attn_full[:, : 3 * model_width], preferred_element_type=jnp.float32
    ).reshape(slot_count, local_tok, model_width)
    grad_input, grad_scale_one, grad_shift_one = jax.vjp(norm_mod, features, scale_one, shift_one)[
        1
    ](grad_h_one)
    input_grad = grad_input + grad_first
    grad_mod = jnp.concatenate(
        [
            grad_shift_one[:, 0, :],
            grad_scale_one[:, 0, :],
            grad_gate_one,
            grad_shift_two[:, 0, :],
            grad_scale_two[:, 0, :],
            grad_gate_two,
        ],
        axis=-1,
    )
    bin_terms = lax.dot_general(onehot, grad_mod, (((0,), (0,)), ((), ())), precision=PRECISE)
    grad_bins = lax.psum(bin_terms, ("fsdp", "blk"))
    table_term = jnp.einsum("be,de->bd", grad_bins, mod_weight, precision=PRECISE)
    noise_grad = jax.vjp(jax.nn.silu, noise_table)[1](table_term)[0]
    mod_weight_grad = lax.dot_general(
        activated, grad_bins, (((0,), (0,)), ((), ())), precision=PRECISE
    )
    mod_bias_grad = lax.dynamic_slice_in_dim(
        jnp.sum(grad_bins, axis=0), lax.axis_index("fsdp") * bias_piece, bias_piece
    )
    h_part = h_one
    attn_part = lax.psum_scatter(
        jnp.concatenate(
            [rows_product(h_part, grad_qkv), rows_product(attended, grad_attn_out)], axis=1
        ).astype(jnp.bfloat16),
        "fsdp",
        scatter_dimension=0,
        tiled=True,
    )
    h_part = h_two
    mlp_part = lax.psum_scatter(
        jnp.concatenate(
            [rows_product(h_part, grad_pre), rows_product(grad_mlp, hidden)], axis=1
        ).astype(jnp.bfloat16),
        "fsdp",
        scatter_dimension=0,
        tiled=True,
    )
    attn_weight_grad, mlp_weight_grad = (
        lax.psum(attn_part, "blk").astype(jnp.float32),
        lax.psum(mlp_part, "blk").astype(jnp.float32),
    )
    return (
        block_out,
        input_grad,
        attn_weight_grad,
        mlp_weight_grad,
        noise_grad,
        mod_weight_grad,
        mod_bias_grad,
    )


MESH_ID = pl.DeviceIdType.MESH
VMEM_BYTES = 56 * 1024 * 1024


def contract(left, right, left_dim, right_dim):
    return lax.dot_general(
        left, right, (((left_dim,), (right_dim,)), ((), ())), preferred_element_type=jnp.float32
    )


def plane_places():
    mine = lax.axis_index("fsdp")
    plane = lax.axis_index("blk")
    core = lax.rem(mine, 2)
    col = lax.rem(mine // 2, 2)
    row = mine // 4

    def at(flip):
        flip_row, flip_col, flip_core = flip // 4, (flip // 2) % 2, flip % 2
        new_row = 1 - row if flip_row else row
        new_col = 1 - col if flip_col else col
        new_core = 1 - core if flip_core else core
        return new_row * 4 + new_col * 2 + new_core

    return mine, plane, at


def greet(places):
    barrier = pltpu.get_barrier_semaphore()
    for place in places:
        pl.semaphore_signal(barrier, inc=1, device_id=place, device_id_type=MESH_ID)
    pl.semaphore_wait(barrier, len(places))


def remote(src, dst, send_sem, recv_sem, place):
    return pltpu.make_async_remote_copy(
        src_ref=src,
        dst_ref=dst,
        send_sem=send_sem,
        recv_sem=recv_sem,
        device_id=place,
        device_id_type=MESH_ID,
    )


PIECES = 4


def softmax_rows(queries, key_rows):
    scores = contract(queries, key_rows, 1, 1) * HD ** (-0.5)
    exponent = jnp.exp(scores - jnp.max(scores, axis=-1, keepdims=True))
    return exponent / jnp.sum(exponent, axis=-1, keepdims=True)


def rms_scale(features):
    return lax.rsqrt(jnp.mean(features * features, axis=-1, keepdims=True) + EPSILON)


CHUNKS = 12
FIRST = 4
EARLY = 8
HALF_ROWS = 128
BAND = 32


def flipped(mine, flip):
    total = 0
    for bit in (1, 2, 4):
        total = total + lax.rem(mine // bit + flip // bit, 2) * bit
    return total


def bands(count, step):
    @pl.loop(0, count // BAND)
    def _(index):
        step(pl.ds(pl.multiple_of(index * BAND, BAND), BAND))


def plain(ref, rows):
    return ref[rows, :].astype(jnp.float32)


def column_products(source, right, cols, staged, result, load_sems, store_sems, pieces=None, hook=None):
    rows = cols.shape[-1]
    count = result.shape[0]

    def load(block):
        slot = lax.rem(block, 2)
        return pltpu.make_async_copy(
            source.at[:, :, pl.ds(pl.multiple_of(block * rows, rows), rows)],
            cols.at[slot],
            load_sems.at[slot],
        )

    def store(block):
        slot = lax.rem(block, 2)
        return pltpu.make_async_copy(
            staged.at[slot, pl.ds(0, count)], result.at[:, block], store_sems.at[slot]
        )

    load(0).start()

    @pl.loop(0, 8)
    def _(block):
        slot = lax.rem(block, 2)
        load(block).wait()

        @pl.when(block < 7)
        def _():
            load(block + 1).start()

        @pl.when(block >= 2)
        def _():
            store(block - 2).wait()

        if hook:
            hook(block)
        product = contract(cols[slot].reshape(8 * rows, rows), right[...], 0, 0)
        for number in range(count):
            begins = pieces[number] if pieces else (number * rows,)
            size = rows // len(begins)
            for index, begin in enumerate(begins):
                staged[slot, number, :, index * size : (index + 1) * size] = product[
                    :, begin : begin + size
                ].astype(jnp.bfloat16)
        store(block).start()

    store(6).wait()
    store(7).wait()


GELU_SCALE = (2.0 / math.pi) ** 0.5


def gelu_and_slope(pre):
    squared = pre * pre
    bend = jnp.tanh(GELU_SCALE * (pre + 0.044715 * (squared * pre)))
    rise = 0.5 * (1.0 + bend)
    slope = rise + 0.5 * pre * (1.0 - bend * bend) * (GELU_SCALE * (1.0 + 3.0 * 0.044715 * squared))
    return pre * rise, slope


class Plane:
    def __init__(self):
        self.mine, self.place, self.at = plane_places()

    def to(self, flip):
        return (self.at(flip), self.place)

    def got(self, ref, sem):
        remote(ref, ref, sem, sem, (self.mine, self.place)).wait_recv()

    def gone(self, ref, sem):
        remote(ref, ref, sem, sem, (self.mine, self.place)).wait_send()


def scatter_flow(plane, own_of, fetch, peer, far, near, sems, finish):
    core_recv, far_send, far_recv, near_send, near_recv = sems
    rows = near.shape[1]
    half = rows // 2
    sent = []

    def add(slot, start, count, extra=None):
        own = own_of(slot)

        def step(band):
            at = pl.ds(pl.multiple_of(start + band.start, BAND), BAND)
            total = plain(own, at) + plain(peer.at[slot], at)
            if extra is not None:
                total = total + plain(extra, band)
            peer[slot, at, :] = total.astype(jnp.bfloat16)

        bands(count, step)

    def send(src, dst, flip, send_sem, recv_sem):
        copy = remote(src, dst, send_sem, recv_sem, plane.to(flip))
        copy.start()
        sent.append(copy)

    def send_near(slot, part):
        at = pl.ds(part * half, half)
        index = (slot - 1) * 2 + part
        send(
            peer.at[slot, at],
            near.at[slot - 1, at],
            2 * slot,
            near_send.at[index],
            near_recv.at[index],
        )

    fetch(3)
    plane.got(peer.at[3], core_recv.at[3])
    add(3, 0, rows)
    send(peer.at[3, pl.ds(0, half)], far.at[0], 2, far_send.at[0], far_recv.at[0])
    send(peer.at[3, pl.ds(half, half)], far.at[1], 4, far_send.at[1], far_recv.at[1])
    fetch(1)
    plane.got(peer.at[1], core_recv.at[1])
    add(1, 0, half)
    send_near(1, 0)
    fetch(2)
    plane.got(peer.at[2], core_recv.at[2])
    add(2, half, half)
    send_near(2, 1)
    yield
    plane.got(far.at[0], far_recv.at[0])
    add(2, 0, half, far.at[0])
    send_near(2, 0)
    plane.got(far.at[1], far_recv.at[1])
    add(1, half, half, far.at[1])
    send_near(1, 1)
    fetch(0)
    plane.got(peer.at[0], core_recv.at[0])
    yield
    for slot, part in ((1, 0), (2, 1), (2, 0), (1, 1)):
        at = pl.ds(part * half, half)
        plane.got(near.at[slot - 1, at], near_recv.at[(slot - 1) * 2 + part])
        if (slot, part) == (2, 1):
            yield
    own = own_of(0)

    def step(at):
        finish(
            at,
            plain(own, at)
            + plain(peer.at[0], at)
            + plain(near.at[0], at)
            + plain(near.at[1], at),
        )

    bands(rows, step)
    for copy in sent:
        copy.wait_send()


def back_kernel(
    down_low,
    up_weight,
    hidden_all,
    slope_all,
    grad_mlp_all,
    h_two_all,
    first_grads,
    h_all,
    qkv_all,
    attended_all,
    qkv_weight,
    out_weight,
    features,
    first_sum,
    attn_out,
    grad_out,
    mod,
    shares,
    token_out,
    token_grad,
    mod_out,
    more,
    partial_out,
    land_a,
    land_b,
    first_buf,
    second_buf,
    stage,
    own_pair,
    image_buf,
    grad_all,
    down_buf,
    grad_first,
    saved_grad,
    cols_buf,
    qkv_buf,
    attended_buf,
    staged_buf,
    out_sum,
    sum_buf,
    in_buf,
    half_buf,
    half_in,
    mod_sum,
    mod_land,
    core_send,
    core_recv,
    far_send,
    far_recv,
    near_send,
    near_recv,
    stage_sems,
    gather_send,
    gather_recv,
    load_sems,
    weight_sems,
    z_sems,
    x_sems,
    zload_sems,
    token_sems,
    mod_sems,
    mod_gather_sems,
):
    plane = Plane()
    mine, place = plane.mine, plane.place
    rows, width = features.shape
    at = plane.at
    own_grad, image_out = own_pair.at[0], own_pair.at[1]
    is_mid = (place == 1) | (place == 2)
    my_half = pl.ds(pl.multiple_of(jnp.where(place == 2, HALF_ROWS, 0), HALF_ROWS), HALF_ROWS)
    other_half = pl.ds(pl.multiple_of(jnp.where(place == 2, 0, HALF_ROWS), HALF_ROWS), HALF_ROWS)
    partner = (mine, 3 - place)
    outer = (mine, jnp.where(place == 1, 0, 3))
    inner = (mine, jnp.where(place == 0, 1, 2))
    others = [lax.rem(place + step, 4) for step in (1, 2, 3)]
    greet([plane.to(flip) for flip in range(1, 8)] + [(mine, other) for other in others])

    def z_copy(kind, chunk, src, dst, target):
        return remote(src, dst, z_sems.at[0, kind, chunk], z_sems.at[1, kind, chunk], target)

    def own_chunk(chunk):
        return first_grads.at[chunk] if chunk < FIRST else more.at[chunk - FIRST]

    def start_outward(chunk):
        z_copy(0, chunk, own_chunk(chunk), land_a.at[chunk], inner).start()

    def stage_d(k):
        region = shares.at[k, :, other_half]
        plane.got(region, z_sems.at[1, 2, k])
        z_copy(4, k, region, region, outer).start()

    def stage_x(k):
        region = shares.at[k, :, my_half]
        plane.got(region, x_sems.at[1, k])
        z_copy(2, k, region, region, partner).start()
        z_copy(3, k, region, region, outer).start()

    def stage_f(k):
        slot = k % 2
        load = pltpu.make_async_copy(land_b.at[k], half_in, zload_sems.at[2])
        plane.got(land_b.at[k], z_sems.at[1, 1, k])
        load.start()
        if k >= 2:
            plane.gone(half_buf.at[slot, pl.ds(0, 7)], x_sems.at[0, k - 2])
        load.wait()

        @pl.loop(0, 8)
        def _(block):
            half_buf[slot, block] = sum_buf[slot, block, my_half, :] + half_in[block]

        if k == CHUNKS - 1:
            pltpu.make_async_copy(
                half_buf.at[slot], shares.at[k, :, my_half], x_sems.at[1, k]
            ).start()
            return
        pltpu.make_async_copy(
            half_buf.at[slot, mine], shares.at[k, mine, my_half], x_sems.at[1, k]
        ).start()
        for flip in (6, 7, 2, 4, 3, 5, 1):
            remote(
                half_buf.at[slot, at(flip)],
                shares.at[k, mine, my_half],
                x_sems.at[0, k],
                x_sems.at[1, k],
                plane.to(flip),
            ).start()

    def stage_s(k):
        slot = k % 2
        if k >= 2:
            plane.gone(sum_buf.at[slot, :, other_half], z_sems.at[0, 1, k - 2])
        own_load = pltpu.make_async_copy(own_chunk(k), sum_buf.at[slot], zload_sems.at[0])
        own_load.start()
        in_load = pltpu.make_async_copy(land_a.at[k], in_buf, zload_sems.at[1])
        plane.got(land_a.at[k], z_sems.at[1, 0, k])
        in_load.start()
        own_load.wait()
        in_load.wait()

        @pl.loop(0, 8)
        def _(block):
            sum_buf[slot, block] = sum_buf[slot, block] + in_buf[block]

        z_copy(1, k, sum_buf.at[slot, :, other_half], land_b.at[k], partner).start()

    def send_outward(first, last):
        @pl.when(jnp.logical_not(is_mid))
        def _():
            for chunk in range(first, last):
                start_outward(chunk)

    def tick(now):
        k, odd = now // 2, now % 2
        work = [(stage_f, k - 1), (stage_d, k - 3)] if odd else [(stage_s, k), (stage_x, k - 2)]
        work = {
            16: [(stage_s, EARLY)],
            17: [(stage_x, EARLY - 1)],
            18: [(stage_s, EARLY + 1)],
        }.get(now, work)

        @pl.when(is_mid)
        def _():
            for stage, chunk in work:
                if 0 <= chunk < CHUNKS:
                    stage(chunk)

    def ahead():
        @pl.when(is_mid)
        def _():
            stage_x(EARLY - 2)
            stage_f(EARLY - 1)
            stage_d(EARLY - 3)

    send_outward(0, FIRST)

    attended_load = pltpu.make_async_copy(attended_all, attended_buf, load_sems.at[0])
    attended_load.start()
    feed = up_weight.shape[-1]

    pltpu.make_async_copy(
        down_low.at[mine], down_buf.at[mine], weight_sems.at[0, 0]
    ).start()
    for flip in (6, 7, 2, 4, 3, 5, 1):
        remote(
            down_low.at[at(flip)],
            down_buf.at[mine],
            weight_sems.at[0, flip],
            weight_sems.at[1, flip],
            plane.to(flip),
        ).start()
    up_load = pltpu.make_async_copy(up_weight, grad_all.at[:, :, pl.ds(0, feed)], load_sems.at[5])
    up_load.start()
    mod_sum[...] = jnp.zeros_like(mod_sum)
    row = {
        name: number
        for number, name in enumerate(
            ("shift_one", "scale_one", "gate_one", "shift_two", "scale_two", "gate_two", "live")
        )
    }

    def mod_row(name):
        return mod[pl.ds(row[name], 1), :]

    def accumulate(name, value):
        mod_sum[pl.ds(row[name], 1), :] += jnp.sum(value, axis=0, keepdims=True)

    def sems(number):
        return (
            core_recv.at[number],
            far_send.at[number],
            far_recv.at[number],
            near_send.at[number],
            near_recv.at[number],
        )

    def give(src, buf, number, slot):
        remote(
            src, buf.at[slot], core_send.at[number, slot], core_recv.at[number, slot], plane.to(1)
        ).start()

    def staged_flow(source, buf, number, finish):
        for slot in (3, 1, 2, 0):
            give(source.at[at((2 * slot) ^ 1)], buf, number, slot)
        order = {3: 0, 1: 1, 2: 0, 0: 1}

        def load(slot):
            return pltpu.make_async_copy(
                source.at[at(2 * slot)], stage.at[order[slot]], stage_sems.at[number, slot]
            )

        load(3).start()
        load(1).start()

        def fetch(slot):
            if slot == 2:
                load(2).start()
            if slot == 0:
                load(0).start()
            load(slot).wait()

        return scatter_flow(
            plane,
            lambda slot: stage.at[order[slot]],
            fetch,
            buf.at[pl.ds(0, 4)],
            Halves(buf.at[6], rows // 2),
            buf.at[pl.ds(4, 2)],
            sems(number),
            finish,
        )

    def run(flow, first_tick):
        for step, _ in enumerate(flow):
            tick(first_tick + step)

    def finish_out(where, value):
        base = first_sum[where, :]
        own_pair[1, where, :] = (
            mod_row("live") * (base + mod_row("gate_two") * value)
        ).astype(jnp.bfloat16)
        accumulate("gate_two", plain(grad_out, where) * value)

    token_copies = []

    def return_tokens(image, result, number):
        piece = rows // 4
        own = pltpu.make_async_copy(
            image.at[pl.ds(pl.multiple_of(place * piece, piece), piece)],
            result.at[place],
            token_sems.at[0, number, 0],
        )
        own.start()
        token_copies.append(own)
        for step, other in enumerate(others):
            copy = remote(
                image.at[pl.ds(pl.multiple_of(other * piece, piece), piece)],
                result.at[place],
                token_sems.at[0, number, step + 1],
                token_sems.at[1, number, step + 1],
                (mine, other),
            )
            copy.start()
            token_copies.append(copy)


    def back_norm(source, value, scale_name, shift_name):
        inverse = rms_scale(source)
        unit = source * inverse
        inner = value * (1.0 + mod_row(scale_name))
        accumulate(scale_name, value * unit)
        accumulate(shift_name, value)
        return (inner - unit * jnp.mean(inner * unit, axis=-1, keepdims=True)) * inverse

    def finish_feed(where, value):
        total = back_norm(first_sum[where, :], value, "scale_two", "shift_two") + plain(
            grad_out, where
        )
        grad_first[where, :] = total
        accumulate("gate_one", total * plain(attn_out, where))
        low_grad = (mod_row("gate_one") * total).astype(jnp.bfloat16)
        own_pair[0, where, :] = low_grad
        grad_all[mine, where, :] = low_grad

    up_load.wait()
    pltpu.make_async_copy(
        down_low.at[mine], down_buf.at[mine], weight_sems.at[0, 0]
    ).wait()
    for now in range(5):
        tick(now)
    for flip in range(1, 8):
        plane.got(down_buf.at[at(flip)], weight_sems.at[1, flip])
        plane.gone(down_low.at[0], weight_sems.at[0, flip])

    def image_loads(step):
        image, slot = flipped(mine, step), lax.rem(step, 2)
        return [
            pltpu.make_async_copy(
                slope_all.at[image], image_buf.at[slot, :, pl.ds(0, feed)], load_sems.at[6 + slot]
            ),
            pltpu.make_async_copy(grad_mlp_all.at[image], stage.at[slot], load_sems.at[8 + slot]),
        ]

    for load in image_loads(0):
        load.start()

    @pl.loop(0, 8)
    def _(step):
        @pl.when(step == 4)
        def _():
            tick(5)

        slot = lax.rem(step, 2)
        for load in image_loads(step):
            load.wait()

        @pl.when(step < 7)
        def _():
            for load in image_loads(step + 1):
                load.start()

        image_rows = pl.ds(pl.multiple_of(flipped(mine, step) * rows, rows), rows)
        grad_hidden = contract(stage[slot], down_buf[...].reshape(8 * rows, feed), 1, 0)
        saved_grad[image_rows, :] = (
            grad_hidden * image_buf[slot, :, 0:feed].astype(jnp.float32)
        ).astype(jnp.bfloat16)
        up = grad_all[:, :, 0:feed].reshape(8 * rows, feed)
        second_buf[step] = contract(saved_grad[image_rows, :], up, 1, 1).astype(jnp.bfloat16)
        for number in (1, 3, 5, 7):

            @pl.when(step == number)
            def _(number=number):
                give(second_buf.at[number], first_buf, 1, number // 2)


    def hidden_load(step):
        slot = lax.rem(step, 2)
        return pltpu.make_async_copy(
            hidden_all.at[step], image_buf.at[slot, :, pl.ds(0, feed)], load_sems.at[6 + slot]
        )

    def out_store(step):
        slot = lax.rem(step, 2)
        return pltpu.make_async_copy(own_pair.at[slot], partial_out.at[step], load_sems.at[8 + slot])

    def out_products():
        hidden_load(0).start()

        @pl.loop(0, 8)
        def _(step):
            slot = lax.rem(step, 2)
            hidden_load(step).wait()

            @pl.when(step < 7)
            def _():
                hidden_load(step + 1).start()

            @pl.when(step >= 2)
            def _():
                out_store(step - 2).wait()

            own_pair[slot] = contract(
                image_buf[slot, :, 0:feed], down_buf[...].reshape(8 * rows, feed), 1, 1
            ).astype(jnp.bfloat16)
            out_store(step).start()

        out_store(6).wait()
        out_store(7).wait()

    def up_hook(block):
        @pl.when(block == 6)
        def _():
            tick(7)

    def up_products():
        column_products(
            h_two_all,
            saved_grad,
            cols_buf,
            staged_buf,
            more.at[pl.ds(0, 4)],
            load_sems.at[pl.ds(3, 2)],
            load_sems.at[pl.ds(11, 2)],
            hook=up_hook,
        )

    def own_flow(number, finish):
        return scatter_flow(
            plane,
            lambda slot: second_buf.at[2 * slot],
            lambda slot: None,
            first_buf.at[pl.ds(0, 4)],
            Halves(first_buf.at[6], rows // 2),
            first_buf.at[pl.ds(4, 2)],
            sems(number),
            finish,
        )

    tick(6)
    up_products()
    send_outward(FIRST, EARLY)
    for step, _ in enumerate(own_flow(1, finish_feed)):
        tick((8, 10, 11)[step])
        if step == 0:
            tick(9)
    for slot in range(4):
        plane.gone(second_buf.at[slot], core_send.at[1, slot])

    gather = Gather(plane, own_grad, grad_all, gather_send, gather_recv)
    gather.start()

    def qkv_load(step):
        return pltpu.make_async_copy(
            qkv_all.at[flipped(mine, step)], qkv_buf.at[lax.rem(step, 2)], load_sems.at[1 + lax.rem(step, 2)]
        )

    qkv_load(0).start()
    attended_load.wait()
    out_sum[...] = jnp.zeros_like(out_sum)
    columns = qkv_buf.shape[-1]
    third = columns // 3
    scale = HD ** (-0.5)

    @pl.loop(0, 8)
    def _(step):
        for number in range(8):

            @pl.when(step == number)
            def _(number=number):
                if number in (1, 2, 4):
                    tick({1: 12, 2: 13, 4: 15}[number])
                if number == 2:
                    tick(14)
                gather.step(number)
                if number == 7:
                    gather.finish()

        image = flipped(mine, step)
        slot = lax.rem(step, 2)
        qkv_load(step).wait()

        @pl.when(step < 7)
        def _():
            qkv_load(step + 1).start()

        grad = grad_all[image]
        grad_attended = contract(grad, out_weight[...], 1, 1).astype(jnp.bfloat16)
        image_rows = pl.ds(pl.multiple_of(image * rows, rows), rows)
        for head in range(third // HD):
            begin, first = head * HD, 3 * head * HD
            queries = qkv_buf[slot, :, first : first + HD]
            key_rows = qkv_buf[slot, :, first + HD : first + 2 * HD]
            value_rows = qkv_buf[slot, :, first + 2 * HD : first + 3 * HD]
            grad_head = grad_attended[:, begin : begin + HD]
            attention = softmax_rows(queries, key_rows)
            grad_weights = contract(grad_head, value_rows, 1, 1)
            row_delta = jnp.sum(attention * grad_weights, axis=-1, keepdims=True)
            grad_scores = (attention * (grad_weights - row_delta)).astype(jnp.bfloat16)
            saved_grad[image_rows, first : first + HD] = (
                contract(grad_scores, key_rows, 1, 0) * scale
            ).astype(jnp.bfloat16)
            saved_grad[image_rows, first + HD : first + 2 * HD] = (
                contract(grad_scores, queries, 0, 0) * scale
            ).astype(jnp.bfloat16)
            saved_grad[image_rows, first + 2 * HD : first + 3 * HD] = contract(
                attention.astype(jnp.bfloat16), grad_head, 0, 0
            ).astype(jnp.bfloat16)
        out_sum[...] += contract(attended_buf[image], grad, 0, 0)
        second_buf[step] = contract(saved_grad[image_rows, 0:columns], qkv_weight[...], 1, 1).astype(
            jnp.bfloat16
        )
        for number in (1, 3, 5, 7):

            @pl.when(step == number)
            def _(number=number):
                give(second_buf.at[number], first_buf, 2, number // 2)

    ahead()

    for block in range(8):
        in_buf[block] = out_sum[:, block * rows : (block + 1) * rows].astype(jnp.bfloat16)
    out_copy = pltpu.make_async_copy(in_buf, more.at[7], load_sems.at[0])
    out_copy.start()
    column_products(
        h_all,
        saved_grad.at[:, pl.ds(0, columns)],
        cols_buf,
        staged_buf,
        more.at[pl.ds(4, 3)],
        load_sems.at[pl.ds(3, 2)],
        load_sems.at[pl.ds(11, 2)],
        [[(3 * head + number) * HD for head in range(third // HD)] for number in range(3)],
    )

    def finish_input(where, value):
        total = back_norm(plain(features, where), value, "scale_one", "shift_one")
        own_pair[0, where, :] = (total + grad_first[where, :]).astype(jnp.bfloat16)

    out_copy.wait()
    send_outward(EARLY, CHUNKS)
    tick(16)
    tick(17)
    for step, _ in enumerate(own_flow(2, finish_input)):
        for now in ((18, 19), (20,), (21,))[step]:
            tick(now)
        if step == 0:
            out_products()
    return_tokens(own_grad, token_grad, 1)
    for step, _ in enumerate(staged_flow(partial_out, grad_all, 0, finish_out)):
        for now in ((22, 23), (24,), (25,))[step]:
            tick(now)
    return_tokens(image_out, token_out, 0)

    mod_copies = []
    mod_sum[7:8, :] = mod[7:8, :]
    mod_rows = pl.ds(pl.multiple_of(place * 8, 8), 8)
    mod_land[mod_rows, :] = mod_sum[...]
    for step, other in enumerate(others):
        copy = remote(
            mod_sum, mod_land.at[mod_rows], mod_sems.at[0, step], mod_sems.at[1, step], (mine, other)
        )
        copy.start()
        mod_copies.append(copy)
    tick(26)
    for copy in mod_copies:
        copy.wait_recv()
    own = pltpu.make_async_copy(mod_land, mod_out.at[mine], mod_sems.at[0, 3])
    own.start()
    mod_gather = Gather(plane, mod_land, mod_out, mod_gather_sems.at[0], mod_gather_sems.at[1])
    mod_gather.start()
    tick(27)
    mod_gather.middle()
    mod_gather.far()
    for flip in (1, 3, 5, 7):
        mod_gather.crossed(flip)
    mod_gather.finish()
    for now in range(28, 2 * CHUNKS + 6):
        tick(now)
    own.wait()
    for copy in mod_copies:
        copy.wait_send()
    for copy in token_copies:
        copy.wait()
    for number in (0, 2):
        for slot in range(4):
            plane.gone(second_buf.at[slot], core_send.at[number, slot])

    @pl.when(is_mid)
    def _():
        for k in (CHUNKS - 2, CHUNKS - 1):
            plane.gone(sum_buf.at[k % 2, :, other_half], z_sems.at[0, 1, k])
        plane.gone(half_buf.at[0, pl.ds(0, 7)], x_sems.at[0, CHUNKS - 2])
        for k in range(CHUNKS):
            plane.gone(shares.at[k, :, my_half], z_sems.at[0, 2, k])
            plane.gone(shares.at[k, :, my_half], z_sems.at[0, 3, k])
            plane.gone(shares.at[k, :, other_half], z_sems.at[0, 4, k])

    @pl.when(jnp.logical_not(is_mid))
    def _():
        first = pl.ds(pl.multiple_of(jnp.where(place == 0, 0, HALF_ROWS), HALF_ROWS), HALF_ROWS)
        second = pl.ds(pl.multiple_of(jnp.where(place == 0, HALF_ROWS, 0), HALF_ROWS), HALF_ROWS)
        for k in range(CHUNKS):
            plane.gone(land_a.at[k], z_sems.at[0, 0, k])
            plane.got(shares.at[k, :, first], z_sems.at[1, 3, k])
            plane.got(shares.at[k, :, second], z_sems.at[1, 4, k])


def back_part(*operands):
    h_all, qkv_weight = operands[7], operands[10]
    _, rows, width = h_all.shape
    columns = qkv_weight.shape[1]
    feed = operands[1].shape[-1]
    low, full = jnp.bfloat16, jnp.float32
    dma = pltpu.SemaphoreType.DMA
    anywhere, inside = pl.BlockSpec(memory_space=pl.ANY), pl.BlockSpec(memory_space=pltpu.VMEM)
    return pl.pallas_call(
        back_kernel,
        out_shape=[
            jax.ShapeDtypeStruct((CHUNKS, 8, rows, rows), low),
            jax.ShapeDtypeStruct((4, rows // 4, width), low),
            jax.ShapeDtypeStruct((4, rows // 4, width), low),
            jax.ShapeDtypeStruct((8, 32, width), full),
            jax.ShapeDtypeStruct((CHUNKS - FIRST, 8, rows, rows), low),
            jax.ShapeDtypeStruct((8, rows, width), low),
            jax.ShapeDtypeStruct((CHUNKS, 8, rows, rows), low),
            jax.ShapeDtypeStruct((CHUNKS, 8, HALF_ROWS, rows), low),
        ],
        in_specs=[anywhere] * 10 + [inside] * 7,
        out_specs=[anywhere] * 8,
        scratch_shapes=[
            pltpu.VMEM((7, rows, width), low),
            pltpu.VMEM((8, rows, width), low),
            pltpu.VMEM((2, rows, width), low),
            pltpu.VMEM((2, rows, width), low),
            pltpu.VMEM((2, rows, feed), low),
            pltpu.VMEM((8, rows, width), low),
            pltpu.VMEM((8, rows, feed), low),
            pltpu.VMEM((rows, width), full),
            pltpu.VMEM((8 * rows, feed), low),
            pltpu.VMEM((2, 8, rows, rows), low),
            pltpu.VMEM((2, rows, columns), low),
            pltpu.VMEM((8, rows, columns // 3), low),
            pltpu.VMEM((2, 4, rows, rows), low),
            pltpu.VMEM((columns // 3, width), full),
            pltpu.VMEM((2, 8, rows, rows), low),
            pltpu.VMEM((8, rows, rows), low),
            pltpu.VMEM((2, 8, HALF_ROWS, rows), low),
            pltpu.VMEM((8, HALF_ROWS, rows), low),
            pltpu.VMEM((8, width), full),
            pltpu.VMEM((32, width), full),
            dma((3, 4)),
            dma((3, 4)),
            dma((3, 2)),
            dma((3, 2)),
            dma((3, 4)),
            dma((3, 4)),
            dma((2, 4)),
            dma((7 * PIECES,)),
            dma((7 * PIECES,)),
            dma((13,)),
            dma((2, 8)),
            dma((2, 5, CHUNKS)),
            dma((2, CHUNKS)),
            dma((3,)),
            dma((2, 2, 4)),
            dma((2, 4)),
            dma((2, 7 * PIECES)),
        ],
        compiler_params=pltpu.CompilerParams(
            collective_id=4, has_side_effects=True, vmem_limit_bytes=63 * 1024 * 1024
        ),
        name="back_part",
    )(*operands)


class Gather:
    def __init__(self, plane, own, result, send_sems, recv_sems):
        self.plane, self.own, self.result = plane, own, result
        self.send_sems, self.recv_sems = send_sems, recv_sems
        self.piece = own.shape[0] // PIECES

    def put(self, src, owner, part, flip, slot):
        remote(
            src,
            self.result.at[owner, pl.ds(part * self.piece, self.piece)],
            self.send_sems.at[slot],
            self.recv_sems.at[slot],
            self.plane.to(flip),
        ).start()

    def arrived(self, flip, part, slot):
        ref = self.result.at[self.plane.at(flip), pl.ds(part * self.piece, self.piece)]
        self.plane.got(ref, self.recv_sems.at[slot])
        return ref

    def start(self):
        mine = self.plane.mine
        for part in range(PIECES):
            src = self.own.at[pl.ds(part * self.piece, self.piece)]
            self.put(src, mine, part, 2, part)
            self.put(src, mine, part, 4, PIECES + part)
            self.put(src, mine, part, 1, 3 * PIECES + part)

    def middle(self):
        at = self.plane.at
        for part in range(PIECES):
            got = self.arrived(2, part, part)
            if part < PIECES // 2:
                self.put(got, at(2), part, 4, 2 * PIECES + part)
            self.put(got, at(2), part, 1, 4 * PIECES + part)
            got = self.arrived(4, part, PIECES + part)
            if part >= PIECES // 2:
                self.put(got, at(4), part, 2, 2 * PIECES + part)
            self.put(got, at(4), part, 1, 5 * PIECES + part)

    def far(self):
        for part in range(PIECES):
            got = self.arrived(6, part, 2 * PIECES + part)
            self.put(got, self.plane.at(6), part, 1, 6 * PIECES + part)

    def crossed(self, flip):
        for part in range(PIECES):
            self.arrived(flip, part, (3 + flip // 2) * PIECES + part)

    def step(self, number):
        if number == 2:
            self.middle()
        if number == 6:
            self.far()
        if number % 2:
            self.crossed(number)

    def finish(self):
        for slot in range(7 * PIECES):
            self.plane.gone(self.own.at[pl.ds(0, self.piece)], self.send_sems.at[slot])


class Halves:
    def __init__(self, ref, half):
        self.ref, self.half = ref, half

    @property
    def at(self):
        return self

    def __getitem__(self, number):
        return self.ref.at[pl.ds(number * self.half, self.half)]


def front_kernel(
    bin_ids,
    image_counts,
    noise,
    mod_bias,
    block_input,
    cotangent,
    attn_weight,
    mlp_weight,
    mod_weight,
    qkv_weight,
    out_weight,
    up_weight,
    down_low,
    h_one_all,
    h_two_all,
    grad_mlp_all,
    qkv_all,
    attended_all,
    hidden_all,
    slope_all,
    first_grads,
    features,
    first_sum,
    attn_out,
    grad_out,
    mod,
    load_buf,
    qkv_stage,
    up_stage,
    weight_buf,
    hidden_buf,
    cols_buf,
    staged_buf,
    h_all,
    qkv_buf,
    attended_buf,
    part_buf,
    scatter_buf,
    own_h,
    own_grad,
    own_next,
    bin_row,
    bin_land,
    mod_part,
    mod_land,
    load_sems,
    token_sems,
    bin_sems,
    mod_sems,
    weight_sems,
    beside_sems,
    gather_sems,
    core_send,
    core_recv,
    far_send,
    far_recv,
    near_send,
    near_recv,
    copy_sems,
):
    plane = Plane()
    mine, place, at = plane.mine, plane.place, plane.at
    rows, width = own_h.shape
    feed = up_stage.shape[-1]
    columns = qkv_stage.shape[-1]
    third = columns // 3
    piece = rows // 4
    others = [lax.rem(place + step, 4) for step in (1, 2, 3)]
    flips = (6, 7, 2, 4, 3, 5, 1, 0)
    greet([plane.to(flip) for flip in range(1, 8)] + [(mine, other) for other in others])

    token_copies = []
    my_rows = pl.ds(pl.multiple_of(place * piece, piece), piece)
    for number, (source, result) in enumerate(((block_input, features), (cotangent, grad_out))):
        copies = [
            pltpu.make_async_copy(
                source.at[place], result.at[my_rows], token_sems.at[0, number, 0]
            )
        ]
        for step, other in enumerate(others):
            copies.append(
                remote(
                    source.at[other],
                    result.at[my_rows],
                    token_sems.at[0, number, step + 1],
                    token_sems.at[1, number, step + 1],
                    (mine, other),
                )
            )
        for copy in copies:
            copy.start()
        token_copies.append(copies)

    lanes = lax.broadcasted_iota(jnp.int32, bin_row.shape, 1)
    bin_row[...] = jnp.where(lanes == bin_ids[place], 1.0, 0.0).astype(jnp.float32)
    bin_land[mine] = bin_row[...]
    bin_copies = [
        remote(
            bin_row, bin_land.at[mine], bin_sems.at[0, flip], bin_sems.at[1, flip], plane.to(flip)
        )
        for flip in range(1, 8)
    ]
    for copy in bin_copies:
        copy.start()

    parity = lax.rem(place, 2)
    beside = (mine, place + 1 - 2 * parity)

    def half_of(size):
        return pl.ds(pl.multiple_of(parity * size, size), size)

    def load_columns(source, slot, begins, size):
        return [
            pltpu.make_async_copy(
                source.at[:, pl.ds(pl.multiple_of(begin, HD), size)],
                load_buf.at[slot, :, pl.ds(number * size, size)],
                load_sems.at[slot, number],
            )
            for number, begin in enumerate(begins)
        ]

    def cast_and_send(source, begins_of, size, stage, result, kind):
        loads = [
            load_columns(source, step % 2, begins_of(at(flip)), size)
            for step, flip in enumerate(flips)
        ]
        total = size * len(loads[0])
        half = half_of(total)
        for load in loads[0]:
            load.start()
        for step, flip in enumerate(flips):
            if step + 1 < len(flips):
                for load in loads[step + 1]:
                    load.start()
            for load in loads[step]:
                load.wait()

            def cast(band, step=step):
                stage[step, band, 0:total] = load_buf[step % 2, band, 0:total].astype(jnp.bfloat16)

            bands(rows, cast)
            src = stage.at[step, :, pl.ds(0, total)]
            if flip:
                remote(
                    src,
                    result.at[mine, :, half],
                    weight_sems.at[0, kind, flip],
                    weight_sems.at[1, kind, flip],
                    plane.to(flip),
                ).start()
            else:
                pltpu.make_async_copy(
                    src, result.at[mine, :, half], weight_sems.at[0, kind, 0]
                ).start()

    def pass_on(stage, result, kind, total):
        half = half_of(total)
        pltpu.make_async_copy(
            stage.at[7, :, pl.ds(0, total)], result.at[mine, :, half], weight_sems.at[0, kind, 0]
        ).wait()
        for flip in (1, 2, 3, 4, 5, 6, 7, 0):
            piece = result.at[at(flip), :, half]
            if flip:
                plane.got(piece, weight_sems.at[1, kind, flip])
            remote(
                piece,
                piece,
                beside_sems.at[0, kind, flip],
                beside_sems.at[1, kind, flip],
                beside,
            ).start()

    def weights_ready(stage, result, kind, total):
        for flip in range(8):
            piece = result.at[at(flip), :, half_of(total)]
            plane.got(piece, beside_sems.at[1, kind, flip])
            plane.gone(piece, beside_sems.at[0, kind, flip])
            if flip:
                plane.gone(stage.at[0, :, pl.ds(0, total)], weight_sems.at[0, kind, flip])

    cast_and_send(
        attn_weight,
        lambda owner: [number * width + owner * third + parity * HD for number in range(3)],
        HD,
        qkv_stage,
        qkv_weight,
        0,
    )

    cast_and_send(
        mlp_weight,
        lambda owner: [owner * feed + parity * (feed // 2)],
        feed // 2,
        up_stage,
        up_weight,
        1,
    )

    for copy in bin_copies:
        copy.wait_recv()
    bins = noise.shape[0]
    activated = noise[...] / (1.0 + jnp.exp(-noise[...]))
    chosen = jnp.dot(
        bin_land[:, 0, :bins], activated, precision=PRECISE, preferred_element_type=jnp.float32
    )

    def load_mod(number):
        return pltpu.make_async_copy(
            mod_weight.at[:, pl.ds(number * width, width)],
            load_buf.at[number % 2],
            load_sems.at[number % 2, 0],
        )

    load_mod(0).start()
    mod_part[...] = jnp.zeros_like(mod_part)
    for number in range(6):
        if number < 5:
            load_mod(number + 1).start()
        load_mod(number).wait()
        mod_part[:, number, :] = jnp.dot(
            chosen, load_buf[number % 2], precision=PRECISE, preferred_element_type=jnp.float32
        )
    quarter = width // 4
    for number in range(3):
        index = 3 * mine + number
        where = pl.ds(pl.multiple_of(lax.rem(index, 4) * quarter, quarter), quarter)
        for image in range(8):
            mod_part[image, pl.ds(index // 4, 1), where] += mod_bias[
                :, number * quarter : (number + 1) * quarter
            ]
    mod_copies = [
        remote(
            mod_part.at[at(flip)],
            mod_land.at[mine],
            mod_sems.at[0, flip],
            mod_sems.at[1, flip],
            plane.to(flip),
        )
        for flip in range(1, 8)
    ]
    for copy in mod_copies:
        copy.start()
    pass_on(qkv_stage, qkv_weight, 0, 3 * HD)
    mod_land[mine] = mod_part[mine]
    for copy in mod_copies:
        copy.wait_recv()
    total = mod_land[0]
    for number in range(1, 8):
        total = total + mod_land[number]
    mod[...] = total
    live = jnp.where(place < image_counts[0], 1.0, 0.0).astype(jnp.float32)
    mod[6:7, :] = jnp.full((1, width), 1.0, jnp.float32) * live
    mod[7:8, :] = jnp.zeros((1, width), jnp.float32)
    mod[7:8, :128] = bin_row[0:1, :]

    def mod_row(number):
        return mod[number : number + 1, :]

    def tokens_arrived(number):
        for copy in token_copies[number]:
            if copy is token_copies[number][0]:
                copy.wait()
            else:
                copy.wait_recv()

    tokens_arrived(0)

    def first_norm(band):
        source = plain(features, band)
        normed = (source * rms_scale(source) * (1.0 + mod_row(1)) + mod_row(0)).astype(jnp.bfloat16)
        own_h[band, :] = normed
        h_all[mine, band, :] = normed

    bands(rows, first_norm)
    h_gather = Gather(plane, own_h, h_all, gather_sems.at[0, 0], gather_sems.at[0, 1])
    h_gather.start()

    tokens_arrived(1)

    def feed_grad(band):
        scaled = plain(grad_out, band) * mod_row(6)
        grad_out[band, :] = scaled.astype(jnp.bfloat16)
        own_grad[band, :] = (mod_row(5) * scaled).astype(jnp.bfloat16)

    bands(rows, feed_grad)
    grad_own = pltpu.make_async_copy(own_grad, grad_mlp_all.at[mine], copy_sems.at[0])
    grad_own.start()
    grad_gather = Gather(plane, own_grad, grad_mlp_all, gather_sems.at[1, 0], gather_sems.at[1, 1])
    grad_gather.start()
    def down_load(owner):
        return pltpu.make_async_copy(
            mlp_weight.at[:, pl.ds((8 + owner) * feed, feed)],
            load_buf.at[owner % 2, :, pl.ds(0, feed)],
            load_sems.at[owner % 2, 0],
        )

    def down_store(owner):
        return pltpu.make_async_copy(
            part_buf.at[owner, :, pl.ds(0, feed)], down_low.at[owner], copy_sems.at[6 + owner]
        )

    down_load(0).start()
    for owner in range(8):
        if owner < 7:
            down_load(owner + 1).start()
        down_load(owner).wait()

        def cast_down(band, owner=owner):
            part_buf[owner, band, 0:feed] = load_buf[owner % 2, band, 0:feed].astype(jnp.bfloat16)

        bands(rows, cast_down)
        down_store(owner).start()
    for owner in range(8):
        down_store(owner).wait()
    load = pltpu.make_async_copy(
        attn_weight.at[:, pl.ds(3 * width, width)], load_buf.at[0], load_sems.at[0, 0]
    )
    load.start()
    load.wait()

    def cast_out(band):
        out_weight[band, :] = load_buf[0, band, :].astype(jnp.bfloat16)

    bands(rows, cast_out)

    weights_ready(qkv_stage, qkv_weight, 0, 3 * HD)
    load = pltpu.make_async_copy(qkv_weight, weight_buf, copy_sems.at[1])
    load.start()
    load.wait()

    @pl.loop(0, 8)
    def _(step):
        for number in range(8):

            @pl.when(step == number)
            def _(number=number):
                h_gather.step(number)

        image = flipped(mine, step)
        pltpu.make_async_copy(h_all.at[image], h_one_all.at[image], copy_sems.at[2]).start()
        projected = contract(
            h_all[image], weight_buf[...].reshape(8 * rows, columns), 1, 0
        ).astype(jnp.bfloat16)
        qkv_buf[image] = projected
        for head in range(third // HD):
            begin, first = head * HD, 3 * head * HD
            queries = projected[:, first : first + HD]
            key_rows = projected[:, first + HD : first + 2 * HD]
            value_rows = projected[:, first + 2 * HD : first + 3 * HD]
            attention = softmax_rows(queries, key_rows).astype(jnp.bfloat16)
            attended_buf[image, :, begin : begin + HD] = contract(
                attention, value_rows, 1, 0
            ).astype(jnp.bfloat16)
        part_buf[step] = contract(attended_buf[image], out_weight[...], 1, 0).astype(jnp.bfloat16)
        pltpu.make_async_copy(h_all.at[image], h_one_all.at[image], copy_sems.at[2]).wait()

        @pl.when(step == 7)
        def _():
            h_gather.finish()

        for number in (1, 3, 5, 7):

            @pl.when(step == number)
            def _(number=number):
                slot = number // 2
                remote(
                    part_buf.at[number],
                    scatter_buf.at[slot],
                    core_send.at[slot],
                    core_recv.at[slot],
                    plane.to(1),
                ).start()

    pass_on(up_stage, up_weight, 1, feed // 2)
    keeps = [
        pltpu.make_async_copy(qkv_buf, qkv_all, copy_sems.at[3]),
        pltpu.make_async_copy(attended_buf, attended_all, copy_sems.at[4]),
    ]
    for copy in keeps:
        copy.start()

    def second_norm(band, value):
        attn_out[band, :] = value.astype(jnp.bfloat16)
        source = plain(features, band) + mod_row(2) * value
        first_sum[band, :] = source
        normed = (source * rms_scale(source) * (1.0 + mod_row(4)) + mod_row(3)).astype(jnp.bfloat16)
        own_next[band, :] = normed
        h_all[mine, band, :] = normed

    flow = scatter_flow(
        plane,
        lambda slot: part_buf.at[2 * slot],
        lambda slot: None,
        scatter_buf.at[pl.ds(0, 4)],
        Halves(scatter_buf.at[6], rows // 2),
        scatter_buf.at[pl.ds(4, 2)],
        (core_recv, far_send, far_recv, near_send, near_recv),
        second_norm,
    )
    for number, _ in enumerate(flow):
        if number == 1:
            grad_gather.middle()
    for slot in range(4):
        plane.gone(part_buf.at[slot], core_send.at[slot])
    next_gather = Gather(plane, own_next, h_all, gather_sems.at[2, 0], gather_sems.at[2, 1])
    next_gather.start()
    grad_gather.far()
    weights_ready(up_stage, up_weight, 1, feed // 2)
    load = pltpu.make_async_copy(up_weight, up_stage, copy_sems.at[1])
    load.start()
    load.wait()

    @pl.loop(0, 8)
    def _(step):
        for number in range(8):

            @pl.when(step == number)
            def _(number=number):
                next_gather.step(number)

        image = flipped(mine, step)
        pre = contract(h_all[image], up_stage[...].reshape(8 * rows, feed), 1, 0)
        hidden, slope = gelu_and_slope(pre)
        hidden_buf[pl.ds(pl.multiple_of(image * rows, rows), rows), :] = hidden.astype(jnp.bfloat16)
        part_buf[image, :, 0:feed] = slope.astype(jnp.bfloat16)

    keeps.append(pltpu.make_async_copy(h_all, h_two_all, copy_sems.at[2]))
    keeps.append(pltpu.make_async_copy(hidden_buf, hidden_all, copy_sems.at[5]))
    keeps.append(
        pltpu.make_async_copy(part_buf.at[:, :, pl.ds(0, feed)], slope_all, copy_sems.at[1])
    )
    for copy in keeps[-3:]:
        copy.start()
    for flip in (1, 3, 5, 7):
        grad_gather.crossed(flip)
    grad_own.wait()
    column_products(
        grad_mlp_all,
        hidden_buf,
        cols_buf,
        staged_buf,
        first_grads,
        copy_sems.at[pl.ds(6, 2)],
        copy_sems.at[pl.ds(8, 2)],
    )
    for gather in (grad_gather, next_gather):
        gather.finish()
    for copy in keeps:
        copy.wait()
    for copies in token_copies:
        for copy in copies[1:]:
            copy.wait_send()
    for copy in bin_copies + mod_copies:
        copy.wait_send()


def front_part(
    bin_ids,
    image_counts,
    noise,
    mod_bias,
    block_input,
    cotangent,
    attn_weight,
    mlp_weight,
    mod_weight,
):
    slots, local_tok, width = block_input.shape
    rows = slots * local_tok
    columns, feed = 3 * width // 8, mlp_weight.shape[1] // 16
    low, full = jnp.bfloat16, jnp.float32
    dma = pltpu.SemaphoreType.DMA
    anywhere, inside = pl.BlockSpec(memory_space=pl.ANY), pl.BlockSpec(memory_space=pltpu.VMEM)
    scalars = pl.BlockSpec(memory_space=pltpu.SMEM)
    return pl.pallas_call(
        front_kernel,
        out_shape=[
            jax.ShapeDtypeStruct((8, rows, columns), low),
            jax.ShapeDtypeStruct((rows, width), low),
            jax.ShapeDtypeStruct((8, rows, feed), low),
            jax.ShapeDtypeStruct((8, rows, feed), low),
            jax.ShapeDtypeStruct((8, rows, width), low),
            jax.ShapeDtypeStruct((8, rows, width), low),
            jax.ShapeDtypeStruct((8, rows, width), low),
            jax.ShapeDtypeStruct((8, rows, columns), low),
            jax.ShapeDtypeStruct((8, rows, columns // 3), low),
            jax.ShapeDtypeStruct((8 * rows, feed), low),
            jax.ShapeDtypeStruct((8, rows, feed), low),
            jax.ShapeDtypeStruct((FIRST, 8, rows, rows), low),
            jax.ShapeDtypeStruct((rows, width), low),
            jax.ShapeDtypeStruct((rows, width), full),
            jax.ShapeDtypeStruct((rows, width), low),
            jax.ShapeDtypeStruct((rows, width), low),
            jax.ShapeDtypeStruct((8, width), full),
        ],
        in_specs=[scalars] * 2 + [inside] * 2 + [anywhere] * 5,
        out_specs=[anywhere, inside] + [anywhere] * 10 + [inside] * 5,
        scratch_shapes=[
            pltpu.VMEM((2, rows, width), full),
            pltpu.VMEM((8, rows, columns), low),
            pltpu.VMEM((8, rows, feed), low),
            pltpu.VMEM((8, rows, columns), low),
            pltpu.VMEM((8 * rows, feed), low),
            pltpu.VMEM((2, 8, rows, rows), low),
            pltpu.VMEM((2, 4, rows, rows), low),
            pltpu.VMEM((8, rows, width), low),
            pltpu.VMEM((8, rows, columns), low),
            pltpu.VMEM((8, rows, columns // 3), low),
            pltpu.VMEM((8, rows, width), low),
            pltpu.VMEM((7, rows, width), low),
            pltpu.VMEM((rows, width), low),
            pltpu.VMEM((rows, width), low),
            pltpu.VMEM((rows, width), low),
            pltpu.VMEM((8, 128), full),
            pltpu.VMEM((8, 8, 128), full),
            pltpu.VMEM((8, 8, width), full),
            pltpu.VMEM((8, 8, width), full),
            dma((2, 3)),
            dma((2, 2, 4)),
            dma((2, 8)),
            dma((2, 8)),
            dma((2, 2, 8)),
            dma((2, 2, 8)),
            dma((3, 2, 7 * PIECES)),
            dma((4,)),
            dma((4,)),
            dma((2,)),
            dma((2,)),
            dma((4,)),
            dma((4,)),
            dma((14,)),
        ],
        compiler_params=pltpu.CompilerParams(
            collective_id=5, has_side_effects=True, vmem_limit_bytes=63 * 1024 * 1024
        ),
        name="front_part",
    )(
        bin_ids,
        image_counts,
        noise,
        mod_bias,
        block_input,
        cotangent,
        attn_weight,
        mlp_weight,
        mod_weight,
    )


def tail_kernel(
    mlp_ref,
    attn_ref,
    rows_ref,
    onehot_ref,
    noise_ref,
    weight_ref,
    out_ref,
    grad_ref,
    mlp_grad_ref,
    attn_grad_ref,
    weight_grad_ref,
    noise_grad_ref,
    bias_ref,
    block_out_ref,
    input_grad_ref,
    chosen,
    total,
):
    step = pl.program_id(0)
    size = mlp_ref.shape[-1]
    for number in range(4):
        mlp_grad_ref[:, number * size : (number + 1) * size] = mlp_ref[number, 0].astype(
            jnp.float32
        )
    for number in range(2):
        attn_grad_ref[:, number * size : (number + 1) * size] = attn_ref[0, number].astype(
            jnp.float32
        )
    block_out_ref[...] = out_ref[...]
    input_grad_ref[...] = grad_ref[...].astype(jnp.float32)
    noise = noise_ref[...]
    onehot = onehot_ref[...]
    rise = 1.0 / (1.0 + jnp.exp(-noise))

    @pl.when(step == 0)
    def _():
        chosen[...] = jnp.dot(
            onehot, noise * rise, precision=PRECISE, preferred_element_type=jnp.float32
        )
        total[...] = jnp.zeros_like(total)

    grads = rows_ref[...]
    bias_ref[...] = jnp.broadcast_to(jnp.sum(grads, axis=0, keepdims=True), bias_ref.shape)
    low = grads.astype(jnp.bfloat16)
    weight_grad_ref[...] = contract(chosen[...].astype(jnp.bfloat16), low, 0, 0)
    total[...] += contract(weight_ref[...].astype(jnp.bfloat16), low, 1, 1)

    @pl.when(step == pl.num_programs(0) - 1)
    def _():
        table = lax.dot_general(
            onehot,
            total[...],
            (((0,), (1,)), ((), ())),
            precision=PRECISE,
            preferred_element_type=jnp.float32,
        )
        noise_grad_ref[...] = table * (rise + noise * rise * (1.0 - rise))


def tail_part(shares, image_rows, onehot, noise, weight, token_out, token_grad):
    steps = 16
    rows = shares.shape[2]
    images = image_rows.shape[0]
    depth, columns = weight.shape
    part = columns // steps
    slots, local_tok, width = token_out.shape
    token_spec = pl.BlockSpec((1, local_tok, width // 4), lambda step: (step // 4, 0, step % 4))
    return pl.pallas_call(
        tail_kernel,
        grid=(steps,),
        out_shape=[
            jax.ShapeDtypeStruct((rows, 64 * rows), jnp.float32),
            jax.ShapeDtypeStruct((rows, 32 * rows), jnp.float32),
            jax.ShapeDtypeStruct(weight.shape, jnp.float32),
            jax.ShapeDtypeStruct(noise.shape, jnp.float32),
            jax.ShapeDtypeStruct((8, columns), jnp.float32),
            jax.ShapeDtypeStruct(token_out.shape, jnp.bfloat16),
            jax.ShapeDtypeStruct(token_grad.shape, jnp.float32),
        ],
        in_specs=[
            pl.BlockSpec((4, 1, rows, rows), lambda step: (1 - step // 8, step % 8, 0, 0)),
            pl.BlockSpec((1, 2, rows, rows), lambda step: (EARLY + step // 4, step % 4, 0, 0)),
            pl.BlockSpec((images, part), lambda step: (0, step)),
            pl.BlockSpec(onehot.shape, lambda step: (0, 0)),
            pl.BlockSpec(noise.shape, lambda step: (0, 0)),
            pl.BlockSpec((depth, part), lambda step: (0, step)),
            token_spec,
            token_spec,
        ],
        out_specs=[
            pl.BlockSpec((rows, 4 * rows), lambda step: (0, step)),
            pl.BlockSpec((rows, 2 * rows), lambda step: (0, step)),
            pl.BlockSpec((depth, part), lambda step: (0, step)),
            pl.BlockSpec(noise.shape, lambda step: (0, 0)),
            pl.BlockSpec((8, part), lambda step: (0, step)),
            token_spec,
            token_spec,
        ],
        scratch_shapes=[
            pltpu.VMEM((images, depth), jnp.float32),
            pltpu.VMEM((depth, images), jnp.float32),
        ],
        compiler_params=pltpu.CompilerParams(vmem_limit_bytes=VMEM_BYTES),
        name="tail_part",
    )(shares, shares, image_rows, onehot, noise, weight, token_out, token_grad)


def plane_body(
    block_input,
    cotangent,
    bin_ids,
    image_counts,
    attn_weight,
    mlp_weight,
    noise_table,
    mod_weight,
    mod_bias,
):
    model_width = block_input.shape[2]
    rows = attn_weight.shape[0]
    bins = noise_table.shape[0]
    bias_piece = mod_bias.shape[0]
    mine = lax.axis_index("fsdp")
    (
        qkv_weight,
        out_weight,
        up_weight,
        down_low,
        h_one_all,
        h_two_all,
        grad_mlp_all,
        qkv_all,
        attended_all,
        hidden_all,
        slope_all,
        first_grads,
        features,
        first_sum,
        attn_out,
        grad_out,
        mod_rows,
    ) = front_part(
        bin_ids,
        image_counts,
        noise_table,
        mod_bias.reshape(1, bias_piece),
        block_input,
        cotangent,
        attn_weight,
        mlp_weight,
        mod_weight,
    )

    def flat(array):
        return array.reshape(-1, array.shape[-1])

    shares, token_out, token_grad, mod_out, _, _, _, _ = back_part(
        down_low,
        up_weight,
        hidden_all.reshape(8, rows, -1),
        slope_all,
        grad_mlp_all,
        h_two_all,
        first_grads,
        h_one_all,
        qkv_all,
        attended_all,
        flat(qkv_weight),
        out_weight,
        features,
        first_sum,
        attn_out,
        grad_out,
        mod_rows,
    )
    mod_out = mod_out.reshape(8, 4, 8, model_width)
    onehot_all = mod_out[:, :, 7, :bins].reshape(-1, bins)
    (
        mlp_weight_grad,
        attn_weight_grad,
        mod_weight_grad,
        noise_grad,
        bias_sums,
        block_out,
        input_grad,
    ) = tail_part(
        shares,
        mod_out[:, :, :6].reshape(-1, 6 * model_width),
        onehot_all,
        noise_table,
        mod_weight,
        token_out,
        token_grad,
    )
    mod_bias_grad = lax.dynamic_slice_in_dim(bias_sums[0], mine * bias_piece, bias_piece)
    return (
        block_out,
        input_grad,
        attn_weight_grad,
        mlp_weight_grad,
        noise_grad,
        mod_weight_grad,
        mod_bias_grad,
    )


def solution(mesh):
    fits = mesh.shape["fsdp"] == 8 and mesh.shape["blk"] == 4
    return jax.shard_map(
        plane_body if fits else body,
        mesh=mesh,
        in_specs=(
            P("fsdp", "blk", None),
            P("fsdp", "blk", None),
            P("fsdp"),
            P("fsdp"),
            P("fsdp", None),
            P("fsdp", None),
            P(None, "fsdp"),
            P("fsdp", None),
            P("fsdp"),
        ),
        out_specs=(
            P("fsdp", "blk", None),
            P("fsdp", "blk", None),
            P("fsdp", None),
            P("fsdp", None),
            P(None, "fsdp"),
            P("fsdp", None),
            P("fsdp"),
        ),
        check_vma=False,
    )
```

```python
import functools
import math

import jax
import jax.numpy as jnp
from jax import lax
from jax.experimental import pallas as pl
from jax.experimental.pallas import tpu as pltpu
from jax.sharding import PartitionSpec as P

HD = 128


EPSILON = 1e-06
PRECISE = lax.Precision.HIGHEST


def norm_mod(features, scaling, shifting):
    normed = features * lax.rsqrt(jnp.mean(features * features, axis=-1, keepdims=True) + EPSILON)
    return normed * (1.0 + scaling) + shifting


def rows_product(left_rows, right_rows):
    return lax.dot_general(
        left_rows, right_rows, (((0,), (0,)), ((), ())), preferred_element_type=jnp.float32
    )


def body(
    block_input,
    cotangent,
    bin_ids,
    image_counts,
    attn_weight,
    mlp_weight,
    noise_table,
    mod_weight,
    mod_bias,
):
    slot_count, local_tok, model_width = block_input.shape
    row_count = slot_count * local_tok
    feed_width = mlp_weight.shape[1] // 2
    head_count = model_width // HD
    blk_size = lax.axis_size("blk")
    image_tok = local_tok * blk_size
    score_scale = HD ** (-0.5)
    bias_piece = mod_bias.shape[0]
    activated = jax.nn.silu(noise_table)
    partial_mod = jnp.dot(activated, mod_weight, precision=PRECISE)
    bias_full = lax.dynamic_update_slice_in_dim(
        jnp.zeros((6 * model_width,), jnp.float32), mod_bias, lax.axis_index("fsdp") * bias_piece, 0
    )
    mod_table = lax.psum(partial_mod + bias_full[None, :], "fsdp")
    onehot = (
        bin_ids[:, None] == jnp.arange(noise_table.shape[0], dtype=jnp.int32)[None, :]
    ).astype(jnp.float32)
    mod_image = jnp.dot(onehot, mod_table, precision=PRECISE)
    shift_one, scale_one, gate_one, shift_two, scale_two, gate_two = [
        member[:, None, :] for member in jnp.split(mod_image, 6, axis=-1)
    ]
    live_mask = (jnp.arange(slot_count) < image_counts[0]).astype(jnp.float32)[:, None, None]
    features = block_input.astype(jnp.float32)
    h_one = (
        norm_mod(features, scale_one, shift_one)
        .astype(jnp.bfloat16)
        .reshape(row_count, model_width)
    )
    attn_full = lax.all_gather(attn_weight.astype(jnp.bfloat16), "fsdp", axis=0, tiled=True)
    projected = jnp.dot(
        h_one, attn_full[:, : 3 * model_width], preferred_element_type=jnp.float32
    ).astype(jnp.bfloat16)
    queries = projected[:, :model_width].reshape(slot_count, local_tok, head_count, HD)
    key_rows = projected[:, model_width : 2 * model_width].reshape(
        slot_count, local_tok, model_width
    )
    value_rows = projected[:, 2 * model_width :].reshape(slot_count, local_tok, model_width)
    all_keys, all_values = (
        lax.all_gather(key_rows, "blk", axis=1, tiled=True),
        lax.all_gather(value_rows, "blk", axis=1, tiled=True),
    )
    all_keys = all_keys.reshape(slot_count, image_tok, head_count, HD)
    all_values = all_values.reshape(slot_count, image_tok, head_count, HD)

    def scores_of(query_rows):
        return (
            jnp.einsum("sqhd,skhd->shqk", query_rows, all_keys, preferred_element_type=jnp.float32)
            * score_scale
        )

    scores = scores_of(queries)
    maximum = jnp.max(scores, axis=-1, keepdims=True)
    exponent = jnp.exp(scores - maximum)
    denominator = jnp.sum(exponent, axis=-1, keepdims=True)
    attention = exponent / denominator
    log_total = maximum + jnp.log(denominator)
    attended = (
        jnp.einsum(
            "shqk,skhd->sqhd",
            attention.astype(jnp.bfloat16),
            all_values,
            preferred_element_type=jnp.float32,
        )
        .astype(jnp.bfloat16)
        .reshape(row_count, model_width)
    )
    attn_out = jnp.dot(
        attended, attn_full[:, 3 * model_width :], preferred_element_type=jnp.float32
    ).reshape(slot_count, local_tok, model_width)
    first_sum = features + gate_one * attn_out
    h_two = (
        norm_mod(first_sum, scale_two, shift_two)
        .astype(jnp.bfloat16)
        .reshape(row_count, model_width)
    )
    mlp_full = lax.all_gather(mlp_weight.astype(jnp.bfloat16), "fsdp", axis=0, tiled=True)
    pre_gelu = jnp.dot(h_two, mlp_full[:, :feed_width], preferred_element_type=jnp.float32)
    hidden = jax.nn.gelu(pre_gelu).astype(jnp.bfloat16)
    mlp_out = jnp.einsum(
        "rf,df->rd", hidden, mlp_full[:, feed_width:], preferred_element_type=jnp.float32
    ).reshape(slot_count, local_tok, model_width)
    second_sum = first_sum + gate_two * mlp_out
    block_out = (live_mask * second_sum).astype(jnp.bfloat16)
    grad_out = cotangent.astype(jnp.float32) * live_mask
    grad_mlp = (gate_two * grad_out).astype(jnp.bfloat16).reshape(row_count, model_width)
    grad_gate_two = jnp.sum(grad_out * mlp_out, axis=1)
    grad_hidden = jnp.dot(grad_mlp, mlp_full[:, feed_width:], preferred_element_type=jnp.float32)
    grad_pre = jax.vjp(jax.nn.gelu, pre_gelu)[1](grad_hidden)[0].astype(jnp.bfloat16)
    grad_h_two = jnp.einsum(
        "rf,df->rd", grad_pre, mlp_full[:, :feed_width], preferred_element_type=jnp.float32
    ).reshape(slot_count, local_tok, model_width)
    grad_first, grad_scale_two, grad_shift_two = jax.vjp(norm_mod, first_sum, scale_two, shift_two)[
        1
    ](grad_h_two)
    grad_first = grad_first + grad_out
    grad_attn_out = (gate_one * grad_first).astype(jnp.bfloat16).reshape(row_count, model_width)
    grad_gate_one = jnp.sum(grad_first * attn_out, axis=1)
    grad_attended = jnp.einsum(
        "rd,ed->re",
        grad_attn_out,
        attn_full[:, 3 * model_width :],
        preferred_element_type=jnp.float32,
    ).astype(jnp.bfloat16)
    grad_heads = grad_attended.reshape(slot_count, local_tok, head_count, HD)
    recomputed = jnp.exp(scores_of(queries) - log_total)
    grad_weights = jnp.einsum(
        "sqhd,skhd->shqk", grad_heads, all_values, preferred_element_type=jnp.float32
    )
    row_delta = jnp.sum(recomputed * grad_weights, axis=-1, keepdims=True)
    grad_scores = (recomputed * (grad_weights - row_delta)).astype(jnp.bfloat16)
    grad_queries = (
        jnp.einsum("shqk,skhd->sqhd", grad_scores, all_keys, preferred_element_type=jnp.float32)
        * score_scale
    )
    grad_keys_all = (
        jnp.einsum("shqk,sqhd->skhd", grad_scores, queries, preferred_element_type=jnp.float32)
        * score_scale
    )
    grad_values_all = jnp.einsum(
        "shqk,sqhd->skhd",
        recomputed.astype(jnp.bfloat16),
        grad_heads,
        preferred_element_type=jnp.float32,
    )
    grad_keys, grad_values = (
        lax.psum_scatter(
            grad_keys_all.reshape(slot_count, image_tok, model_width).astype(jnp.bfloat16),
            "blk",
            scatter_dimension=1,
            tiled=True,
        ).astype(jnp.float32),
        lax.psum_scatter(
            grad_values_all.reshape(slot_count, image_tok, model_width).astype(jnp.bfloat16),
            "blk",
            scatter_dimension=1,
            tiled=True,
        ).astype(jnp.float32),
    )
    grad_qkv = jnp.concatenate(
        [
            grad_queries.reshape(row_count, model_width).astype(jnp.bfloat16),
            grad_keys.reshape(row_count, model_width).astype(jnp.bfloat16),
            grad_values.reshape(row_count, model_width).astype(jnp.bfloat16),
        ],
        axis=1,
    )
    grad_h_one = jnp.einsum(
        "rc,dc->rd", grad_qkv, attn_full[:, : 3 * model_width], preferred_element_type=jnp.float32
    ).reshape(slot_count, local_tok, model_width)
    grad_input, grad_scale_one, grad_shift_one = jax.vjp(norm_mod, features, scale_one, shift_one)[
        1
    ](grad_h_one)
    input_grad = grad_input + grad_first
    grad_mod = jnp.concatenate(
        [
            grad_shift_one[:, 0, :],
            grad_scale_one[:, 0, :],
            grad_gate_one,
            grad_shift_two[:, 0, :],
            grad_scale_two[:, 0, :],
            grad_gate_two,
        ],
        axis=-1,
    )
    bin_terms = lax.dot_general(onehot, grad_mod, (((0,), (0,)), ((), ())), precision=PRECISE)
    grad_bins = lax.psum(bin_terms, ("fsdp", "blk"))
    table_term = jnp.einsum("be,de->bd", grad_bins, mod_weight, precision=PRECISE)
    noise_grad = jax.vjp(jax.nn.silu, noise_table)[1](table_term)[0]
    mod_weight_grad = lax.dot_general(
        activated, grad_bins, (((0,), (0,)), ((), ())), precision=PRECISE
    )
    mod_bias_grad = lax.dynamic_slice_in_dim(
        jnp.sum(grad_bins, axis=0), lax.axis_index("fsdp") * bias_piece, bias_piece
    )
    h_part = h_one
    attn_part = lax.psum_scatter(
        jnp.concatenate(
            [rows_product(h_part, grad_qkv), rows_product(attended, grad_attn_out)], axis=1
        ).astype(jnp.bfloat16),
        "fsdp",
        scatter_dimension=0,
        tiled=True,
    )
    h_part = h_two
    mlp_part = lax.psum_scatter(
        jnp.concatenate(
            [rows_product(h_part, grad_pre), rows_product(grad_mlp, hidden)], axis=1
        ).astype(jnp.bfloat16),
        "fsdp",
        scatter_dimension=0,
        tiled=True,
    )
    attn_weight_grad, mlp_weight_grad = (
        lax.psum(attn_part, "blk").astype(jnp.float32),
        lax.psum(mlp_part, "blk").astype(jnp.float32),
    )
    return (
        block_out,
        input_grad,
        attn_weight_grad,
        mlp_weight_grad,
        noise_grad,
        mod_weight_grad,
        mod_bias_grad,
    )


MESH_ID = pl.DeviceIdType.MESH
VMEM_BYTES = 56 * 1024 * 1024


def contract(left, right, left_dim, right_dim):
    return lax.dot_general(
        left, right, (((left_dim,), (right_dim,)), ((), ())), preferred_element_type=jnp.float32
    )


def plane_places():
    mine = lax.axis_index("fsdp")
    plane = lax.axis_index("blk")
    core = lax.rem(mine, 2)
    col = lax.rem(mine // 2, 2)
    row = mine // 4

    def at(flip):
        flip_row, flip_col, flip_core = flip // 4, (flip // 2) % 2, flip % 2
        new_row = 1 - row if flip_row else row
        new_col = 1 - col if flip_col else col
        new_core = 1 - core if flip_core else core
        return new_row * 4 + new_col * 2 + new_core

    return mine, plane, at


def greet(places):
    barrier = pltpu.get_barrier_semaphore()
    for place in places:
        pl.semaphore_signal(barrier, inc=1, device_id=place, device_id_type=MESH_ID)
    pl.semaphore_wait(barrier, len(places))


def remote(src, dst, send_sem, recv_sem, place):
    return pltpu.make_async_remote_copy(
        src_ref=src,
        dst_ref=dst,
        send_sem=send_sem,
        recv_sem=recv_sem,
        device_id=place,
        device_id_type=MESH_ID,
    )


PIECES = 4


def softmax_rows(queries, key_rows):
    scores = contract(queries, key_rows, 1, 1) * HD ** (-0.5)
    exponent = jnp.exp(scores - jnp.max(scores, axis=-1, keepdims=True))
    return exponent / jnp.sum(exponent, axis=-1, keepdims=True)


def rms_scale(features):
    return lax.rsqrt(jnp.mean(features * features, axis=-1, keepdims=True) + EPSILON)


CHUNKS = 12
FIRST = 4
EARLY = 8
HALF_ROWS = 128
BAND = 32


def flipped(mine, flip):
    total = 0
    for bit in (1, 2, 4):
        total = total + lax.rem(mine // bit + flip // bit, 2) * bit
    return total


def bands(count, step):
    @pl.loop(0, count // BAND)
    def _(index):
        step(pl.ds(pl.multiple_of(index * BAND, BAND), BAND))


def plain(ref, rows):
    return ref[rows, :].astype(jnp.float32)


def column_products(source, right, cols, staged, result, load_sems, store_sems, pieces=None, hook=None):
    rows = cols.shape[-1]
    count = result.shape[0]

    def load(block):
        slot = lax.rem(block, 2)
        return pltpu.make_async_copy(
            source.at[:, :, pl.ds(pl.multiple_of(block * rows, rows), rows)],
            cols.at[slot],
            load_sems.at[slot],
        )

    def store(block):
        slot = lax.rem(block, 2)
        return pltpu.make_async_copy(
            staged.at[slot, pl.ds(0, count)], result.at[:, block], store_sems.at[slot]
        )

    load(0).start()

    @pl.loop(0, 8)
    def _(block):
        slot = lax.rem(block, 2)
        load(block).wait()

        @pl.when(block < 7)
        def _():
            load(block + 1).start()

        @pl.when(block >= 2)
        def _():
            store(block - 2).wait()

        if hook:
            hook(block)
        product = contract(cols[slot].reshape(8 * rows, rows), right[...], 0, 0)
        for number in range(count):
            begins = pieces[number] if pieces else (number * rows,)
            size = rows // len(begins)
            for index, begin in enumerate(begins):
                staged[slot, number, :, index * size : (index + 1) * size] = product[
                    :, begin : begin + size
                ].astype(jnp.bfloat16)
        store(block).start()

    store(6).wait()
    store(7).wait()


GELU_SCALE = (2.0 / math.pi) ** 0.5


def gelu_and_slope(pre):
    squared = pre * pre
    bend = jnp.tanh(GELU_SCALE * (pre + 0.044715 * (squared * pre)))
    rise = 0.5 * (1.0 + bend)
    slope = rise + 0.5 * pre * (1.0 - bend * bend) * (GELU_SCALE * (1.0 + 3.0 * 0.044715 * squared))
    return pre * rise, slope


class Plane:
    def __init__(self):
        self.mine, self.place, self.at = plane_places()

    def to(self, flip):
        return (self.at(flip), self.place)

    def got(self, ref, sem):
        remote(ref, ref, sem, sem, (self.mine, self.place)).wait_recv()

    def gone(self, ref, sem):
        remote(ref, ref, sem, sem, (self.mine, self.place)).wait_send()


def scatter_flow(plane, own_of, fetch, peer, far, near, sems, finish):
    core_recv, far_send, far_recv, near_send, near_recv = sems
    rows = near.shape[1]
    half = rows // 2
    sent = []

    def add(slot, start, count, extra=None):
        own = own_of(slot)

        def step(band):
            at = pl.ds(pl.multiple_of(start + band.start, BAND), BAND)
            total = plain(own, at) + plain(peer.at[slot], at)
            if extra is not None:
                total = total + plain(extra, band)
            peer[slot, at, :] = total.astype(jnp.bfloat16)

        bands(count, step)

    def send(src, dst, flip, send_sem, recv_sem):
        copy = remote(src, dst, send_sem, recv_sem, plane.to(flip))
        copy.start()
        sent.append(copy)

    def send_near(slot, part):
        at = pl.ds(part * half, half)
        index = (slot - 1) * 2 + part
        send(
            peer.at[slot, at],
            near.at[slot - 1, at],
            2 * slot,
            near_send.at[index],
            near_recv.at[index],
        )

    fetch(3)
    plane.got(peer.at[3], core_recv.at[3])
    add(3, 0, rows)
    send(peer.at[3, pl.ds(0, half)], far.at[0], 2, far_send.at[0], far_recv.at[0])
    send(peer.at[3, pl.ds(half, half)], far.at[1], 4, far_send.at[1], far_recv.at[1])
    fetch(1)
    plane.got(peer.at[1], core_recv.at[1])
    add(1, 0, half)
    send_near(1, 0)
    fetch(2)
    plane.got(peer.at[2], core_recv.at[2])
    add(2, half, half)
    send_near(2, 1)
    yield
    plane.got(far.at[0], far_recv.at[0])
    add(2, 0, half, far.at[0])
    send_near(2, 0)
    plane.got(far.at[1], far_recv.at[1])
    add(1, half, half, far.at[1])
    send_near(1, 1)
    fetch(0)
    plane.got(peer.at[0], core_recv.at[0])
    yield
    for slot, part in ((1, 0), (2, 1), (2, 0), (1, 1)):
        at = pl.ds(part * half, half)
        plane.got(near.at[slot - 1, at], near_recv.at[(slot - 1) * 2 + part])
        if (slot, part) == (2, 1):
            yield
    own = own_of(0)

    def step(at):
        finish(
            at,
            plain(own, at)
            + plain(peer.at[0], at)
            + plain(near.at[0], at)
            + plain(near.at[1], at),
        )

    bands(rows, step)
    for copy in sent:
        copy.wait_send()


def back_kernel(
    down_low,
    up_weight,
    hidden_all,
    slope_all,
    grad_mlp_all,
    h_two_all,
    first_grads,
    h_all,
    qkv_all,
    attended_all,
    qkv_weight_in,
    out_weight_in,
    features_in,
    first_sum_in,
    attn_out_in,
    grad_out_in,
    mod,
    shares,
    token_out,
    token_grad,
    mod_out,
    more,
    partial_out,
    land_a,
    land_b,
    first_buf,
    second_buf,
    stage,
    own_pair,
    image_buf,
    grad_all,
    down_buf,
    grad_first,
    saved_grad,
    cols_buf,
    qkv_buf,
    attended_buf,
    staged_buf,
    out_sum,
    sum_buf,
    in_buf,
    half_buf,
    half_in,
    mod_sum,
    mod_land,
    qkv_weight,
    out_weight,
    features,
    first_sum,
    attn_out,
    grad_out,
    core_send,
    core_recv,
    far_send,
    far_recv,
    near_send,
    near_recv,
    stage_sems,
    gather_send,
    gather_recv,
    load_sems,
    weight_sems,
    z_sems,
    x_sems,
    zload_sems,
    token_sems,
    mod_sems,
    mod_gather_sems,
):
    plane = Plane()
    mine, place = plane.mine, plane.place
    rows, width = features.shape
    at = plane.at
    own_grad, image_out = own_pair.at[0], own_pair.at[1]
    is_mid = (place == 1) | (place == 2)
    my_half = pl.ds(pl.multiple_of(jnp.where(place == 2, HALF_ROWS, 0), HALF_ROWS), HALF_ROWS)
    other_half = pl.ds(pl.multiple_of(jnp.where(place == 2, 0, HALF_ROWS), HALF_ROWS), HALF_ROWS)
    partner = (mine, 3 - place)
    outer = (mine, jnp.where(place == 1, 0, 3))
    inner = (mine, jnp.where(place == 0, 1, 2))
    others = [lax.rem(place + step, 4) for step in (1, 2, 3)]
    greet([plane.to(flip) for flip in range(1, 8)] + [(mine, other) for other in others])

    def z_copy(kind, chunk, src, dst, target):
        return remote(src, dst, z_sems.at[0, kind, chunk], z_sems.at[1, kind, chunk], target)

    def own_chunk(chunk):
        return first_grads.at[chunk] if chunk < FIRST else more.at[chunk - FIRST]

    def start_outward(chunk):
        z_copy(0, chunk, own_chunk(chunk), land_a.at[chunk], inner).start()

    def stage_d(k):
        region = shares.at[k, :, other_half]
        plane.got(region, z_sems.at[1, 2, k])
        z_copy(4, k, region, region, outer).start()

    def stage_x(k):
        region = shares.at[k, :, my_half]
        plane.got(region, x_sems.at[1, k])
        z_copy(2, k, region, region, partner).start()
        z_copy(3, k, region, region, outer).start()

    def stage_f(k):
        slot = k % 2
        load = pltpu.make_async_copy(land_b.at[k], half_in, zload_sems.at[2])
        plane.got(land_b.at[k], z_sems.at[1, 1, k])
        load.start()
        if k >= 2:
            plane.gone(half_buf.at[slot, pl.ds(0, 7)], x_sems.at[0, k - 2])
        load.wait()

        @pl.loop(0, 8)
        def _(block):
            half_buf[slot, block] = sum_buf[slot, block, my_half, :] + half_in[block]

        if k == CHUNKS - 1:
            pltpu.make_async_copy(
                half_buf.at[slot], shares.at[k, :, my_half], x_sems.at[1, k]
            ).start()
            return
        pltpu.make_async_copy(
            half_buf.at[slot, mine], shares.at[k, mine, my_half], x_sems.at[1, k]
        ).start()
        for flip in (6, 7, 2, 4, 3, 5, 1):
            remote(
                half_buf.at[slot, at(flip)],
                shares.at[k, mine, my_half],
                x_sems.at[0, k],
                x_sems.at[1, k],
                plane.to(flip),
            ).start()

    def stage_s(k):
        slot = k % 2
        if k >= 2:
            plane.gone(sum_buf.at[slot, :, other_half], z_sems.at[0, 1, k - 2])
        own_load = pltpu.make_async_copy(own_chunk(k), sum_buf.at[slot], zload_sems.at[0])
        own_load.start()
        in_load = pltpu.make_async_copy(land_a.at[k], in_buf, zload_sems.at[1])
        plane.got(land_a.at[k], z_sems.at[1, 0, k])
        in_load.start()
        own_load.wait()
        in_load.wait()

        @pl.loop(0, 8)
        def _(block):
            sum_buf[slot, block] = sum_buf[slot, block] + in_buf[block]

        z_copy(1, k, sum_buf.at[slot, :, other_half], land_b.at[k], partner).start()

    def send_outward(first, last):
        @pl.when(jnp.logical_not(is_mid))
        def _():
            for chunk in range(first, last):
                start_outward(chunk)

    def tick(now):
        k, odd = now // 2, now % 2
        work = [(stage_f, k - 1), (stage_d, k - 3)] if odd else [(stage_s, k), (stage_x, k - 2)]
        work = {
            16: [(stage_s, EARLY)],
            17: [(stage_x, EARLY - 1)],
            18: [(stage_s, EARLY + 1)],
        }.get(now, work)

        @pl.when(is_mid)
        def _():
            for stage, chunk in work:
                if 0 <= chunk < CHUNKS:
                    stage(chunk)

    def ahead():
        @pl.when(is_mid)
        def _():
            stage_x(EARLY - 2)
            stage_f(EARLY - 1)
            stage_d(EARLY - 3)

    send_outward(0, FIRST)

    attended_load = pltpu.make_async_copy(attended_all, attended_buf, load_sems.at[0])
    attended_load.start()
    fetches = [
        pltpu.make_async_copy(source, result, load_sems.at[13 + number])
        for number, (source, result) in enumerate(
            (
                (first_sum_in, first_sum),
                (grad_out_in, grad_out),
                (attn_out_in, attn_out),
                (out_weight_in, out_weight),
                (qkv_weight_in, qkv_weight),
                (features_in, features),
            )
        )
    ]
    feed = up_weight.shape[-1]

    pltpu.make_async_copy(
        down_low.at[mine], down_buf.at[mine], weight_sems.at[0, 0]
    ).start()
    for flip in (6, 7, 2, 4, 3, 5, 1):
        remote(
            down_low.at[at(flip)],
            down_buf.at[mine],
            weight_sems.at[0, flip],
            weight_sems.at[1, flip],
            plane.to(flip),
        ).start()
    up_load = pltpu.make_async_copy(up_weight, grad_all.at[:, :, pl.ds(0, feed)], load_sems.at[5])
    up_load.start()
    for fetch in fetches:
        fetch.start()
    mod_sum[...] = jnp.zeros_like(mod_sum)
    row = {
        name: number
        for number, name in enumerate(
            ("shift_one", "scale_one", "gate_one", "shift_two", "scale_two", "gate_two", "live")
        )
    }

    def mod_row(name):
        return mod[pl.ds(row[name], 1), :]

    def accumulate(name, value):
        mod_sum[pl.ds(row[name], 1), :] += jnp.sum(value, axis=0, keepdims=True)

    def sems(number):
        return (
            core_recv.at[number],
            far_send.at[number],
            far_recv.at[number],
            near_send.at[number],
            near_recv.at[number],
        )

    def give(src, buf, number, slot):
        remote(
            src, buf.at[slot], core_send.at[number, slot], core_recv.at[number, slot], plane.to(1)
        ).start()

    def staged_flow(source, buf, number, finish):
        for slot in (3, 1, 2, 0):
            give(source.at[at((2 * slot) ^ 1)], buf, number, slot)
        order = {3: 0, 1: 1, 2: 0, 0: 1}

        def load(slot):
            return pltpu.make_async_copy(
                source.at[at(2 * slot)], stage.at[order[slot]], stage_sems.at[number, slot]
            )

        load(3).start()
        load(1).start()

        def fetch(slot):
            if slot == 2:
                load(2).start()
            if slot == 0:
                load(0).start()
            load(slot).wait()

        return scatter_flow(
            plane,
            lambda slot: stage.at[order[slot]],
            fetch,
            buf.at[pl.ds(0, 4)],
            Halves(buf.at[6], rows // 2),
            buf.at[pl.ds(4, 2)],
            sems(number),
            finish,
        )

    def run(flow, first_tick):
        for step, _ in enumerate(flow):
            tick(first_tick + step)

    def finish_out(where, value):
        base = first_sum[where, :]
        own_pair[1, where, :] = (
            mod_row("live") * (base + mod_row("gate_two") * value)
        ).astype(jnp.bfloat16)
        accumulate("gate_two", plain(grad_out, where) * value)

    token_copies = []

    def return_tokens(image, result, number):
        piece = rows // 4
        own = pltpu.make_async_copy(
            image.at[pl.ds(pl.multiple_of(place * piece, piece), piece)],
            result.at[place],
            token_sems.at[0, number, 0],
        )
        own.start()
        token_copies.append(own)
        for step, other in enumerate(others):
            copy = remote(
                image.at[pl.ds(pl.multiple_of(other * piece, piece), piece)],
                result.at[place],
                token_sems.at[0, number, step + 1],
                token_sems.at[1, number, step + 1],
                (mine, other),
            )
            copy.start()
            token_copies.append(copy)


    def back_norm(source, value, scale_name, shift_name):
        inverse = rms_scale(source)
        unit = source * inverse
        inner = value * (1.0 + mod_row(scale_name))
        accumulate(scale_name, value * unit)
        accumulate(shift_name, value)
        return (inner - unit * jnp.mean(inner * unit, axis=-1, keepdims=True)) * inverse

    def finish_feed(where, value):
        total = back_norm(first_sum[where, :], value, "scale_two", "shift_two") + plain(
            grad_out, where
        )
        grad_first[where, :] = total
        accumulate("gate_one", total * plain(attn_out, where))
        low_grad = (mod_row("gate_one") * total).astype(jnp.bfloat16)
        own_pair[0, where, :] = low_grad
        grad_all[mine, where, :] = low_grad

    up_load.wait()
    pltpu.make_async_copy(
        down_low.at[mine], down_buf.at[mine], weight_sems.at[0, 0]
    ).wait()
    for now in range(5):
        tick(now)
    for flip in range(1, 8):
        plane.got(down_buf.at[at(flip)], weight_sems.at[1, flip])
        plane.gone(down_low.at[0], weight_sems.at[0, flip])

    def image_loads(step):
        image, slot = flipped(mine, step), lax.rem(step, 2)
        return [
            pltpu.make_async_copy(
                slope_all.at[image], image_buf.at[slot, :, pl.ds(0, feed)], load_sems.at[6 + slot]
            ),
            pltpu.make_async_copy(grad_mlp_all.at[image], stage.at[slot], load_sems.at[8 + slot]),
        ]

    for load in image_loads(0):
        load.start()

    @pl.loop(0, 8)
    def _(step):
        @pl.when(step == 4)
        def _():
            tick(5)

        slot = lax.rem(step, 2)
        for load in image_loads(step):
            load.wait()

        @pl.when(step < 7)
        def _():
            for load in image_loads(step + 1):
                load.start()

        image_rows = pl.ds(pl.multiple_of(flipped(mine, step) * rows, rows), rows)
        grad_hidden = contract(stage[slot], down_buf[...].reshape(8 * rows, feed), 1, 0)
        saved_grad[image_rows, :] = (
            grad_hidden * image_buf[slot, :, 0:feed].astype(jnp.float32)
        ).astype(jnp.bfloat16)
        up = grad_all[:, :, 0:feed].reshape(8 * rows, feed)
        second_buf[step] = contract(saved_grad[image_rows, :], up, 1, 1).astype(jnp.bfloat16)
        for number in (1, 3, 5, 7):

            @pl.when(step == number)
            def _(number=number):
                give(second_buf.at[number], first_buf, 1, number // 2)


    def hidden_load(step):
        slot = lax.rem(step, 2)
        return pltpu.make_async_copy(
            hidden_all.at[step], image_buf.at[slot, :, pl.ds(0, feed)], load_sems.at[6 + slot]
        )

    def out_store(step):
        slot = lax.rem(step, 2)
        return pltpu.make_async_copy(own_pair.at[slot], partial_out.at[step], load_sems.at[8 + slot])

    def out_products():
        hidden_load(0).start()

        @pl.loop(0, 8)
        def _(step):
            slot = lax.rem(step, 2)
            hidden_load(step).wait()

            @pl.when(step < 7)
            def _():
                hidden_load(step + 1).start()

            @pl.when(step >= 2)
            def _():
                out_store(step - 2).wait()

            own_pair[slot] = contract(
                image_buf[slot, :, 0:feed], down_buf[...].reshape(8 * rows, feed), 1, 1
            ).astype(jnp.bfloat16)
            out_store(step).start()

        out_store(6).wait()
        out_store(7).wait()

    def up_hook(block):
        @pl.when(block == 6)
        def _():
            tick(7)

    def up_products():
        column_products(
            h_two_all,
            saved_grad,
            cols_buf,
            staged_buf,
            more.at[pl.ds(0, 4)],
            load_sems.at[pl.ds(3, 2)],
            load_sems.at[pl.ds(11, 2)],
            hook=up_hook,
        )

    def own_flow(number, finish):
        return scatter_flow(
            plane,
            lambda slot: second_buf.at[2 * slot],
            lambda slot: None,
            first_buf.at[pl.ds(0, 4)],
            Halves(first_buf.at[6], rows // 2),
            first_buf.at[pl.ds(4, 2)],
            sems(number),
            finish,
        )

    tick(6)
    up_products()
    send_outward(FIRST, EARLY)
    for fetch in fetches:
        fetch.wait()
    for step, _ in enumerate(own_flow(1, finish_feed)):
        tick((8, 10, 11)[step])
        if step == 0:
            tick(9)
    for slot in range(4):
        plane.gone(second_buf.at[slot], core_send.at[1, slot])

    gather = Gather(plane, own_grad, grad_all, gather_send, gather_recv)
    gather.start()

    def qkv_load(step):
        return pltpu.make_async_copy(
            qkv_all.at[flipped(mine, step)], qkv_buf.at[lax.rem(step, 2)], load_sems.at[1 + lax.rem(step, 2)]
        )

    qkv_load(0).start()
    attended_load.wait()
    out_sum[...] = jnp.zeros_like(out_sum)
    columns = qkv_buf.shape[-1]
    third = columns // 3
    scale = HD ** (-0.5)

    @pl.loop(0, 8)
    def _(step):
        for number in range(8):

            @pl.when(step == number)
            def _(number=number):
                if number in (1, 2, 4):
                    tick({1: 12, 2: 13, 4: 15}[number])
                if number == 2:
                    tick(14)
                gather.step(number)
                if number == 7:
                    gather.finish()

        image = flipped(mine, step)
        slot = lax.rem(step, 2)
        qkv_load(step).wait()

        @pl.when(step < 7)
        def _():
            qkv_load(step + 1).start()

        grad = grad_all[image]
        grad_attended = contract(grad, out_weight[...], 1, 1).astype(jnp.bfloat16)
        image_rows = pl.ds(pl.multiple_of(image * rows, rows), rows)
        for head in range(third // HD):
            begin, first = head * HD, 3 * head * HD
            queries = qkv_buf[slot, :, first : first + HD]
            key_rows = qkv_buf[slot, :, first + HD : first + 2 * HD]
            value_rows = qkv_buf[slot, :, first + 2 * HD : first + 3 * HD]
            grad_head = grad_attended[:, begin : begin + HD]
            attention = softmax_rows(queries, key_rows)
            grad_weights = contract(grad_head, value_rows, 1, 1)
            row_delta = jnp.sum(attention * grad_weights, axis=-1, keepdims=True)
            grad_scores = (attention * (grad_weights - row_delta)).astype(jnp.bfloat16)
            saved_grad[image_rows, first : first + HD] = (
                contract(grad_scores, key_rows, 1, 0) * scale
            ).astype(jnp.bfloat16)
            saved_grad[image_rows, first + HD : first + 2 * HD] = (
                contract(grad_scores, queries, 0, 0) * scale
            ).astype(jnp.bfloat16)
            saved_grad[image_rows, first + 2 * HD : first + 3 * HD] = contract(
                attention.astype(jnp.bfloat16), grad_head, 0, 0
            ).astype(jnp.bfloat16)
        out_sum[...] += contract(attended_buf[image], grad, 0, 0)
        second_buf[step] = contract(saved_grad[image_rows, 0:columns], qkv_weight[...], 1, 1).astype(
            jnp.bfloat16
        )
        for number in (1, 3, 5, 7):

            @pl.when(step == number)
            def _(number=number):
                give(second_buf.at[number], first_buf, 2, number // 2)

    ahead()

    for block in range(8):
        in_buf[block] = out_sum[:, block * rows : (block + 1) * rows].astype(jnp.bfloat16)
    out_copy = pltpu.make_async_copy(in_buf, more.at[7], load_sems.at[0])
    out_copy.start()
    column_products(
        h_all,
        saved_grad.at[:, pl.ds(0, columns)],
        cols_buf,
        staged_buf,
        more.at[pl.ds(4, 3)],
        load_sems.at[pl.ds(3, 2)],
        load_sems.at[pl.ds(11, 2)],
        [[(3 * head + number) * HD for head in range(third // HD)] for number in range(3)],
    )

    def finish_input(where, value):
        total = back_norm(plain(features, where), value, "scale_one", "shift_one")
        own_pair[0, where, :] = (total + grad_first[where, :]).astype(jnp.bfloat16)

    out_copy.wait()
    send_outward(EARLY, CHUNKS)
    tick(16)
    tick(17)
    for step, _ in enumerate(own_flow(2, finish_input)):
        for now in ((18, 19), (20,), (21,))[step]:
            tick(now)
        if step == 0:
            out_products()
    return_tokens(own_grad, token_grad, 1)
    for step, _ in enumerate(staged_flow(partial_out, grad_all, 0, finish_out)):
        for now in ((22, 23), (24,), (25,))[step]:
            tick(now)
    return_tokens(image_out, token_out, 0)

    mod_copies = []
    mod_sum[7:8, :] = mod[7:8, :]
    mod_rows = pl.ds(pl.multiple_of(place * 8, 8), 8)
    mod_land[mod_rows, :] = mod_sum[...]
    for step, other in enumerate(others):
        copy = remote(
            mod_sum, mod_land.at[mod_rows], mod_sems.at[0, step], mod_sems.at[1, step], (mine, other)
        )
        copy.start()
        mod_copies.append(copy)
    tick(26)
    for copy in mod_copies:
        copy.wait_recv()
    own = pltpu.make_async_copy(mod_land, mod_out.at[mine], mod_sems.at[0, 3])
    own.start()
    mod_gather = Gather(plane, mod_land, mod_out, mod_gather_sems.at[0], mod_gather_sems.at[1])
    mod_gather.start()
    tick(27)
    mod_gather.middle()
    mod_gather.far()
    for flip in (1, 3, 5, 7):
        mod_gather.crossed(flip)
    mod_gather.finish()
    for now in range(28, 2 * CHUNKS + 6):
        tick(now)
    own.wait()
    for copy in mod_copies:
        copy.wait_send()
    for copy in token_copies:
        copy.wait()
    for number in (0, 2):
        for slot in range(4):
            plane.gone(second_buf.at[slot], core_send.at[number, slot])

    @pl.when(is_mid)
    def _():
        for k in (CHUNKS - 2, CHUNKS - 1):
            plane.gone(sum_buf.at[k % 2, :, other_half], z_sems.at[0, 1, k])
        plane.gone(half_buf.at[0, pl.ds(0, 7)], x_sems.at[0, CHUNKS - 2])
        for k in range(CHUNKS):
            plane.gone(shares.at[k, :, my_half], z_sems.at[0, 2, k])
            plane.gone(shares.at[k, :, my_half], z_sems.at[0, 3, k])
            plane.gone(shares.at[k, :, other_half], z_sems.at[0, 4, k])

    @pl.when(jnp.logical_not(is_mid))
    def _():
        first = pl.ds(pl.multiple_of(jnp.where(place == 0, 0, HALF_ROWS), HALF_ROWS), HALF_ROWS)
        second = pl.ds(pl.multiple_of(jnp.where(place == 0, HALF_ROWS, 0), HALF_ROWS), HALF_ROWS)
        for k in range(CHUNKS):
            plane.gone(land_a.at[k], z_sems.at[0, 0, k])
            plane.got(shares.at[k, :, first], z_sems.at[1, 3, k])
            plane.got(shares.at[k, :, second], z_sems.at[1, 4, k])


def back_part(*operands):
    h_all, qkv_weight = operands[7], operands[10]
    _, rows, width = h_all.shape
    columns = qkv_weight.shape[1]
    feed = operands[1].shape[-1]
    low, full = jnp.bfloat16, jnp.float32
    dma = pltpu.SemaphoreType.DMA
    anywhere, inside = pl.BlockSpec(memory_space=pl.ANY), pl.BlockSpec(memory_space=pltpu.VMEM)
    return pl.pallas_call(
        back_kernel,
        out_shape=[
            jax.ShapeDtypeStruct((CHUNKS, 8, rows, rows), low),
            jax.ShapeDtypeStruct((4, rows // 4, width), low),
            jax.ShapeDtypeStruct((4, rows // 4, width), low),
            jax.ShapeDtypeStruct((8, 32, width), full),
            jax.ShapeDtypeStruct((CHUNKS - FIRST, 8, rows, rows), low),
            jax.ShapeDtypeStruct((8, rows, width), low),
            jax.ShapeDtypeStruct((CHUNKS, 8, rows, rows), low),
            jax.ShapeDtypeStruct((CHUNKS, 8, HALF_ROWS, rows), low),
        ],
        in_specs=[anywhere] * 16 + [inside],
        out_specs=[anywhere] * 8,
        scratch_shapes=[
            pltpu.VMEM((7, rows, width), low),
            pltpu.VMEM((8, rows, width), low),
            pltpu.VMEM((2, rows, width), low),
            pltpu.VMEM((2, rows, width), low),
            pltpu.VMEM((2, rows, feed), low),
            pltpu.VMEM((8, rows, width), low),
            pltpu.VMEM((8, rows, feed), low),
            pltpu.VMEM((rows, width), full),
            pltpu.VMEM((8 * rows, feed), low),
            pltpu.VMEM((2, 8, rows, rows), low),
            pltpu.VMEM((2, rows, columns), low),
            pltpu.VMEM((8, rows, columns // 3), low),
            pltpu.VMEM((2, 4, rows, rows), low),
            pltpu.VMEM((columns // 3, width), full),
            pltpu.VMEM((2, 8, rows, rows), low),
            pltpu.VMEM((8, rows, rows), low),
            pltpu.VMEM((2, 8, HALF_ROWS, rows), low),
            pltpu.VMEM((8, HALF_ROWS, rows), low),
            pltpu.VMEM((8, width), full),
            pltpu.VMEM((32, width), full),
            pltpu.VMEM((8 * rows, columns), low),
            pltpu.VMEM((rows, width), low),
            pltpu.VMEM((rows, width), low),
            pltpu.VMEM((rows, width), full),
            pltpu.VMEM((rows, width), low),
            pltpu.VMEM((rows, width), low),
            dma((3, 4)),
            dma((3, 4)),
            dma((3, 2)),
            dma((3, 2)),
            dma((3, 4)),
            dma((3, 4)),
            dma((2, 4)),
            dma((7 * PIECES,)),
            dma((7 * PIECES,)),
            dma((19,)),
            dma((2, 8)),
            dma((2, 5, CHUNKS)),
            dma((2, CHUNKS)),
            dma((3,)),
            dma((2, 2, 4)),
            dma((2, 4)),
            dma((2, 7 * PIECES)),
        ],
        compiler_params=pltpu.CompilerParams(
            collective_id=4, has_side_effects=True, vmem_limit_bytes=63 * 1024 * 1024
        ),
        name="back_part",
    )(*operands)


class Gather:
    def __init__(self, plane, own, result, send_sems, recv_sems):
        self.plane, self.own, self.result = plane, own, result
        self.send_sems, self.recv_sems = send_sems, recv_sems
        self.piece = own.shape[0] // PIECES

    def put(self, src, owner, part, flip, slot):
        remote(
            src,
            self.result.at[owner, pl.ds(part * self.piece, self.piece)],
            self.send_sems.at[slot],
            self.recv_sems.at[slot],
            self.plane.to(flip),
        ).start()

    def arrived(self, flip, part, slot):
        ref = self.result.at[self.plane.at(flip), pl.ds(part * self.piece, self.piece)]
        self.plane.got(ref, self.recv_sems.at[slot])
        return ref

    def start(self):
        mine = self.plane.mine
        for part in range(PIECES):
            src = self.own.at[pl.ds(part * self.piece, self.piece)]
            self.put(src, mine, part, 2, part)
            self.put(src, mine, part, 4, PIECES + part)
            self.put(src, mine, part, 1, 3 * PIECES + part)

    def middle(self):
        at = self.plane.at
        for part in range(PIECES):
            got = self.arrived(2, part, part)
            if part < PIECES // 2:
                self.put(got, at(2), part, 4, 2 * PIECES + part)
            self.put(got, at(2), part, 1, 4 * PIECES + part)
            got = self.arrived(4, part, PIECES + part)
            if part >= PIECES // 2:
                self.put(got, at(4), part, 2, 2 * PIECES + part)
            self.put(got, at(4), part, 1, 5 * PIECES + part)

    def far(self):
        for part in range(PIECES):
            got = self.arrived(6, part, 2 * PIECES + part)
            self.put(got, self.plane.at(6), part, 1, 6 * PIECES + part)

    def crossed(self, flip):
        for part in range(PIECES):
            self.arrived(flip, part, (3 + flip // 2) * PIECES + part)

    def step(self, number):
        if number == 2:
            self.middle()
        if number == 6:
            self.far()
        if number % 2:
            self.crossed(number)

    def finish(self):
        for slot in range(7 * PIECES):
            self.plane.gone(self.own.at[pl.ds(0, self.piece)], self.send_sems.at[slot])


class Halves:
    def __init__(self, ref, half):
        self.ref, self.half = ref, half

    @property
    def at(self):
        return self

    def __getitem__(self, number):
        return self.ref.at[pl.ds(number * self.half, self.half)]


def front_kernel(
    bin_ids,
    image_counts,
    noise,
    mod_bias,
    block_input,
    cotangent,
    attn_weight,
    mlp_weight,
    mod_weight,
    qkv_weight,
    out_weight_out,
    up_weight,
    down_low,
    h_one_all,
    h_two_all,
    grad_mlp_all,
    qkv_all,
    attended_all,
    hidden_all,
    slope_all,
    first_grads,
    features_out,
    first_sum_out,
    attn_out_out,
    grad_out_out,
    mod_out,
    load_buf,
    qkv_stage,
    up_stage,
    weight_buf,
    hidden_buf,
    cols_buf,
    staged_buf,
    h_all,
    qkv_buf,
    attended_buf,
    part_buf,
    scatter_buf,
    own_h,
    own_grad,
    own_next,
    bin_row,
    bin_land,
    mod_part,
    mod_land,
    out_weight,
    features,
    first_sum,
    attn_out,
    grad_out,
    mod,
    load_sems,
    token_sems,
    bin_sems,
    mod_sems,
    weight_sems,
    beside_sems,
    gather_sems,
    core_send,
    core_recv,
    far_send,
    far_recv,
    near_send,
    near_recv,
    copy_sems,
):
    plane = Plane()
    mine, place, at = plane.mine, plane.place, plane.at
    rows, width = own_h.shape
    feed = up_stage.shape[-1]
    columns = qkv_stage.shape[-1]
    third = columns // 3
    piece = rows // 4
    others = [lax.rem(place + step, 4) for step in (1, 2, 3)]
    flips = (6, 7, 2, 4, 3, 5, 1, 0)
    greet([plane.to(flip) for flip in range(1, 8)] + [(mine, other) for other in others])

    results = [
        pltpu.make_async_copy(source, result, copy_sems.at[14 + number])
        for number, (source, result) in enumerate(
            (
                (mod, mod_out),
                (features, features_out),
                (grad_out, grad_out_out),
                (out_weight, out_weight_out),
                (first_sum, first_sum_out),
                (attn_out, attn_out_out),
            )
        )
    ]

    token_copies = []
    my_rows = pl.ds(pl.multiple_of(place * piece, piece), piece)
    for number, (source, result) in enumerate(((block_input, features), (cotangent, grad_out))):
        copies = [
            pltpu.make_async_copy(
                source.at[place], result.at[my_rows], token_sems.at[0, number, 0]
            )
        ]
        for step, other in enumerate(others):
            copies.append(
                remote(
                    source.at[other],
                    result.at[my_rows],
                    token_sems.at[0, number, step + 1],
                    token_sems.at[1, number, step + 1],
                    (mine, other),
                )
            )
        for copy in copies:
            copy.start()
        token_copies.append(copies)

    lanes = lax.broadcasted_iota(jnp.int32, bin_row.shape, 1)
    bin_row[...] = jnp.where(lanes == bin_ids[place], 1.0, 0.0).astype(jnp.float32)
    bin_land[mine] = bin_row[...]
    bin_copies = [
        remote(
            bin_row, bin_land.at[mine], bin_sems.at[0, flip], bin_sems.at[1, flip], plane.to(flip)
        )
        for flip in range(1, 8)
    ]
    for copy in bin_copies:
        copy.start()

    parity = lax.rem(place, 2)
    beside = (mine, place + 1 - 2 * parity)

    def half_of(size):
        return pl.ds(pl.multiple_of(parity * size, size), size)

    def load_columns(source, slot, begins, size):
        return [
            pltpu.make_async_copy(
                source.at[:, pl.ds(pl.multiple_of(begin, HD), size)],
                load_buf.at[slot, :, pl.ds(number * size, size)],
                load_sems.at[slot, number],
            )
            for number, begin in enumerate(begins)
        ]

    def cast_and_send(source, begins_of, size, stage, result, kind):
        loads = [
            load_columns(source, step % 2, begins_of(at(flip)), size)
            for step, flip in enumerate(flips)
        ]
        total = size * len(loads[0])
        half = half_of(total)
        for load in loads[0]:
            load.start()
        for step, flip in enumerate(flips):
            if step + 1 < len(flips):
                for load in loads[step + 1]:
                    load.start()
            for load in loads[step]:
                load.wait()

            def cast(band, step=step):
                stage[step, band, 0:total] = load_buf[step % 2, band, 0:total].astype(jnp.bfloat16)

            bands(rows, cast)
            src = stage.at[step, :, pl.ds(0, total)]
            if flip:
                remote(
                    src,
                    result.at[mine, :, half],
                    weight_sems.at[0, kind, flip],
                    weight_sems.at[1, kind, flip],
                    plane.to(flip),
                ).start()
            else:
                pltpu.make_async_copy(
                    src, result.at[mine, :, half], weight_sems.at[0, kind, 0]
                ).start()

    def pass_on(stage, result, kind, total):
        half = half_of(total)
        pltpu.make_async_copy(
            stage.at[7, :, pl.ds(0, total)], result.at[mine, :, half], weight_sems.at[0, kind, 0]
        ).wait()
        for flip in (1, 2, 3, 4, 5, 6, 7, 0):
            piece = result.at[at(flip), :, half]
            if flip:
                plane.got(piece, weight_sems.at[1, kind, flip])
            remote(
                piece,
                piece,
                beside_sems.at[0, kind, flip],
                beside_sems.at[1, kind, flip],
                beside,
            ).start()

    def weights_ready(stage, result, kind, total):
        for flip in range(8):
            piece = result.at[at(flip), :, half_of(total)]
            plane.got(piece, beside_sems.at[1, kind, flip])
            plane.gone(piece, beside_sems.at[0, kind, flip])
            if flip:
                plane.gone(stage.at[0, :, pl.ds(0, total)], weight_sems.at[0, kind, flip])

    cast_and_send(
        attn_weight,
        lambda owner: [number * width + owner * third + parity * HD for number in range(3)],
        HD,
        qkv_stage,
        qkv_weight,
        0,
    )

    cast_and_send(
        mlp_weight,
        lambda owner: [owner * feed + parity * (feed // 2)],
        feed // 2,
        up_stage,
        up_weight,
        1,
    )

    for copy in bin_copies:
        copy.wait_recv()
    bins = noise.shape[0]
    activated = noise[...] / (1.0 + jnp.exp(-noise[...]))
    chosen = jnp.dot(
        bin_land[:, 0, :bins], activated, precision=PRECISE, preferred_element_type=jnp.float32
    )

    def load_mod(number):
        return pltpu.make_async_copy(
            mod_weight.at[:, pl.ds(number * width, width)],
            load_buf.at[number % 2],
            load_sems.at[number % 2, 0],
        )

    load_mod(0).start()
    mod_part[...] = jnp.zeros_like(mod_part)
    for number in range(6):
        if number < 5:
            load_mod(number + 1).start()
        load_mod(number).wait()
        mod_part[:, number, :] = jnp.dot(
            chosen, load_buf[number % 2], precision=PRECISE, preferred_element_type=jnp.float32
        )
    quarter = width // 4
    for number in range(3):
        index = 3 * mine + number
        where = pl.ds(pl.multiple_of(lax.rem(index, 4) * quarter, quarter), quarter)
        for image in range(8):
            mod_part[image, pl.ds(index // 4, 1), where] += mod_bias[
                :, number * quarter : (number + 1) * quarter
            ]
    mod_copies = [
        remote(
            mod_part.at[at(flip)],
            mod_land.at[mine],
            mod_sems.at[0, flip],
            mod_sems.at[1, flip],
            plane.to(flip),
        )
        for flip in range(1, 8)
    ]
    for copy in mod_copies:
        copy.start()
    pass_on(qkv_stage, qkv_weight, 0, 3 * HD)
    mod_land[mine] = mod_part[mine]
    for copy in mod_copies:
        copy.wait_recv()
    total = mod_land[0]
    for number in range(1, 8):
        total = total + mod_land[number]
    mod[...] = total
    live = jnp.where(place < image_counts[0], 1.0, 0.0).astype(jnp.float32)
    mod[6:7, :] = jnp.full((1, width), 1.0, jnp.float32) * live
    mod[7:8, :] = jnp.zeros((1, width), jnp.float32)
    mod[7:8, :128] = bin_row[0:1, :]
    results[0].start()

    def mod_row(number):
        return mod[number : number + 1, :]

    def tokens_arrived(number):
        for copy in token_copies[number]:
            if copy is token_copies[number][0]:
                copy.wait()
            else:
                copy.wait_recv()

    tokens_arrived(0)
    results[1].start()

    def first_norm(band):
        source = plain(features, band)
        normed = (source * rms_scale(source) * (1.0 + mod_row(1)) + mod_row(0)).astype(jnp.bfloat16)
        own_h[band, :] = normed
        h_all[mine, band, :] = normed

    bands(rows, first_norm)
    h_gather = Gather(plane, own_h, h_all, gather_sems.at[0, 0], gather_sems.at[0, 1])
    h_gather.start()

    tokens_arrived(1)

    def feed_grad(band):
        scaled = plain(grad_out, band) * mod_row(6)
        grad_out[band, :] = scaled.astype(jnp.bfloat16)
        own_grad[band, :] = (mod_row(5) * scaled).astype(jnp.bfloat16)

    bands(rows, feed_grad)
    results[2].start()
    grad_own = pltpu.make_async_copy(own_grad, grad_mlp_all.at[mine], copy_sems.at[0])
    grad_own.start()
    grad_gather = Gather(plane, own_grad, grad_mlp_all, gather_sems.at[1, 0], gather_sems.at[1, 1])
    grad_gather.start()
    def down_load(owner):
        return pltpu.make_async_copy(
            mlp_weight.at[:, pl.ds((8 + owner) * feed, feed)],
            load_buf.at[owner % 2, :, pl.ds(0, feed)],
            load_sems.at[owner % 2, 0],
        )

    def down_store(owner):
        return pltpu.make_async_copy(
            part_buf.at[owner, :, pl.ds(0, feed)], down_low.at[owner], copy_sems.at[6 + owner]
        )

    down_load(0).start()
    for owner in range(8):
        if owner < 7:
            down_load(owner + 1).start()
        down_load(owner).wait()

        def cast_down(band, owner=owner):
            part_buf[owner, band, 0:feed] = load_buf[owner % 2, band, 0:feed].astype(jnp.bfloat16)

        bands(rows, cast_down)
        down_store(owner).start()
    for owner in range(8):
        down_store(owner).wait()
    load = pltpu.make_async_copy(
        attn_weight.at[:, pl.ds(3 * width, width)], load_buf.at[0], load_sems.at[0, 0]
    )
    load.start()
    load.wait()

    def cast_out(band):
        out_weight[band, :] = load_buf[0, band, :].astype(jnp.bfloat16)

    bands(rows, cast_out)
    results[3].start()

    weights_ready(qkv_stage, qkv_weight, 0, 3 * HD)
    load = pltpu.make_async_copy(qkv_weight, weight_buf, copy_sems.at[1])
    load.start()
    load.wait()

    @pl.loop(0, 8)
    def _(step):
        for number in range(8):

            @pl.when(step == number)
            def _(number=number):
                h_gather.step(number)

        image = flipped(mine, step)
        pltpu.make_async_copy(h_all.at[image], h_one_all.at[image], copy_sems.at[2]).start()
        projected = contract(
            h_all[image], weight_buf[...].reshape(8 * rows, columns), 1, 0
        ).astype(jnp.bfloat16)
        qkv_buf[image] = projected
        for head in range(third // HD):
            begin, first = head * HD, 3 * head * HD
            queries = projected[:, first : first + HD]
            key_rows = projected[:, first + HD : first + 2 * HD]
            value_rows = projected[:, first + 2 * HD : first + 3 * HD]
            attention = softmax_rows(queries, key_rows).astype(jnp.bfloat16)
            attended_buf[image, :, begin : begin + HD] = contract(
                attention, value_rows, 1, 0
            ).astype(jnp.bfloat16)
        part_buf[step] = contract(attended_buf[image], out_weight[...], 1, 0).astype(jnp.bfloat16)
        pltpu.make_async_copy(h_all.at[image], h_one_all.at[image], copy_sems.at[2]).wait()

        @pl.when(step == 7)
        def _():
            h_gather.finish()

        for number in (1, 3, 5, 7):

            @pl.when(step == number)
            def _(number=number):
                slot = number // 2
                remote(
                    part_buf.at[number],
                    scatter_buf.at[slot],
                    core_send.at[slot],
                    core_recv.at[slot],
                    plane.to(1),
                ).start()

    pass_on(up_stage, up_weight, 1, feed // 2)
    keeps = [
        pltpu.make_async_copy(qkv_buf, qkv_all, copy_sems.at[3]),
        pltpu.make_async_copy(attended_buf, attended_all, copy_sems.at[4]),
    ]
    for copy in keeps:
        copy.start()

    def second_norm(band, value):
        attn_out[band, :] = value.astype(jnp.bfloat16)
        source = plain(features, band) + mod_row(2) * value
        first_sum[band, :] = source
        normed = (source * rms_scale(source) * (1.0 + mod_row(4)) + mod_row(3)).astype(jnp.bfloat16)
        own_next[band, :] = normed
        h_all[mine, band, :] = normed

    flow = scatter_flow(
        plane,
        lambda slot: part_buf.at[2 * slot],
        lambda slot: None,
        scatter_buf.at[pl.ds(0, 4)],
        Halves(scatter_buf.at[6], rows // 2),
        scatter_buf.at[pl.ds(4, 2)],
        (core_recv, far_send, far_recv, near_send, near_recv),
        second_norm,
    )
    for number, _ in enumerate(flow):
        if number == 1:
            grad_gather.middle()
    for slot in range(4):
        plane.gone(part_buf.at[slot], core_send.at[slot])
    next_gather = Gather(plane, own_next, h_all, gather_sems.at[2, 0], gather_sems.at[2, 1])
    next_gather.start()
    results[4].start()
    results[5].start()
    grad_gather.far()
    weights_ready(up_stage, up_weight, 1, feed // 2)
    load = pltpu.make_async_copy(up_weight, up_stage, copy_sems.at[1])
    load.start()
    load.wait()

    @pl.loop(0, 8)
    def _(step):
        for number in range(8):

            @pl.when(step == number)
            def _(number=number):
                next_gather.step(number)

        image = flipped(mine, step)
        pre = contract(h_all[image], up_stage[...].reshape(8 * rows, feed), 1, 0)
        hidden, slope = gelu_and_slope(pre)
        hidden_buf[pl.ds(pl.multiple_of(image * rows, rows), rows), :] = hidden.astype(jnp.bfloat16)
        part_buf[image, :, 0:feed] = slope.astype(jnp.bfloat16)

    keeps.append(pltpu.make_async_copy(h_all, h_two_all, copy_sems.at[2]))
    keeps.append(pltpu.make_async_copy(hidden_buf, hidden_all, copy_sems.at[5]))
    keeps.append(
        pltpu.make_async_copy(part_buf.at[:, :, pl.ds(0, feed)], slope_all, copy_sems.at[1])
    )
    for copy in keeps[-3:]:
        copy.start()
    for flip in (1, 3, 5, 7):
        grad_gather.crossed(flip)
    grad_own.wait()
    column_products(
        grad_mlp_all,
        hidden_buf,
        cols_buf,
        staged_buf,
        first_grads,
        copy_sems.at[pl.ds(6, 2)],
        copy_sems.at[pl.ds(8, 2)],
    )
    for gather in (grad_gather, next_gather):
        gather.finish()
    for copy in keeps + results:
        copy.wait()
    for copies in token_copies:
        for copy in copies[1:]:
            copy.wait_send()
    for copy in bin_copies + mod_copies:
        copy.wait_send()


def front_part(
    bin_ids,
    image_counts,
    noise,
    mod_bias,
    block_input,
    cotangent,
    attn_weight,
    mlp_weight,
    mod_weight,
):
    slots, local_tok, width = block_input.shape
    rows = slots * local_tok
    columns, feed = 3 * width // 8, mlp_weight.shape[1] // 16
    low, full = jnp.bfloat16, jnp.float32
    dma = pltpu.SemaphoreType.DMA
    anywhere, inside = pl.BlockSpec(memory_space=pl.ANY), pl.BlockSpec(memory_space=pltpu.VMEM)
    scalars = pl.BlockSpec(memory_space=pltpu.SMEM)
    return pl.pallas_call(
        front_kernel,
        out_shape=[
            jax.ShapeDtypeStruct((8, rows, columns), low),
            jax.ShapeDtypeStruct((rows, width), low),
            jax.ShapeDtypeStruct((8, rows, feed), low),
            jax.ShapeDtypeStruct((8, rows, feed), low),
            jax.ShapeDtypeStruct((8, rows, width), low),
            jax.ShapeDtypeStruct((8, rows, width), low),
            jax.ShapeDtypeStruct((8, rows, width), low),
            jax.ShapeDtypeStruct((8, rows, columns), low),
            jax.ShapeDtypeStruct((8, rows, columns // 3), low),
            jax.ShapeDtypeStruct((8 * rows, feed), low),
            jax.ShapeDtypeStruct((8, rows, feed), low),
            jax.ShapeDtypeStruct((FIRST, 8, rows, rows), low),
            jax.ShapeDtypeStruct((rows, width), low),
            jax.ShapeDtypeStruct((rows, width), full),
            jax.ShapeDtypeStruct((rows, width), low),
            jax.ShapeDtypeStruct((rows, width), low),
            jax.ShapeDtypeStruct((8, width), full),
        ],
        in_specs=[scalars] * 2 + [inside] * 2 + [anywhere] * 5,
        out_specs=[anywhere] * 17,
        scratch_shapes=[
            pltpu.VMEM((2, rows, width), full),
            pltpu.VMEM((8, rows, columns), low),
            pltpu.VMEM((8, rows, feed), low),
            pltpu.VMEM((8, rows, columns), low),
            pltpu.VMEM((8 * rows, feed), low),
            pltpu.VMEM((2, 8, rows, rows), low),
            pltpu.VMEM((2, 4, rows, rows), low),
            pltpu.VMEM((8, rows, width), low),
            pltpu.VMEM((8, rows, columns), low),
            pltpu.VMEM((8, rows, columns // 3), low),
            pltpu.VMEM((8, rows, width), low),
            pltpu.VMEM((7, rows, width), low),
            pltpu.VMEM((rows, width), low),
            pltpu.VMEM((rows, width), low),
            pltpu.VMEM((rows, width), low),
            pltpu.VMEM((8, 128), full),
            pltpu.VMEM((8, 8, 128), full),
            pltpu.VMEM((8, 8, width), full),
            pltpu.VMEM((8, 8, width), full),
            pltpu.VMEM((rows, width), low),
            pltpu.VMEM((rows, width), low),
            pltpu.VMEM((rows, width), full),
            pltpu.VMEM((rows, width), low),
            pltpu.VMEM((rows, width), low),
            pltpu.VMEM((8, width), full),
            dma((2, 3)),
            dma((2, 2, 4)),
            dma((2, 8)),
            dma((2, 8)),
            dma((2, 2, 8)),
            dma((2, 2, 8)),
            dma((3, 2, 7 * PIECES)),
            dma((4,)),
            dma((4,)),
            dma((2,)),
            dma((2,)),
            dma((4,)),
            dma((4,)),
            dma((20,)),
        ],
        compiler_params=pltpu.CompilerParams(
            collective_id=5, has_side_effects=True, vmem_limit_bytes=63 * 1024 * 1024
        ),
        name="front_part",
    )(
        bin_ids,
        image_counts,
        noise,
        mod_bias,
        block_input,
        cotangent,
        attn_weight,
        mlp_weight,
        mod_weight,
    )


def tail_kernel(
    mlp_ref,
    attn_ref,
    rows_ref,
    noise_ref,
    weight_ref,
    out_ref,
    grad_ref,
    mlp_grad_ref,
    attn_grad_ref,
    weight_grad_ref,
    noise_grad_ref,
    bias_ref,
    block_out_ref,
    input_grad_ref,
    chosen,
    total,
    flat_rows,
    onehot_rows,
):
    step = pl.program_id(0)
    size = mlp_ref.shape[-1]
    for number in range(4):
        mlp_grad_ref[:, number * size : (number + 1) * size] = mlp_ref[number, 0].astype(
            jnp.float32
        )
    for number in range(2):
        attn_grad_ref[:, number * size : (number + 1) * size] = attn_ref[0, number].astype(
            jnp.float32
        )
    block_out_ref[...] = out_ref[...]
    input_grad_ref[...] = grad_ref[...].astype(jnp.float32)
    noise = noise_ref[...]
    rise = 1.0 / (1.0 + jnp.exp(-noise))
    part = weight_ref.shape[1]

    @pl.when(step == 0)
    def _():
        width = rows_ref.shape[2]
        for row in range(6):
            flat_rows[:, row * width : (row + 1) * width] = rows_ref[:, row, :]
        onehot = rows_ref[:, 7, : noise.shape[0]]
        onehot_rows[...] = onehot
        chosen[...] = jnp.dot(
            onehot, noise * rise, precision=PRECISE, preferred_element_type=jnp.float32
        )
        total[...] = jnp.zeros_like(total)

    grads = flat_rows[:, pl.ds(pl.multiple_of(step * part, 128), part)]
    bias_ref[...] = jnp.broadcast_to(jnp.sum(grads, axis=0, keepdims=True), bias_ref.shape)
    low = grads.astype(jnp.bfloat16)
    weight_grad_ref[...] = contract(chosen[...].astype(jnp.bfloat16), low, 0, 0)
    total[...] += contract(weight_ref[...].astype(jnp.bfloat16), low, 1, 1)

    @pl.when(step == pl.num_programs(0) - 1)
    def _():
        table = lax.dot_general(
            onehot_rows[...],
            total[...],
            (((0,), (1,)), ((), ())),
            precision=PRECISE,
            preferred_element_type=jnp.float32,
        )
        noise_grad_ref[...] = table * (rise + noise * rise * (1.0 - rise))


def tail_part(shares, image_rows, noise, weight, token_out, token_grad):
    steps = 16
    rows = shares.shape[2]
    images = image_rows.shape[0]
    depth, columns = weight.shape
    part = columns // steps
    slots, local_tok, width = token_out.shape
    token_spec = pl.BlockSpec((1, local_tok, width // 4), lambda step: (step // 4, 0, step % 4))
    return pl.pallas_call(
        tail_kernel,
        grid=(steps,),
        out_shape=[
            jax.ShapeDtypeStruct((rows, 64 * rows), jnp.float32),
            jax.ShapeDtypeStruct((rows, 32 * rows), jnp.float32),
            jax.ShapeDtypeStruct(weight.shape, jnp.float32),
            jax.ShapeDtypeStruct(noise.shape, jnp.float32),
            jax.ShapeDtypeStruct((8, columns), jnp.float32),
            jax.ShapeDtypeStruct(token_out.shape, jnp.bfloat16),
            jax.ShapeDtypeStruct(token_grad.shape, jnp.float32),
        ],
        in_specs=[
            pl.BlockSpec((4, 1, rows, rows), lambda step: (1 - step // 8, step % 8, 0, 0)),
            pl.BlockSpec((1, 2, rows, rows), lambda step: (EARLY + step // 4, step % 4, 0, 0)),
            pl.BlockSpec(image_rows.shape, lambda step: (0, 0, 0)),
            pl.BlockSpec(noise.shape, lambda step: (0, 0)),
            pl.BlockSpec((depth, part), lambda step: (0, step)),
            token_spec,
            token_spec,
        ],
        out_specs=[
            pl.BlockSpec((rows, 4 * rows), lambda step: (0, step)),
            pl.BlockSpec((rows, 2 * rows), lambda step: (0, step)),
            pl.BlockSpec((depth, part), lambda step: (0, step)),
            pl.BlockSpec(noise.shape, lambda step: (0, 0)),
            pl.BlockSpec((8, part), lambda step: (0, step)),
            token_spec,
            token_spec,
        ],
        scratch_shapes=[
            pltpu.VMEM((images, depth), jnp.float32),
            pltpu.VMEM((depth, images), jnp.float32),
            pltpu.VMEM((images, columns), jnp.float32),
            pltpu.VMEM((images, noise.shape[0]), jnp.float32),
        ],
        compiler_params=pltpu.CompilerParams(vmem_limit_bytes=VMEM_BYTES),
        name="tail_part",
    )(shares, shares, image_rows, noise, weight, token_out, token_grad)


def plane_body(
    block_input,
    cotangent,
    bin_ids,
    image_counts,
    attn_weight,
    mlp_weight,
    noise_table,
    mod_weight,
    mod_bias,
):
    model_width = block_input.shape[2]
    rows = attn_weight.shape[0]
    bias_piece = mod_bias.shape[0]
    mine = lax.axis_index("fsdp")
    (
        qkv_weight,
        out_weight,
        up_weight,
        down_low,
        h_one_all,
        h_two_all,
        grad_mlp_all,
        qkv_all,
        attended_all,
        hidden_all,
        slope_all,
        first_grads,
        features,
        first_sum,
        attn_out,
        grad_out,
        mod_rows,
    ) = front_part(
        bin_ids,
        image_counts,
        noise_table,
        mod_bias.reshape(1, bias_piece),
        block_input,
        cotangent,
        attn_weight,
        mlp_weight,
        mod_weight,
    )

    def flat(array):
        return array.reshape(-1, array.shape[-1])

    shares, token_out, token_grad, mod_out, _, _, _, _ = back_part(
        down_low,
        up_weight,
        hidden_all.reshape(8, rows, -1),
        slope_all,
        grad_mlp_all,
        h_two_all,
        first_grads,
        h_one_all,
        qkv_all,
        attended_all,
        flat(qkv_weight),
        out_weight,
        features,
        first_sum,
        attn_out,
        grad_out,
        mod_rows,
    )
    (
        mlp_weight_grad,
        attn_weight_grad,
        mod_weight_grad,
        noise_grad,
        bias_sums,
        block_out,
        input_grad,
    ) = tail_part(
        shares,
        mod_out.reshape(-1, 8, model_width),
        noise_table,
        mod_weight,
        token_out,
        token_grad,
    )
    mod_bias_grad = lax.dynamic_slice_in_dim(bias_sums[0], mine * bias_piece, bias_piece)
    return (
        block_out,
        input_grad,
        attn_weight_grad,
        mlp_weight_grad,
        noise_grad,
        mod_weight_grad,
        mod_bias_grad,
    )


def solution(mesh):
    fits = mesh.shape["fsdp"] == 8 and mesh.shape["blk"] == 4
    return jax.shard_map(
        plane_body if fits else body,
        mesh=mesh,
        in_specs=(
            P("fsdp", "blk", None),
            P("fsdp", "blk", None),
            P("fsdp"),
            P("fsdp"),
            P("fsdp", None),
            P("fsdp", None),
            P(None, "fsdp"),
            P("fsdp", None),
            P("fsdp"),
        ),
        out_specs=(
            P("fsdp", "blk", None),
            P("fsdp", "blk", None),
            P("fsdp", None),
            P("fsdp", None),
            P(None, "fsdp"),
            P("fsdp", None),
            P("fsdp"),
        ),
        check_vma=False,
    )
```

```python
import functools
import math

import jax
import jax.numpy as jnp
from jax import lax
from jax.experimental import pallas as pl
from jax.experimental.pallas import tpu as pltpu
from jax.sharding import PartitionSpec as P

HD = 128


EPSILON = 1e-06
PRECISE = lax.Precision.HIGHEST


def norm_mod(features, scaling, shifting):
    normed = features * lax.rsqrt(jnp.mean(features * features, axis=-1, keepdims=True) + EPSILON)
    return normed * (1.0 + scaling) + shifting


def rows_product(left_rows, right_rows):
    return lax.dot_general(
        left_rows, right_rows, (((0,), (0,)), ((), ())), preferred_element_type=jnp.float32
    )


def body(
    block_input,
    cotangent,
    bin_ids,
    image_counts,
    attn_weight,
    mlp_weight,
    noise_table,
    mod_weight,
    mod_bias,
):
    slot_count, local_tok, model_width = block_input.shape
    row_count = slot_count * local_tok
    feed_width = mlp_weight.shape[1] // 2
    head_count = model_width // HD
    blk_size = lax.axis_size("blk")
    image_tok = local_tok * blk_size
    score_scale = HD ** (-0.5)
    bias_piece = mod_bias.shape[0]
    activated = jax.nn.silu(noise_table)
    partial_mod = jnp.dot(activated, mod_weight, precision=PRECISE)
    bias_full = lax.dynamic_update_slice_in_dim(
        jnp.zeros((6 * model_width,), jnp.float32), mod_bias, lax.axis_index("fsdp") * bias_piece, 0
    )
    mod_table = lax.psum(partial_mod + bias_full[None, :], "fsdp")
    onehot = (
        bin_ids[:, None] == jnp.arange(noise_table.shape[0], dtype=jnp.int32)[None, :]
    ).astype(jnp.float32)
    mod_image = jnp.dot(onehot, mod_table, precision=PRECISE)
    shift_one, scale_one, gate_one, shift_two, scale_two, gate_two = [
        member[:, None, :] for member in jnp.split(mod_image, 6, axis=-1)
    ]
    live_mask = (jnp.arange(slot_count) < image_counts[0]).astype(jnp.float32)[:, None, None]
    features = block_input.astype(jnp.float32)
    h_one = (
        norm_mod(features, scale_one, shift_one)
        .astype(jnp.bfloat16)
        .reshape(row_count, model_width)
    )
    attn_full = lax.all_gather(attn_weight.astype(jnp.bfloat16), "fsdp", axis=0, tiled=True)
    projected = jnp.dot(
        h_one, attn_full[:, : 3 * model_width], preferred_element_type=jnp.float32
    ).astype(jnp.bfloat16)
    queries = projected[:, :model_width].reshape(slot_count, local_tok, head_count, HD)
    key_rows = projected[:, model_width : 2 * model_width].reshape(
        slot_count, local_tok, model_width
    )
    value_rows = projected[:, 2 * model_width :].reshape(slot_count, local_tok, model_width)
    all_keys, all_values = (
        lax.all_gather(key_rows, "blk", axis=1, tiled=True),
        lax.all_gather(value_rows, "blk", axis=1, tiled=True),
    )
    all_keys = all_keys.reshape(slot_count, image_tok, head_count, HD)
    all_values = all_values.reshape(slot_count, image_tok, head_count, HD)

    def scores_of(query_rows):
        return (
            jnp.einsum("sqhd,skhd->shqk", query_rows, all_keys, preferred_element_type=jnp.float32)
            * score_scale
        )

    scores = scores_of(queries)
    maximum = jnp.max(scores, axis=-1, keepdims=True)
    exponent = jnp.exp(scores - maximum)
    denominator = jnp.sum(exponent, axis=-1, keepdims=True)
    attention = exponent / denominator
    log_total = maximum + jnp.log(denominator)
    attended = (
        jnp.einsum(
            "shqk,skhd->sqhd",
            attention.astype(jnp.bfloat16),
            all_values,
            preferred_element_type=jnp.float32,
        )
        .astype(jnp.bfloat16)
        .reshape(row_count, model_width)
    )
    attn_out = jnp.dot(
        attended, attn_full[:, 3 * model_width :], preferred_element_type=jnp.float32
    ).reshape(slot_count, local_tok, model_width)
    first_sum = features + gate_one * attn_out
    h_two = (
        norm_mod(first_sum, scale_two, shift_two)
        .astype(jnp.bfloat16)
        .reshape(row_count, model_width)
    )
    mlp_full = lax.all_gather(mlp_weight.astype(jnp.bfloat16), "fsdp", axis=0, tiled=True)
    pre_gelu = jnp.dot(h_two, mlp_full[:, :feed_width], preferred_element_type=jnp.float32)
    hidden = jax.nn.gelu(pre_gelu).astype(jnp.bfloat16)
    mlp_out = jnp.einsum(
        "rf,df->rd", hidden, mlp_full[:, feed_width:], preferred_element_type=jnp.float32
    ).reshape(slot_count, local_tok, model_width)
    second_sum = first_sum + gate_two * mlp_out
    block_out = (live_mask * second_sum).astype(jnp.bfloat16)
    grad_out = cotangent.astype(jnp.float32) * live_mask
    grad_mlp = (gate_two * grad_out).astype(jnp.bfloat16).reshape(row_count, model_width)
    grad_gate_two = jnp.sum(grad_out * mlp_out, axis=1)
    grad_hidden = jnp.dot(grad_mlp, mlp_full[:, feed_width:], preferred_element_type=jnp.float32)
    grad_pre = jax.vjp(jax.nn.gelu, pre_gelu)[1](grad_hidden)[0].astype(jnp.bfloat16)
    grad_h_two = jnp.einsum(
        "rf,df->rd", grad_pre, mlp_full[:, :feed_width], preferred_element_type=jnp.float32
    ).reshape(slot_count, local_tok, model_width)
    grad_first, grad_scale_two, grad_shift_two = jax.vjp(norm_mod, first_sum, scale_two, shift_two)[
        1
    ](grad_h_two)
    grad_first = grad_first + grad_out
    grad_attn_out = (gate_one * grad_first).astype(jnp.bfloat16).reshape(row_count, model_width)
    grad_gate_one = jnp.sum(grad_first * attn_out, axis=1)
    grad_attended = jnp.einsum(
        "rd,ed->re",
        grad_attn_out,
        attn_full[:, 3 * model_width :],
        preferred_element_type=jnp.float32,
    ).astype(jnp.bfloat16)
    grad_heads = grad_attended.reshape(slot_count, local_tok, head_count, HD)
    recomputed = jnp.exp(scores_of(queries) - log_total)
    grad_weights = jnp.einsum(
        "sqhd,skhd->shqk", grad_heads, all_values, preferred_element_type=jnp.float32
    )
    row_delta = jnp.sum(recomputed * grad_weights, axis=-1, keepdims=True)
    grad_scores = (recomputed * (grad_weights - row_delta)).astype(jnp.bfloat16)
    grad_queries = (
        jnp.einsum("shqk,skhd->sqhd", grad_scores, all_keys, preferred_element_type=jnp.float32)
        * score_scale
    )
    grad_keys_all = (
        jnp.einsum("shqk,sqhd->skhd", grad_scores, queries, preferred_element_type=jnp.float32)
        * score_scale
    )
    grad_values_all = jnp.einsum(
        "shqk,sqhd->skhd",
        recomputed.astype(jnp.bfloat16),
        grad_heads,
        preferred_element_type=jnp.float32,
    )
    grad_keys, grad_values = (
        lax.psum_scatter(
            grad_keys_all.reshape(slot_count, image_tok, model_width).astype(jnp.bfloat16),
            "blk",
            scatter_dimension=1,
            tiled=True,
        ).astype(jnp.float32),
        lax.psum_scatter(
            grad_values_all.reshape(slot_count, image_tok, model_width).astype(jnp.bfloat16),
            "blk",
            scatter_dimension=1,
            tiled=True,
        ).astype(jnp.float32),
    )
    grad_qkv = jnp.concatenate(
        [
            grad_queries.reshape(row_count, model_width).astype(jnp.bfloat16),
            grad_keys.reshape(row_count, model_width).astype(jnp.bfloat16),
            grad_values.reshape(row_count, model_width).astype(jnp.bfloat16),
        ],
        axis=1,
    )
    grad_h_one = jnp.einsum(
        "rc,dc->rd", grad_qkv, attn_full[:, : 3 * model_width], preferred_element_type=jnp.float32
    ).reshape(slot_count, local_tok, model_width)
    grad_input, grad_scale_one, grad_shift_one = jax.vjp(norm_mod, features, scale_one, shift_one)[
        1
    ](grad_h_one)
    input_grad = grad_input + grad_first
    grad_mod = jnp.concatenate(
        [
            grad_shift_one[:, 0, :],
            grad_scale_one[:, 0, :],
            grad_gate_one,
            grad_shift_two[:, 0, :],
            grad_scale_two[:, 0, :],
            grad_gate_two,
        ],
        axis=-1,
    )
    bin_terms = lax.dot_general(onehot, grad_mod, (((0,), (0,)), ((), ())), precision=PRECISE)
    grad_bins = lax.psum(bin_terms, ("fsdp", "blk"))
    table_term = jnp.einsum("be,de->bd", grad_bins, mod_weight, precision=PRECISE)
    noise_grad = jax.vjp(jax.nn.silu, noise_table)[1](table_term)[0]
    mod_weight_grad = lax.dot_general(
        activated, grad_bins, (((0,), (0,)), ((), ())), precision=PRECISE
    )
    mod_bias_grad = lax.dynamic_slice_in_dim(
        jnp.sum(grad_bins, axis=0), lax.axis_index("fsdp") * bias_piece, bias_piece
    )
    h_part = h_one
    attn_part = lax.psum_scatter(
        jnp.concatenate(
            [rows_product(h_part, grad_qkv), rows_product(attended, grad_attn_out)], axis=1
        ).astype(jnp.bfloat16),
        "fsdp",
        scatter_dimension=0,
        tiled=True,
    )
    h_part = h_two
    mlp_part = lax.psum_scatter(
        jnp.concatenate(
            [rows_product(h_part, grad_pre), rows_product(grad_mlp, hidden)], axis=1
        ).astype(jnp.bfloat16),
        "fsdp",
        scatter_dimension=0,
        tiled=True,
    )
    attn_weight_grad, mlp_weight_grad = (
        lax.psum(attn_part, "blk").astype(jnp.float32),
        lax.psum(mlp_part, "blk").astype(jnp.float32),
    )
    return (
        block_out,
        input_grad,
        attn_weight_grad,
        mlp_weight_grad,
        noise_grad,
        mod_weight_grad,
        mod_bias_grad,
    )


MESH_ID = pl.DeviceIdType.MESH
VMEM_BYTES = 56 * 1024 * 1024


def contract(left, right, left_dim, right_dim):
    return lax.dot_general(
        left, right, (((left_dim,), (right_dim,)), ((), ())), preferred_element_type=jnp.float32
    )


def plane_places():
    mine = lax.axis_index("fsdp")
    plane = lax.axis_index("blk")
    core = lax.rem(mine, 2)
    col = lax.rem(mine // 2, 2)
    row = mine // 4

    def at(flip):
        flip_row, flip_col, flip_core = flip // 4, (flip // 2) % 2, flip % 2
        new_row = 1 - row if flip_row else row
        new_col = 1 - col if flip_col else col
        new_core = 1 - core if flip_core else core
        return new_row * 4 + new_col * 2 + new_core

    return mine, plane, at


def greet(places):
    barrier = pltpu.get_barrier_semaphore()
    for place in places:
        pl.semaphore_signal(barrier, inc=1, device_id=place, device_id_type=MESH_ID)
    pl.semaphore_wait(barrier, len(places))


def remote(src, dst, send_sem, recv_sem, place):
    return pltpu.make_async_remote_copy(
        src_ref=src,
        dst_ref=dst,
        send_sem=send_sem,
        recv_sem=recv_sem,
        device_id=place,
        device_id_type=MESH_ID,
    )


PIECES = 4


def softmax_rows(queries, key_rows):
    scores = contract(queries, key_rows, 1, 1) * HD ** (-0.5)
    exponent = jnp.exp(scores - jnp.max(scores, axis=-1, keepdims=True))
    return exponent / jnp.sum(exponent, axis=-1, keepdims=True)


def rms_scale(features):
    return lax.rsqrt(jnp.mean(features * features, axis=-1, keepdims=True) + EPSILON)


CHUNKS = 12
FIRST = 4
EARLY = 8
HALF_ROWS = 128
BAND = 32


def flipped(mine, flip):
    total = 0
    for bit in (1, 2, 4):
        total = total + lax.rem(mine // bit + flip // bit, 2) * bit
    return total


def bands(count, step):
    @pl.loop(0, count // BAND)
    def _(index):
        step(pl.ds(pl.multiple_of(index * BAND, BAND), BAND))


def plain(ref, rows):
    return ref[rows, :].astype(jnp.float32)


def column_products(source, right, cols, staged, result, load_sems, store_sems, pieces=None, hook=None):
    rows = cols.shape[-1]
    count = result.shape[0]

    def load(block):
        slot = lax.rem(block, 2)
        return pltpu.make_async_copy(
            source.at[:, :, pl.ds(pl.multiple_of(block * rows, rows), rows)],
            cols.at[slot],
            load_sems.at[slot],
        )

    def store(block):
        slot = lax.rem(block, 2)
        return pltpu.make_async_copy(
            staged.at[slot, pl.ds(0, count)], result.at[:, block], store_sems.at[slot]
        )

    load(0).start()

    @pl.loop(0, 8)
    def _(block):
        slot = lax.rem(block, 2)
        load(block).wait()

        @pl.when(block < 7)
        def _():
            load(block + 1).start()

        @pl.when(block >= 2)
        def _():
            store(block - 2).wait()

        if hook:
            hook(block)
        product = contract(cols[slot].reshape(8 * rows, rows), right[...], 0, 0)
        for number in range(count):
            begins = pieces[number] if pieces else (number * rows,)
            size = rows // len(begins)
            for index, begin in enumerate(begins):
                staged[slot, number, :, index * size : (index + 1) * size] = product[
                    :, begin : begin + size
                ].astype(jnp.bfloat16)
        store(block).start()

    store(6).wait()
    store(7).wait()


GELU_SCALE = (2.0 / math.pi) ** 0.5


def gelu_and_slope(pre):
    squared = pre * pre
    bend = jnp.tanh(GELU_SCALE * (pre + 0.044715 * (squared * pre)))
    rise = 0.5 * (1.0 + bend)
    slope = rise + 0.5 * pre * (1.0 - bend * bend) * (GELU_SCALE * (1.0 + 3.0 * 0.044715 * squared))
    return pre * rise, slope


class Plane:
    def __init__(self):
        self.mine, self.place, self.at = plane_places()

    def to(self, flip):
        return (self.at(flip), self.place)

    def got(self, ref, sem):
        remote(ref, ref, sem, sem, (self.mine, self.place)).wait_recv()

    def gone(self, ref, sem):
        remote(ref, ref, sem, sem, (self.mine, self.place)).wait_send()


def scatter_flow(plane, own_of, fetch, peer, far, near, sems, finish):
    core_recv, far_send, far_recv, near_send, near_recv = sems
    rows = near.shape[1]
    half = rows // 2
    sent = []

    def add(slot, start, count, extra=None):
        own = own_of(slot)

        def step(band):
            at = pl.ds(pl.multiple_of(start + band.start, BAND), BAND)
            total = plain(own, at) + plain(peer.at[slot], at)
            if extra is not None:
                total = total + plain(extra, band)
            peer[slot, at, :] = total.astype(jnp.bfloat16)

        bands(count, step)

    def send(src, dst, flip, send_sem, recv_sem):
        copy = remote(src, dst, send_sem, recv_sem, plane.to(flip))
        copy.start()
        sent.append(copy)

    def send_near(slot, part):
        at = pl.ds(part * half, half)
        index = (slot - 1) * 2 + part
        send(
            peer.at[slot, at],
            near.at[slot - 1, at],
            2 * slot,
            near_send.at[index],
            near_recv.at[index],
        )

    fetch(3)
    plane.got(peer.at[3], core_recv.at[3])
    add(3, 0, rows)
    send(peer.at[3, pl.ds(0, half)], far.at[0], 2, far_send.at[0], far_recv.at[0])
    send(peer.at[3, pl.ds(half, half)], far.at[1], 4, far_send.at[1], far_recv.at[1])
    fetch(1)
    plane.got(peer.at[1], core_recv.at[1])
    add(1, 0, half)
    send_near(1, 0)
    fetch(2)
    plane.got(peer.at[2], core_recv.at[2])
    add(2, half, half)
    send_near(2, 1)
    yield
    plane.got(far.at[0], far_recv.at[0])
    add(2, 0, half, far.at[0])
    send_near(2, 0)
    plane.got(far.at[1], far_recv.at[1])
    add(1, half, half, far.at[1])
    send_near(1, 1)
    fetch(0)
    plane.got(peer.at[0], core_recv.at[0])
    yield
    for slot, part in ((1, 0), (2, 1), (2, 0), (1, 1)):
        at = pl.ds(part * half, half)
        plane.got(near.at[slot - 1, at], near_recv.at[(slot - 1) * 2 + part])
        if (slot, part) == (2, 1):
            yield
    own = own_of(0)

    def step(at):
        finish(
            at,
            plain(own, at)
            + plain(peer.at[0], at)
            + plain(near.at[0], at)
            + plain(near.at[1], at),
        )

    bands(rows, step)
    for copy in sent:
        copy.wait_send()


def back_kernel(
    down_low,
    up_weight,
    hidden_all,
    slope_all,
    grad_mlp_all,
    h_two_all,
    first_grads,
    h_all,
    qkv_all,
    attended_all,
    qkv_weight_in,
    out_weight_in,
    features_in,
    first_sum_in,
    attn_out_in,
    grad_out_in,
    mod,
    shares,
    token_out,
    token_grad,
    mod_out,
    more,
    partial_out,
    land_a,
    land_b,
    first_buf,
    second_buf,
    stage,
    own_pair,
    image_buf,
    grad_all,
    down_buf,
    grad_first,
    saved_grad,
    cols_buf,
    qkv_buf,
    attended_buf,
    staged_buf,
    out_sum,
    sum_buf,
    in_buf,
    half_buf,
    half_in,
    mod_sum,
    mod_land,
    qkv_weight,
    out_weight,
    features,
    first_sum,
    attn_out,
    grad_out,
    core_send,
    core_recv,
    far_send,
    far_recv,
    near_send,
    near_recv,
    stage_sems,
    gather_send,
    gather_recv,
    load_sems,
    weight_sems,
    z_sems,
    x_sems,
    zload_sems,
    token_sems,
    mod_sems,
    mod_gather_sems,
):
    plane = Plane()
    mine, place = plane.mine, plane.place
    rows, width = features.shape
    at = plane.at
    own_grad, image_out = own_pair.at[0], own_pair.at[1]
    is_mid = (place == 1) | (place == 2)
    my_half = pl.ds(pl.multiple_of(jnp.where(place == 2, HALF_ROWS, 0), HALF_ROWS), HALF_ROWS)
    other_half = pl.ds(pl.multiple_of(jnp.where(place == 2, 0, HALF_ROWS), HALF_ROWS), HALF_ROWS)
    partner = (mine, 3 - place)
    outer = (mine, jnp.where(place == 1, 0, 3))
    inner = (mine, jnp.where(place == 0, 1, 2))
    others = [lax.rem(place + step, 4) for step in (1, 2, 3)]
    greet([plane.to(flip) for flip in range(1, 8)] + [(mine, other) for other in others])

    def z_copy(kind, chunk, src, dst, target):
        return remote(src, dst, z_sems.at[0, kind, chunk], z_sems.at[1, kind, chunk], target)

    def own_chunk(chunk):
        return first_grads.at[chunk] if chunk < FIRST else more.at[chunk - FIRST]

    def start_outward(chunk):
        z_copy(0, chunk, own_chunk(chunk), land_a.at[chunk], inner).start()

    def stage_d(k):
        region = shares.at[k, :, other_half]
        plane.got(region, z_sems.at[1, 2, k])
        z_copy(4, k, region, region, outer).start()

    def stage_x(k):
        region = shares.at[k, :, my_half]
        plane.got(region, x_sems.at[1, k])
        z_copy(2, k, region, region, partner).start()
        z_copy(3, k, region, region, outer).start()

    def stage_f(k):
        slot = k % 2
        load = pltpu.make_async_copy(land_b.at[k], half_in, zload_sems.at[2])
        plane.got(land_b.at[k], z_sems.at[1, 1, k])
        load.start()
        if k >= 2 and k - 2 != EARLY:
            plane.gone(half_buf.at[slot, pl.ds(0, 7)], x_sems.at[0, k - 2])
        load.wait()

        @pl.loop(0, 8)
        def _(block):
            half_buf[slot, block] = sum_buf[slot, block, my_half, :] + half_in[block]

        if k == EARLY:
            pltpu.make_async_copy(
                half_buf.at[slot], shares.at[k, :, my_half], x_sems.at[1, k]
            ).start()
            return
        pltpu.make_async_copy(
            half_buf.at[slot, mine], shares.at[k, mine, my_half], x_sems.at[1, k]
        ).start()
        for flip in (6, 7, 2, 4, 3, 5, 1):
            remote(
                half_buf.at[slot, at(flip)],
                shares.at[k, mine, my_half],
                x_sems.at[0, k],
                x_sems.at[1, k],
                plane.to(flip),
            ).start()

    def stage_s(k):
        slot = k % 2
        if k >= 2:
            plane.gone(sum_buf.at[slot, :, other_half], z_sems.at[0, 1, k - 2])
        own_load = pltpu.make_async_copy(own_chunk(k), sum_buf.at[slot], zload_sems.at[0])
        own_load.start()
        in_load = pltpu.make_async_copy(land_a.at[k], in_buf, zload_sems.at[1])
        plane.got(land_a.at[k], z_sems.at[1, 0, k])
        in_load.start()
        own_load.wait()
        in_load.wait()

        @pl.loop(0, 8)
        def _(block):
            sum_buf[slot, block] = sum_buf[slot, block] + in_buf[block]

        z_copy(1, k, sum_buf.at[slot, :, other_half], land_b.at[k], partner).start()

    def send_outward(first, last):
        @pl.when(jnp.logical_not(is_mid))
        def _():
            for chunk in range(first, last):
                start_outward(chunk)

    def tick(now):
        k, odd = now // 2, now % 2
        work = [(stage_f, k - 1), (stage_d, k - 3)] if odd else [(stage_s, k), (stage_x, k - 2)]
        work = {
            16: [(stage_s, EARLY)],
            17: [(stage_x, EARLY - 1)],
            18: [(stage_s, EARLY + 1)],
        }.get(now, work)

        @pl.when(is_mid)
        def _():
            for stage, chunk in work:
                if 0 <= chunk < CHUNKS:
                    stage(chunk)

    def ahead():
        @pl.when(is_mid)
        def _():
            stage_x(EARLY - 2)
            stage_f(EARLY - 1)
            stage_d(EARLY - 3)

    send_outward(0, FIRST)

    attended_load = pltpu.make_async_copy(attended_all, attended_buf, load_sems.at[0])
    attended_load.start()
    fetches = [
        pltpu.make_async_copy(source, result, load_sems.at[13 + number])
        for number, (source, result) in enumerate(
            (
                (first_sum_in, first_sum),
                (grad_out_in, grad_out),
                (attn_out_in, attn_out),
                (out_weight_in, out_weight),
                (qkv_weight_in, qkv_weight),
                (features_in, features),
            )
        )
    ]
    feed = up_weight.shape[-1]

    pltpu.make_async_copy(
        down_low.at[mine], down_buf.at[mine], weight_sems.at[0, 0]
    ).start()
    for flip in (6, 7, 2, 4, 3, 5, 1):
        remote(
            down_low.at[at(flip)],
            down_buf.at[mine],
            weight_sems.at[0, flip],
            weight_sems.at[1, flip],
            plane.to(flip),
        ).start()
    up_load = pltpu.make_async_copy(up_weight, grad_all.at[:, :, pl.ds(0, feed)], load_sems.at[5])
    up_load.start()
    for fetch in fetches:
        fetch.start()
    mod_sum[...] = jnp.zeros_like(mod_sum)
    row = {
        name: number
        for number, name in enumerate(
            ("shift_one", "scale_one", "gate_one", "shift_two", "scale_two", "gate_two", "live")
        )
    }

    def mod_row(name):
        return mod[pl.ds(row[name], 1), :]

    def accumulate(name, value):
        mod_sum[pl.ds(row[name], 1), :] += jnp.sum(value, axis=0, keepdims=True)

    def sems(number):
        return (
            core_recv.at[number],
            far_send.at[number],
            far_recv.at[number],
            near_send.at[number],
            near_recv.at[number],
        )

    def give(src, buf, number, slot):
        remote(
            src, buf.at[slot], core_send.at[number, slot], core_recv.at[number, slot], plane.to(1)
        ).start()

    def staged_flow(source, buf, number, finish):
        for slot in (3, 1, 2, 0):
            give(source.at[at((2 * slot) ^ 1)], buf, number, slot)
        order = {3: 0, 1: 1, 2: 0, 0: 1}

        def load(slot):
            return pltpu.make_async_copy(
                source.at[at(2 * slot)], stage.at[order[slot]], stage_sems.at[number, slot]
            )

        load(3).start()
        load(1).start()

        def fetch(slot):
            if slot == 2:
                load(2).start()
            if slot == 0:
                load(0).start()
            load(slot).wait()

        return scatter_flow(
            plane,
            lambda slot: stage.at[order[slot]],
            fetch,
            buf.at[pl.ds(0, 4)],
            Halves(buf.at[6], rows // 2),
            buf.at[pl.ds(4, 2)],
            sems(number),
            finish,
        )

    def run(flow, first_tick):
        for step, _ in enumerate(flow):
            tick(first_tick + step)

    def finish_out(where, value):
        base = first_sum[where, :]
        own_pair[1, where, :] = (
            mod_row("live") * (base + mod_row("gate_two") * value)
        ).astype(jnp.bfloat16)
        accumulate("gate_two", plain(grad_out, where) * value)

    token_copies = []

    def return_tokens(image, result, number):
        piece = rows // 4
        own = pltpu.make_async_copy(
            image.at[pl.ds(pl.multiple_of(place * piece, piece), piece)],
            result.at[place],
            token_sems.at[0, number, 0],
        )
        own.start()
        token_copies.append(own)
        for step, other in enumerate(others):
            copy = remote(
                image.at[pl.ds(pl.multiple_of(other * piece, piece), piece)],
                result.at[place],
                token_sems.at[0, number, step + 1],
                token_sems.at[1, number, step + 1],
                (mine, other),
            )
            copy.start()
            token_copies.append(copy)


    def back_norm(source, value, scale_name, shift_name):
        inverse = rms_scale(source)
        unit = source * inverse
        inner = value * (1.0 + mod_row(scale_name))
        accumulate(scale_name, value * unit)
        accumulate(shift_name, value)
        return (inner - unit * jnp.mean(inner * unit, axis=-1, keepdims=True)) * inverse

    def finish_feed(where, value):
        total = back_norm(first_sum[where, :], value, "scale_two", "shift_two") + plain(
            grad_out, where
        )
        grad_first[where, :] = total
        accumulate("gate_one", total * plain(attn_out, where))
        low_grad = (mod_row("gate_one") * total).astype(jnp.bfloat16)
        own_pair[0, where, :] = low_grad
        grad_all[mine, where, :] = low_grad

    up_load.wait()
    pltpu.make_async_copy(
        down_low.at[mine], down_buf.at[mine], weight_sems.at[0, 0]
    ).wait()
    for now in range(5):
        tick(now)
    for flip in range(1, 8):
        plane.got(down_buf.at[at(flip)], weight_sems.at[1, flip])
        plane.gone(down_low.at[0], weight_sems.at[0, flip])

    def image_loads(step):
        image, slot = flipped(mine, step), lax.rem(step, 2)
        return [
            pltpu.make_async_copy(
                slope_all.at[image], image_buf.at[slot, :, pl.ds(0, feed)], load_sems.at[6 + slot]
            ),
            pltpu.make_async_copy(grad_mlp_all.at[image], stage.at[slot], load_sems.at[8 + slot]),
        ]

    for load in image_loads(0):
        load.start()

    @pl.loop(0, 8)
    def _(step):
        @pl.when(step == 4)
        def _():
            tick(5)

        slot = lax.rem(step, 2)
        for load in image_loads(step):
            load.wait()

        @pl.when(step < 7)
        def _():
            for load in image_loads(step + 1):
                load.start()

        image_rows = pl.ds(pl.multiple_of(flipped(mine, step) * rows, rows), rows)
        grad_hidden = contract(stage[slot], down_buf[...].reshape(8 * rows, feed), 1, 0)
        saved_grad[image_rows, :] = (
            grad_hidden * image_buf[slot, :, 0:feed].astype(jnp.float32)
        ).astype(jnp.bfloat16)
        up = grad_all[:, :, 0:feed].reshape(8 * rows, feed)
        second_buf[step] = contract(saved_grad[image_rows, :], up, 1, 1).astype(jnp.bfloat16)
        for number in (1, 3, 5, 7):

            @pl.when(step == number)
            def _(number=number):
                give(second_buf.at[number], first_buf, 1, number // 2)


    def hidden_load(step):
        slot = lax.rem(step, 2)
        return pltpu.make_async_copy(
            hidden_all.at[step], image_buf.at[slot, :, pl.ds(0, feed)], load_sems.at[6 + slot]
        )

    def out_store(step):
        slot = lax.rem(step, 2)
        return pltpu.make_async_copy(own_pair.at[slot], partial_out.at[step], load_sems.at[8 + slot])

    def out_products():
        hidden_load(0).start()

        @pl.loop(0, 8)
        def _(step):
            slot = lax.rem(step, 2)
            hidden_load(step).wait()

            @pl.when(step < 7)
            def _():
                hidden_load(step + 1).start()

            @pl.when(step >= 2)
            def _():
                out_store(step - 2).wait()

            own_pair[slot] = contract(
                image_buf[slot, :, 0:feed], down_buf[...].reshape(8 * rows, feed), 1, 1
            ).astype(jnp.bfloat16)
            out_store(step).start()

        out_store(6).wait()
        out_store(7).wait()

    def up_hook(block):
        @pl.when(block == 6)
        def _():
            tick(7)

    def up_products():
        column_products(
            h_two_all,
            saved_grad,
            cols_buf,
            staged_buf,
            more.at[pl.ds(0, 4)],
            load_sems.at[pl.ds(3, 2)],
            load_sems.at[pl.ds(11, 2)],
            hook=up_hook,
        )

    def own_flow(number, finish):
        return scatter_flow(
            plane,
            lambda slot: second_buf.at[2 * slot],
            lambda slot: None,
            first_buf.at[pl.ds(0, 4)],
            Halves(first_buf.at[6], rows // 2),
            first_buf.at[pl.ds(4, 2)],
            sems(number),
            finish,
        )

    tick(6)
    up_products()
    send_outward(FIRST, EARLY)
    for fetch in fetches:
        fetch.wait()
    for step, _ in enumerate(own_flow(1, finish_feed)):
        tick((8, 10, 11)[step])
        if step == 0:
            tick(9)
    for slot in range(4):
        plane.gone(second_buf.at[slot], core_send.at[1, slot])

    gather = Gather(plane, own_grad, grad_all, gather_send, gather_recv)
    gather.start()

    def qkv_load(step):
        return pltpu.make_async_copy(
            qkv_all.at[flipped(mine, step)], qkv_buf.at[lax.rem(step, 2)], load_sems.at[1 + lax.rem(step, 2)]
        )

    qkv_load(0).start()
    attended_load.wait()
    out_sum[...] = jnp.zeros_like(out_sum)
    columns = qkv_buf.shape[-1]
    third = columns // 3
    scale = HD ** (-0.5)

    @pl.loop(0, 8)
    def _(step):
        for number in range(8):

            @pl.when(step == number)
            def _(number=number):
                if number in (1, 2, 4):
                    tick({1: 12, 2: 13, 4: 15}[number])
                if number == 2:
                    tick(14)
                gather.step(number)
                if number == 7:
                    gather.finish()

        image = flipped(mine, step)
        slot = lax.rem(step, 2)
        qkv_load(step).wait()

        @pl.when(step < 7)
        def _():
            qkv_load(step + 1).start()

        grad = grad_all[image]
        grad_attended = contract(grad, out_weight[...], 1, 1).astype(jnp.bfloat16)
        image_rows = pl.ds(pl.multiple_of(image * rows, rows), rows)
        for head in range(third // HD):
            begin, first = head * HD, 3 * head * HD
            queries = qkv_buf[slot, :, first : first + HD]
            key_rows = qkv_buf[slot, :, first + HD : first + 2 * HD]
            value_rows = qkv_buf[slot, :, first + 2 * HD : first + 3 * HD]
            grad_head = grad_attended[:, begin : begin + HD]
            attention = softmax_rows(queries, key_rows)
            grad_weights = contract(grad_head, value_rows, 1, 1)
            row_delta = jnp.sum(attention * grad_weights, axis=-1, keepdims=True)
            grad_scores = (attention * (grad_weights - row_delta)).astype(jnp.bfloat16)
            saved_grad[image_rows, first : first + HD] = (
                contract(grad_scores, key_rows, 1, 0) * scale
            ).astype(jnp.bfloat16)
            saved_grad[image_rows, first + HD : first + 2 * HD] = (
                contract(grad_scores, queries, 0, 0) * scale
            ).astype(jnp.bfloat16)
            saved_grad[image_rows, first + 2 * HD : first + 3 * HD] = contract(
                attention.astype(jnp.bfloat16), grad_head, 0, 0
            ).astype(jnp.bfloat16)
        out_sum[...] += contract(attended_buf[image], grad, 0, 0)
        second_buf[step] = contract(saved_grad[image_rows, 0:columns], qkv_weight[...], 1, 1).astype(
            jnp.bfloat16
        )
        for number in (1, 3, 5, 7):

            @pl.when(step == number)
            def _(number=number):
                give(second_buf.at[number], first_buf, 2, number // 2)

    ahead()

    for block in range(8):
        in_buf[block] = out_sum[:, block * rows : (block + 1) * rows].astype(jnp.bfloat16)
    out_copy = pltpu.make_async_copy(in_buf, more.at[4], load_sems.at[0])
    out_copy.start()
    out_copy.wait()
    send_outward(EARLY, EARLY + 1)
    tick(16)
    def late_hook(block):
        @pl.when(block == 3)
        def _():
            tick(17)

    column_products(
        h_all,
        saved_grad.at[:, pl.ds(0, columns)],
        cols_buf,
        staged_buf,
        more.at[pl.ds(5, 3)],
        load_sems.at[pl.ds(3, 2)],
        load_sems.at[pl.ds(11, 2)],
        [[(3 * head + number) * HD for head in range(third // HD)] for number in range(3)],
        late_hook,
    )

    def finish_input(where, value):
        total = back_norm(plain(features, where), value, "scale_one", "shift_one")
        own_pair[0, where, :] = (total + grad_first[where, :]).astype(jnp.bfloat16)

    send_outward(EARLY + 1, CHUNKS)
    for step, _ in enumerate(own_flow(2, finish_input)):
        for now in ((18, 19), (20,), (21,))[step]:
            tick(now)
        if step == 0:
            out_products()
    return_tokens(own_grad, token_grad, 1)
    for step, _ in enumerate(staged_flow(partial_out, grad_all, 0, finish_out)):
        for now in ((22, 23), (24,), (25,))[step]:
            tick(now)
    return_tokens(image_out, token_out, 0)

    mod_copies = []
    mod_sum[7:8, :] = mod[7:8, :]
    mod_rows = pl.ds(pl.multiple_of(place * 8, 8), 8)
    mod_land[mod_rows, :] = mod_sum[...]
    for step, other in enumerate(others):
        copy = remote(
            mod_sum, mod_land.at[mod_rows], mod_sems.at[0, step], mod_sems.at[1, step], (mine, other)
        )
        copy.start()
        mod_copies.append(copy)
    tick(26)
    for copy in mod_copies:
        copy.wait_recv()
    own = pltpu.make_async_copy(mod_land, mod_out.at[mine], mod_sems.at[0, 3])
    own.start()
    mod_gather = Gather(plane, mod_land, mod_out, mod_gather_sems.at[0], mod_gather_sems.at[1])
    mod_gather.start()
    tick(27)
    mod_gather.middle()
    mod_gather.far()
    for flip in (1, 3, 5, 7):
        mod_gather.crossed(flip)
    mod_gather.finish()
    for now in range(28, 2 * CHUNKS + 6):
        tick(now)
    own.wait()
    for copy in mod_copies:
        copy.wait_send()
    for copy in token_copies:
        copy.wait()
    for number in (0, 2):
        for slot in range(4):
            plane.gone(second_buf.at[slot], core_send.at[number, slot])

    @pl.when(is_mid)
    def _():
        for k in (CHUNKS - 2, CHUNKS - 1):
            plane.gone(sum_buf.at[k % 2, :, other_half], z_sems.at[0, 1, k])
        for k in (CHUNKS - 2, CHUNKS - 1):
            plane.gone(half_buf.at[k % 2, pl.ds(0, 7)], x_sems.at[0, k])
        for k in range(CHUNKS):
            plane.gone(shares.at[k, :, my_half], z_sems.at[0, 2, k])
            plane.gone(shares.at[k, :, my_half], z_sems.at[0, 3, k])
            plane.gone(shares.at[k, :, other_half], z_sems.at[0, 4, k])

    @pl.when(jnp.logical_not(is_mid))
    def _():
        first = pl.ds(pl.multiple_of(jnp.where(place == 0, 0, HALF_ROWS), HALF_ROWS), HALF_ROWS)
        second = pl.ds(pl.multiple_of(jnp.where(place == 0, HALF_ROWS, 0), HALF_ROWS), HALF_ROWS)
        for k in range(CHUNKS):
            plane.gone(land_a.at[k], z_sems.at[0, 0, k])
            plane.got(shares.at[k, :, first], z_sems.at[1, 3, k])
            plane.got(shares.at[k, :, second], z_sems.at[1, 4, k])


def back_part(*operands):
    h_all, qkv_weight = operands[7], operands[10]
    _, rows, width = h_all.shape
    columns = qkv_weight.shape[1]
    feed = operands[1].shape[-1]
    low, full = jnp.bfloat16, jnp.float32
    dma = pltpu.SemaphoreType.DMA
    anywhere, inside = pl.BlockSpec(memory_space=pl.ANY), pl.BlockSpec(memory_space=pltpu.VMEM)
    return pl.pallas_call(
        back_kernel,
        out_shape=[
            jax.ShapeDtypeStruct((CHUNKS, 8, rows, rows), low),
            jax.ShapeDtypeStruct((4, rows // 4, width), low),
            jax.ShapeDtypeStruct((4, rows // 4, width), low),
            jax.ShapeDtypeStruct((8, 32, width), full),
            jax.ShapeDtypeStruct((CHUNKS - FIRST, 8, rows, rows), low),
            jax.ShapeDtypeStruct((8, rows, width), low),
            jax.ShapeDtypeStruct((CHUNKS, 8, rows, rows), low),
            jax.ShapeDtypeStruct((CHUNKS, 8, HALF_ROWS, rows), low),
        ],
        in_specs=[anywhere] * 16 + [inside],
        out_specs=[anywhere] * 8,
        scratch_shapes=[
            pltpu.VMEM((7, rows, width), low),
            pltpu.VMEM((8, rows, width), low),
            pltpu.VMEM((2, rows, width), low),
            pltpu.VMEM((2, rows, width), low),
            pltpu.VMEM((2, rows, feed), low),
            pltpu.VMEM((8, rows, width), low),
            pltpu.VMEM((8, rows, feed), low),
            pltpu.VMEM((rows, width), full),
            pltpu.VMEM((8 * rows, feed), low),
            pltpu.VMEM((2, 8, rows, rows), low),
            pltpu.VMEM((2, rows, columns), low),
            pltpu.VMEM((8, rows, columns // 3), low),
            pltpu.VMEM((2, 4, rows, rows), low),
            pltpu.VMEM((columns // 3, width), full),
            pltpu.VMEM((2, 8, rows, rows), low),
            pltpu.VMEM((8, rows, rows), low),
            pltpu.VMEM((2, 8, HALF_ROWS, rows), low),
            pltpu.VMEM((8, HALF_ROWS, rows), low),
            pltpu.VMEM((8, width), full),
            pltpu.VMEM((32, width), full),
            pltpu.VMEM((8 * rows, columns), low),
            pltpu.VMEM((rows, width), low),
            pltpu.VMEM((rows, width), low),
            pltpu.VMEM((rows, width), full),
            pltpu.VMEM((rows, width), low),
            pltpu.VMEM((rows, width), low),
            dma((3, 4)),
            dma((3, 4)),
            dma((3, 2)),
            dma((3, 2)),
            dma((3, 4)),
            dma((3, 4)),
            dma((2, 4)),
            dma((7 * PIECES,)),
            dma((7 * PIECES,)),
            dma((19,)),
            dma((2, 8)),
            dma((2, 5, CHUNKS)),
            dma((2, CHUNKS)),
            dma((3,)),
            dma((2, 2, 4)),
            dma((2, 4)),
            dma((2, 7 * PIECES)),
        ],
        compiler_params=pltpu.CompilerParams(
            collective_id=4, has_side_effects=True, vmem_limit_bytes=63 * 1024 * 1024
        ),
        name="back_part",
    )(*operands)


class Gather:
    def __init__(self, plane, own, result, send_sems, recv_sems):
        self.plane, self.own, self.result = plane, own, result
        self.send_sems, self.recv_sems = send_sems, recv_sems
        self.piece = own.shape[0] // PIECES

    def put(self, src, owner, part, flip, slot):
        remote(
            src,
            self.result.at[owner, pl.ds(part * self.piece, self.piece)],
            self.send_sems.at[slot],
            self.recv_sems.at[slot],
            self.plane.to(flip),
        ).start()

    def arrived(self, flip, part, slot):
        ref = self.result.at[self.plane.at(flip), pl.ds(part * self.piece, self.piece)]
        self.plane.got(ref, self.recv_sems.at[slot])
        return ref

    def start(self):
        mine = self.plane.mine
        for part in range(PIECES):
            src = self.own.at[pl.ds(part * self.piece, self.piece)]
            self.put(src, mine, part, 2, part)
            self.put(src, mine, part, 4, PIECES + part)
            self.put(src, mine, part, 1, 3 * PIECES + part)

    def middle(self):
        at = self.plane.at
        for part in range(PIECES):
            got = self.arrived(2, part, part)
            if part < PIECES // 2:
                self.put(got, at(2), part, 4, 2 * PIECES + part)
            self.put(got, at(2), part, 1, 4 * PIECES + part)
            got = self.arrived(4, part, PIECES + part)
            if part >= PIECES // 2:
                self.put(got, at(4), part, 2, 2 * PIECES + part)
            self.put(got, at(4), part, 1, 5 * PIECES + part)

    def far(self):
        for part in range(PIECES):
            got = self.arrived(6, part, 2 * PIECES + part)
            self.put(got, self.plane.at(6), part, 1, 6 * PIECES + part)

    def crossed(self, flip):
        for part in range(PIECES):
            self.arrived(flip, part, (3 + flip // 2) * PIECES + part)

    def step(self, number):
        if number == 2:
            self.middle()
        if number == 6:
            self.far()
        if number % 2:
            self.crossed(number)

    def finish(self):
        for slot in range(7 * PIECES):
            self.plane.gone(self.own.at[pl.ds(0, self.piece)], self.send_sems.at[slot])


class Halves:
    def __init__(self, ref, half):
        self.ref, self.half = ref, half

    @property
    def at(self):
        return self

    def __getitem__(self, number):
        return self.ref.at[pl.ds(number * self.half, self.half)]


def front_kernel(
    bin_ids,
    image_counts,
    noise,
    mod_bias,
    block_input,
    cotangent,
    attn_weight,
    mlp_weight,
    mod_weight,
    qkv_weight,
    out_weight_out,
    up_weight,
    down_low,
    h_one_all,
    h_two_all,
    grad_mlp_all,
    qkv_all,
    attended_all,
    hidden_all,
    slope_all,
    first_grads,
    features_out,
    first_sum_out,
    attn_out_out,
    grad_out_out,
    mod_out,
    load_buf,
    qkv_stage,
    up_stage,
    weight_buf,
    hidden_buf,
    cols_buf,
    staged_buf,
    h_all,
    qkv_buf,
    attended_buf,
    part_buf,
    scatter_buf,
    own_h,
    own_grad,
    own_next,
    bin_row,
    bin_land,
    mod_part,
    mod_land,
    out_weight,
    features,
    first_sum,
    attn_out,
    grad_out,
    mod,
    load_sems,
    token_sems,
    bin_sems,
    mod_sems,
    weight_sems,
    beside_sems,
    gather_sems,
    core_send,
    core_recv,
    far_send,
    far_recv,
    near_send,
    near_recv,
    copy_sems,
):
    plane = Plane()
    mine, place, at = plane.mine, plane.place, plane.at
    rows, width = own_h.shape
    feed = up_stage.shape[-1]
    columns = qkv_stage.shape[-1]
    third = columns // 3
    piece = rows // 4
    others = [lax.rem(place + step, 4) for step in (1, 2, 3)]
    flips = (6, 7, 2, 4, 3, 5, 1, 0)
    greet([plane.to(flip) for flip in range(1, 8)] + [(mine, other) for other in others])

    results = [
        pltpu.make_async_copy(source, result, copy_sems.at[14 + number])
        for number, (source, result) in enumerate(
            (
                (mod, mod_out),
                (features, features_out),
                (grad_out, grad_out_out),
                (out_weight, out_weight_out),
                (first_sum, first_sum_out),
                (attn_out, attn_out_out),
            )
        )
    ]

    token_copies = []
    my_rows = pl.ds(pl.multiple_of(place * piece, piece), piece)
    for number, (source, result) in enumerate(((block_input, features), (cotangent, grad_out))):
        copies = [
            pltpu.make_async_copy(
                source.at[place], result.at[my_rows], token_sems.at[0, number, 0]
            )
        ]
        for step, other in enumerate(others):
            copies.append(
                remote(
                    source.at[other],
                    result.at[my_rows],
                    token_sems.at[0, number, step + 1],
                    token_sems.at[1, number, step + 1],
                    (mine, other),
                )
            )
        for copy in copies:
            copy.start()
        token_copies.append(copies)

    lanes = lax.broadcasted_iota(jnp.int32, bin_row.shape, 1)
    bin_row[...] = jnp.where(lanes == bin_ids[place], 1.0, 0.0).astype(jnp.float32)
    bin_land[mine] = bin_row[...]
    bin_copies = [
        remote(
            bin_row, bin_land.at[mine], bin_sems.at[0, flip], bin_sems.at[1, flip], plane.to(flip)
        )
        for flip in range(1, 8)
    ]
    for copy in bin_copies:
        copy.start()

    parity = lax.rem(place, 2)
    beside = (mine, place + 1 - 2 * parity)

    def half_of(size):
        return pl.ds(pl.multiple_of(parity * size, size), size)

    def load_columns(source, slot, begins, size):
        return [
            pltpu.make_async_copy(
                source.at[:, pl.ds(pl.multiple_of(begin, HD), size)],
                load_buf.at[slot, :, pl.ds(number * size, size)],
                load_sems.at[slot, number],
            )
            for number, begin in enumerate(begins)
        ]

    def cast_and_send(source, begins_of, size, stage, result, kind):
        loads = [
            load_columns(source, step % 2, begins_of(at(flip)), size)
            for step, flip in enumerate(flips)
        ]
        total = size * len(loads[0])
        half = half_of(total)
        for load in loads[0]:
            load.start()
        for step, flip in enumerate(flips):
            if step + 1 < len(flips):
                for load in loads[step + 1]:
                    load.start()
            for load in loads[step]:
                load.wait()

            def cast(band, step=step):
                stage[step, band, 0:total] = load_buf[step % 2, band, 0:total].astype(jnp.bfloat16)

            bands(rows, cast)
            src = stage.at[step, :, pl.ds(0, total)]
            if flip:
                remote(
                    src,
                    result.at[mine, :, half],
                    weight_sems.at[0, kind, flip],
                    weight_sems.at[1, kind, flip],
                    plane.to(flip),
                ).start()
            else:
                pltpu.make_async_copy(
                    src, result.at[mine, :, half], weight_sems.at[0, kind, 0]
                ).start()

    def pass_on(stage, result, kind, total):
        half = half_of(total)
        pltpu.make_async_copy(
            stage.at[7, :, pl.ds(0, total)], result.at[mine, :, half], weight_sems.at[0, kind, 0]
        ).wait()
        for flip in (1, 2, 3, 4, 5, 6, 7, 0):
            piece = result.at[at(flip), :, half]
            if flip:
                plane.got(piece, weight_sems.at[1, kind, flip])
            remote(
                piece,
                piece,
                beside_sems.at[0, kind, flip],
                beside_sems.at[1, kind, flip],
                beside,
            ).start()

    def weights_ready(stage, result, kind, total):
        for flip in range(8):
            piece = result.at[at(flip), :, half_of(total)]
            plane.got(piece, beside_sems.at[1, kind, flip])
            plane.gone(piece, beside_sems.at[0, kind, flip])
            if flip:
                plane.gone(stage.at[0, :, pl.ds(0, total)], weight_sems.at[0, kind, flip])

    cast_and_send(
        attn_weight,
        lambda owner: [number * width + owner * third + parity * HD for number in range(3)],
        HD,
        qkv_stage,
        qkv_weight,
        0,
    )

    cast_and_send(
        mlp_weight,
        lambda owner: [owner * feed + parity * (feed // 2)],
        feed // 2,
        up_stage,
        up_weight,
        1,
    )

    for copy in bin_copies:
        copy.wait_recv()
    bins = noise.shape[0]
    activated = noise[...] / (1.0 + jnp.exp(-noise[...]))
    chosen = jnp.dot(
        bin_land[:, 0, :bins], activated, precision=PRECISE, preferred_element_type=jnp.float32
    )

    def load_mod(number):
        return pltpu.make_async_copy(
            mod_weight.at[:, pl.ds(number * width, width)],
            load_buf.at[number % 2],
            load_sems.at[number % 2, 0],
        )

    load_mod(0).start()
    mod_part[...] = jnp.zeros_like(mod_part)
    for number in range(6):
        if number < 5:
            load_mod(number + 1).start()
        load_mod(number).wait()
        mod_part[:, number, :] = jnp.dot(
            chosen, load_buf[number % 2], precision=PRECISE, preferred_element_type=jnp.float32
        )
    quarter = width // 4
    for number in range(3):
        index = 3 * mine + number
        where = pl.ds(pl.multiple_of(lax.rem(index, 4) * quarter, quarter), quarter)
        for image in range(8):
            mod_part[image, pl.ds(index // 4, 1), where] += mod_bias[
                :, number * quarter : (number + 1) * quarter
            ]
    mod_copies = [
        remote(
            mod_part.at[at(flip)],
            mod_land.at[mine],
            mod_sems.at[0, flip],
            mod_sems.at[1, flip],
            plane.to(flip),
        )
        for flip in range(1, 8)
    ]
    for copy in mod_copies:
        copy.start()
    pass_on(qkv_stage, qkv_weight, 0, 3 * HD)
    mod_land[mine] = mod_part[mine]
    for copy in mod_copies:
        copy.wait_recv()
    total = mod_land[0]
    for number in range(1, 8):
        total = total + mod_land[number]
    mod[...] = total
    live = jnp.where(place < image_counts[0], 1.0, 0.0).astype(jnp.float32)
    mod[6:7, :] = jnp.full((1, width), 1.0, jnp.float32) * live
    mod[7:8, :] = jnp.zeros((1, width), jnp.float32)
    mod[7:8, :128] = bin_row[0:1, :]
    results[0].start()

    def mod_row(number):
        return mod[number : number + 1, :]

    def tokens_arrived(number):
        for copy in token_copies[number]:
            if copy is token_copies[number][0]:
                copy.wait()
            else:
                copy.wait_recv()

    tokens_arrived(0)
    results[1].start()

    def first_norm(band):
        source = plain(features, band)
        normed = (source * rms_scale(source) * (1.0 + mod_row(1)) + mod_row(0)).astype(jnp.bfloat16)
        own_h[band, :] = normed
        h_all[mine, band, :] = normed

    bands(rows, first_norm)
    h_gather = Gather(plane, own_h, h_all, gather_sems.at[0, 0], gather_sems.at[0, 1])
    h_gather.start()

    tokens_arrived(1)

    def feed_grad(band):
        scaled = plain(grad_out, band) * mod_row(6)
        grad_out[band, :] = scaled.astype(jnp.bfloat16)
        own_grad[band, :] = (mod_row(5) * scaled).astype(jnp.bfloat16)

    bands(rows, feed_grad)
    results[2].start()
    grad_own = pltpu.make_async_copy(own_grad, grad_mlp_all.at[mine], copy_sems.at[0])
    grad_own.start()
    grad_gather = Gather(plane, own_grad, grad_mlp_all, gather_sems.at[1, 0], gather_sems.at[1, 1])
    grad_gather.start()
    def down_load(owner):
        return pltpu.make_async_copy(
            mlp_weight.at[:, pl.ds((8 + owner) * feed, feed)],
            load_buf.at[owner % 2, :, pl.ds(0, feed)],
            load_sems.at[owner % 2, 0],
        )

    def down_store(owner):
        return pltpu.make_async_copy(
            part_buf.at[owner, :, pl.ds(0, feed)], down_low.at[owner], copy_sems.at[6 + owner]
        )

    down_load(0).start()
    for owner in range(8):
        if owner < 7:
            down_load(owner + 1).start()
        down_load(owner).wait()

        def cast_down(band, owner=owner):
            part_buf[owner, band, 0:feed] = load_buf[owner % 2, band, 0:feed].astype(jnp.bfloat16)

        bands(rows, cast_down)
        down_store(owner).start()
    for owner in range(8):
        down_store(owner).wait()
    load = pltpu.make_async_copy(
        attn_weight.at[:, pl.ds(3 * width, width)], load_buf.at[0], load_sems.at[0, 0]
    )
    load.start()
    load.wait()

    def cast_out(band):
        out_weight[band, :] = load_buf[0, band, :].astype(jnp.bfloat16)

    bands(rows, cast_out)
    results[3].start()

    weights_ready(qkv_stage, qkv_weight, 0, 3 * HD)
    load = pltpu.make_async_copy(qkv_weight, weight_buf, copy_sems.at[1])
    load.start()
    load.wait()

    @pl.loop(0, 8)
    def _(step):
        for number in range(8):

            @pl.when(step == number)
            def _(number=number):
                h_gather.step(number)

        image = flipped(mine, step)
        pltpu.make_async_copy(h_all.at[image], h_one_all.at[image], copy_sems.at[2]).start()
        projected = contract(
            h_all[image], weight_buf[...].reshape(8 * rows, columns), 1, 0
        ).astype(jnp.bfloat16)
        qkv_buf[image] = projected
        for head in range(third // HD):
            begin, first = head * HD, 3 * head * HD
            queries = projected[:, first : first + HD]
            key_rows = projected[:, first + HD : first + 2 * HD]
            value_rows = projected[:, first + 2 * HD : first + 3 * HD]
            attention = softmax_rows(queries, key_rows).astype(jnp.bfloat16)
            attended_buf[image, :, begin : begin + HD] = contract(
                attention, value_rows, 1, 0
            ).astype(jnp.bfloat16)
        part_buf[step] = contract(attended_buf[image], out_weight[...], 1, 0).astype(jnp.bfloat16)
        pltpu.make_async_copy(h_all.at[image], h_one_all.at[image], copy_sems.at[2]).wait()

        @pl.when(step == 7)
        def _():
            h_gather.finish()

        for number in (1, 3, 5, 7):

            @pl.when(step == number)
            def _(number=number):
                slot = number // 2
                remote(
                    part_buf.at[number],
                    scatter_buf.at[slot],
                    core_send.at[slot],
                    core_recv.at[slot],
                    plane.to(1),
                ).start()

    pass_on(up_stage, up_weight, 1, feed // 2)
    keeps = [
        pltpu.make_async_copy(qkv_buf, qkv_all, copy_sems.at[3]),
        pltpu.make_async_copy(attended_buf, attended_all, copy_sems.at[4]),
    ]
    for copy in keeps:
        copy.start()

    def second_norm(band, value):
        attn_out[band, :] = value.astype(jnp.bfloat16)
        source = plain(features, band) + mod_row(2) * value
        first_sum[band, :] = source
        normed = (source * rms_scale(source) * (1.0 + mod_row(4)) + mod_row(3)).astype(jnp.bfloat16)
        own_next[band, :] = normed
        h_all[mine, band, :] = normed

    flow = scatter_flow(
        plane,
        lambda slot: part_buf.at[2 * slot],
        lambda slot: None,
        scatter_buf.at[pl.ds(0, 4)],
        Halves(scatter_buf.at[6], rows // 2),
        scatter_buf.at[pl.ds(4, 2)],
        (core_recv, far_send, far_recv, near_send, near_recv),
        second_norm,
    )
    for number, _ in enumerate(flow):
        if number == 1:
            grad_gather.middle()
    for slot in range(4):
        plane.gone(part_buf.at[slot], core_send.at[slot])
    next_gather = Gather(plane, own_next, h_all, gather_sems.at[2, 0], gather_sems.at[2, 1])
    next_gather.start()
    results[4].start()
    results[5].start()
    grad_gather.far()
    weights_ready(up_stage, up_weight, 1, feed // 2)
    load = pltpu.make_async_copy(up_weight, up_stage, copy_sems.at[1])
    load.start()
    load.wait()

    @pl.loop(0, 8)
    def _(step):
        for number in range(8):

            @pl.when(step == number)
            def _(number=number):
                next_gather.step(number)

        image = flipped(mine, step)
        pre = contract(h_all[image], up_stage[...].reshape(8 * rows, feed), 1, 0)
        hidden, slope = gelu_and_slope(pre)
        hidden_buf[pl.ds(pl.multiple_of(image * rows, rows), rows), :] = hidden.astype(jnp.bfloat16)
        part_buf[image, :, 0:feed] = slope.astype(jnp.bfloat16)

    keeps.append(pltpu.make_async_copy(h_all, h_two_all, copy_sems.at[2]))
    keeps.append(pltpu.make_async_copy(hidden_buf, hidden_all, copy_sems.at[5]))
    keeps.append(
        pltpu.make_async_copy(part_buf.at[:, :, pl.ds(0, feed)], slope_all, copy_sems.at[1])
    )
    for copy in keeps[-3:]:
        copy.start()
    for flip in (1, 3, 5, 7):
        grad_gather.crossed(flip)
    grad_own.wait()
    column_products(
        grad_mlp_all,
        hidden_buf,
        cols_buf,
        staged_buf,
        first_grads,
        copy_sems.at[pl.ds(6, 2)],
        copy_sems.at[pl.ds(8, 2)],
    )
    for gather in (grad_gather, next_gather):
        gather.finish()
    for copy in keeps + results:
        copy.wait()
    for copies in token_copies:
        for copy in copies[1:]:
            copy.wait_send()
    for copy in bin_copies + mod_copies:
        copy.wait_send()


def front_part(
    bin_ids,
    image_counts,
    noise,
    mod_bias,
    block_input,
    cotangent,
    attn_weight,
    mlp_weight,
    mod_weight,
):
    slots, local_tok, width = block_input.shape
    rows = slots * local_tok
    columns, feed = 3 * width // 8, mlp_weight.shape[1] // 16
    low, full = jnp.bfloat16, jnp.float32
    dma = pltpu.SemaphoreType.DMA
    anywhere, inside = pl.BlockSpec(memory_space=pl.ANY), pl.BlockSpec(memory_space=pltpu.VMEM)
    scalars = pl.BlockSpec(memory_space=pltpu.SMEM)
    return pl.pallas_call(
        front_kernel,
        out_shape=[
            jax.ShapeDtypeStruct((8, rows, columns), low),
            jax.ShapeDtypeStruct((rows, width), low),
            jax.ShapeDtypeStruct((8, rows, feed), low),
            jax.ShapeDtypeStruct((8, rows, feed), low),
            jax.ShapeDtypeStruct((8, rows, width), low),
            jax.ShapeDtypeStruct((8, rows, width), low),
            jax.ShapeDtypeStruct((8, rows, width), low),
            jax.ShapeDtypeStruct((8, rows, columns), low),
            jax.ShapeDtypeStruct((8, rows, columns // 3), low),
            jax.ShapeDtypeStruct((8 * rows, feed), low),
            jax.ShapeDtypeStruct((8, rows, feed), low),
            jax.ShapeDtypeStruct((FIRST, 8, rows, rows), low),
            jax.ShapeDtypeStruct((rows, width), low),
            jax.ShapeDtypeStruct((rows, width), full),
            jax.ShapeDtypeStruct((rows, width), low),
            jax.ShapeDtypeStruct((rows, width), low),
            jax.ShapeDtypeStruct((8, width), full),
        ],
        in_specs=[scalars] * 2 + [inside] * 2 + [anywhere] * 5,
        out_specs=[anywhere] * 17,
        scratch_shapes=[
            pltpu.VMEM((2, rows, width), full),
            pltpu.VMEM((8, rows, columns), low),
            pltpu.VMEM((8, rows, feed), low),
            pltpu.VMEM((8, rows, columns), low),
            pltpu.VMEM((8 * rows, feed), low),
            pltpu.VMEM((2, 8, rows, rows), low),
            pltpu.VMEM((2, 4, rows, rows), low),
            pltpu.VMEM((8, rows, width), low),
            pltpu.VMEM((8, rows, columns), low),
            pltpu.VMEM((8, rows, columns // 3), low),
            pltpu.VMEM((8, rows, width), low),
            pltpu.VMEM((7, rows, width), low),
            pltpu.VMEM((rows, width), low),
            pltpu.VMEM((rows, width), low),
            pltpu.VMEM((rows, width), low),
            pltpu.VMEM((8, 128), full),
            pltpu.VMEM((8, 8, 128), full),
            pltpu.VMEM((8, 8, width), full),
            pltpu.VMEM((8, 8, width), full),
            pltpu.VMEM((rows, width), low),
            pltpu.VMEM((rows, width), low),
            pltpu.VMEM((rows, width), full),
            pltpu.VMEM((rows, width), low),
            pltpu.VMEM((rows, width), low),
            pltpu.VMEM((8, width), full),
            dma((2, 3)),
            dma((2, 2, 4)),
            dma((2, 8)),
            dma((2, 8)),
            dma((2, 2, 8)),
            dma((2, 2, 8)),
            dma((3, 2, 7 * PIECES)),
            dma((4,)),
            dma((4,)),
            dma((2,)),
            dma((2,)),
            dma((4,)),
            dma((4,)),
            dma((20,)),
        ],
        compiler_params=pltpu.CompilerParams(
            collective_id=5, has_side_effects=True, vmem_limit_bytes=63 * 1024 * 1024
        ),
        name="front_part",
    )(
        bin_ids,
        image_counts,
        noise,
        mod_bias,
        block_input,
        cotangent,
        attn_weight,
        mlp_weight,
        mod_weight,
    )


def tail_kernel(
    mlp_ref,
    attn_ref,
    rows_ref,
    noise_ref,
    weight_ref,
    out_ref,
    grad_ref,
    mlp_grad_ref,
    attn_grad_ref,
    weight_grad_ref,
    noise_grad_ref,
    bias_ref,
    block_out_ref,
    input_grad_ref,
    chosen,
    total,
    flat_rows,
    onehot_rows,
):
    step = pl.program_id(0)
    size = mlp_ref.shape[-1]
    for number in range(4):
        mlp_grad_ref[:, number * size : (number + 1) * size] = mlp_ref[number, 0].astype(
            jnp.float32
        )
    for number in range(2):
        attn_grad_ref[:, number * size : (number + 1) * size] = attn_ref[0, number].astype(
            jnp.float32
        )
    block_out_ref[...] = out_ref[...]
    input_grad_ref[...] = grad_ref[...].astype(jnp.float32)
    noise = noise_ref[...]
    rise = 1.0 / (1.0 + jnp.exp(-noise))
    part = weight_ref.shape[1]

    @pl.when(step == 0)
    def _():
        width = rows_ref.shape[2]
        for row in range(6):
            flat_rows[:, row * width : (row + 1) * width] = rows_ref[:, row, :]
        onehot = rows_ref[:, 7, : noise.shape[0]]
        onehot_rows[...] = onehot
        chosen[...] = jnp.dot(
            onehot, noise * rise, precision=PRECISE, preferred_element_type=jnp.float32
        )
        total[...] = jnp.zeros_like(total)

    grads = flat_rows[:, pl.ds(pl.multiple_of(step * part, 128), part)]
    bias_ref[...] = jnp.broadcast_to(jnp.sum(grads, axis=0, keepdims=True), bias_ref.shape)
    low = grads.astype(jnp.bfloat16)
    weight_grad_ref[...] = contract(chosen[...].astype(jnp.bfloat16), low, 0, 0)
    total[...] += contract(weight_ref[...].astype(jnp.bfloat16), low, 1, 1)

    @pl.when(step == pl.num_programs(0) - 1)
    def _():
        table = lax.dot_general(
            onehot_rows[...],
            total[...],
            (((0,), (1,)), ((), ())),
            precision=PRECISE,
            preferred_element_type=jnp.float32,
        )
        noise_grad_ref[...] = table * (rise + noise * rise * (1.0 - rise))


def tail_part(shares, image_rows, noise, weight, token_out, token_grad):
    steps = 16
    rows = shares.shape[2]
    images = image_rows.shape[0]
    depth, columns = weight.shape
    part = columns // steps
    slots, local_tok, width = token_out.shape
    token_spec = pl.BlockSpec((1, local_tok, width // 4), lambda step: (step // 4, 0, step % 4))
    return pl.pallas_call(
        tail_kernel,
        grid=(steps,),
        out_shape=[
            jax.ShapeDtypeStruct((rows, 64 * rows), jnp.float32),
            jax.ShapeDtypeStruct((rows, 32 * rows), jnp.float32),
            jax.ShapeDtypeStruct(weight.shape, jnp.float32),
            jax.ShapeDtypeStruct(noise.shape, jnp.float32),
            jax.ShapeDtypeStruct((8, columns), jnp.float32),
            jax.ShapeDtypeStruct(token_out.shape, jnp.bfloat16),
            jax.ShapeDtypeStruct(token_grad.shape, jnp.float32),
        ],
        in_specs=[
            pl.BlockSpec((4, 1, rows, rows), lambda step: (1 - step // 8, step % 8, 0, 0)),
            pl.BlockSpec((1, 2, rows, rows), lambda step: (EARLY + (step // 4 + 1) % 4, step % 4, 0, 0)),
            pl.BlockSpec(image_rows.shape, lambda step: (0, 0, 0)),
            pl.BlockSpec(noise.shape, lambda step: (0, 0)),
            pl.BlockSpec((depth, part), lambda step: (0, step)),
            token_spec,
            token_spec,
        ],
        out_specs=[
            pl.BlockSpec((rows, 4 * rows), lambda step: (0, step)),
            pl.BlockSpec((rows, 2 * rows), lambda step: (0, step)),
            pl.BlockSpec((depth, part), lambda step: (0, step)),
            pl.BlockSpec(noise.shape, lambda step: (0, 0)),
            pl.BlockSpec((8, part), lambda step: (0, step)),
            token_spec,
            token_spec,
        ],
        scratch_shapes=[
            pltpu.VMEM((images, depth), jnp.float32),
            pltpu.VMEM((depth, images), jnp.float32),
            pltpu.VMEM((images, columns), jnp.float32),
            pltpu.VMEM((images, noise.shape[0]), jnp.float32),
        ],
        compiler_params=pltpu.CompilerParams(vmem_limit_bytes=VMEM_BYTES),
        name="tail_part",
    )(shares, shares, image_rows, noise, weight, token_out, token_grad)


def plane_body(
    block_input,
    cotangent,
    bin_ids,
    image_counts,
    attn_weight,
    mlp_weight,
    noise_table,
    mod_weight,
    mod_bias,
):
    model_width = block_input.shape[2]
    rows = attn_weight.shape[0]
    bias_piece = mod_bias.shape[0]
    mine = lax.axis_index("fsdp")
    (
        qkv_weight,
        out_weight,
        up_weight,
        down_low,
        h_one_all,
        h_two_all,
        grad_mlp_all,
        qkv_all,
        attended_all,
        hidden_all,
        slope_all,
        first_grads,
        features,
        first_sum,
        attn_out,
        grad_out,
        mod_rows,
    ) = front_part(
        bin_ids,
        image_counts,
        noise_table,
        mod_bias.reshape(1, bias_piece),
        block_input,
        cotangent,
        attn_weight,
        mlp_weight,
        mod_weight,
    )

    def flat(array):
        return array.reshape(-1, array.shape[-1])

    shares, token_out, token_grad, mod_out, _, _, _, _ = back_part(
        down_low,
        up_weight,
        hidden_all.reshape(8, rows, -1),
        slope_all,
        grad_mlp_all,
        h_two_all,
        first_grads,
        h_one_all,
        qkv_all,
        attended_all,
        flat(qkv_weight),
        out_weight,
        features,
        first_sum,
        attn_out,
        grad_out,
        mod_rows,
    )
    (
        mlp_weight_grad,
        attn_weight_grad,
        mod_weight_grad,
        noise_grad,
        bias_sums,
        block_out,
        input_grad,
    ) = tail_part(
        shares,
        mod_out.reshape(-1, 8, model_width),
        noise_table,
        mod_weight,
        token_out,
        token_grad,
    )
    mod_bias_grad = lax.dynamic_slice_in_dim(bias_sums[0], mine * bias_piece, bias_piece)
    return (
        block_out,
        input_grad,
        attn_weight_grad,
        mlp_weight_grad,
        noise_grad,
        mod_weight_grad,
        mod_bias_grad,
    )


def solution(mesh):
    fits = mesh.shape["fsdp"] == 8 and mesh.shape["blk"] == 4
    return jax.shard_map(
        plane_body if fits else body,
        mesh=mesh,
        in_specs=(
            P("fsdp", "blk", None),
            P("fsdp", "blk", None),
            P("fsdp"),
            P("fsdp"),
            P("fsdp", None),
            P("fsdp", None),
            P(None, "fsdp"),
            P("fsdp", None),
            P("fsdp"),
        ),
        out_specs=(
            P("fsdp", "blk", None),
            P("fsdp", "blk", None),
            P("fsdp", None),
            P("fsdp", None),
            P(None, "fsdp"),
            P("fsdp", None),
            P("fsdp"),
        ),
        check_vma=False,
    )
```

```python
import functools
import math

import jax
import jax.numpy as jnp
from jax import lax
from jax.experimental import pallas as pl
from jax.experimental.pallas import tpu as pltpu
from jax.sharding import PartitionSpec as P

HD = 128


EPSILON = 1e-06
PRECISE = lax.Precision.HIGHEST


def norm_mod(features, scaling, shifting):
    normed = features * lax.rsqrt(jnp.mean(features * features, axis=-1, keepdims=True) + EPSILON)
    return normed * (1.0 + scaling) + shifting


def rows_product(left_rows, right_rows):
    return lax.dot_general(
        left_rows, right_rows, (((0,), (0,)), ((), ())), preferred_element_type=jnp.float32
    )


def body(
    block_input,
    cotangent,
    bin_ids,
    image_counts,
    attn_weight,
    mlp_weight,
    noise_table,
    mod_weight,
    mod_bias,
):
    slot_count, local_tok, model_width = block_input.shape
    row_count = slot_count * local_tok
    feed_width = mlp_weight.shape[1] // 2
    head_count = model_width // HD
    blk_size = lax.axis_size("blk")
    image_tok = local_tok * blk_size
    score_scale = HD ** (-0.5)
    bias_piece = mod_bias.shape[0]
    activated = jax.nn.silu(noise_table)
    partial_mod = jnp.dot(activated, mod_weight, precision=PRECISE)
    bias_full = lax.dynamic_update_slice_in_dim(
        jnp.zeros((6 * model_width,), jnp.float32), mod_bias, lax.axis_index("fsdp") * bias_piece, 0
    )
    mod_table = lax.psum(partial_mod + bias_full[None, :], "fsdp")
    onehot = (
        bin_ids[:, None] == jnp.arange(noise_table.shape[0], dtype=jnp.int32)[None, :]
    ).astype(jnp.float32)
    mod_image = jnp.dot(onehot, mod_table, precision=PRECISE)
    shift_one, scale_one, gate_one, shift_two, scale_two, gate_two = [
        member[:, None, :] for member in jnp.split(mod_image, 6, axis=-1)
    ]
    live_mask = (jnp.arange(slot_count) < image_counts[0]).astype(jnp.float32)[:, None, None]
    features = block_input.astype(jnp.float32)
    h_one = (
        norm_mod(features, scale_one, shift_one)
        .astype(jnp.bfloat16)
        .reshape(row_count, model_width)
    )
    attn_full = lax.all_gather(attn_weight.astype(jnp.bfloat16), "fsdp", axis=0, tiled=True)
    projected = jnp.dot(
        h_one, attn_full[:, : 3 * model_width], preferred_element_type=jnp.float32
    ).astype(jnp.bfloat16)
    queries = projected[:, :model_width].reshape(slot_count, local_tok, head_count, HD)
    key_rows = projected[:, model_width : 2 * model_width].reshape(
        slot_count, local_tok, model_width
    )
    value_rows = projected[:, 2 * model_width :].reshape(slot_count, local_tok, model_width)
    all_keys, all_values = (
        lax.all_gather(key_rows, "blk", axis=1, tiled=True),
        lax.all_gather(value_rows, "blk", axis=1, tiled=True),
    )
    all_keys = all_keys.reshape(slot_count, image_tok, head_count, HD)
    all_values = all_values.reshape(slot_count, image_tok, head_count, HD)

    def scores_of(query_rows):
        return (
            jnp.einsum("sqhd,skhd->shqk", query_rows, all_keys, preferred_element_type=jnp.float32)
            * score_scale
        )

    scores = scores_of(queries)
    maximum = jnp.max(scores, axis=-1, keepdims=True)
    exponent = jnp.exp(scores - maximum)
    denominator = jnp.sum(exponent, axis=-1, keepdims=True)
    attention = exponent / denominator
    log_total = maximum + jnp.log(denominator)
    attended = (
        jnp.einsum(
            "shqk,skhd->sqhd",
            attention.astype(jnp.bfloat16),
            all_values,
            preferred_element_type=jnp.float32,
        )
        .astype(jnp.bfloat16)
        .reshape(row_count, model_width)
    )
    attn_out = jnp.dot(
        attended, attn_full[:, 3 * model_width :], preferred_element_type=jnp.float32
    ).reshape(slot_count, local_tok, model_width)
    first_sum = features + gate_one * attn_out
    h_two = (
        norm_mod(first_sum, scale_two, shift_two)
        .astype(jnp.bfloat16)
        .reshape(row_count, model_width)
    )
    mlp_full = lax.all_gather(mlp_weight.astype(jnp.bfloat16), "fsdp", axis=0, tiled=True)
    pre_gelu = jnp.dot(h_two, mlp_full[:, :feed_width], preferred_element_type=jnp.float32)
    hidden = jax.nn.gelu(pre_gelu).astype(jnp.bfloat16)
    mlp_out = jnp.einsum(
        "rf,df->rd", hidden, mlp_full[:, feed_width:], preferred_element_type=jnp.float32
    ).reshape(slot_count, local_tok, model_width)
    second_sum = first_sum + gate_two * mlp_out
    block_out = (live_mask * second_sum).astype(jnp.bfloat16)
    grad_out = cotangent.astype(jnp.float32) * live_mask
    grad_mlp = (gate_two * grad_out).astype(jnp.bfloat16).reshape(row_count, model_width)
    grad_gate_two = jnp.sum(grad_out * mlp_out, axis=1)
    grad_hidden = jnp.dot(grad_mlp, mlp_full[:, feed_width:], preferred_element_type=jnp.float32)
    grad_pre = jax.vjp(jax.nn.gelu, pre_gelu)[1](grad_hidden)[0].astype(jnp.bfloat16)
    grad_h_two = jnp.einsum(
        "rf,df->rd", grad_pre, mlp_full[:, :feed_width], preferred_element_type=jnp.float32
    ).reshape(slot_count, local_tok, model_width)
    grad_first, grad_scale_two, grad_shift_two = jax.vjp(norm_mod, first_sum, scale_two, shift_two)[
        1
    ](grad_h_two)
    grad_first = grad_first + grad_out
    grad_attn_out = (gate_one * grad_first).astype(jnp.bfloat16).reshape(row_count, model_width)
    grad_gate_one = jnp.sum(grad_first * attn_out, axis=1)
    grad_attended = jnp.einsum(
        "rd,ed->re",
        grad_attn_out,
        attn_full[:, 3 * model_width :],
        preferred_element_type=jnp.float32,
    ).astype(jnp.bfloat16)
    grad_heads = grad_attended.reshape(slot_count, local_tok, head_count, HD)
    recomputed = jnp.exp(scores_of(queries) - log_total)
    grad_weights = jnp.einsum(
        "sqhd,skhd->shqk", grad_heads, all_values, preferred_element_type=jnp.float32
    )
    row_delta = jnp.sum(recomputed * grad_weights, axis=-1, keepdims=True)
    grad_scores = (recomputed * (grad_weights - row_delta)).astype(jnp.bfloat16)
    grad_queries = (
        jnp.einsum("shqk,skhd->sqhd", grad_scores, all_keys, preferred_element_type=jnp.float32)
        * score_scale
    )
    grad_keys_all = (
        jnp.einsum("shqk,sqhd->skhd", grad_scores, queries, preferred_element_type=jnp.float32)
        * score_scale
    )
    grad_values_all = jnp.einsum(
        "shqk,sqhd->skhd",
        recomputed.astype(jnp.bfloat16),
        grad_heads,
        preferred_element_type=jnp.float32,
    )
    grad_keys, grad_values = (
        lax.psum_scatter(
            grad_keys_all.reshape(slot_count, image_tok, model_width).astype(jnp.bfloat16),
            "blk",
            scatter_dimension=1,
            tiled=True,
        ).astype(jnp.float32),
        lax.psum_scatter(
            grad_values_all.reshape(slot_count, image_tok, model_width).astype(jnp.bfloat16),
            "blk",
            scatter_dimension=1,
            tiled=True,
        ).astype(jnp.float32),
    )
    grad_qkv = jnp.concatenate(
        [
            grad_queries.reshape(row_count, model_width).astype(jnp.bfloat16),
            grad_keys.reshape(row_count, model_width).astype(jnp.bfloat16),
            grad_values.reshape(row_count, model_width).astype(jnp.bfloat16),
        ],
        axis=1,
    )
    grad_h_one = jnp.einsum(
        "rc,dc->rd", grad_qkv, attn_full[:, : 3 * model_width], preferred_element_type=jnp.float32
    ).reshape(slot_count, local_tok, model_width)
    grad_input, grad_scale_one, grad_shift_one = jax.vjp(norm_mod, features, scale_one, shift_one)[
        1
    ](grad_h_one)
    input_grad = grad_input + grad_first
    grad_mod = jnp.concatenate(
        [
            grad_shift_one[:, 0, :],
            grad_scale_one[:, 0, :],
            grad_gate_one,
            grad_shift_two[:, 0, :],
            grad_scale_two[:, 0, :],
            grad_gate_two,
        ],
        axis=-1,
    )
    bin_terms = lax.dot_general(onehot, grad_mod, (((0,), (0,)), ((), ())), precision=PRECISE)
    grad_bins = lax.psum(bin_terms, ("fsdp", "blk"))
    table_term = jnp.einsum("be,de->bd", grad_bins, mod_weight, precision=PRECISE)
    noise_grad = jax.vjp(jax.nn.silu, noise_table)[1](table_term)[0]
    mod_weight_grad = lax.dot_general(
        activated, grad_bins, (((0,), (0,)), ((), ())), precision=PRECISE
    )
    mod_bias_grad = lax.dynamic_slice_in_dim(
        jnp.sum(grad_bins, axis=0), lax.axis_index("fsdp") * bias_piece, bias_piece
    )
    h_part = h_one
    attn_part = lax.psum_scatter(
        jnp.concatenate(
            [rows_product(h_part, grad_qkv), rows_product(attended, grad_attn_out)], axis=1
        ).astype(jnp.bfloat16),
        "fsdp",
        scatter_dimension=0,
        tiled=True,
    )
    h_part = h_two
    mlp_part = lax.psum_scatter(
        jnp.concatenate(
            [rows_product(h_part, grad_pre), rows_product(grad_mlp, hidden)], axis=1
        ).astype(jnp.bfloat16),
        "fsdp",
        scatter_dimension=0,
        tiled=True,
    )
    attn_weight_grad, mlp_weight_grad = (
        lax.psum(attn_part, "blk").astype(jnp.float32),
        lax.psum(mlp_part, "blk").astype(jnp.float32),
    )
    return (
        block_out,
        input_grad,
        attn_weight_grad,
        mlp_weight_grad,
        noise_grad,
        mod_weight_grad,
        mod_bias_grad,
    )


MESH_ID = pl.DeviceIdType.MESH
VMEM_BYTES = 56 * 1024 * 1024


def contract(left, right, left_dim, right_dim):
    return lax.dot_general(
        left, right, (((left_dim,), (right_dim,)), ((), ())), preferred_element_type=jnp.float32
    )


def plane_places():
    mine = lax.axis_index("fsdp")
    plane = lax.axis_index("blk")
    core = lax.rem(mine, 2)
    col = lax.rem(mine // 2, 2)
    row = mine // 4

    def at(flip):
        flip_row, flip_col, flip_core = flip // 4, (flip // 2) % 2, flip % 2
        new_row = 1 - row if flip_row else row
        new_col = 1 - col if flip_col else col
        new_core = 1 - core if flip_core else core
        return new_row * 4 + new_col * 2 + new_core

    return mine, plane, at


def greet(places):
    barrier = pltpu.get_barrier_semaphore()
    for place in places:
        pl.semaphore_signal(barrier, inc=1, device_id=place, device_id_type=MESH_ID)
    pl.semaphore_wait(barrier, len(places))


def remote(src, dst, send_sem, recv_sem, place):
    return pltpu.make_async_remote_copy(
        src_ref=src,
        dst_ref=dst,
        send_sem=send_sem,
        recv_sem=recv_sem,
        device_id=place,
        device_id_type=MESH_ID,
    )


PIECES = 4


def softmax_rows(queries, key_rows):
    scores = contract(queries, key_rows, 1, 1) * HD ** (-0.5)
    exponent = jnp.exp(scores - jnp.max(scores, axis=-1, keepdims=True))
    return exponent / jnp.sum(exponent, axis=-1, keepdims=True)


def rms_scale(features):
    return lax.rsqrt(jnp.mean(features * features, axis=-1, keepdims=True) + EPSILON)


CHUNKS = 12
FIRST = 4
EARLY = 8
HALF_ROWS = 128
BAND = 32


def flipped(mine, flip):
    total = 0
    for bit in (1, 2, 4):
        total = total + lax.rem(mine // bit + flip // bit, 2) * bit
    return total


def bands(count, step):
    @pl.loop(0, count // BAND)
    def _(index):
        step(pl.ds(pl.multiple_of(index * BAND, BAND), BAND))


def plain(ref, rows):
    return ref[rows, :].astype(jnp.float32)


def column_products(source, right, cols, staged, result, load_sems, store_sems, pieces=None, hook=None):
    rows = cols.shape[-1]
    count = result.shape[0]

    def load(block):
        slot = lax.rem(block, 2)
        return pltpu.make_async_copy(
            source.at[:, :, pl.ds(pl.multiple_of(block * rows, rows), rows)],
            cols.at[slot],
            load_sems.at[slot],
        )

    def store(block):
        slot = lax.rem(block, 2)
        return pltpu.make_async_copy(
            staged.at[slot, pl.ds(0, count)], result.at[:, block], store_sems.at[slot]
        )

    load(0).start()

    @pl.loop(0, 8)
    def _(block):
        slot = lax.rem(block, 2)
        load(block).wait()

        @pl.when(block < 7)
        def _():
            load(block + 1).start()

        @pl.when(block >= 2)
        def _():
            store(block - 2).wait()

        if hook:
            hook(block)
        product = contract(cols[slot].reshape(8 * rows, rows), right[...], 0, 0)
        for number in range(count):
            begins = pieces[number] if pieces else (number * rows,)
            size = rows // len(begins)
            for index, begin in enumerate(begins):
                staged[slot, number, :, index * size : (index + 1) * size] = product[
                    :, begin : begin + size
                ].astype(jnp.bfloat16)
        store(block).start()

    store(6).wait()
    store(7).wait()


GELU_SCALE = (2.0 / math.pi) ** 0.5


def gelu_and_slope(pre):
    squared = pre * pre
    bend = jnp.tanh(GELU_SCALE * (pre + 0.044715 * (squared * pre)))
    rise = 0.5 * (1.0 + bend)
    slope = rise + 0.5 * pre * (1.0 - bend * bend) * (GELU_SCALE * (1.0 + 3.0 * 0.044715 * squared))
    return pre * rise, slope


class Plane:
    def __init__(self):
        self.mine, self.place, self.at = plane_places()

    def to(self, flip):
        return (self.at(flip), self.place)

    def got(self, ref, sem):
        remote(ref, ref, sem, sem, (self.mine, self.place)).wait_recv()

    def gone(self, ref, sem):
        remote(ref, ref, sem, sem, (self.mine, self.place)).wait_send()


def scatter_flow(plane, own_of, fetch, peer, far, near, sems, finish):
    core_recv, far_send, far_recv, near_send, near_recv = sems
    rows = near.shape[1]
    half = rows // 2
    sent = []

    def add(slot, start, count, extra=None):
        own = own_of(slot)

        def step(band):
            at = pl.ds(pl.multiple_of(start + band.start, BAND), BAND)
            total = plain(own, at) + plain(peer.at[slot], at)
            if extra is not None:
                total = total + plain(extra, band)
            peer[slot, at, :] = total.astype(jnp.bfloat16)

        bands(count, step)

    def send(src, dst, flip, send_sem, recv_sem):
        copy = remote(src, dst, send_sem, recv_sem, plane.to(flip))
        copy.start()
        sent.append(copy)

    def send_near(slot, part):
        at = pl.ds(part * half, half)
        index = (slot - 1) * 2 + part
        send(
            peer.at[slot, at],
            near.at[slot - 1, at],
            2 * slot,
            near_send.at[index],
            near_recv.at[index],
        )

    fetch(3)
    plane.got(peer.at[3], core_recv.at[3])
    add(3, 0, rows)
    send(peer.at[3, pl.ds(0, half)], far.at[0], 2, far_send.at[0], far_recv.at[0])
    send(peer.at[3, pl.ds(half, half)], far.at[1], 4, far_send.at[1], far_recv.at[1])
    fetch(1)
    plane.got(peer.at[1], core_recv.at[1])
    add(1, 0, half)
    send_near(1, 0)
    fetch(2)
    plane.got(peer.at[2], core_recv.at[2])
    add(2, half, half)
    send_near(2, 1)
    yield
    plane.got(far.at[0], far_recv.at[0])
    add(2, 0, half, far.at[0])
    send_near(2, 0)
    plane.got(far.at[1], far_recv.at[1])
    add(1, half, half, far.at[1])
    send_near(1, 1)
    fetch(0)
    plane.got(peer.at[0], core_recv.at[0])
    yield
    for slot, part in ((1, 0), (2, 1), (2, 0), (1, 1)):
        at = pl.ds(part * half, half)
        plane.got(near.at[slot - 1, at], near_recv.at[(slot - 1) * 2 + part])
        if (slot, part) == (2, 1):
            yield
    own = own_of(0)

    def step(at):
        finish(
            at,
            plain(own, at)
            + plain(peer.at[0], at)
            + plain(near.at[0], at)
            + plain(near.at[1], at),
        )

    bands(rows, step)
    for copy in sent:
        copy.wait_send()


def back_kernel(
    down_low,
    up_weight,
    hidden_all,
    slope_all,
    grad_mlp_all,
    h_two_all,
    first_grads,
    h_all,
    qkv_all,
    attended_all,
    qkv_weight_in,
    out_weight_in,
    features_in,
    first_sum_in,
    attn_out_in,
    grad_out_in,
    mod,
    shares,
    token_out,
    token_grad,
    mod_out,
    more,
    partial_out,
    land_a,
    land_b,
    first_buf,
    second_buf,
    stage,
    own_pair,
    image_buf,
    grad_all,
    down_buf,
    grad_first,
    saved_grad,
    cols_buf,
    qkv_buf,
    attended_buf,
    staged_buf,
    out_sum,
    sum_buf,
    in_buf,
    half_buf,
    half_in,
    mod_sum,
    mod_land,
    qkv_weight,
    out_weight,
    features,
    first_sum,
    attn_out,
    grad_out,
    core_send,
    core_recv,
    far_send,
    far_recv,
    near_send,
    near_recv,
    stage_sems,
    gather_send,
    gather_recv,
    load_sems,
    weight_sems,
    z_sems,
    x_sems,
    zload_sems,
    token_sems,
    mod_sems,
    mod_gather_sems,
):
    plane = Plane()
    mine, place = plane.mine, plane.place
    rows, width = features.shape
    at = plane.at
    own_grad, image_out = own_pair.at[0], own_pair.at[1]
    is_mid = (place == 1) | (place == 2)
    my_half = pl.ds(pl.multiple_of(jnp.where(place == 2, HALF_ROWS, 0), HALF_ROWS), HALF_ROWS)
    other_half = pl.ds(pl.multiple_of(jnp.where(place == 2, 0, HALF_ROWS), HALF_ROWS), HALF_ROWS)
    partner = (mine, 3 - place)
    outer = (mine, jnp.where(place == 1, 0, 3))
    inner = (mine, jnp.where(place == 0, 1, 2))
    others = [lax.rem(place + step, 4) for step in (1, 2, 3)]
    greet([plane.to(flip) for flip in range(1, 8)] + [(mine, other) for other in others])

    def z_copy(kind, chunk, src, dst, target):
        return remote(src, dst, z_sems.at[0, kind, chunk], z_sems.at[1, kind, chunk], target)

    def own_chunk(chunk):
        return first_grads.at[chunk] if chunk < FIRST else more.at[chunk - FIRST]

    def start_outward(chunk):
        z_copy(0, chunk, own_chunk(chunk), land_a.at[chunk], inner).start()

    def stage_d(k):
        region = shares.at[k, :, other_half]
        plane.got(region, z_sems.at[1, 2, k])
        z_copy(4, k, region, region, outer).start()

    def stage_x(k):
        region = shares.at[k, :, my_half]
        plane.got(region, x_sems.at[1, k])
        z_copy(2, k, region, region, partner).start()
        z_copy(3, k, region, region, outer).start()

    def stage_f(k):
        slot = k % 2
        load = pltpu.make_async_copy(land_b.at[k], half_in, zload_sems.at[2])
        plane.got(land_b.at[k], z_sems.at[1, 1, k])
        load.start()
        if k >= 2 and k - 2 != EARLY:
            plane.gone(half_buf.at[slot, pl.ds(0, 7)], x_sems.at[0, k - 2])
        load.wait()

        @pl.loop(0, 8)
        def _(block):
            half_buf[slot, block] = sum_buf[slot, block, my_half, :] + half_in[block]

        if k == EARLY:
            pltpu.make_async_copy(
                half_buf.at[slot], shares.at[k, :, my_half], x_sems.at[1, k]
            ).start()
            return
        pltpu.make_async_copy(
            half_buf.at[slot, mine], shares.at[k, mine, my_half], x_sems.at[1, k]
        ).start()
        for flip in (6, 7, 2, 4, 3, 5, 1):
            remote(
                half_buf.at[slot, at(flip)],
                shares.at[k, mine, my_half],
                x_sems.at[0, k],
                x_sems.at[1, k],
                plane.to(flip),
            ).start()

    def stage_s(k):
        slot = k % 2
        if k >= 2:
            plane.gone(sum_buf.at[slot, :, other_half], z_sems.at[0, 1, k - 2])
        own_load = pltpu.make_async_copy(own_chunk(k), sum_buf.at[slot], zload_sems.at[0])
        own_load.start()
        in_load = pltpu.make_async_copy(land_a.at[k], in_buf, zload_sems.at[1])
        plane.got(land_a.at[k], z_sems.at[1, 0, k])
        in_load.start()
        own_load.wait()
        in_load.wait()

        @pl.loop(0, 8)
        def _(block):
            sum_buf[slot, block] = sum_buf[slot, block] + in_buf[block]

        z_copy(1, k, sum_buf.at[slot, :, other_half], land_b.at[k], partner).start()

    def send_outward(first, last):
        @pl.when(jnp.logical_not(is_mid))
        def _():
            for chunk in range(first, last):
                start_outward(chunk)

    def tick(now):
        k, odd = now // 2, now % 2
        work = [(stage_f, k - 1), (stage_d, k - 3)] if odd else [(stage_s, k), (stage_x, k - 2)]
        work = {
            16: [(stage_s, EARLY)],
            17: [(stage_x, EARLY - 1)],
            18: [(stage_s, EARLY + 1)],
        }.get(now, work)

        @pl.when(is_mid)
        def _():
            for stage, chunk in work:
                if 0 <= chunk < CHUNKS:
                    stage(chunk)

    def ahead():
        @pl.when(is_mid)
        def _():
            stage_x(EARLY - 2)
            stage_f(EARLY - 1)
            stage_d(EARLY - 3)

    send_outward(0, FIRST)

    attended_load = pltpu.make_async_copy(attended_all, attended_buf, load_sems.at[0])
    attended_load.start()
    fetches = [
        pltpu.make_async_copy(source, result, load_sems.at[13 + number])
        for number, (source, result) in enumerate(
            (
                (first_sum_in, first_sum),
                (grad_out_in, grad_out),
                (attn_out_in, attn_out),
                (out_weight_in, out_weight),
                (qkv_weight_in, qkv_weight),
                (features_in, features),
            )
        )
    ]
    feed = up_weight.shape[-1]

    pltpu.make_async_copy(
        down_low.at[mine], down_buf.at[mine], weight_sems.at[0, 0]
    ).start()
    for flip in (6, 7, 2, 4, 3, 5, 1):
        remote(
            down_low.at[at(flip)],
            down_buf.at[mine],
            weight_sems.at[0, flip],
            weight_sems.at[1, flip],
            plane.to(flip),
        ).start()
    up_load = pltpu.make_async_copy(up_weight, grad_all.at[:, :, pl.ds(0, feed)], load_sems.at[5])
    up_load.start()
    for fetch in fetches:
        fetch.start()
    mod_sum[...] = jnp.zeros_like(mod_sum)
    row = {
        name: number
        for number, name in enumerate(
            ("shift_one", "scale_one", "gate_one", "shift_two", "scale_two", "gate_two", "live")
        )
    }

    def mod_row(name):
        return mod[pl.ds(row[name], 1), :]

    def accumulate(name, value):
        mod_sum[pl.ds(row[name], 1), :] += jnp.sum(value, axis=0, keepdims=True)

    def sems(number):
        return (
            core_recv.at[number],
            far_send.at[number],
            far_recv.at[number],
            near_send.at[number],
            near_recv.at[number],
        )

    def give(src, buf, number, slot):
        remote(
            src, buf.at[slot], core_send.at[number, slot], core_recv.at[number, slot], plane.to(1)
        ).start()

    def staged_flow(source, buf, number, finish):
        for slot in (3, 1, 2, 0):
            give(source.at[at((2 * slot) ^ 1)], buf, number, slot)
        order = {3: 0, 1: 1, 2: 0, 0: 1}

        def load(slot):
            return pltpu.make_async_copy(
                source.at[at(2 * slot)], stage.at[order[slot]], stage_sems.at[number, slot]
            )

        load(3).start()
        load(1).start()

        def fetch(slot):
            if slot == 2:
                load(2).start()
            if slot == 0:
                load(0).start()
            load(slot).wait()

        return scatter_flow(
            plane,
            lambda slot: stage.at[order[slot]],
            fetch,
            buf.at[pl.ds(0, 4)],
            Halves(buf.at[6], rows // 2),
            buf.at[pl.ds(4, 2)],
            sems(number),
            finish,
        )

    def run(flow, first_tick):
        for step, _ in enumerate(flow):
            tick(first_tick + step)

    def finish_out(where, value):
        base = first_sum[where, :]
        own_pair[1, where, :] = (
            mod_row("live") * (base + mod_row("gate_two") * value)
        ).astype(jnp.bfloat16)
        accumulate("gate_two", plain(grad_out, where) * value)

    token_copies = []

    def return_tokens(image, result, number):
        piece = rows // 4
        own = pltpu.make_async_copy(
            image.at[pl.ds(pl.multiple_of(place * piece, piece), piece)],
            result.at[place],
            token_sems.at[0, number, 0],
        )
        own.start()
        token_copies.append(own)
        for step, other in enumerate(others):
            copy = remote(
                image.at[pl.ds(pl.multiple_of(other * piece, piece), piece)],
                result.at[place],
                token_sems.at[0, number, step + 1],
                token_sems.at[1, number, step + 1],
                (mine, other),
            )
            copy.start()
            token_copies.append(copy)


    def back_norm(source, value, scale_name, shift_name):
        inverse = rms_scale(source)
        unit = source * inverse
        inner = value * (1.0 + mod_row(scale_name))
        accumulate(scale_name, value * unit)
        accumulate(shift_name, value)
        return (inner - unit * jnp.mean(inner * unit, axis=-1, keepdims=True)) * inverse

    def finish_feed(where, value):
        total = back_norm(first_sum[where, :], value, "scale_two", "shift_two") + plain(
            grad_out, where
        )
        grad_first[where, :] = total
        accumulate("gate_one", total * plain(attn_out, where))
        low_grad = (mod_row("gate_one") * total).astype(jnp.bfloat16)
        own_pair[0, where, :] = low_grad
        grad_all[mine, where, :] = low_grad

    up_load.wait()
    pltpu.make_async_copy(
        down_low.at[mine], down_buf.at[mine], weight_sems.at[0, 0]
    ).wait()
    for now in range(5):
        tick(now)
    for flip in range(1, 8):
        plane.got(down_buf.at[at(flip)], weight_sems.at[1, flip])
        plane.gone(down_low.at[0], weight_sems.at[0, flip])

    def image_loads(step):
        image, slot = flipped(mine, step), lax.rem(step, 2)
        return [
            pltpu.make_async_copy(
                slope_all.at[image], image_buf.at[slot, :, pl.ds(0, feed)], load_sems.at[6 + slot]
            ),
            pltpu.make_async_copy(grad_mlp_all.at[image], stage.at[slot], load_sems.at[8 + slot]),
        ]

    for load in image_loads(0):
        load.start()

    @pl.loop(0, 8)
    def _(step):
        @pl.when(step == 4)
        def _():
            tick(5)

        slot = lax.rem(step, 2)
        for load in image_loads(step):
            load.wait()

        @pl.when(step < 7)
        def _():
            for load in image_loads(step + 1):
                load.start()

        image_rows = pl.ds(pl.multiple_of(flipped(mine, step) * rows, rows), rows)
        grad_hidden = contract(stage[slot], down_buf[...].reshape(8 * rows, feed), 1, 0)
        saved_grad[image_rows, :] = (
            grad_hidden * image_buf[slot, :, 0:feed].astype(jnp.float32)
        ).astype(jnp.bfloat16)
        up = grad_all[:, :, 0:feed].reshape(8 * rows, feed)
        second_buf[step] = contract(saved_grad[image_rows, :], up, 1, 1).astype(jnp.bfloat16)
        for number in (1, 3, 5, 7):

            @pl.when(step == number)
            def _(number=number):
                give(second_buf.at[number], first_buf, 1, number // 2)


    def hidden_load(step):
        slot = lax.rem(step, 2)
        return pltpu.make_async_copy(
            hidden_all.at[step], image_buf.at[slot, :, pl.ds(0, feed)], load_sems.at[6 + slot]
        )

    def out_store(step):
        slot = lax.rem(step, 2)
        return pltpu.make_async_copy(own_pair.at[slot], partial_out.at[step], load_sems.at[8 + slot])

    def out_products():
        hidden_load(0).start()

        @pl.loop(0, 8)
        def _(step):
            slot = lax.rem(step, 2)
            hidden_load(step).wait()

            @pl.when(step < 7)
            def _():
                hidden_load(step + 1).start()

            @pl.when(step >= 2)
            def _():
                out_store(step - 2).wait()

            own_pair[slot] = contract(
                image_buf[slot, :, 0:feed], down_buf[...].reshape(8 * rows, feed), 1, 1
            ).astype(jnp.bfloat16)
            out_store(step).start()

        out_store(6).wait()
        out_store(7).wait()

    def up_hook(block):
        @pl.when(block == 6)
        def _():
            tick(7)

    def up_products():
        column_products(
            h_two_all,
            saved_grad,
            cols_buf,
            staged_buf,
            more.at[pl.ds(0, 4)],
            load_sems.at[pl.ds(3, 2)],
            load_sems.at[pl.ds(11, 2)],
            hook=up_hook,
        )

    def own_flow(number, finish):
        return scatter_flow(
            plane,
            lambda slot: second_buf.at[2 * slot],
            lambda slot: None,
            first_buf.at[pl.ds(0, 4)],
            Halves(first_buf.at[6], rows // 2),
            first_buf.at[pl.ds(4, 2)],
            sems(number),
            finish,
        )

    tick(6)
    up_products()
    send_outward(FIRST, EARLY)
    for fetch in fetches:
        fetch.wait()
    for step, _ in enumerate(own_flow(1, finish_feed)):
        tick((8, 10, 11)[step])
        if step == 0:
            tick(9)
    for slot in range(4):
        plane.gone(second_buf.at[slot], core_send.at[1, slot])

    gather = Gather(plane, own_grad, grad_all, gather_send, gather_recv)
    gather.start()

    def qkv_load(step):
        return pltpu.make_async_copy(
            qkv_all.at[flipped(mine, step)], qkv_buf.at[lax.rem(step, 2)], load_sems.at[1 + lax.rem(step, 2)]
        )

    qkv_load(0).start()
    attended_load.wait()
    out_sum[...] = jnp.zeros_like(out_sum)
    columns = qkv_buf.shape[-1]
    third = columns // 3
    scale = HD ** (-0.5)

    @pl.loop(0, 8)
    def _(step):
        for number in range(8):

            @pl.when(step == number)
            def _(number=number):
                if number in (1, 2, 4):
                    tick({1: 12, 2: 13, 4: 15}[number])
                if number == 2:
                    tick(14)
                gather.step(number)
                if number == 7:
                    gather.finish()

        image = flipped(mine, step)
        slot = lax.rem(step, 2)
        qkv_load(step).wait()

        @pl.when(step < 7)
        def _():
            qkv_load(step + 1).start()

        grad = grad_all[image]
        grad_attended = contract(grad, out_weight[...], 1, 1).astype(jnp.bfloat16)
        image_rows = pl.ds(pl.multiple_of(image * rows, rows), rows)
        for head in range(third // HD):
            begin, first = head * HD, 3 * head * HD
            queries = qkv_buf[slot, :, first : first + HD]
            key_rows = qkv_buf[slot, :, first + HD : first + 2 * HD]
            value_rows = qkv_buf[slot, :, first + 2 * HD : first + 3 * HD]
            grad_head = grad_attended[:, begin : begin + HD]
            attention = softmax_rows(queries, key_rows)
            grad_weights = contract(grad_head, value_rows, 1, 1)
            row_delta = jnp.sum(attention * grad_weights, axis=-1, keepdims=True)
            grad_scores = (attention * (grad_weights - row_delta)).astype(jnp.bfloat16)
            saved_grad[image_rows, first : first + HD] = (
                contract(grad_scores, key_rows, 1, 0) * scale
            ).astype(jnp.bfloat16)
            saved_grad[image_rows, first + HD : first + 2 * HD] = (
                contract(grad_scores, queries, 0, 0) * scale
            ).astype(jnp.bfloat16)
            saved_grad[image_rows, first + 2 * HD : first + 3 * HD] = contract(
                attention.astype(jnp.bfloat16), grad_head, 0, 0
            ).astype(jnp.bfloat16)
        out_sum[...] += contract(attended_buf[image], grad, 0, 0)
        second_buf[step] = contract(saved_grad[image_rows, 0:columns], qkv_weight[...], 1, 1).astype(
            jnp.bfloat16
        )
        for number in (1, 3, 5, 7):

            @pl.when(step == number)
            def _(number=number):
                give(second_buf.at[number], first_buf, 2, number // 2)

    ahead()

    for block in range(8):
        in_buf[block] = out_sum[:, block * rows : (block + 1) * rows].astype(jnp.bfloat16)
    out_copy = pltpu.make_async_copy(in_buf, more.at[4], load_sems.at[0])
    out_copy.start()
    out_copy.wait()
    send_outward(EARLY, EARLY + 1)
    tick(16)
    def late_hook(block):
        @pl.when(block == 3)
        def _():
            tick(17)

    column_products(
        h_all,
        saved_grad.at[:, pl.ds(0, columns)],
        cols_buf,
        staged_buf,
        more.at[pl.ds(5, 3)],
        load_sems.at[pl.ds(3, 2)],
        load_sems.at[pl.ds(11, 2)],
        [[(3 * head + number) * HD for head in range(third // HD)] for number in range(3)],
        late_hook,
    )

    def finish_input(where, value):
        total = back_norm(plain(features, where), value, "scale_one", "shift_one")
        own_pair[0, where, :] = (total + grad_first[where, :]).astype(jnp.bfloat16)

    send_outward(EARLY + 1, CHUNKS)
    for step, _ in enumerate(own_flow(2, finish_input)):
        for now in ((18, 19), (20,), (21,))[step]:
            tick(now)
        if step == 0:
            out_products()
    return_tokens(own_grad, token_grad, 1)
    for step, _ in enumerate(staged_flow(partial_out, grad_all, 0, finish_out)):
        for now in ((22, 23), (24,), (25,))[step]:
            tick(now)
    return_tokens(image_out, token_out, 0)

    mod_copies = []
    mod_sum[7:8, :] = mod[7:8, :]
    mod_rows = pl.ds(pl.multiple_of(place * 8, 8), 8)
    mod_land[mod_rows, :] = mod_sum[...]
    for step, other in enumerate(others):
        copy = remote(
            mod_sum, mod_land.at[mod_rows], mod_sems.at[0, step], mod_sems.at[1, step], (mine, other)
        )
        copy.start()
        mod_copies.append(copy)
    tick(26)
    for copy in mod_copies:
        copy.wait_recv()
    own = pltpu.make_async_copy(mod_land, mod_out.at[mine], mod_sems.at[0, 3])
    own.start()
    mod_gather = Gather(plane, mod_land, mod_out, mod_gather_sems.at[0], mod_gather_sems.at[1])
    mod_gather.start()
    tick(27)
    mod_gather.middle()
    mod_gather.far()
    for flip in (1, 3, 5, 7):
        mod_gather.crossed(flip)
    mod_gather.finish()
    for now in range(28, 2 * CHUNKS + 6):
        tick(now)
    own.wait()
    for copy in mod_copies:
        copy.wait_send()
    for copy in token_copies:
        copy.wait()
    for number in (0, 2):
        for slot in range(4):
            plane.gone(second_buf.at[slot], core_send.at[number, slot])

    @pl.when(is_mid)
    def _():
        for k in (CHUNKS - 2, CHUNKS - 1):
            plane.gone(sum_buf.at[k % 2, :, other_half], z_sems.at[0, 1, k])
        for k in (CHUNKS - 2, CHUNKS - 1):
            plane.gone(half_buf.at[k % 2, pl.ds(0, 7)], x_sems.at[0, k])
        for k in range(CHUNKS):
            plane.gone(shares.at[k, :, my_half], z_sems.at[0, 2, k])
            plane.gone(shares.at[k, :, my_half], z_sems.at[0, 3, k])
            plane.gone(shares.at[k, :, other_half], z_sems.at[0, 4, k])

    @pl.when(jnp.logical_not(is_mid))
    def _():
        first = pl.ds(pl.multiple_of(jnp.where(place == 0, 0, HALF_ROWS), HALF_ROWS), HALF_ROWS)
        second = pl.ds(pl.multiple_of(jnp.where(place == 0, HALF_ROWS, 0), HALF_ROWS), HALF_ROWS)
        for k in range(CHUNKS):
            plane.gone(land_a.at[k], z_sems.at[0, 0, k])
            plane.got(shares.at[k, :, first], z_sems.at[1, 3, k])
            plane.got(shares.at[k, :, second], z_sems.at[1, 4, k])


def back_part(*operands):
    h_all, qkv_weight = operands[7], operands[10]
    _, rows, width = h_all.shape
    columns = qkv_weight.shape[1]
    feed = operands[1].shape[-1]
    low, full = jnp.bfloat16, jnp.float32
    dma = pltpu.SemaphoreType.DMA
    anywhere, inside = pl.BlockSpec(memory_space=pl.ANY), pl.BlockSpec(memory_space=pltpu.VMEM)
    return pl.pallas_call(
        back_kernel,
        out_shape=[
            jax.ShapeDtypeStruct((CHUNKS, 8, rows, rows), low),
            jax.ShapeDtypeStruct((4, rows // 4, width), low),
            jax.ShapeDtypeStruct((4, rows // 4, width), low),
            jax.ShapeDtypeStruct((8, 32, width), full),
            jax.ShapeDtypeStruct((CHUNKS - FIRST, 8, rows, rows), low),
            jax.ShapeDtypeStruct((8, rows, width), low),
            jax.ShapeDtypeStruct((CHUNKS, 8, rows, rows), low),
            jax.ShapeDtypeStruct((CHUNKS, 8, HALF_ROWS, rows), low),
        ],
        in_specs=[anywhere] * 16 + [inside],
        out_specs=[anywhere] * 8,
        scratch_shapes=[
            pltpu.VMEM((7, rows, width), low),
            pltpu.VMEM((8, rows, width), low),
            pltpu.VMEM((2, rows, width), low),
            pltpu.VMEM((2, rows, width), low),
            pltpu.VMEM((2, rows, feed), low),
            pltpu.VMEM((8, rows, width), low),
            pltpu.VMEM((8, rows, feed), low),
            pltpu.VMEM((rows, width), full),
            pltpu.VMEM((8 * rows, feed), low),
            pltpu.VMEM((2, 8, rows, rows), low),
            pltpu.VMEM((2, rows, columns), low),
            pltpu.VMEM((8, rows, columns // 3), low),
            pltpu.VMEM((2, 4, rows, rows), low),
            pltpu.VMEM((columns // 3, width), full),
            pltpu.VMEM((2, 8, rows, rows), low),
            pltpu.VMEM((8, rows, rows), low),
            pltpu.VMEM((2, 8, HALF_ROWS, rows), low),
            pltpu.VMEM((8, HALF_ROWS, rows), low),
            pltpu.VMEM((8, width), full),
            pltpu.VMEM((32, width), full),
            pltpu.VMEM((8 * rows, columns), low),
            pltpu.VMEM((rows, width), low),
            pltpu.VMEM((rows, width), low),
            pltpu.VMEM((rows, width), full),
            pltpu.VMEM((rows, width), low),
            pltpu.VMEM((rows, width), low),
            dma((3, 4)),
            dma((3, 4)),
            dma((3, 2)),
            dma((3, 2)),
            dma((3, 4)),
            dma((3, 4)),
            dma((2, 4)),
            dma((7 * PIECES,)),
            dma((7 * PIECES,)),
            dma((19,)),
            dma((2, 8)),
            dma((2, 5, CHUNKS)),
            dma((2, CHUNKS)),
            dma((3,)),
            dma((2, 2, 4)),
            dma((2, 4)),
            dma((2, 7 * PIECES)),
        ],
        compiler_params=pltpu.CompilerParams(
            collective_id=4, has_side_effects=True, vmem_limit_bytes=63 * 1024 * 1024
        ),
        name="back_part",
    )(*operands)


class Gather:
    def __init__(self, plane, own, result, send_sems, recv_sems):
        self.plane, self.own, self.result = plane, own, result
        self.send_sems, self.recv_sems = send_sems, recv_sems
        self.piece = own.shape[0] // PIECES

    def put(self, src, owner, part, flip, slot):
        remote(
            src,
            self.result.at[owner, pl.ds(part * self.piece, self.piece)],
            self.send_sems.at[slot],
            self.recv_sems.at[slot],
            self.plane.to(flip),
        ).start()

    def arrived(self, flip, part, slot):
        ref = self.result.at[self.plane.at(flip), pl.ds(part * self.piece, self.piece)]
        self.plane.got(ref, self.recv_sems.at[slot])
        return ref

    def start(self):
        mine = self.plane.mine
        for part in range(PIECES):
            src = self.own.at[pl.ds(part * self.piece, self.piece)]
            self.put(src, mine, part, 2, part)
            self.put(src, mine, part, 4, PIECES + part)
            self.put(src, mine, part, 1, 3 * PIECES + part)

    def middle(self):
        at = self.plane.at
        for part in range(PIECES):
            got = self.arrived(2, part, part)
            if part < PIECES // 2:
                self.put(got, at(2), part, 4, 2 * PIECES + part)
            self.put(got, at(2), part, 1, 4 * PIECES + part)
            got = self.arrived(4, part, PIECES + part)
            if part >= PIECES // 2:
                self.put(got, at(4), part, 2, 2 * PIECES + part)
            self.put(got, at(4), part, 1, 5 * PIECES + part)

    def far(self):
        for part in range(PIECES):
            got = self.arrived(6, part, 2 * PIECES + part)
            self.put(got, self.plane.at(6), part, 1, 6 * PIECES + part)

    def crossed(self, flip):
        for part in range(PIECES):
            self.arrived(flip, part, (3 + flip // 2) * PIECES + part)

    def step(self, number):
        if number == 2:
            self.middle()
        if number == 6:
            self.far()
        if number % 2:
            self.crossed(number)

    def finish(self):
        for slot in range(7 * PIECES):
            self.plane.gone(self.own.at[pl.ds(0, self.piece)], self.send_sems.at[slot])


class Halves:
    def __init__(self, ref, half):
        self.ref, self.half = ref, half

    @property
    def at(self):
        return self

    def __getitem__(self, number):
        return self.ref.at[pl.ds(number * self.half, self.half)]


def front_kernel(
    bin_ids,
    image_counts,
    noise,
    mod_bias,
    block_input,
    cotangent,
    attn_weight,
    mlp_weight,
    mod_weight,
    qkv_weight,
    out_weight_out,
    up_weight,
    down_low,
    h_one_all,
    h_two_all,
    grad_mlp_all,
    qkv_all,
    attended_all,
    hidden_all,
    slope_all,
    first_grads,
    features_out,
    first_sum_out,
    attn_out_out,
    grad_out_out,
    mod_out,
    load_buf,
    qkv_stage,
    up_stage,
    weight_buf,
    hidden_buf,
    cols_buf,
    staged_buf,
    h_all,
    qkv_buf,
    attended_buf,
    part_buf,
    scatter_buf,
    own_h,
    own_grad,
    own_next,
    bin_row,
    bin_land,
    mod_part,
    mod_land,
    out_weight,
    features,
    first_sum,
    attn_out,
    grad_out,
    mod,
    load_sems,
    token_sems,
    bin_sems,
    mod_sems,
    weight_sems,
    beside_sems,
    gather_sems,
    core_send,
    core_recv,
    far_send,
    far_recv,
    near_send,
    near_recv,
    copy_sems,
):
    plane = Plane()
    mine, place, at = plane.mine, plane.place, plane.at
    rows, width = own_h.shape
    feed = up_stage.shape[-1]
    columns = qkv_stage.shape[-1]
    third = columns // 3
    piece = rows // 4
    others = [lax.rem(place + step, 4) for step in (1, 2, 3)]
    flips = (6, 7, 2, 4, 3, 5, 1, 0)
    greet([plane.to(flip) for flip in range(1, 8)] + [(mine, other) for other in others])

    results = [
        pltpu.make_async_copy(source, result, copy_sems.at[14 + number])
        for number, (source, result) in enumerate(
            (
                (mod, mod_out),
                (features, features_out),
                (grad_out, grad_out_out),
                (out_weight, out_weight_out),
                (first_sum, first_sum_out),
                (attn_out, attn_out_out),
            )
        )
    ]

    token_copies = []
    my_rows = pl.ds(pl.multiple_of(place * piece, piece), piece)
    for number, (source, result) in enumerate(((block_input, features), (cotangent, grad_out))):
        copies = [
            pltpu.make_async_copy(
                source.at[place], result.at[my_rows], token_sems.at[0, number, 0]
            )
        ]
        for step, other in enumerate(others):
            copies.append(
                remote(
                    source.at[other],
                    result.at[my_rows],
                    token_sems.at[0, number, step + 1],
                    token_sems.at[1, number, step + 1],
                    (mine, other),
                )
            )
        for copy in copies:
            copy.start()
        token_copies.append(copies)

    lanes = lax.broadcasted_iota(jnp.int32, bin_row.shape, 1)
    bin_row[...] = jnp.where(lanes == bin_ids[place], 1.0, 0.0).astype(jnp.float32)
    bin_land[mine] = bin_row[...]
    bin_copies = [
        remote(
            bin_row, bin_land.at[mine], bin_sems.at[0, flip], bin_sems.at[1, flip], plane.to(flip)
        )
        for flip in range(1, 8)
    ]
    for copy in bin_copies:
        copy.start()

    parity = lax.rem(place, 2)
    beside = (mine, place + 1 - 2 * parity)

    def half_of(size):
        return pl.ds(pl.multiple_of(parity * size, size), size)

    def load_columns(source, slot, begins, size):
        return [
            pltpu.make_async_copy(
                source.at[:, pl.ds(pl.multiple_of(begin, HD), size)],
                load_buf.at[slot, :, pl.ds(number * size, size)],
                load_sems.at[slot, number],
            )
            for number, begin in enumerate(begins)
        ]

    def cast_and_send(source, begins_of, size, stage, result, kind):
        loads = [
            load_columns(source, step % 2, begins_of(at(flip)), size)
            for step, flip in enumerate(flips)
        ]
        total = size * len(loads[0])
        half = half_of(total)
        for load in loads[0]:
            load.start()
        for step, flip in enumerate(flips):
            if step + 1 < len(flips):
                for load in loads[step + 1]:
                    load.start()
            for load in loads[step]:
                load.wait()

            def cast(band, step=step):
                stage[step, band, 0:total] = load_buf[step % 2, band, 0:total].astype(jnp.bfloat16)

            bands(rows, cast)
            src = stage.at[step, :, pl.ds(0, total)]
            if flip:
                remote(
                    src,
                    result.at[mine, :, half],
                    weight_sems.at[0, kind, flip],
                    weight_sems.at[1, kind, flip],
                    plane.to(flip),
                ).start()
            else:
                pltpu.make_async_copy(
                    src, result.at[mine, :, half], weight_sems.at[0, kind, 0]
                ).start()

    def pass_on(stage, result, kind, total):
        half = half_of(total)
        pltpu.make_async_copy(
            stage.at[7, :, pl.ds(0, total)], result.at[mine, :, half], weight_sems.at[0, kind, 0]
        ).wait()
        for flip in (1, 2, 3, 4, 5, 6, 7, 0):
            piece = result.at[at(flip), :, half]
            if flip:
                plane.got(piece, weight_sems.at[1, kind, flip])
            remote(
                piece,
                piece,
                beside_sems.at[0, kind, flip],
                beside_sems.at[1, kind, flip],
                beside,
            ).start()

    def weights_ready(stage, result, kind, total):
        for flip in range(8):
            piece = result.at[at(flip), :, half_of(total)]
            plane.got(piece, beside_sems.at[1, kind, flip])
            plane.gone(piece, beside_sems.at[0, kind, flip])
            if flip:
                plane.gone(stage.at[0, :, pl.ds(0, total)], weight_sems.at[0, kind, flip])

    cast_and_send(
        attn_weight,
        lambda owner: [number * width + owner * third + parity * HD for number in range(3)],
        HD,
        qkv_stage,
        qkv_weight,
        0,
    )

    cast_and_send(
        mlp_weight,
        lambda owner: [owner * feed + parity * (feed // 2)],
        feed // 2,
        up_stage,
        up_weight,
        1,
    )

    for copy in bin_copies:
        copy.wait_recv()
    bins = noise.shape[0]
    activated = noise[...] / (1.0 + jnp.exp(-noise[...]))
    chosen = jnp.dot(
        bin_land[:, 0, :bins], activated, precision=PRECISE, preferred_element_type=jnp.float32
    )

    def load_mod(number):
        return pltpu.make_async_copy(
            mod_weight.at[:, pl.ds(number * width, width)],
            load_buf.at[number % 2],
            load_sems.at[number % 2, 0],
        )

    load_mod(0).start()
    mod_part[...] = jnp.zeros_like(mod_part)
    for number in range(6):
        if number < 5:
            load_mod(number + 1).start()
        load_mod(number).wait()
        mod_part[:, number, :] = jnp.dot(
            chosen, load_buf[number % 2], precision=PRECISE, preferred_element_type=jnp.float32
        )
    quarter = width // 4
    for number in range(3):
        index = 3 * mine + number
        where = pl.ds(pl.multiple_of(lax.rem(index, 4) * quarter, quarter), quarter)
        for image in range(8):
            mod_part[image, pl.ds(index // 4, 1), where] += mod_bias[
                :, number * quarter : (number + 1) * quarter
            ]
    mod_copies = [
        remote(
            mod_part.at[at(flip)],
            mod_land.at[mine],
            mod_sems.at[0, flip],
            mod_sems.at[1, flip],
            plane.to(flip),
        )
        for flip in range(1, 8)
    ]
    for copy in mod_copies:
        copy.start()
    pass_on(qkv_stage, qkv_weight, 0, 3 * HD)
    mod_land[mine] = mod_part[mine]
    for copy in mod_copies:
        copy.wait_recv()
    total = mod_land[0]
    for number in range(1, 8):
        total = total + mod_land[number]
    mod[...] = total
    live = jnp.where(place < image_counts[0], 1.0, 0.0).astype(jnp.float32)
    mod[6:7, :] = jnp.full((1, width), 1.0, jnp.float32) * live
    mod[7:8, :] = jnp.zeros((1, width), jnp.float32)
    mod[7:8, :128] = bin_row[0:1, :]
    results[0].start()

    def mod_row(number):
        return mod[number : number + 1, :]

    def tokens_arrived(number):
        for copy in token_copies[number]:
            if copy is token_copies[number][0]:
                copy.wait()
            else:
                copy.wait_recv()

    tokens_arrived(0)
    results[1].start()

    def first_norm(band):
        source = plain(features, band)
        normed = (source * rms_scale(source) * (1.0 + mod_row(1)) + mod_row(0)).astype(jnp.bfloat16)
        own_h[band, :] = normed
        h_all[mine, band, :] = normed

    bands(rows, first_norm)
    h_gather = Gather(plane, own_h, h_all, gather_sems.at[0, 0], gather_sems.at[0, 1])
    h_gather.start()

    tokens_arrived(1)

    def feed_grad(band):
        scaled = plain(grad_out, band) * mod_row(6)
        grad_out[band, :] = scaled.astype(jnp.bfloat16)
        own_grad[band, :] = (mod_row(5) * scaled).astype(jnp.bfloat16)

    bands(rows, feed_grad)
    results[2].start()
    grad_own = pltpu.make_async_copy(own_grad, grad_mlp_all.at[mine], copy_sems.at[0])
    grad_own.start()
    grad_gather = Gather(plane, own_grad, grad_mlp_all, gather_sems.at[1, 0], gather_sems.at[1, 1])
    grad_gather.start()
    def down_load(owner):
        return pltpu.make_async_copy(
            mlp_weight.at[:, pl.ds((8 + owner) * feed, feed)],
            load_buf.at[owner % 2, :, pl.ds(0, feed)],
            load_sems.at[owner % 2, 0],
        )

    def down_store(owner):
        return pltpu.make_async_copy(
            part_buf.at[owner, :, pl.ds(0, feed)], down_low.at[owner], copy_sems.at[6 + owner]
        )

    down_load(0).start()
    for owner in range(8):
        if owner < 7:
            down_load(owner + 1).start()
        down_load(owner).wait()

        def cast_down(band, owner=owner):
            part_buf[owner, band, 0:feed] = load_buf[owner % 2, band, 0:feed].astype(jnp.bfloat16)

        bands(rows, cast_down)
        down_store(owner).start()
    for owner in range(8):
        down_store(owner).wait()
    load = pltpu.make_async_copy(
        attn_weight.at[:, pl.ds(3 * width, width)], load_buf.at[0], load_sems.at[0, 0]
    )
    load.start()
    load.wait()

    def cast_out(band):
        out_weight[band, :] = load_buf[0, band, :].astype(jnp.bfloat16)

    bands(rows, cast_out)
    results[3].start()

    weights_ready(qkv_stage, qkv_weight, 0, 3 * HD)
    load = pltpu.make_async_copy(qkv_weight, weight_buf, copy_sems.at[1])
    load.start()
    load.wait()

    @pl.loop(0, 8)
    def _(step):
        for number in range(8):

            @pl.when(step == number)
            def _(number=number):
                h_gather.step(number)

        image = flipped(mine, step)
        pltpu.make_async_copy(h_all.at[image], h_one_all.at[image], copy_sems.at[2]).start()
        projected = contract(
            h_all[image], weight_buf[...].reshape(8 * rows, columns), 1, 0
        ).astype(jnp.bfloat16)
        qkv_buf[image] = projected
        for head in range(third // HD):
            begin, first = head * HD, 3 * head * HD
            queries = projected[:, first : first + HD]
            key_rows = projected[:, first + HD : first + 2 * HD]
            value_rows = projected[:, first + 2 * HD : first + 3 * HD]
            attention = softmax_rows(queries, key_rows).astype(jnp.bfloat16)
            attended_buf[image, :, begin : begin + HD] = contract(
                attention, value_rows, 1, 0
            ).astype(jnp.bfloat16)
        part_buf[step] = contract(attended_buf[image], out_weight[...], 1, 0).astype(jnp.bfloat16)
        pltpu.make_async_copy(h_all.at[image], h_one_all.at[image], copy_sems.at[2]).wait()

        @pl.when(step == 7)
        def _():
            h_gather.finish()

        for number in (1, 3, 5, 7):

            @pl.when(step == number)
            def _(number=number):
                slot = number // 2
                remote(
                    part_buf.at[number],
                    scatter_buf.at[slot],
                    core_send.at[slot],
                    core_recv.at[slot],
                    plane.to(1),
                ).start()

    pass_on(up_stage, up_weight, 1, feed // 2)
    keeps = [
        pltpu.make_async_copy(qkv_buf, qkv_all, copy_sems.at[3]),
        pltpu.make_async_copy(attended_buf, attended_all, copy_sems.at[4]),
    ]
    for copy in keeps:
        copy.start()

    def second_norm(band, value):
        attn_out[band, :] = value.astype(jnp.bfloat16)
        source = plain(features, band) + mod_row(2) * value
        first_sum[band, :] = source
        normed = (source * rms_scale(source) * (1.0 + mod_row(4)) + mod_row(3)).astype(jnp.bfloat16)
        own_next[band, :] = normed
        h_all[mine, band, :] = normed

    flow = scatter_flow(
        plane,
        lambda slot: part_buf.at[2 * slot],
        lambda slot: None,
        scatter_buf.at[pl.ds(0, 4)],
        Halves(scatter_buf.at[6], rows // 2),
        scatter_buf.at[pl.ds(4, 2)],
        (core_recv, far_send, far_recv, near_send, near_recv),
        second_norm,
    )
    for number, _ in enumerate(flow):
        if number == 1:
            grad_gather.middle()
    for slot in range(4):
        plane.gone(part_buf.at[slot], core_send.at[slot])
    next_gather = Gather(plane, own_next, h_all, gather_sems.at[2, 0], gather_sems.at[2, 1])
    next_gather.start()
    results[4].start()
    results[5].start()
    grad_gather.far()
    weights_ready(up_stage, up_weight, 1, feed // 2)
    load = pltpu.make_async_copy(up_weight, up_stage, copy_sems.at[1])
    load.start()
    load.wait()

    @pl.loop(0, 8)
    def _(step):
        for number in range(8):

            @pl.when(step == number)
            def _(number=number):
                next_gather.step(number)

        image = flipped(mine, step)
        pre = contract(h_all[image], up_stage[...].reshape(8 * rows, feed), 1, 0)
        hidden, slope = gelu_and_slope(pre)
        hidden_buf[pl.ds(pl.multiple_of(image * rows, rows), rows), :] = hidden.astype(jnp.bfloat16)
        part_buf[image, :, 0:feed] = slope.astype(jnp.bfloat16)

    keeps.append(pltpu.make_async_copy(h_all, h_two_all, copy_sems.at[2]))
    keeps.append(pltpu.make_async_copy(hidden_buf, hidden_all, copy_sems.at[5]))
    keeps.append(
        pltpu.make_async_copy(part_buf.at[:, :, pl.ds(0, feed)], slope_all, copy_sems.at[1])
    )
    for copy in keeps[-3:]:
        copy.start()
    for flip in (1, 3, 5, 7):
        grad_gather.crossed(flip)
    grad_own.wait()
    column_products(
        grad_mlp_all,
        hidden_buf,
        cols_buf,
        staged_buf,
        first_grads,
        copy_sems.at[pl.ds(6, 2)],
        copy_sems.at[pl.ds(8, 2)],
    )
    for gather in (grad_gather, next_gather):
        gather.finish()
    for copy in keeps + results:
        copy.wait()
    for copies in token_copies:
        for copy in copies[1:]:
            copy.wait_send()
    for copy in bin_copies + mod_copies:
        copy.wait_send()


def front_part(
    bin_ids,
    image_counts,
    noise,
    mod_bias,
    block_input,
    cotangent,
    attn_weight,
    mlp_weight,
    mod_weight,
):
    slots, local_tok, width = block_input.shape
    rows = slots * local_tok
    columns, feed = 3 * width // 8, mlp_weight.shape[1] // 16
    low, full = jnp.bfloat16, jnp.float32
    dma = pltpu.SemaphoreType.DMA
    anywhere, inside = pl.BlockSpec(memory_space=pl.ANY), pl.BlockSpec(memory_space=pltpu.VMEM)
    scalars = pl.BlockSpec(memory_space=pltpu.SMEM)
    return pl.pallas_call(
        front_kernel,
        out_shape=[
            jax.ShapeDtypeStruct((8, rows, columns), low),
            jax.ShapeDtypeStruct((rows, width), low),
            jax.ShapeDtypeStruct((8, rows, feed), low),
            jax.ShapeDtypeStruct((8, rows, feed), low),
            jax.ShapeDtypeStruct((8, rows, width), low),
            jax.ShapeDtypeStruct((8, rows, width), low),
            jax.ShapeDtypeStruct((8, rows, width), low),
            jax.ShapeDtypeStruct((8, rows, columns), low),
            jax.ShapeDtypeStruct((8, rows, columns // 3), low),
            jax.ShapeDtypeStruct((8 * rows, feed), low),
            jax.ShapeDtypeStruct((8, rows, feed), low),
            jax.ShapeDtypeStruct((FIRST, 8, rows, rows), low),
            jax.ShapeDtypeStruct((rows, width), low),
            jax.ShapeDtypeStruct((rows, width), full),
            jax.ShapeDtypeStruct((rows, width), low),
            jax.ShapeDtypeStruct((rows, width), low),
            jax.ShapeDtypeStruct((8, width), full),
        ],
        in_specs=[scalars] * 2 + [inside] * 2 + [anywhere] * 5,
        out_specs=[anywhere] * 17,
        scratch_shapes=[
            pltpu.VMEM((2, rows, width), full),
            pltpu.VMEM((8, rows, columns), low),
            pltpu.VMEM((8, rows, feed), low),
            pltpu.VMEM((8, rows, columns), low),
            pltpu.VMEM((8 * rows, feed), low),
            pltpu.VMEM((2, 8, rows, rows), low),
            pltpu.VMEM((2, 4, rows, rows), low),
            pltpu.VMEM((8, rows, width), low),
            pltpu.VMEM((8, rows, columns), low),
            pltpu.VMEM((8, rows, columns // 3), low),
            pltpu.VMEM((8, rows, width), low),
            pltpu.VMEM((7, rows, width), low),
            pltpu.VMEM((rows, width), low),
            pltpu.VMEM((rows, width), low),
            pltpu.VMEM((rows, width), low),
            pltpu.VMEM((8, 128), full),
            pltpu.VMEM((8, 8, 128), full),
            pltpu.VMEM((8, 8, width), full),
            pltpu.VMEM((8, 8, width), full),
            pltpu.VMEM((rows, width), low),
            pltpu.VMEM((rows, width), low),
            pltpu.VMEM((rows, width), full),
            pltpu.VMEM((rows, width), low),
            pltpu.VMEM((rows, width), low),
            pltpu.VMEM((8, width), full),
            dma((2, 3)),
            dma((2, 2, 4)),
            dma((2, 8)),
            dma((2, 8)),
            dma((2, 2, 8)),
            dma((2, 2, 8)),
            dma((3, 2, 7 * PIECES)),
            dma((4,)),
            dma((4,)),
            dma((2,)),
            dma((2,)),
            dma((4,)),
            dma((4,)),
            dma((20,)),
        ],
        compiler_params=pltpu.CompilerParams(
            collective_id=5, has_side_effects=True, vmem_limit_bytes=63 * 1024 * 1024
        ),
        name="front_part",
    )(
        bin_ids,
        image_counts,
        noise,
        mod_bias,
        block_input,
        cotangent,
        attn_weight,
        mlp_weight,
        mod_weight,
    )


def tail_kernel(
    mlp_ref,
    attn_ref,
    rows_ref,
    noise_ref,
    weight_ref,
    out_ref,
    grad_ref,
    mlp_grad_ref,
    attn_grad_ref,
    weight_grad_ref,
    noise_grad_ref,
    bias_ref,
    block_out_ref,
    input_grad_ref,
    chosen,
    total,
    flat_rows,
    onehot_rows,
):
    step = pl.program_id(0)
    size = mlp_ref.shape[-1]
    for number in range(8):
        mlp_grad_ref[:, number * size : (number + 1) * size] = mlp_ref[
            number % 4, number // 4
        ].astype(jnp.float32)
    for number in range(4):
        attn_grad_ref[:, number * size : (number + 1) * size] = attn_ref[0, number].astype(
            jnp.float32
        )
    block_out_ref[...] = out_ref[...]
    input_grad_ref[...] = grad_ref[...].astype(jnp.float32)
    noise = noise_ref[...]
    rise = 1.0 / (1.0 + jnp.exp(-noise))
    part = weight_ref.shape[1]

    @pl.when(step == 0)
    def _():
        width = rows_ref.shape[2]
        for row in range(6):
            flat_rows[:, row * width : (row + 1) * width] = rows_ref[:, row, :]
        onehot = rows_ref[:, 7, : noise.shape[0]]
        onehot_rows[...] = onehot
        chosen[...] = jnp.dot(
            onehot, noise * rise, precision=PRECISE, preferred_element_type=jnp.float32
        )
        total[...] = jnp.zeros_like(total)

    grads = flat_rows[:, pl.ds(pl.multiple_of(step * part, 128), part)]
    bias_ref[...] = jnp.broadcast_to(jnp.sum(grads, axis=0, keepdims=True), bias_ref.shape)
    low = grads.astype(jnp.bfloat16)
    weight_grad_ref[...] = contract(chosen[...].astype(jnp.bfloat16), low, 0, 0)
    total[...] += contract(weight_ref[...].astype(jnp.bfloat16), low, 1, 1)

    @pl.when(step == pl.num_programs(0) - 1)
    def _():
        table = lax.dot_general(
            onehot_rows[...],
            total[...],
            (((0,), (1,)), ((), ())),
            precision=PRECISE,
            preferred_element_type=jnp.float32,
        )
        noise_grad_ref[...] = table * (rise + noise * rise * (1.0 - rise))


def tail_part(shares, image_rows, noise, weight, token_out, token_grad):
    steps = 8
    rows = shares.shape[2]
    images = image_rows.shape[0]
    depth, columns = weight.shape
    part = columns // steps
    slots, local_tok, width = token_out.shape
    token_spec = pl.BlockSpec((1, local_tok, width // 2), lambda step: (step // 2, 0, step % 2))
    return pl.pallas_call(
        tail_kernel,
        grid=(steps,),
        out_shape=[
            jax.ShapeDtypeStruct((rows, 64 * rows), jnp.float32),
            jax.ShapeDtypeStruct((rows, 32 * rows), jnp.float32),
            jax.ShapeDtypeStruct(weight.shape, jnp.float32),
            jax.ShapeDtypeStruct(noise.shape, jnp.float32),
            jax.ShapeDtypeStruct((8, columns), jnp.float32),
            jax.ShapeDtypeStruct(token_out.shape, jnp.bfloat16),
            jax.ShapeDtypeStruct(token_grad.shape, jnp.float32),
        ],
        in_specs=[
            pl.BlockSpec((4, 2, rows, rows), lambda step: (1 - step // 4, step % 4, 0, 0)),
            pl.BlockSpec((1, 4, rows, rows), lambda step: (EARLY + (step // 2 + 1) % 4, step % 2, 0, 0)),
            pl.BlockSpec(image_rows.shape, lambda step: (0, 0, 0)),
            pl.BlockSpec(noise.shape, lambda step: (0, 0)),
            pl.BlockSpec((depth, part), lambda step: (0, step)),
            token_spec,
            token_spec,
        ],
        out_specs=[
            pl.BlockSpec((rows, 8 * rows), lambda step: (0, step)),
            pl.BlockSpec((rows, 4 * rows), lambda step: (0, step)),
            pl.BlockSpec((depth, part), lambda step: (0, step)),
            pl.BlockSpec(noise.shape, lambda step: (0, 0)),
            pl.BlockSpec((8, part), lambda step: (0, step)),
            token_spec,
            token_spec,
        ],
        scratch_shapes=[
            pltpu.VMEM((images, depth), jnp.float32),
            pltpu.VMEM((depth, images), jnp.float32),
            pltpu.VMEM((images, columns), jnp.float32),
            pltpu.VMEM((images, noise.shape[0]), jnp.float32),
        ],
        compiler_params=pltpu.CompilerParams(vmem_limit_bytes=VMEM_BYTES),
        name="tail_part",
    )(shares, shares, image_rows, noise, weight, token_out, token_grad)


def plane_body(
    block_input,
    cotangent,
    bin_ids,
    image_counts,
    attn_weight,
    mlp_weight,
    noise_table,
    mod_weight,
    mod_bias,
):
    model_width = block_input.shape[2]
    rows = attn_weight.shape[0]
    bias_piece = mod_bias.shape[0]
    mine = lax.axis_index("fsdp")
    (
        qkv_weight,
        out_weight,
        up_weight,
        down_low,
        h_one_all,
        h_two_all,
        grad_mlp_all,
        qkv_all,
        attended_all,
        hidden_all,
        slope_all,
        first_grads,
        features,
        first_sum,
        attn_out,
        grad_out,
        mod_rows,
    ) = front_part(
        bin_ids,
        image_counts,
        noise_table,
        mod_bias.reshape(1, bias_piece),
        block_input,
        cotangent,
        attn_weight,
        mlp_weight,
        mod_weight,
    )

    def flat(array):
        return array.reshape(-1, array.shape[-1])

    shares, token_out, token_grad, mod_out, _, _, _, _ = back_part(
        down_low,
        up_weight,
        hidden_all.reshape(8, rows, -1),
        slope_all,
        grad_mlp_all,
        h_two_all,
        first_grads,
        h_one_all,
        qkv_all,
        attended_all,
        flat(qkv_weight),
        out_weight,
        features,
        first_sum,
        attn_out,
        grad_out,
        mod_rows,
    )
    (
        mlp_weight_grad,
        attn_weight_grad,
        mod_weight_grad,
        noise_grad,
        bias_sums,
        block_out,
        input_grad,
    ) = tail_part(
        shares,
        mod_out.reshape(-1, 8, model_width),
        noise_table,
        mod_weight,
        token_out,
        token_grad,
    )
    mod_bias_grad = lax.dynamic_slice_in_dim(bias_sums[0], mine * bias_piece, bias_piece)
    return (
        block_out,
        input_grad,
        attn_weight_grad,
        mlp_weight_grad,
        noise_grad,
        mod_weight_grad,
        mod_bias_grad,
    )


def solution(mesh):
    fits = mesh.shape["fsdp"] == 8 and mesh.shape["blk"] == 4
    return jax.shard_map(
        plane_body if fits else body,
        mesh=mesh,
        in_specs=(
            P("fsdp", "blk", None),
            P("fsdp", "blk", None),
            P("fsdp"),
            P("fsdp"),
            P("fsdp", None),
            P("fsdp", None),
            P(None, "fsdp"),
            P("fsdp", None),
            P("fsdp"),
        ),
        out_specs=(
            P("fsdp", "blk", None),
            P("fsdp", "blk", None),
            P("fsdp", None),
            P("fsdp", None),
            P(None, "fsdp"),
            P("fsdp", None),
            P("fsdp"),
        ),
        check_vma=False,
    )
```
